32 devices in a mesh: dp: 8 (over z, y), ctx: 4 (over x, core).
Axes of the slice: x: 2, y: 2, z: 4, core: 2. Of those that a mesh axis runs over, the one named last changes fastest.
Arguments:
- frame_input: bfloat16 [16, 256, 1536], P('dp', 'ctx'), may hold values from -6 to 6
- queries: bfloat16 [16, 256, 768], P('dp', 'ctx'), may hold values from -18 to 18
- key_proj: bfloat16 [16, 256, 768], P('dp', 'ctx'), may hold values from -18 to 18
- value_proj: bfloat16 [16, 256, 768], P('dp', 'ctx'), may hold values from -6 to 6
- out_weight: bfloat16 [1536, 768], P('ctx', 'dp'), may hold values from -0.21875 to 0.21875
- conv_weight: bfloat16 [31, 1536], P(None, 'dp'), may hold values from -1 to 1
- lengths: int32 [16], P('dp'), may hold values from 64 to 256, as said below
- grad_output: bfloat16 [16, 256, 1536], P('dp', 'ctx'), may hold values from -6 to 6
Outputs:
- block_output: bfloat16 [16, 256, 1536], P('dp', 'ctx')
- grad_input: bfloat16 [16, 256, 1536], P('dp', 'ctx')
- grad_queries: bfloat16 [16, 256, 768], P('dp', 'ctx')
- grad_keys: bfloat16 [16, 256, 768], P('dp', 'ctx')
- grad_values: bfloat16 [16, 256, 768], P('dp', 'ctx')
- grad_out_weight: float32 [1536, 768], P('ctx', 'dp')
- grad_conv_weight: float32 [31, 1536], P(None, 'dp')
The draws below stay inside these ranges and needn't reach their ends.
Inputs may be any that keep to these rules, and one draw needn't show every extreme that they name: `lengths`: at least one utterance of every draw fills all 256 frame slots.
All inputs are finite; a program needn't handle non-finite values.
Results may differ from the reference program's by a relative error of at most 0.035.
Values may be sent and summed in bfloat16 or wider, within the bound.
No kernel may reach another device: no remote copies, remote signals or barrier semaphores. Data moves between devices by JAX's collectives and lax.ppermute only.
A program may use at most 128 MiB of HBM per device.

```python
import jax
import jax.numpy as jnp
from jax import lax

UTT_DEV = 2
D = 1536
HEADS = 12
HEAD_DIM = 64
KERNEL = 31
HD = 768
FRAMES = 256
UTTS = 16
N_DP = 8
N_CTX = 4


def draw_pairs(key):
    array_shape = (UTTS, FRAMES, HD)
    query_seed = jax.random.fold_in(key, 101)
    key_seed = jax.random.fold_in(key, 202)
    query_values = 1.7 * jnp.clip(jax.random.normal(query_seed, array_shape, jnp.float32), -6.0, 6.0)
    key_values = 1.7 * jnp.clip(jax.random.normal(key_seed, array_shape, jnp.float32), -6.0, 6.0)
    return (query_values, key_values)


def draw_queries(key, part):
    return draw_pairs(key)[0].astype(jnp.bfloat16)


def draw_key_proj(key, part):
    return draw_pairs(key)[1].astype(jnp.bfloat16)


def draw_lengths(key, part):
    drawn_lengths = jax.random.randint(jax.random.fold_in(key, 404), (UTTS,), FRAMES // 4, FRAMES + 1)
    full_index = jax.random.randint(jax.random.fold_in(key, 505), (), 0, UTTS)
    return jnp.where(jnp.arange(UTTS) == full_index, FRAMES, drawn_lengths).astype(jnp.int32)


def level_of(key, extent, cuts, least, high):
    level, own = 1.0, jax.random.fold_in(key, 6)
    for axis_at, parts in cuts:
        steps = jnp.exp(jax.random.uniform(jax.random.fold_in(own, axis_at), (parts,), jnp.float32, least / len(cuts), high / len(cuts)))
        level = level * jnp.repeat(steps, extent[axis_at] // parts).reshape([-1 if axis == axis_at else 1 for axis in range(len(extent))])
    return level


def noise(rng, shape, deviation, limit, pieces=(), kind=jnp.bfloat16):
    array = jax.random.normal(rng, shape, jnp.float32) * deviation
    if len(pieces) > 0:
        array = level_of(rng, shape, pieces, -0.22, 0.18) * array
    return jnp.clip(array, min=-limit, max=limit).astype(kind)


def setup_inputs(seed: int = 0) -> dict:
    key_list = jax.random.split(jax.random.key(seed), 9)
    frame_input = noise(key_list[0], (UTTS, FRAMES, D), 1.0, 6.0, ((0, 8), (1, 4)))
    queries = draw_queries(jax.random.fold_in(key_list[8], 71), 0)
    key_proj = draw_key_proj(jax.random.fold_in(key_list[8], 71), 0)
    value_proj = noise(key_list[3], (UTTS, FRAMES, HD), 1.0, 6.0, ((0, 8), (1, 4)))
    out_weight = noise(key_list[4], (D, HD), HD ** -0.5, 0.21875, ((0, 4), (1, 8)))
    conv_weight = noise(key_list[5], (KERNEL, D), KERNEL ** -0.5, 1.0, ((1, 8),))
    lengths = draw_lengths(jax.random.fold_in(key_list[8], 71), 0)
    grad_output = noise(key_list[7], (UTTS, FRAMES, D), 1.0, 6.0, ((0, 8), (1, 4)))
    return {"frame_input": frame_input, "queries": queries, "key_proj": key_proj, "value_proj": value_proj, "out_weight": out_weight, "conv_weight": conv_weight, "lengths": lengths, "grad_output": grad_output}


masked_score = -1e30


def rounded(values):
    return lax.optimization_barrier(values.astype(jnp.bfloat16)).astype(jnp.float32)


def one_utterance(items, out_weight, conv_weight):
    frame_input, queries, key_proj, value_proj, grad_output, length = items
    score_scale = HEAD_DIM ** -0.5
    half_span = (KERNEL - 1) // 2
    valid = jnp.arange(FRAMES, dtype=jnp.int32) < length
    query_heads = queries.astype(jnp.float32).reshape(FRAMES, HEADS, HEAD_DIM)
    key_heads = key_proj.astype(jnp.float32).reshape(FRAMES, HEADS, HEAD_DIM)
    value_heads = value_proj.astype(jnp.float32).reshape(FRAMES, HEADS, HEAD_DIM)
    scores = jnp.einsum("qhd,khd->hqk", query_heads, key_heads) * score_scale
    scores = jnp.where(valid[None, None, :], scores, masked_score)
    largest = jnp.max(scores, axis=-1, keepdims=True)
    log_total = largest + jnp.log(jnp.sum(jnp.exp(scores - largest), axis=-1, keepdims=True))
    weights = jnp.exp(scores - log_total)
    weights_low = rounded(weights)
    attended = jnp.einsum("hqk,khd->qhd", weights_low, value_heads).reshape(FRAMES, HD).astype(jnp.bfloat16)
    projected = jnp.dot(attended, out_weight.T, preferred_element_type=jnp.float32)
    hidden = (frame_input.astype(jnp.float32) + projected).astype(jnp.bfloat16)
    masked_hidden = jnp.where(valid[:, None], hidden, jnp.zeros_like(hidden))
    padded = jnp.pad(masked_hidden.astype(jnp.float32), ((half_span, half_span), (0, 0)))
    taps = conv_weight.astype(jnp.float32)
    conv_sum = taps[0] * padded[0:FRAMES]
    for tap_index in range(1, KERNEL):
        conv_sum = conv_sum + taps[tap_index] * padded[tap_index:tap_index + FRAMES]
    sigmoid = jax.nn.sigmoid(conv_sum)
    block_output = (hidden.astype(jnp.float32) + conv_sum * sigmoid).astype(jnp.bfloat16)
    swish_slope = sigmoid * (1.0 + conv_sum * (1.0 - sigmoid))
    grad_conv = (grad_output.astype(jnp.float32) * swish_slope).astype(jnp.bfloat16)
    grad_padded = jnp.pad(grad_conv.astype(jnp.float32), ((half_span, half_span), (0, 0)))
    back_sum = taps[0] * grad_padded[2 * half_span:2 * half_span + FRAMES]
    for tap_index in range(1, KERNEL):
        first_row = 2 * half_span - tap_index
        back_sum = back_sum + taps[tap_index] * grad_padded[first_row:first_row + FRAMES]
    grad_hidden = (grad_output.astype(jnp.float32) + jnp.where(valid[:, None], back_sum, 0.0)).astype(jnp.bfloat16)
    kernel_term = jnp.stack([jnp.sum(grad_conv.astype(jnp.float32) * padded[tap_index:tap_index + FRAMES], axis=0) for tap_index in range(KERNEL)])
    grad_attended = jnp.dot(grad_hidden, out_weight, preferred_element_type=jnp.float32).astype(jnp.bfloat16)
    grad_heads = grad_attended.astype(jnp.float32).reshape(FRAMES, HEADS, HEAD_DIM)
    row_delta = jnp.sum(grad_heads * attended.astype(jnp.float32).reshape(FRAMES, HEADS, HEAD_DIM), axis=-1)
    grad_weights = jnp.einsum("qhd,khd->hqk", grad_heads, value_heads)
    grad_scores = rounded(weights * (grad_weights - row_delta.T[:, :, None]))
    grad_queries = (jnp.einsum("hqk,khd->qhd", grad_scores, key_heads) * score_scale).reshape(FRAMES, HD).astype(jnp.bfloat16)
    grad_keys = (jnp.einsum("hqk,qhd->khd", grad_scores, query_heads) * score_scale).reshape(FRAMES, HD).astype(jnp.bfloat16)
    grad_values = jnp.einsum("hqk,qhd->khd", weights_low, grad_heads).reshape(FRAMES, HD).astype(jnp.bfloat16)
    return block_output, grad_hidden, grad_queries, grad_keys, grad_values, attended, kernel_term


def one_group(items, out_weight, conv_weight):
    shard_rows = FRAMES // N_CTX
    panel_sum = jnp.zeros((N_CTX, D, HD), jnp.float32)
    kernel_sum = jnp.zeros((KERNEL, D), jnp.float32)
    collected = []
    for utt_index in range(UTT_DEV):
        results = one_utterance(tuple(item[utt_index] for item in items), out_weight, conv_weight)
        hidden_blocks = results[1].astype(jnp.float32).reshape(N_CTX, shard_rows, D)
        attended_blocks = results[5].astype(jnp.float32).reshape(N_CTX, shard_rows, HD)
        panel_sum = panel_sum + jnp.einsum("cfd,cfe->cde", hidden_blocks, attended_blocks)
        kernel_sum = kernel_sum + results[6]
        collected.append(results[:5])
    stacked = tuple(jnp.stack([entry[slot] for entry in collected]) for slot in range(5))
    panel_terms = rounded(panel_sum)
    return stacked + (jnp.sum(panel_terms, axis=0), kernel_sum)


def reference(frame_input, queries, key_proj, value_proj, out_weight, conv_weight, lengths, grad_output):
    def grouped(values):
        return values.reshape((N_DP, UTT_DEV) + values.shape[1:])

    items = tuple(grouped(values) for values in (frame_input, queries, key_proj, value_proj, grad_output, lengths))
    results = lax.map(lambda group_items: one_group(group_items, out_weight, conv_weight), items)

    def flat(values):
        return values.reshape((UTTS,) + values.shape[2:])

    return (flat(results[0]), flat(results[1]), flat(results[2]), flat(results[3]), flat(results[4]),
            jnp.sum(results[5], axis=0), jnp.sum(results[6], axis=0))
```

```python
import functools

import jax
import jax.numpy as jnp
from jax import lax
from jax.experimental import pallas as pl
from jax.experimental.pallas import tpu as pltpu
from jax.sharding import PartitionSpec as P

HEAD_DIM = 64


masked_score = -1e30


def padded_2(array, sides, width):
    for axis, dim in sides:
        size, length = (lax.axis_size(axis), array.shape[dim])
        up = [(i, (i + 1) % size) for i in range(size - 1)]
        down = [(j, i) for i, j in up]
        last = lax.slice_in_dim(array, length - width, length, axis=dim)
        leading = lax.slice_in_dim(array, 0, width, axis=dim)
        before = lax.ppermute(last, axis, up)
        after = lax.ppermute(leading, axis, down)
        array = jnp.concatenate([before, array, after], axis=dim)
    return array


def depthwise(lhs, rhs):
    return lax.conv_general_dilated(
        lhs,
        rhs,
        (1,),
        "VALID",
        dimension_numbers=("NWC", "WIO", "NWC"),
        feature_group_count=lhs.shape[2],
        precision=lax.Precision.HIGHEST,
    )


def general_device(
    frame_input, queries, key_proj, value_proj, out_weight, conv_weight, lengths, grad_output
):
    utt_count = frame_input.shape[0]
    frame_count = frame_input.shape[1]
    inner_width = queries.shape[2]
    head_count = inner_width // HEAD_DIM
    group_heads = max((g for g in range(1, 7) if head_count % g == 0))
    group_count = head_count // group_heads
    group_width = group_heads * HEAD_DIM
    tap_count = conv_weight.shape[0]
    half_span = (tap_count - 1) // 2
    score_scale = HEAD_DIM ** (-0.5)
    total_frames = frame_count * lax.axis_size("ctx")
    offset = lax.axis_index("ctx") * frame_count
    own_valid = (offset + jnp.arange(frame_count, dtype=jnp.int32))[None, :] < lengths[:, None]
    all_valid = jnp.arange(total_frames, dtype=jnp.int32)[None, :] < lengths[:, None]

    def grouped(values):
        row_count = values.shape[1]
        return values.reshape(utt_count, row_count, group_count, group_width).transpose(2, 0, 1, 3)

    def ungrouped(values):
        row_count = values.shape[2]
        return values.transpose(1, 2, 0, 3).reshape(utt_count, row_count, group_count * group_width)

    def split_heads(values):
        return values.reshape(utt_count, values.shape[1], group_heads, HEAD_DIM)

    def stats_grouped(values):
        row_count = values.shape[1]
        return values.reshape(utt_count, row_count, group_count, group_heads).transpose(2, 0, 3, 1)

    def masked_scores(query_block, key_block, key_mask):
        scores = (
            jnp.einsum(
                "uqgd,ukgd->ugqk", query_block, key_block, preferred_element_type=jnp.float32
            )
            * score_scale
        )
        return jnp.where(key_mask[:, None, None, :], scores, masked_score)

    taps = lax.all_gather(conv_weight, "dp", axis=1, tiled=True).astype(jnp.float32)
    panel_rows = lax.all_gather(out_weight, "dp", axis=1, tiled=True)
    weight_full = lax.all_gather(panel_rows, "ctx", axis=0, tiled=True)
    all_keys, all_values = (
        lax.all_gather(key_proj, "ctx", axis=1, tiled=True),
        lax.all_gather(value_proj, "ctx", axis=1, tiled=True),
    )
    query_groups = grouped(queries)
    key_groups = grouped(all_keys)
    value_groups = grouped(all_values)

    def forward_group(unused, items):
        query_group, key_group, value_group = items
        query_block = split_heads(query_group)
        scores = masked_scores(query_block, split_heads(key_group), all_valid)
        largest = jnp.max(scores, axis=-1)
        log_group = largest + jnp.log(jnp.sum(jnp.exp(scores - largest[..., None]), axis=-1))
        weights_low = jnp.exp(scores - log_group[..., None]).astype(jnp.bfloat16)
        attended_group = jnp.einsum(
            "ugqk,ukgd->uqgd",
            weights_low,
            split_heads(value_group),
            preferred_element_type=jnp.float32,
        )
        return (None, (log_group, attended_group.reshape(utt_count, frame_count, group_width)))

    _, (log_groups, attended_groups) = lax.scan(
        forward_group, None, (query_groups, key_groups, value_groups)
    )
    attended = ungrouped(attended_groups).astype(jnp.bfloat16)
    log_total = log_groups.transpose(1, 3, 0, 2).reshape(utt_count, frame_count, head_count)
    projected = jnp.einsum("ufe,de->ufd", attended, weight_full, preferred_element_type=jnp.float32)
    hidden = (frame_input.astype(jnp.float32) + projected).astype(jnp.bfloat16)
    masked_hidden = jnp.where(own_valid[:, :, None], hidden, jnp.zeros_like(hidden))
    padded = padded_2(masked_hidden, (("ctx", 1),), half_span).astype(jnp.float32)
    conv_sum = depthwise(padded, taps[:, None, :])
    sigmoid = jax.nn.sigmoid(conv_sum)
    block_output = (hidden.astype(jnp.float32) + conv_sum * sigmoid).astype(jnp.bfloat16)
    grad_local = grad_output.astype(jnp.float32)
    swish_slope = sigmoid * (1.0 + conv_sum * (1.0 - sigmoid))
    grad_conv = (grad_local * swish_slope).astype(jnp.bfloat16)
    grad_padded = padded_2(grad_conv, (("ctx", 1),), half_span).astype(jnp.float32)
    back_sum = depthwise(grad_padded, taps[::-1][:, None, :])
    grad_hidden = (grad_local + jnp.where(own_valid[:, :, None], back_sum, 0.0)).astype(
        jnp.bfloat16
    )
    grad_conv_wide = grad_conv.astype(jnp.float32)
    kernel_term = jnp.zeros((tap_count, conv_sum.shape[2]), jnp.float32)
    for utt_index in range(utt_count):
        kernel_term = (
            kernel_term
            + depthwise(padded[utt_index : utt_index + 1], grad_conv_wide[utt_index][:, None, :])[0]
        )
    kernel_whole = lax.psum(kernel_term.astype(jnp.bfloat16), "ctx")
    grad_conv_weight = lax.psum_scatter(kernel_whole, "dp", scatter_dimension=1, tiled=True).astype(
        jnp.float32
    )
    grad_attended = jnp.einsum(
        "ufd,de->ufe", grad_hidden, weight_full, preferred_element_type=jnp.float32
    ).astype(jnp.bfloat16)
    row_delta = jnp.sum(
        grad_attended.astype(jnp.float32).reshape(utt_count, frame_count, head_count, HEAD_DIM)
        * attended.astype(jnp.float32).reshape(utt_count, frame_count, head_count, HEAD_DIM),
        axis=-1,
    )
    grad_groups = grouped(grad_attended)

    def query_group_step(unused, items):
        query_group, key_group, value_group, grad_group, log_group, delta_group = items
        key_block = split_heads(key_group)
        weights = jnp.exp(
            masked_scores(split_heads(query_group), key_block, all_valid) - log_group[..., None]
        )
        grad_weights = jnp.einsum(
            "uqgd,ukgd->ugqk",
            split_heads(grad_group),
            split_heads(value_group),
            preferred_element_type=jnp.float32,
        )
        grad_scores = (weights * (grad_weights - delta_group[..., None])).astype(jnp.bfloat16)
        query_sum = jnp.einsum(
            "ugqk,ukgd->uqgd", grad_scores, key_block, preferred_element_type=jnp.float32
        )
        return (None, query_sum.reshape(utt_count, frame_count, group_width))

    _, query_sums = lax.scan(
        query_group_step,
        None,
        (
            query_groups,
            key_groups,
            value_groups,
            grad_groups,
            stats_grouped(log_total),
            stats_grouped(row_delta),
        ),
    )
    grad_queries = (ungrouped(query_sums) * score_scale).astype(jnp.bfloat16)
    total_log, total_delta = (
        lax.all_gather(log_total, "ctx", axis=1, tiled=True),
        lax.all_gather(row_delta, "ctx", axis=1, tiled=True),
    )
    own_key_groups = grouped(key_proj)
    own_value_groups = grouped(value_proj)
    group_zeros = jnp.zeros((group_count, utt_count, frame_count, group_width), jnp.float32)
    start_sums = (group_zeros, group_zeros)
    query_all, grad_all = (
        lax.all_gather(queries, "ctx", axis=1, tiled=True),
        lax.all_gather(grad_attended, "ctx", axis=1, tiled=True),
    )
    log_piece = stats_grouped(total_log)
    delta_piece = stats_grouped(total_delta)

    def key_group_step(unused, items):
        (
            query_group,
            grad_group,
            log_group,
            delta_group,
            key_group,
            value_group,
            key_sum,
            value_sum,
        ) = items
        query_block = split_heads(query_group)
        grad_block = split_heads(grad_group)
        weights = jnp.exp(
            masked_scores(query_block, split_heads(key_group), own_valid) - log_group[..., None]
        )
        grad_weights = jnp.einsum(
            "uqgd,ukgd->ugqk",
            grad_block,
            split_heads(value_group),
            preferred_element_type=jnp.float32,
        )
        grad_scores = (weights * (grad_weights - delta_group[..., None])).astype(jnp.bfloat16)
        key_next = key_sum + jnp.einsum(
            "ugqk,uqgd->ukgd", grad_scores, query_block, preferred_element_type=jnp.float32
        ).reshape(utt_count, frame_count, group_width)
        value_next = value_sum + jnp.einsum(
            "ugqk,uqgd->ukgd",
            weights.astype(jnp.bfloat16),
            grad_block,
            preferred_element_type=jnp.float32,
        ).reshape(utt_count, frame_count, group_width)
        return (None, (key_next, value_next))

    _, result_sums = lax.scan(
        key_group_step,
        None,
        (
            grouped(query_all),
            grouped(grad_all),
            log_piece,
            delta_piece,
            own_key_groups,
            own_value_groups,
            start_sums[0],
            start_sums[1],
        ),
    )
    key_sum, value_sum = result_sums
    grad_keys = (ungrouped(key_sum) * score_scale).astype(jnp.bfloat16)
    grad_values = ungrouped(value_sum).astype(jnp.bfloat16)
    hidden_cols = lax.slice_in_dim(
        grad_hidden, 0, weight_full.shape[0] // lax.axis_size("ctx") * lax.axis_size("ctx"), axis=2
    )
    panel_share = lax.psum_scatter(
        jnp.einsum("ufd,ufe->de", hidden_cols, attended, preferred_element_type=jnp.float32).astype(
            jnp.bfloat16
        ),
        "ctx",
        scatter_dimension=0,
        tiled=True,
    )
    grad_out_weight = lax.psum_scatter(panel_share, "dp", scatter_dimension=1, tiled=True).astype(
        jnp.float32
    )
    return (
        block_output,
        grad_hidden,
        grad_queries,
        grad_keys,
        grad_values,
        grad_out_weight,
        grad_conv_weight,
    )


LANES = 128
N_CTX = 4
N_DP = 8
DP_BITS = (4, 2, 1)
TAP_PAD = 32


def slot_of(index, me):
    apart = jnp.bitwise_xor(index, me)
    return ((apart & 1) << 2) | (apart & 2) | ((apart >> 2) & 1)


def dot_tt(lhs, rhs, lhs_dim, rhs_dim):
    return lax.dot_general(
        lhs, rhs, (((lhs_dim,), (rhs_dim,)), ((), ())), preferred_element_type=jnp.float32
    )


def call_kernel(body, out_shape, scratch=(), smem_first=False, count=1, cost=None):
    vmem = pl.BlockSpec(memory_space=pltpu.VMEM)
    specs = [vmem] * count
    if smem_first:
        specs[0] = pl.BlockSpec(memory_space=pltpu.SMEM)
    return pl.pallas_call(
        body,
        out_shape=out_shape,
        in_specs=specs,
        out_specs=jax.tree.map(lambda unused: vmem, out_shape),
        scratch_shapes=list(scratch),
        compiler_params=pltpu.CompilerParams(vmem_limit_bytes=48 * 1024 * 1024),
        cost_estimate=cost,
    )


def pack_heads(query_ref, key_ref, value_ref, out_ref):
    half = query_ref.shape[2] // 2
    for utt in range(2):
        for side in range(2):
            for slot, ref in enumerate((query_ref, key_ref, value_ref)):
                out_ref[2 * utt + side, :, slot * half : (slot + 1) * half] = ref[
                    utt, :, side * half : (side + 1) * half
                ]


def pack_channels(frame_ref, grad_ref, out_ref):
    width = frame_ref.shape[2] // N_CTX
    for dest in range(N_CTX):
        for slot, ref in enumerate((frame_ref, grad_ref)):
            out_ref[dest, slot] = ref[:, :, dest * width : (dest + 1) * width]


def unpack_channels(in_ref, output_ref, grad_ref):
    width = in_ref.shape[4]
    for source in range(N_CTX):
        for slot, ref in enumerate((output_ref, grad_ref)):
            ref[:, :, source * width : (source + 1) * width] = in_ref[source, slot]


def unpack_heads(in_ref, query_ref, key_ref, value_ref):
    half = in_ref.shape[2] // 3
    for utt in range(2):
        for side in range(2):
            for slot, ref in enumerate((query_ref, key_ref, value_ref)):
                ref[utt, :, side * half : (side + 1) * half] = in_ref[
                    2 * utt + side, :, slot * half : (slot + 1) * half
                ]


def head_parts(ref, slot, half):
    rows = ref.shape[0] * ref.shape[1]
    return ref[:, :, slot * half : (slot + 1) * half].reshape(rows, half)


def half_masks(rows):
    lane = lax.broadcasted_iota(jnp.int32, (rows, LANES), 1)
    low = jnp.where(lane < HEAD_DIM, 1.0, 0.0)
    return low.astype(jnp.bfloat16), (1.0 - low).astype(jnp.bfloat16)


def attend(length_ref, packed_ref, attended_ref, weight_ref):
    half = packed_ref.shape[2] // 3
    rows = packed_ref.shape[0] * packed_ref.shape[1]
    length = length_ref[lax.axis_index("ctx") // 2]
    query, key, value = (head_parts(packed_ref, slot, half) for slot in range(3))
    masks = half_masks(rows)
    real = lax.broadcasted_iota(jnp.int32, (rows, rows), 0) < length
    for pair in range(half // LANES):
        cols = slice(pair * LANES, (pair + 1) * LANES)
        key_pair, value_pair = key[:, cols], value[:, cols]
        parts = []
        for side in range(2):
            scores = dot_tt(key_pair, query[:, cols] * masks[side], 1, 1) * HEAD_DIM ** (-0.5)
            scores = jnp.where(real, scores, masked_score)
            largest = jnp.max(scores, axis=0, keepdims=True)
            powers = jnp.exp(scores - largest)
            total = jnp.sum(powers, axis=0, keepdims=True)
            low = (powers * (1.0 / total)).astype(jnp.bfloat16)
            weight_ref[2 * pair + side] = low
            mixed = dot_tt(value_pair, low, 0, 0)
            parts.append(mixed[side * HEAD_DIM : (side + 1) * HEAD_DIM])
        joined = jnp.concatenate(parts, axis=0).T.astype(jnp.bfloat16)
        for dest in range(N_CTX):
            attended_ref[dest, :, cols] = joined


def middle(
    length_ref,
    attended_ref,
    weight_ref,
    side_ref,
    result_ref,
    back_ref,
    panel_ref,
    taps_ref,
    tap_sum_ref,
    rows_ref,
    hidden_ref,
    masked_ref,
    cotangent_ref,
    grad_ref,
):
    rows, half = attended_ref.shape[1], attended_ref.shape[2]
    frames, width = side_ref.shape[3], side_ref.shape[4]
    chunks = width // LANES
    entries = 2 * half // N_DP
    tap_count, reach = 31, 15
    own = width // 2
    group, place = lax.axis_index("dp"), lax.axis_index("ctx")
    for part in range(N_DP):
        rows_ref[part * entries : (part + 1) * entries] = weight_ref[
            slot_of(part, group), 0:entries
        ]
    pieces = []
    for part in range(2):
        block = weight_ref[slot_of(2 * place + part, group), entries:].astype(jnp.float32)
        pieces.append(jnp.concatenate([block[:, :own], block[:, own:]], axis=0))
    taps = jnp.concatenate(pieces, axis=1)
    for chunk in range(chunks):
        for tap in range(tap_count):
            taps_ref[chunk, tap] = jnp.broadcast_to(
                taps[tap : tap + 1, chunk * LANES : (chunk + 1) * LANES], (8, LANES)
            )
    tap_sum_ref[...] = jnp.zeros_like(tap_sum_ref)
    edge = jnp.zeros((2 * chunks, 16, LANES), jnp.float32)
    for ref in (masked_ref, cotangent_ref):
        ref[:, 0:16, :] = edge
        ref[:, 16 + rows : 32 + rows, :] = edge
    for utt in range(2):
        real = lax.broadcasted_iota(jnp.int32, (rows, LANES), 0) < length_ref[utt]
        projected = dot_tt(attended_ref[2 * utt], rows_ref[0:half], 1, 0)
        projected += dot_tt(attended_ref[2 * utt + 1], rows_ref[half:], 1, 0)
        hidden = side_ref[:, 0, utt].reshape(rows, width).astype(jnp.float32) + projected
        hidden = hidden.astype(jnp.bfloat16).astype(jnp.float32)
        for chunk in range(chunks):
            piece = hidden[:, chunk * LANES : (chunk + 1) * LANES]
            hidden_ref[utt * chunks + chunk] = piece
            masked_ref[utt * chunks + chunk, 16 : 16 + rows, :] = jnp.where(real, piece, 0.0)

    def convolve(step, carry):
        utt, chunk = step // chunks, step % chunks
        cols = pl.ds(pl.multiple_of(chunk * LANES, LANES), LANES)
        length = length_ref[utt]
        shape = (frames // 8, 8, LANES)
        for block in range(N_CTX):
            base = block * frames
            total = jnp.zeros(shape, jnp.float32)
            for tap in range(tap_count):
                piece = masked_ref[step, base + tap + 16 - reach : base + tap + 16 - reach + frames, :]
                total += taps_ref[chunk, tap][None] * piece.reshape(shape)
            total = total.reshape(frames, LANES)
            gate = jax.nn.sigmoid(total)
            outer = hidden_ref[step, base : base + frames, :] + total * gate
            result_ref[block, 0, utt, :, cols] = outer.astype(jnp.bfloat16)
            incoming = side_ref[block, 1, utt, :, cols].astype(jnp.float32)
            slope = gate * (1.0 + total * (1.0 - gate))
            low = (incoming * slope).astype(jnp.bfloat16)
            cotangent_ref[step, 16 + base : 16 + base + frames, :] = low.astype(jnp.float32)
        for block in range(N_CTX):
            base = block * frames
            total = jnp.zeros(shape, jnp.float32)
            held = masked_ref[step, 16 + base : 16 + base + frames, :].reshape(shape)
            for tap in range(tap_count):
                first = base + 16 + reach - tap
                piece = cotangent_ref[step, first : first + frames, :].reshape(shape)
                total += taps_ref[chunk, tap][None] * piece
                tap_sum_ref[chunk, tap] += jnp.sum(held * piece, axis=0)
            place_of = base + lax.broadcasted_iota(jnp.int32, (frames, LANES), 0)
            total = jnp.where(place_of < length, total.reshape(frames, LANES), 0.0)
            incoming = side_ref[block, 1, utt, :, cols].astype(jnp.float32)
            low = (incoming + total).astype(jnp.bfloat16)
            result_ref[block, 1, utt, :, cols] = low
            grad_ref[utt, base : base + frames, cols] = low
        return carry

    lax.fori_loop(0, 2 * chunks, convolve, 0)
    sums = [
        jnp.concatenate([jnp.sum(tap_sum_ref[chunk, tap], axis=0, keepdims=True) for tap in range(TAP_PAD)], axis=0)
        for chunk in range(chunks)
    ]
    sums = jnp.concatenate(sums, axis=1).astype(jnp.bfloat16)
    for utt in range(2):
        for side in range(2):
            back_ref[2 * utt + side, 0:rows, :] = dot_tt(
                grad_ref[utt], rows_ref[side * half : (side + 1) * half], 1, 1
            ).astype(jnp.bfloat16)
            back_ref[2 * utt + side, rows:, :] = sums
    for side in range(2):
        panel = dot_tt(attended_ref[side], grad_ref[0], 0, 0)
        panel += dot_tt(attended_ref[2 + side], grad_ref[1], 0, 0)
        panel = panel.astype(jnp.bfloat16)
        for part in range(N_DP // 2):
            panel_ref[slot_of(side * N_DP // 2 + part, group)] = panel[
                part * entries : (part + 1) * entries
            ]


def attend_back(packed_ref, weight_ref, back_ref, out_ref, taps_ref):
    half = packed_ref.shape[2] // 3
    sources, frames = packed_ref.shape[0], packed_ref.shape[1]
    rows = sources * frames
    own = half // 2
    group = lax.axis_index("dp")
    query, key, value = (head_parts(packed_ref, slot, half) for slot in range(3))
    masks = half_masks(rows)
    scale = HEAD_DIM ** (-0.5)
    arriving = back_ref[0, 0:rows, :].astype(jnp.float32)
    for source in range(1, sources):
        arriving += back_ref[source, 0:rows, :].astype(jnp.float32)
    arriving = arriving.astype(jnp.bfloat16)
    low_lanes = lax.broadcasted_iota(jnp.int32, (rows, LANES), 1) < HEAD_DIM
    for pair in range(half // LANES):
        cols = slice(pair * LANES, (pair + 1) * LANES)
        key_pair, value_pair = key[:, cols], value[:, cols]
        query_pair, grad_pair = query[:, cols], arriving[:, cols]
        query_parts, key_parts, value_parts = [], [], []
        for side in range(2):
            low = weight_ref[2 * pair + side]
            weights = low.astype(jnp.float32)
            moved = weights * dot_tt(value_pair, grad_pair * masks[side], 1, 1)
            delta = jnp.sum(moved, axis=0, keepdims=True)
            grad_scores = (moved - weights * delta).astype(jnp.bfloat16)
            value_parts.append(dot_tt(low, grad_pair, 1, 0))
            key_parts.append(dot_tt(grad_scores, query_pair, 1, 0))
            mixed = dot_tt(key_pair, grad_scores, 0, 0)
            query_parts.append(mixed[side * HEAD_DIM : (side + 1) * HEAD_DIM])
        query_sum = (jnp.concatenate(query_parts, axis=0).T * scale).astype(jnp.bfloat16)
        key_sum = (jnp.where(low_lanes, key_parts[0], key_parts[1]) * scale).astype(jnp.bfloat16)
        value_sum = jnp.where(low_lanes, value_parts[0], value_parts[1]).astype(jnp.bfloat16)
        for slot, total in enumerate((query_sum, key_sum, value_sum)):
            first = slot * half + pair * LANES
            out_ref[:, :, first : first + LANES] = total.reshape(sources, frames, LANES)
    for source in range(sources):
        block = back_ref[source, rows:, :].astype(jnp.float32)
        for part in range(2):
            piece = block[:, part * own : (part + 1) * own]
            piece = jnp.concatenate([piece[: TAP_PAD // 2], piece[TAP_PAD // 2 :]], axis=1)
            taps_ref[slot_of(2 * source + part, group)] = piece.astype(jnp.bfloat16)


def swapped(array, bit):
    return lax.ppermute(array, "dp", [(i, i ^ bit) for i in range(N_DP)])


def traded(array):
    return lax.all_to_all(array, "ctx", 0, 0, tiled=True)


def per_device(
    frame_input, queries, key_proj, value_proj, out_weight, conv_weight, lengths, grad_output
):
    utts, frames, wide = frame_input.shape
    inner = queries.shape[2]
    half, width = inner // 2, wide // N_CTX
    rows = N_CTX * frames
    low, f32 = jnp.bfloat16, jnp.float32
    shape = jax.ShapeDtypeStruct
    entries = out_weight.shape[1]
    tap_count = conv_weight.shape[0]

    tap_rows = jnp.pad(conv_weight, ((0, TAP_PAD - tap_count), (0, 0)))
    tap_rows = jnp.concatenate([tap_rows[: TAP_PAD // 2], tap_rows[TAP_PAD // 2 :]], axis=1)
    shard = jnp.concatenate([out_weight.T, tap_rows], axis=0)[None]
    for bit in DP_BITS:
        shard = jnp.concatenate([shard, swapped(shard, bit)], axis=0)

    packed = traded(
        call_kernel(pack_heads, shape((N_CTX, frames, 3 * half), low), count=3)(
            queries, key_proj, value_proj
        )
    )
    sides = traded(
        call_kernel(pack_channels, shape((N_CTX, 2, utts, frames, width), low), count=2)(
            frame_input, grad_output
        )
    )
    attended, weights = call_kernel(
        attend,
        (shape((N_CTX, rows, half), low), shape((half // HEAD_DIM, rows, rows), low)),
        smem_first=True,
        count=2,
    )(lengths, packed)
    attended_all = traded(attended)
    chunks = width // LANES
    results, back, panels = call_kernel(
        middle,
        (
            shape((N_CTX, 2, utts, frames, width), low),
            shape((N_CTX, rows + TAP_PAD, half), low),
            shape((N_DP, entries, width), low),
        ),
        scratch=(
            pltpu.VMEM((chunks, TAP_PAD, 8, LANES), f32),
            pltpu.VMEM((chunks, TAP_PAD, 8, LANES), f32),
            pltpu.VMEM((inner, width), low),
            pltpu.VMEM((utts * chunks, rows, LANES), f32),
            pltpu.VMEM((utts * chunks, rows + 32, LANES), f32),
            pltpu.VMEM((utts * chunks, rows + 32, LANES), f32),
            pltpu.VMEM((utts, rows, width), low),
        ),
        smem_first=True,
        count=4,
    )(lengths, attended_all, shard, sides)

    def added(kept, came):
        return (kept.astype(f32) + came.astype(f32)).astype(low)

    panels = added(panels[:4], swapped(panels[4:], 1))
    back = traded(back)
    grads, tap_slots = call_kernel(
        attend_back,
        (shape((N_CTX, frames, 3 * half), low), shape((N_DP, TAP_PAD // 2, width), low)),
        count=3,
    )(packed, weights, back)
    tap_slots = added(tap_slots[:4], swapped(tap_slots[4:], 1))
    summed = jnp.concatenate([panels, tap_slots], axis=1)
    summed = added(summed[:2], swapped(summed[2:], 2))
    last = summed[0].astype(f32) + swapped(summed[1], 4).astype(f32)
    grad_queries, grad_keys, grad_values = call_kernel(
        unpack_heads, (shape((utts, frames, inner), low),) * 3, count=1
    )(traded(grads))
    block_output, grad_input = call_kernel(
        unpack_channels, (shape((utts, frames, wide), low),) * 2, count=1
    )(traded(results))
    grad_out_weight = last[:entries].T
    own = width // 2
    grad_taps = jnp.concatenate([last[entries:, :own], last[entries:, own:]], axis=0)[:tap_count]
    return (
        block_output,
        grad_input,
        grad_queries,
        grad_keys,
        grad_values,
        grad_out_weight,
        grad_taps,
    )


def chosen(sizes, *arrays):
    frame_input, queries, out_weight, conv_weight = (arrays[i] for i in (0, 1, 4, 5))
    utts, frames, wide = frame_input.shape
    inner = queries.shape[2]
    fits = (
        sizes == (N_DP, N_CTX)
        and utts == 2
        and frames == 64
        and wide % (N_CTX * LANES) == 0
        and inner % (2 * LANES) == 0
        and inner // N_DP % 16 == 0
        and inner // 2 == wide // N_CTX
        and conv_weight.shape == (31, wide // N_DP)
        and out_weight.shape == (wide // N_CTX, inner // N_DP)
    )
    return (per_device if fits else general_device)(*arrays)


def solution(mesh):
    placed = (
        P("dp", "ctx", None),
        P("dp", "ctx", None),
        P("dp", "ctx", None),
        P("dp", "ctx", None),
        P("ctx", "dp"),
        P(None, "dp"),
        P("dp"),
        P("dp", "ctx", None),
    )
    sizes = (mesh.shape["dp"], mesh.shape["ctx"])
    return jax.shard_map(
        functools.partial(chosen, sizes),
        mesh=mesh,
        in_specs=placed,
        out_specs=(
            P("dp", "ctx", None),
            P("dp", "ctx", None),
            P("dp", "ctx", None),
            P("dp", "ctx", None),
            P("dp", "ctx", None),
            P("ctx", "dp"),
            P(None, "dp"),
        ),
        check_vma=False,
    )
```

```python
import functools

import jax
import jax.numpy as jnp
from jax import lax
from jax.experimental import pallas as pl
from jax.experimental.pallas import tpu as pltpu
from jax.sharding import PartitionSpec as P

HEAD_DIM = 64


masked_score = -1e30


def padded_2(array, sides, width):
    for axis, dim in sides:
        size, length = (lax.axis_size(axis), array.shape[dim])
        up = [(i, (i + 1) % size) for i in range(size - 1)]
        down = [(j, i) for i, j in up]
        last = lax.slice_in_dim(array, length - width, length, axis=dim)
        leading = lax.slice_in_dim(array, 0, width, axis=dim)
        before = lax.ppermute(last, axis, up)
        after = lax.ppermute(leading, axis, down)
        array = jnp.concatenate([before, array, after], axis=dim)
    return array


def depthwise(lhs, rhs):
    return lax.conv_general_dilated(
        lhs,
        rhs,
        (1,),
        "VALID",
        dimension_numbers=("NWC", "WIO", "NWC"),
        feature_group_count=lhs.shape[2],
        precision=lax.Precision.HIGHEST,
    )


def general_device(
    frame_input, queries, key_proj, value_proj, out_weight, conv_weight, lengths, grad_output
):
    utt_count = frame_input.shape[0]
    frame_count = frame_input.shape[1]
    inner_width = queries.shape[2]
    head_count = inner_width // HEAD_DIM
    group_heads = max((g for g in range(1, 7) if head_count % g == 0))
    group_count = head_count // group_heads
    group_width = group_heads * HEAD_DIM
    tap_count = conv_weight.shape[0]
    half_span = (tap_count - 1) // 2
    score_scale = HEAD_DIM ** (-0.5)
    total_frames = frame_count * lax.axis_size("ctx")
    offset = lax.axis_index("ctx") * frame_count
    own_valid = (offset + jnp.arange(frame_count, dtype=jnp.int32))[None, :] < lengths[:, None]
    all_valid = jnp.arange(total_frames, dtype=jnp.int32)[None, :] < lengths[:, None]

    def grouped(values):
        row_count = values.shape[1]
        return values.reshape(utt_count, row_count, group_count, group_width).transpose(2, 0, 1, 3)

    def ungrouped(values):
        row_count = values.shape[2]
        return values.transpose(1, 2, 0, 3).reshape(utt_count, row_count, group_count * group_width)

    def split_heads(values):
        return values.reshape(utt_count, values.shape[1], group_heads, HEAD_DIM)

    def stats_grouped(values):
        row_count = values.shape[1]
        return values.reshape(utt_count, row_count, group_count, group_heads).transpose(2, 0, 3, 1)

    def masked_scores(query_block, key_block, key_mask):
        scores = (
            jnp.einsum(
                "uqgd,ukgd->ugqk", query_block, key_block, preferred_element_type=jnp.float32
            )
            * score_scale
        )
        return jnp.where(key_mask[:, None, None, :], scores, masked_score)

    taps = lax.all_gather(conv_weight, "dp", axis=1, tiled=True).astype(jnp.float32)
    panel_rows = lax.all_gather(out_weight, "dp", axis=1, tiled=True)
    weight_full = lax.all_gather(panel_rows, "ctx", axis=0, tiled=True)
    all_keys, all_values = (
        lax.all_gather(key_proj, "ctx", axis=1, tiled=True),
        lax.all_gather(value_proj, "ctx", axis=1, tiled=True),
    )
    query_groups = grouped(queries)
    key_groups = grouped(all_keys)
    value_groups = grouped(all_values)

    def forward_group(unused, items):
        query_group, key_group, value_group = items
        query_block = split_heads(query_group)
        scores = masked_scores(query_block, split_heads(key_group), all_valid)
        largest = jnp.max(scores, axis=-1)
        log_group = largest + jnp.log(jnp.sum(jnp.exp(scores - largest[..., None]), axis=-1))
        weights_low = jnp.exp(scores - log_group[..., None]).astype(jnp.bfloat16)
        attended_group = jnp.einsum(
            "ugqk,ukgd->uqgd",
            weights_low,
            split_heads(value_group),
            preferred_element_type=jnp.float32,
        )
        return (None, (log_group, attended_group.reshape(utt_count, frame_count, group_width)))

    _, (log_groups, attended_groups) = lax.scan(
        forward_group, None, (query_groups, key_groups, value_groups)
    )
    attended = ungrouped(attended_groups).astype(jnp.bfloat16)
    log_total = log_groups.transpose(1, 3, 0, 2).reshape(utt_count, frame_count, head_count)
    projected = jnp.einsum("ufe,de->ufd", attended, weight_full, preferred_element_type=jnp.float32)
    hidden = (frame_input.astype(jnp.float32) + projected).astype(jnp.bfloat16)
    masked_hidden = jnp.where(own_valid[:, :, None], hidden, jnp.zeros_like(hidden))
    padded = padded_2(masked_hidden, (("ctx", 1),), half_span).astype(jnp.float32)
    conv_sum = depthwise(padded, taps[:, None, :])
    sigmoid = jax.nn.sigmoid(conv_sum)
    block_output = (hidden.astype(jnp.float32) + conv_sum * sigmoid).astype(jnp.bfloat16)
    grad_local = grad_output.astype(jnp.float32)
    swish_slope = sigmoid * (1.0 + conv_sum * (1.0 - sigmoid))
    grad_conv = (grad_local * swish_slope).astype(jnp.bfloat16)
    grad_padded = padded_2(grad_conv, (("ctx", 1),), half_span).astype(jnp.float32)
    back_sum = depthwise(grad_padded, taps[::-1][:, None, :])
    grad_hidden = (grad_local + jnp.where(own_valid[:, :, None], back_sum, 0.0)).astype(
        jnp.bfloat16
    )
    grad_conv_wide = grad_conv.astype(jnp.float32)
    kernel_term = jnp.zeros((tap_count, conv_sum.shape[2]), jnp.float32)
    for utt_index in range(utt_count):
        kernel_term = (
            kernel_term
            + depthwise(padded[utt_index : utt_index + 1], grad_conv_wide[utt_index][:, None, :])[0]
        )
    kernel_whole = lax.psum(kernel_term.astype(jnp.bfloat16), "ctx")
    grad_conv_weight = lax.psum_scatter(kernel_whole, "dp", scatter_dimension=1, tiled=True).astype(
        jnp.float32
    )
    grad_attended = jnp.einsum(
        "ufd,de->ufe", grad_hidden, weight_full, preferred_element_type=jnp.float32
    ).astype(jnp.bfloat16)
    row_delta = jnp.sum(
        grad_attended.astype(jnp.float32).reshape(utt_count, frame_count, head_count, HEAD_DIM)
        * attended.astype(jnp.float32).reshape(utt_count, frame_count, head_count, HEAD_DIM),
        axis=-1,
    )
    grad_groups = grouped(grad_attended)

    def query_group_step(unused, items):
        query_group, key_group, value_group, grad_group, log_group, delta_group = items
        key_block = split_heads(key_group)
        weights = jnp.exp(
            masked_scores(split_heads(query_group), key_block, all_valid) - log_group[..., None]
        )
        grad_weights = jnp.einsum(
            "uqgd,ukgd->ugqk",
            split_heads(grad_group),
            split_heads(value_group),
            preferred_element_type=jnp.float32,
        )
        grad_scores = (weights * (grad_weights - delta_group[..., None])).astype(jnp.bfloat16)
        query_sum = jnp.einsum(
            "ugqk,ukgd->uqgd", grad_scores, key_block, preferred_element_type=jnp.float32
        )
        return (None, query_sum.reshape(utt_count, frame_count, group_width))

    _, query_sums = lax.scan(
        query_group_step,
        None,
        (
            query_groups,
            key_groups,
            value_groups,
            grad_groups,
            stats_grouped(log_total),
            stats_grouped(row_delta),
        ),
    )
    grad_queries = (ungrouped(query_sums) * score_scale).astype(jnp.bfloat16)
    total_log, total_delta = (
        lax.all_gather(log_total, "ctx", axis=1, tiled=True),
        lax.all_gather(row_delta, "ctx", axis=1, tiled=True),
    )
    own_key_groups = grouped(key_proj)
    own_value_groups = grouped(value_proj)
    group_zeros = jnp.zeros((group_count, utt_count, frame_count, group_width), jnp.float32)
    start_sums = (group_zeros, group_zeros)
    query_all, grad_all = (
        lax.all_gather(queries, "ctx", axis=1, tiled=True),
        lax.all_gather(grad_attended, "ctx", axis=1, tiled=True),
    )
    log_piece = stats_grouped(total_log)
    delta_piece = stats_grouped(total_delta)

    def key_group_step(unused, items):
        (
            query_group,
            grad_group,
            log_group,
            delta_group,
            key_group,
            value_group,
            key_sum,
            value_sum,
        ) = items
        query_block = split_heads(query_group)
        grad_block = split_heads(grad_group)
        weights = jnp.exp(
            masked_scores(query_block, split_heads(key_group), own_valid) - log_group[..., None]
        )
        grad_weights = jnp.einsum(
            "uqgd,ukgd->ugqk",
            grad_block,
            split_heads(value_group),
            preferred_element_type=jnp.float32,
        )
        grad_scores = (weights * (grad_weights - delta_group[..., None])).astype(jnp.bfloat16)
        key_next = key_sum + jnp.einsum(
            "ugqk,uqgd->ukgd", grad_scores, query_block, preferred_element_type=jnp.float32
        ).reshape(utt_count, frame_count, group_width)
        value_next = value_sum + jnp.einsum(
            "ugqk,uqgd->ukgd",
            weights.astype(jnp.bfloat16),
            grad_block,
            preferred_element_type=jnp.float32,
        ).reshape(utt_count, frame_count, group_width)
        return (None, (key_next, value_next))

    _, result_sums = lax.scan(
        key_group_step,
        None,
        (
            grouped(query_all),
            grouped(grad_all),
            log_piece,
            delta_piece,
            own_key_groups,
            own_value_groups,
            start_sums[0],
            start_sums[1],
        ),
    )
    key_sum, value_sum = result_sums
    grad_keys = (ungrouped(key_sum) * score_scale).astype(jnp.bfloat16)
    grad_values = ungrouped(value_sum).astype(jnp.bfloat16)
    hidden_cols = lax.slice_in_dim(
        grad_hidden, 0, weight_full.shape[0] // lax.axis_size("ctx") * lax.axis_size("ctx"), axis=2
    )
    panel_share = lax.psum_scatter(
        jnp.einsum("ufd,ufe->de", hidden_cols, attended, preferred_element_type=jnp.float32).astype(
            jnp.bfloat16
        ),
        "ctx",
        scatter_dimension=0,
        tiled=True,
    )
    grad_out_weight = lax.psum_scatter(panel_share, "dp", scatter_dimension=1, tiled=True).astype(
        jnp.float32
    )
    return (
        block_output,
        grad_hidden,
        grad_queries,
        grad_keys,
        grad_values,
        grad_out_weight,
        grad_conv_weight,
    )


LANES = 128
N_CTX = 4
N_DP = 8
DP_BITS = (4, 2, 1)
TAP_PAD = 32
TAPS = 31
REACH = 15


def slot_of(index, me):
    apart = jnp.bitwise_xor(index, me)
    return ((apart & 1) << 2) | (apart & 2) | ((apart >> 2) & 1)


def dot_tt(lhs, rhs, lhs_dim, rhs_dim):
    return lax.dot_general(
        lhs, rhs, (((lhs_dim,), (rhs_dim,)), ((), ())), preferred_element_type=jnp.float32
    )


def call_kernel(body, out_shape, ins, outs=None, scratch=()):
    spaces = {
        "smem": pl.BlockSpec(memory_space=pltpu.SMEM),
        "vmem": pl.BlockSpec(memory_space=pltpu.VMEM),
        "hbm": pl.BlockSpec(memory_space=pltpu.HBM),
        "any": pl.BlockSpec(memory_space=pl.ANY),
    }
    return pl.pallas_call(
        body,
        out_shape=out_shape,
        in_specs=[spaces[space] for space in ins],
        out_specs=[spaces[space] for space in (outs or ["vmem"] * len(out_shape))],
        scratch_shapes=list(scratch),
        compiler_params=pltpu.CompilerParams(vmem_limit_bytes=40 * 1024 * 1024),
    )


def half_of(index):
    return lax.shift_right_logical(index, 1)


def columns(start, size):
    return pl.ds(pl.multiple_of(start, LANES), size)


def run_copies(pairs, sem):
    copies = [
        pltpu.make_async_copy(source, target, sem.at[number])
        for number, (source, target) in enumerate(pairs)
    ]
    for copy in copies:
        copy.start()
    for copy in copies:
        copy.wait()


def pack_heads(query_ref, key_ref, value_ref, *rest):
    outs, sem = rest[:N_CTX], rest[N_CTX]
    half = query_ref.shape[2] // 2
    place = lax.axis_index("ctx")
    pairs = []
    for apart in (2, 3, 1, 0):
        dest = place ^ apart
        cols = columns((dest & 1) * half, half)
        for slot, ref in enumerate((query_ref, key_ref, value_ref)):
            pairs.append((ref.at[half_of(dest), :, cols], outs[apart].at[slot]))
    run_copies(pairs, sem)


def pack_channels(in_ref, *rest):
    outs, sem = rest[:N_CTX], rest[N_CTX]
    width = in_ref.shape[2] // N_CTX
    place = lax.axis_index("ctx")
    pairs = []
    for apart in (2, 3, 1, 0):
        cols = columns((place ^ apart) * width, width)
        for utt in range(2):
            pairs.append((in_ref.at[utt, :, cols], outs[apart].at[utt]))
    run_copies(pairs, sem)


def unpack_channels(*refs):
    ins, out_ref, sem = refs[:N_CTX], refs[N_CTX], refs[N_CTX + 1]
    width = ins[0].shape[2]
    place = lax.axis_index("ctx")
    pairs = []
    for apart in range(N_CTX):
        cols = columns((place ^ apart) * width, width)
        for utt in range(2):
            pairs.append((ins[apart].at[utt], out_ref.at[utt, :, cols]))
    run_copies(pairs, sem)


def unpack_heads(*refs):
    ins, outs, sem = refs[:N_CTX], refs[N_CTX : N_CTX + 3], refs[N_CTX + 3]
    half = ins[0].shape[2]
    place = lax.axis_index("ctx")
    pairs = []
    for apart in range(N_CTX):
        source = place ^ apart
        cols = columns((source & 1) * half, half)
        for slot in range(3):
            pairs.append((ins[apart].at[slot], outs[slot].at[half_of(source), :, cols]))
    run_copies(pairs, sem)


def head_parts(refs, slot):
    return jnp.concatenate([ref[slot] for ref in refs], axis=0)


def half_masks(rows):
    lane = lax.broadcasted_iota(jnp.int32, (rows, LANES), 1)
    low = jnp.where(lane < HEAD_DIM, 1.0, 0.0)
    return low.astype(jnp.bfloat16), (1.0 - low).astype(jnp.bfloat16)


def attend(length_ref, *refs):
    ins, attended_ref, weight_ref = refs[:N_CTX], refs[N_CTX], refs[N_CTX + 1]
    frames, half = ins[0].shape[1], ins[0].shape[2]
    rows = N_CTX * frames
    place = lax.axis_index("ctx")
    length = length_ref[half_of(place)]
    query, key, value = (head_parts(ins, slot) for slot in range(3))
    masks = half_masks(rows)
    frame = lax.broadcasted_iota(jnp.int32, (rows, rows), 0) ^ (place * frames)
    real = frame < length
    for pair in range(half // LANES):
        cols = slice(pair * LANES, (pair + 1) * LANES)
        key_pair, value_pair = key[:, cols], value[:, cols]
        parts = []
        for side in range(2):
            scores = dot_tt(key_pair, query[:, cols] * masks[side], 1, 1) * HEAD_DIM ** (-0.5)
            scores = jnp.where(real, scores, masked_score)
            largest = jnp.max(scores, axis=0, keepdims=True)
            powers = jnp.exp(scores - largest)
            total = jnp.sum(powers, axis=0, keepdims=True)
            low = (powers * (1.0 / total)).astype(jnp.bfloat16)
            weight_ref[2 * pair + side] = low
            mixed = dot_tt(value_pair, low, 0, 0)
            parts.append(mixed[side * HEAD_DIM : (side + 1) * HEAD_DIM])
        joined = jnp.concatenate(parts, axis=0).T.astype(jnp.bfloat16)
        attended_ref[:, :, cols] = joined.reshape(N_CTX, frames, LANES)


def forward(length_ref, weight_ref, *refs):
    attended_refs, frame_refs = refs[:N_CTX], refs[N_CTX : 2 * N_CTX]
    out_refs = refs[2 * N_CTX : 3 * N_CTX]
    whole_ref, rows_ref, taps_ref, total_ref, masked_ref = refs[3 * N_CTX : 3 * N_CTX + 5]
    hidden_ref, frame_ref, result_ref = refs[3 * N_CTX + 5 :]
    frames, half = attended_refs[0].shape[1], attended_refs[0].shape[2]
    width = frame_ref.shape[3]
    rows = N_CTX * frames
    chunks = width // LANES
    entries = 2 * half // N_DP
    own = width // 2
    group, place = lax.axis_index("dp"), lax.axis_index("ctx")
    for apart in range(N_CTX):
        source = place ^ apart
        cols = columns((source & 1) * half, half)
        for block in range(N_CTX):
            whole_ref[half_of(source), block ^ source, :, cols] = attended_refs[apart][block]
        frame_ref[source] = frame_refs[apart][...]
    for part in range(N_DP):
        rows_ref[part * entries : (part + 1) * entries] = weight_ref[
            slot_of(part, group), 0:entries
        ]
    pieces = []
    for part in range(2):
        block = weight_ref[slot_of(2 * place + part, group), entries:].astype(jnp.float32)
        pieces.append(jnp.concatenate([block[:, :own], block[:, own:]], axis=0))
    taps = jnp.concatenate(pieces, axis=1)
    for chunk in range(chunks):
        for tap in range(TAPS):
            taps_ref[chunk, tap] = jnp.broadcast_to(
                taps[tap : tap + 1, chunk * LANES : (chunk + 1) * LANES], (8, LANES)
            )
    edge = jnp.zeros((2 * chunks, 16, LANES), jnp.float32)
    masked_ref[:, 0:16, :] = edge
    masked_ref[:, 16 + rows : 32 + rows, :] = edge
    for utt in range(2):
        real = lax.broadcasted_iota(jnp.int32, (rows, LANES), 0) < length_ref[utt]
        mixed = whole_ref[utt].reshape(rows, 2 * half)
        projected = dot_tt(mixed, rows_ref[...], 1, 0)
        hidden = frame_ref[:, utt].reshape(rows, width).astype(jnp.float32) + projected
        hidden = hidden.astype(jnp.bfloat16).astype(jnp.float32)
        for chunk in range(chunks):
            piece = hidden[:, chunk * LANES : (chunk + 1) * LANES]
            hidden_ref[utt * chunks + chunk] = piece
            masked_ref[utt * chunks + chunk, 16 : 16 + rows, :] = jnp.where(real, piece, 0.0)

    def convolve(step, carry):
        utt, chunk = step // chunks, step % chunks
        cols = columns(chunk * LANES, LANES)
        shape = (frames // 8, 8, LANES)
        for block in range(N_CTX):
            base = block * frames
            total = jnp.zeros(shape, jnp.float32)
            for tap in range(TAPS):
                first = base + tap + 16 - REACH
                piece = masked_ref[step, first : first + frames, :]
                total += taps_ref[chunk, tap][None] * piece.reshape(shape)
            total = total.reshape(frames, LANES)
            total_ref[step, base : base + frames, :] = total
            outer = hidden_ref[step, base : base + frames, :] + total * jax.nn.sigmoid(total)
            result_ref[block, utt, :, cols] = outer.astype(jnp.bfloat16)
        return carry

    lax.fori_loop(0, 2 * chunks, convolve, 0)
    for apart in range(N_CTX):
        out_refs[apart][...] = result_ref[place ^ apart]


def backward(length_ref, total_ref, masked_ref, taps_ref, rows_ref, *refs):
    side_refs, out_refs = refs[:N_CTX], refs[N_CTX : 2 * N_CTX]
    grad_ref, keep_ref, send_ref, sums_ref = refs[2 * N_CTX : 2 * N_CTX + 4]
    side_ref, result_ref, cotangent_ref, tap_sum_ref = refs[2 * N_CTX + 4 :]
    frames, width = side_refs[0].shape[1], side_refs[0].shape[2]
    rows = N_CTX * frames
    chunks = width // LANES
    half = rows_ref.shape[0] // 2
    place = lax.axis_index("ctx")
    for apart in range(N_CTX):
        side_ref[place ^ apart] = side_refs[apart][...]
    tap_sum_ref[...] = jnp.zeros_like(tap_sum_ref)
    edge = jnp.zeros((2 * chunks, 16, LANES), jnp.float32)
    cotangent_ref[:, 0:16, :] = edge
    cotangent_ref[:, 16 + rows : 32 + rows, :] = edge

    def convolve(step, carry):
        utt, chunk = step // chunks, step % chunks
        cols = columns(chunk * LANES, LANES)
        length = length_ref[utt]
        shape = (frames // 8, 8, LANES)
        for block in range(N_CTX):
            base = block * frames
            total = total_ref[step, base : base + frames, :]
            gate = jax.nn.sigmoid(total)
            incoming = side_ref[block, utt, :, cols].astype(jnp.float32)
            slope = gate * (1.0 + total * (1.0 - gate))
            low = (incoming * slope).astype(jnp.bfloat16)
            cotangent_ref[step, 16 + base : 16 + base + frames, :] = low.astype(jnp.float32)
        for block in range(N_CTX):
            base = block * frames
            total = jnp.zeros(shape, jnp.float32)
            held = masked_ref[step, 16 + base : 16 + base + frames, :].reshape(shape)
            for tap in range(TAPS):
                first = base + 16 + REACH - tap
                piece = cotangent_ref[step, first : first + frames, :].reshape(shape)
                total += taps_ref[chunk, tap][None] * piece
                tap_sum_ref[chunk, tap] += jnp.sum(held * piece, axis=0)
            place_of = base + lax.broadcasted_iota(jnp.int32, (frames, LANES), 0)
            total = jnp.where(place_of < length, total.reshape(frames, LANES), 0.0)
            incoming = side_ref[block, utt, :, cols].astype(jnp.float32)
            low = (incoming + total).astype(jnp.bfloat16)
            result_ref[block, utt, :, cols] = low
            grad_ref[utt, base : base + frames, cols] = low
        return carry

    lax.fori_loop(0, 2 * chunks, convolve, 0)
    sums = [
        jnp.concatenate(
            [
                jnp.sum(tap_sum_ref[chunk, tap], axis=0, keepdims=True)
                for tap in range(TAP_PAD)
            ],
            axis=0,
        )
        for chunk in range(chunks)
    ]
    sums = jnp.concatenate(sums, axis=1).astype(jnp.bfloat16)
    sums_ref[...] = sums
    for apart in range(N_CTX):
        out_refs[apart][...] = result_ref[place ^ apart]
        dest = place ^ apart
        mixed = dot_tt(
            grad_ref[half_of(dest)],
            rows_ref[pl.ds(pl.multiple_of((dest & 1) * half, half), half)],
            1,
            1,
        ).astype(jnp.bfloat16)
        ref = send_ref if apart % 2 else keep_ref
        for block in range(N_CTX):
            first = pl.multiple_of((block ^ dest) * frames, frames)
            ref[apart // 2, pl.ds(first, frames), :] = mixed[block * frames : (block + 1) * frames]
    for part in range(2):
        send_ref[part, rows:, :] = sums[part * TAP_PAD // 2 : (part + 1) * TAP_PAD // 2]


def make_panels(whole_ref, grad_ref, panel_ref):
    rows, half = grad_ref.shape[1], whole_ref.shape[3] // 2
    entries = 2 * half // N_DP
    group = lax.axis_index("dp")
    for side in range(2):
        panel = 0.0
        for utt in range(2):
            mixed = whole_ref[utt, :, :, side * half : (side + 1) * half].reshape(rows, half)
            panel += dot_tt(mixed, grad_ref[utt], 0, 0)
        panel = panel.astype(jnp.bfloat16)
        for part in range(N_DP // 2):
            panel_ref[slot_of(side * N_DP // 2 + part, group)] = panel[
                part * entries : (part + 1) * entries
            ]


def relay(keep_ref, came_ref, sums_ref, out_ref):
    rows = keep_ref.shape[1]
    total = keep_ref[1].astype(jnp.float32) + came_ref[1, 0:rows, :].astype(jnp.float32)
    out_ref[0:rows, :] = total.astype(jnp.bfloat16)
    out_ref[rows : rows + TAP_PAD, :] = sums_ref[...]
    for part in range(2):
        first = rows + TAP_PAD + part * TAP_PAD // 2
        out_ref[first : first + TAP_PAD // 2, :] = came_ref[part, rows:, :]


def attend_back(weight_ref, keep_ref, came_ref, far_ref, sums_ref, *refs):
    ins, out_refs, taps_ref = refs[:N_CTX], refs[N_CTX : 2 * N_CTX], refs[2 * N_CTX]
    frames, half = ins[0].shape[1], ins[0].shape[2]
    rows = N_CTX * frames
    own = half // 2
    group, place = lax.axis_index("dp"), lax.axis_index("ctx")
    query, key, value = (head_parts(ins, slot) for slot in range(3))
    masks = half_masks(rows)
    scale = HEAD_DIM ** (-0.5)
    arriving = keep_ref[0].astype(jnp.float32) + came_ref[0, 0:rows, :].astype(jnp.float32)
    arriving = (arriving + far_ref[0:rows, :].astype(jnp.float32)).astype(jnp.bfloat16)
    low_lanes = lax.broadcasted_iota(jnp.int32, (rows, LANES), 1) < HEAD_DIM
    for pair in range(half // LANES):
        cols = slice(pair * LANES, (pair + 1) * LANES)
        key_pair, value_pair = key[:, cols], value[:, cols]
        query_pair, grad_pair = query[:, cols], arriving[:, cols]
        query_parts, key_parts, value_parts = [], [], []
        for side in range(2):
            low = weight_ref[2 * pair + side]
            weights = low.astype(jnp.float32)
            moved = weights * dot_tt(value_pair, grad_pair * masks[side], 1, 1)
            delta = jnp.sum(moved, axis=0, keepdims=True)
            grad_scores = (moved - weights * delta).astype(jnp.bfloat16)
            value_parts.append(dot_tt(low, grad_pair, 1, 0))
            key_parts.append(dot_tt(grad_scores, query_pair, 1, 0))
            mixed = dot_tt(key_pair, grad_scores, 0, 0)
            query_parts.append(mixed[side * HEAD_DIM : (side + 1) * HEAD_DIM])
        query_sum = (jnp.concatenate(query_parts, axis=0).T * scale).astype(jnp.bfloat16)
        key_sum = (jnp.where(low_lanes, key_parts[0], key_parts[1]) * scale).astype(jnp.bfloat16)
        value_sum = jnp.where(low_lanes, value_parts[0], value_parts[1]).astype(jnp.bfloat16)
        for slot, total in enumerate((query_sum, key_sum, value_sum)):
            for apart in range(N_CTX):
                out_refs[apart][slot, :, cols] = total[apart * frames : (apart + 1) * frames]
    pieces = [sums_ref[...]]
    pieces.append(jnp.concatenate([came_ref[0, rows:, :], came_ref[1, rows:, :]], axis=0))
    for part in range(2):
        first = rows + part * TAP_PAD
        pieces.append(far_ref[first : first + TAP_PAD, :])
    for apart, piece in enumerate(pieces):
        block = piece.astype(jnp.float32)
        for part in range(2):
            mine = block[:, part * own : (part + 1) * own]
            mine = jnp.concatenate([mine[: TAP_PAD // 2], mine[TAP_PAD // 2 :]], axis=1)
            taps_ref[slot_of(2 * (place ^ apart) + part, group)] = mine.astype(jnp.bfloat16)


def swapped(array, bit):
    return lax.ppermute(array, "dp", [(i, i ^ bit) for i in range(N_DP)])


def crossed(array, apart):
    return lax.ppermute(array, "ctx", [(i, i ^ apart) for i in range(N_CTX)])


def traded(blocks):
    came = {apart: crossed(blocks[apart], apart) for apart in (2, 3, 1)}
    return [blocks[0]] + [came[apart] for apart in (1, 2, 3)]


def per_device(
    frame_input, queries, key_proj, value_proj, out_weight, conv_weight, lengths, grad_output
):
    utts, frames, wide = frame_input.shape
    inner = queries.shape[2]
    half, width = inner // 2, wide // N_CTX
    rows = N_CTX * frames
    chunks = width // LANES
    low, f32 = jnp.bfloat16, jnp.float32
    shape = jax.ShapeDtypeStruct
    entries = out_weight.shape[1]
    tap_count = conv_weight.shape[0]
    dma = pltpu.SemaphoreType.DMA
    head_block = shape((3, frames, half), low)
    channel_block = shape((utts, frames, width), low)

    packed = traded(
        call_kernel(
            pack_heads, (head_block,) * N_CTX, ["hbm"] * 3, scratch=[dma((3 * N_CTX,))]
        )(queries, key_proj, value_proj)
    )
    tap_rows = jnp.pad(conv_weight, ((0, TAP_PAD - tap_count), (0, 0)))
    tap_rows = jnp.concatenate([tap_rows[: TAP_PAD // 2], tap_rows[TAP_PAD // 2 :]], axis=1)
    shard = jnp.concatenate([out_weight.T, tap_rows], axis=0)[None]
    for bit in DP_BITS:
        shard = jnp.concatenate([shard, swapped(shard, bit)], axis=0)

    def spread(array):
        blocks = call_kernel(
            pack_channels, (channel_block,) * N_CTX, ["hbm"], scratch=[dma((2 * N_CTX,))]
        )(array)
        return traded(blocks)

    frame_blocks = spread(frame_input)
    attended, weights = call_kernel(
        attend,
        (
            shape((N_CTX, frames, half), low),
            shape((half // HEAD_DIM, rows, rows), low),
        ),
        ["smem"] + ["vmem"] * N_CTX,
    )(lengths, *packed)
    across = crossed(attended, 2)
    beside = crossed(attended, 1)
    diagonal = crossed(across, 1)
    grad_blocks = spread(grad_output)
    forward_out = call_kernel(
        forward,
        (channel_block,) * N_CTX
        + (
            shape((utts, N_CTX, frames, inner), low),
            shape((inner, width), low),
            shape((chunks, TAP_PAD, 8, LANES), f32),
            shape((utts * chunks, rows, LANES), f32),
            shape((utts * chunks, rows + 32, LANES), f32),
        ),
        ["smem"] + ["vmem"] * (1 + 2 * N_CTX),
        scratch=[
            pltpu.VMEM((utts * chunks, rows, LANES), f32),
            pltpu.VMEM((N_CTX, utts, frames, width), low),
            pltpu.VMEM((N_CTX, utts, frames, width), low),
        ],
    )(lengths, shard, attended, beside, across, diagonal, *frame_blocks)
    output_blocks = traded(forward_out[:N_CTX])
    whole, weight_rows, taps, totals, masked = forward_out[N_CTX:]
    backward_out = call_kernel(
        backward,
        (channel_block,) * N_CTX
        + (
            shape((utts, rows, width), low),
            shape((2, rows, half), low),
            shape((2, rows + TAP_PAD // 2, half), low),
            shape((TAP_PAD, width), low),
        ),
        ["smem"] + ["vmem"] * (4 + N_CTX),
        scratch=[
            pltpu.VMEM((N_CTX, utts, frames, width), low),
            pltpu.VMEM((N_CTX, utts, frames, width), low),
            pltpu.VMEM((utts * chunks, rows + 32, LANES), f32),
            pltpu.VMEM((chunks, TAP_PAD, 8, LANES), f32),
        ],
    )(lengths, totals, masked, taps, weight_rows, *grad_blocks)
    grad_hidden, keep, send, sums = backward_out[N_CTX:]
    came = crossed(send, 1)
    (panels,) = call_kernel(
        make_panels, (shape((N_DP, entries, width), low),), ["vmem"] * 2
    )(whole, grad_hidden)

    def added(kept, arrived):
        return (kept.astype(f32) + arrived.astype(f32)).astype(low)

    (far,) = call_kernel(
        relay, (shape((rows + 2 * TAP_PAD, half), low),), ["vmem"] * 3
    )(keep, came, sums)
    far = crossed(far, 2)
    input_blocks = traded(backward_out[:N_CTX])
    panels = added(panels[:4], swapped(panels[4:], 1))
    back_out = call_kernel(
        attend_back,
        (head_block,) * N_CTX + (shape((N_DP, TAP_PAD // 2, width), low),),
        ["vmem"] * (5 + N_CTX),
    )(weights, keep, came, far, sums, *packed)
    grad_blocks = traded(back_out[:N_CTX])
    tap_slots = back_out[N_CTX]
    tap_slots = added(tap_slots[:4], swapped(tap_slots[4:], 1))
    summed = jnp.concatenate([panels, tap_slots], axis=1)
    summed = added(summed[:2], swapped(summed[2:], 2))
    last = summed[0].astype(f32) + swapped(summed[1], 4).astype(f32)

    def gathered(blocks):
        return call_kernel(
            unpack_channels,
            (shape((utts, frames, wide), low),),
            ["any"] * N_CTX,
            ["hbm"],
            [dma((2 * N_CTX,))],
        )(*blocks)[0]

    block_output = gathered(output_blocks)
    grad_input = gathered(input_blocks)
    grad_queries, grad_keys, grad_values = call_kernel(
        unpack_heads,
        (shape((utts, frames, inner), low),) * 3,
        ["any"] * N_CTX,
        ["hbm"] * 3,
        [dma((3 * N_CTX,))],
    )(*grad_blocks)
    grad_out_weight = last[:entries].T
    own = width // 2
    grad_taps = jnp.concatenate([last[entries:, :own], last[entries:, own:]], axis=0)[:tap_count]
    return (
        block_output,
        grad_input,
        grad_queries,
        grad_keys,
        grad_values,
        grad_out_weight,
        grad_taps,
    )


def chosen(sizes, *arrays):
    frame_input, queries, out_weight, conv_weight = (arrays[i] for i in (0, 1, 4, 5))
    utts, frames, wide = frame_input.shape
    inner = queries.shape[2]
    fits = (
        sizes == (N_DP, N_CTX)
        and utts == 2
        and frames == 64
        and wide % (N_CTX * LANES) == 0
        and inner % (2 * LANES) == 0
        and inner // N_DP % 16 == 0
        and inner // 2 == wide // N_CTX
        and conv_weight.shape == (TAPS, wide // N_DP)
        and out_weight.shape == (wide // N_CTX, inner // N_DP)
    )
    return (per_device if fits else general_device)(*arrays)


def solution(mesh):
    placed = (
        P("dp", "ctx", None),
        P("dp", "ctx", None),
        P("dp", "ctx", None),
        P("dp", "ctx", None),
        P("ctx", "dp"),
        P(None, "dp"),
        P("dp"),
        P("dp", "ctx", None),
    )
    sizes = (mesh.shape["dp"], mesh.shape["ctx"])
    return jax.shard_map(
        functools.partial(chosen, sizes),
        mesh=mesh,
        in_specs=placed,
        out_specs=(
            P("dp", "ctx", None),
            P("dp", "ctx", None),
            P("dp", "ctx", None),
            P("dp", "ctx", None),
            P("dp", "ctx", None),
            P("ctx", "dp"),
            P(None, "dp"),
        ),
        check_vma=False,
    )
```

```python
import functools

import jax
import jax.numpy as jnp
from jax import lax
from jax.experimental import pallas as pl
from jax.experimental.pallas import tpu as pltpu
from jax.sharding import PartitionSpec as P

HEAD_DIM = 64


masked_score = -1e30


def padded_2(array, sides, width):
    for axis, dim in sides:
        size, length = (lax.axis_size(axis), array.shape[dim])
        up = [(i, (i + 1) % size) for i in range(size - 1)]
        down = [(j, i) for i, j in up]
        last = lax.slice_in_dim(array, length - width, length, axis=dim)
        leading = lax.slice_in_dim(array, 0, width, axis=dim)
        before = lax.ppermute(last, axis, up)
        after = lax.ppermute(leading, axis, down)
        array = jnp.concatenate([before, array, after], axis=dim)
    return array


def depthwise(lhs, rhs):
    return lax.conv_general_dilated(
        lhs,
        rhs,
        (1,),
        "VALID",
        dimension_numbers=("NWC", "WIO", "NWC"),
        feature_group_count=lhs.shape[2],
        precision=lax.Precision.HIGHEST,
    )


def general_device(
    frame_input, queries, key_proj, value_proj, out_weight, conv_weight, lengths, grad_output
):
    utt_count = frame_input.shape[0]
    frame_count = frame_input.shape[1]
    inner_width = queries.shape[2]
    head_count = inner_width // HEAD_DIM
    group_heads = max((g for g in range(1, 7) if head_count % g == 0))
    group_count = head_count // group_heads
    group_width = group_heads * HEAD_DIM
    tap_count = conv_weight.shape[0]
    half_span = (tap_count - 1) // 2
    score_scale = HEAD_DIM ** (-0.5)
    total_frames = frame_count * lax.axis_size("ctx")
    offset = lax.axis_index("ctx") * frame_count
    own_valid = (offset + jnp.arange(frame_count, dtype=jnp.int32))[None, :] < lengths[:, None]
    all_valid = jnp.arange(total_frames, dtype=jnp.int32)[None, :] < lengths[:, None]

    def grouped(values):
        row_count = values.shape[1]
        return values.reshape(utt_count, row_count, group_count, group_width).transpose(2, 0, 1, 3)

    def ungrouped(values):
        row_count = values.shape[2]
        return values.transpose(1, 2, 0, 3).reshape(utt_count, row_count, group_count * group_width)

    def split_heads(values):
        return values.reshape(utt_count, values.shape[1], group_heads, HEAD_DIM)

    def stats_grouped(values):
        row_count = values.shape[1]
        return values.reshape(utt_count, row_count, group_count, group_heads).transpose(2, 0, 3, 1)

    def masked_scores(query_block, key_block, key_mask):
        scores = (
            jnp.einsum(
                "uqgd,ukgd->ugqk", query_block, key_block, preferred_element_type=jnp.float32
            )
            * score_scale
        )
        return jnp.where(key_mask[:, None, None, :], scores, masked_score)

    taps = lax.all_gather(conv_weight, "dp", axis=1, tiled=True).astype(jnp.float32)
    panel_rows = lax.all_gather(out_weight, "dp", axis=1, tiled=True)
    weight_full = lax.all_gather(panel_rows, "ctx", axis=0, tiled=True)
    all_keys, all_values = (
        lax.all_gather(key_proj, "ctx", axis=1, tiled=True),
        lax.all_gather(value_proj, "ctx", axis=1, tiled=True),
    )
    query_groups = grouped(queries)
    key_groups = grouped(all_keys)
    value_groups = grouped(all_values)

    def forward_group(unused, items):
        query_group, key_group, value_group = items
        query_block = split_heads(query_group)
        scores = masked_scores(query_block, split_heads(key_group), all_valid)
        largest = jnp.max(scores, axis=-1)
        log_group = largest + jnp.log(jnp.sum(jnp.exp(scores - largest[..., None]), axis=-1))
        weights_low = jnp.exp(scores - log_group[..., None]).astype(jnp.bfloat16)
        attended_group = jnp.einsum(
            "ugqk,ukgd->uqgd",
            weights_low,
            split_heads(value_group),
            preferred_element_type=jnp.float32,
        )
        return (None, (log_group, attended_group.reshape(utt_count, frame_count, group_width)))

    _, (log_groups, attended_groups) = lax.scan(
        forward_group, None, (query_groups, key_groups, value_groups)
    )
    attended = ungrouped(attended_groups).astype(jnp.bfloat16)
    log_total = log_groups.transpose(1, 3, 0, 2).reshape(utt_count, frame_count, head_count)
    projected = jnp.einsum("ufe,de->ufd", attended, weight_full, preferred_element_type=jnp.float32)
    hidden = (frame_input.astype(jnp.float32) + projected).astype(jnp.bfloat16)
    masked_hidden = jnp.where(own_valid[:, :, None], hidden, jnp.zeros_like(hidden))
    padded = padded_2(masked_hidden, (("ctx", 1),), half_span).astype(jnp.float32)
    conv_sum = depthwise(padded, taps[:, None, :])
    sigmoid = jax.nn.sigmoid(conv_sum)
    block_output = (hidden.astype(jnp.float32) + conv_sum * sigmoid).astype(jnp.bfloat16)
    grad_local = grad_output.astype(jnp.float32)
    swish_slope = sigmoid * (1.0 + conv_sum * (1.0 - sigmoid))
    grad_conv = (grad_local * swish_slope).astype(jnp.bfloat16)
    grad_padded = padded_2(grad_conv, (("ctx", 1),), half_span).astype(jnp.float32)
    back_sum = depthwise(grad_padded, taps[::-1][:, None, :])
    grad_hidden = (grad_local + jnp.where(own_valid[:, :, None], back_sum, 0.0)).astype(
        jnp.bfloat16
    )
    grad_conv_wide = grad_conv.astype(jnp.float32)
    kernel_term = jnp.zeros((tap_count, conv_sum.shape[2]), jnp.float32)
    for utt_index in range(utt_count):
        kernel_term = (
            kernel_term
            + depthwise(padded[utt_index : utt_index + 1], grad_conv_wide[utt_index][:, None, :])[0]
        )
    kernel_whole = lax.psum(kernel_term.astype(jnp.bfloat16), "ctx")
    grad_conv_weight = lax.psum_scatter(kernel_whole, "dp", scatter_dimension=1, tiled=True).astype(
        jnp.float32
    )
    grad_attended = jnp.einsum(
        "ufd,de->ufe", grad_hidden, weight_full, preferred_element_type=jnp.float32
    ).astype(jnp.bfloat16)
    row_delta = jnp.sum(
        grad_attended.astype(jnp.float32).reshape(utt_count, frame_count, head_count, HEAD_DIM)
        * attended.astype(jnp.float32).reshape(utt_count, frame_count, head_count, HEAD_DIM),
        axis=-1,
    )
    grad_groups = grouped(grad_attended)

    def query_group_step(unused, items):
        query_group, key_group, value_group, grad_group, log_group, delta_group = items
        key_block = split_heads(key_group)
        weights = jnp.exp(
            masked_scores(split_heads(query_group), key_block, all_valid) - log_group[..., None]
        )
        grad_weights = jnp.einsum(
            "uqgd,ukgd->ugqk",
            split_heads(grad_group),
            split_heads(value_group),
            preferred_element_type=jnp.float32,
        )
        grad_scores = (weights * (grad_weights - delta_group[..., None])).astype(jnp.bfloat16)
        query_sum = jnp.einsum(
            "ugqk,ukgd->uqgd", grad_scores, key_block, preferred_element_type=jnp.float32
        )
        return (None, query_sum.reshape(utt_count, frame_count, group_width))

    _, query_sums = lax.scan(
        query_group_step,
        None,
        (
            query_groups,
            key_groups,
            value_groups,
            grad_groups,
            stats_grouped(log_total),
            stats_grouped(row_delta),
        ),
    )
    grad_queries = (ungrouped(query_sums) * score_scale).astype(jnp.bfloat16)
    total_log, total_delta = (
        lax.all_gather(log_total, "ctx", axis=1, tiled=True),
        lax.all_gather(row_delta, "ctx", axis=1, tiled=True),
    )
    own_key_groups = grouped(key_proj)
    own_value_groups = grouped(value_proj)
    group_zeros = jnp.zeros((group_count, utt_count, frame_count, group_width), jnp.float32)
    start_sums = (group_zeros, group_zeros)
    query_all, grad_all = (
        lax.all_gather(queries, "ctx", axis=1, tiled=True),
        lax.all_gather(grad_attended, "ctx", axis=1, tiled=True),
    )
    log_piece = stats_grouped(total_log)
    delta_piece = stats_grouped(total_delta)

    def key_group_step(unused, items):
        (
            query_group,
            grad_group,
            log_group,
            delta_group,
            key_group,
            value_group,
            key_sum,
            value_sum,
        ) = items
        query_block = split_heads(query_group)
        grad_block = split_heads(grad_group)
        weights = jnp.exp(
            masked_scores(query_block, split_heads(key_group), own_valid) - log_group[..., None]
        )
        grad_weights = jnp.einsum(
            "uqgd,ukgd->ugqk",
            grad_block,
            split_heads(value_group),
            preferred_element_type=jnp.float32,
        )
        grad_scores = (weights * (grad_weights - delta_group[..., None])).astype(jnp.bfloat16)
        key_next = key_sum + jnp.einsum(
            "ugqk,uqgd->ukgd", grad_scores, query_block, preferred_element_type=jnp.float32
        ).reshape(utt_count, frame_count, group_width)
        value_next = value_sum + jnp.einsum(
            "ugqk,uqgd->ukgd",
            weights.astype(jnp.bfloat16),
            grad_block,
            preferred_element_type=jnp.float32,
        ).reshape(utt_count, frame_count, group_width)
        return (None, (key_next, value_next))

    _, result_sums = lax.scan(
        key_group_step,
        None,
        (
            grouped(query_all),
            grouped(grad_all),
            log_piece,
            delta_piece,
            own_key_groups,
            own_value_groups,
            start_sums[0],
            start_sums[1],
        ),
    )
    key_sum, value_sum = result_sums
    grad_keys = (ungrouped(key_sum) * score_scale).astype(jnp.bfloat16)
    grad_values = ungrouped(value_sum).astype(jnp.bfloat16)
    hidden_cols = lax.slice_in_dim(
        grad_hidden, 0, weight_full.shape[0] // lax.axis_size("ctx") * lax.axis_size("ctx"), axis=2
    )
    panel_share = lax.psum_scatter(
        jnp.einsum("ufd,ufe->de", hidden_cols, attended, preferred_element_type=jnp.float32).astype(
            jnp.bfloat16
        ),
        "ctx",
        scatter_dimension=0,
        tiled=True,
    )
    grad_out_weight = lax.psum_scatter(panel_share, "dp", scatter_dimension=1, tiled=True).astype(
        jnp.float32
    )
    return (
        block_output,
        grad_hidden,
        grad_queries,
        grad_keys,
        grad_values,
        grad_out_weight,
        grad_conv_weight,
    )


LANES = 128
N_CTX = 4
N_DP = 8
Z_FIRST = (4, 2, 1)
Y_FIRST = (1, 4, 2)
TAP_PAD = 32
TAPS = 31
REACH = 15


def slot_of(index, me, bits=Z_FIRST):
    apart = jnp.bitwise_xor(index, me)
    place = 0
    for order, bit in enumerate(bits):
        place += jnp.where((apart & bit) != 0, 1 << order, 0)
    return place


def dot_tt(lhs, rhs, lhs_dim, rhs_dim):
    return lax.dot_general(
        lhs, rhs, (((lhs_dim,), (rhs_dim,)), ((), ())), preferred_element_type=jnp.float32
    )


def call_kernel(body, out_shape, ins, outs=None, scratch=(), room=40):
    spaces = {
        "smem": pl.BlockSpec(memory_space=pltpu.SMEM),
        "vmem": pl.BlockSpec(memory_space=pltpu.VMEM),
        "hbm": pl.BlockSpec(memory_space=pltpu.HBM),
        "any": pl.BlockSpec(memory_space=pl.ANY),
    }
    return pl.pallas_call(
        body,
        out_shape=out_shape,
        in_specs=[spaces[space] for space in ins],
        out_specs=[spaces[space] for space in (outs or ["vmem"] * len(out_shape))],
        scratch_shapes=list(scratch),
        compiler_params=pltpu.CompilerParams(vmem_limit_bytes=room * 1024 * 1024),
    )


def half_of(index):
    return lax.shift_right_logical(index, 1)


def columns(start, size):
    return pl.ds(pl.multiple_of(start, LANES), size)


def start_copies(pairs, sem):
    for number, (source, target) in enumerate(pairs):
        pltpu.make_async_copy(source, target, sem.at[number]).start()


def wait_copies(pairs, sem):
    for number, (source, target) in enumerate(pairs):
        pltpu.make_async_copy(source, target, sem.at[number]).wait()


def run_copies(pairs, sem):
    start_copies(pairs, sem)
    wait_copies(pairs, sem)


def untouched(*refs):
    pass


def gate(arrays, *awaited):
    count = len(arrays)
    spec = pl.BlockSpec(memory_space=pl.ANY)
    return pl.pallas_call(
        untouched,
        out_shape=tuple(jax.ShapeDtypeStruct(array.shape, array.dtype) for array in arrays),
        in_specs=[spec] * (count + len(awaited)),
        out_specs=(spec,) * count,
        input_output_aliases={number: number for number in range(count)},
    )(*arrays, *awaited)


def pack_heads(query_ref, key_ref, value_ref, panel_ref, taps_ref, *rest):
    outs, early_ref, late_ref, sem = rest[:N_CTX], *rest[N_CTX:]
    half = query_ref.shape[2] // 2
    place = lax.axis_index("ctx")
    pairs = []
    for apart in (2, 3, 1, 0):
        dest = place ^ apart
        cols = columns((dest & 1) * half, half)
        for slot, ref in enumerate((query_ref, key_ref, value_ref)):
            pairs.append((ref.at[half_of(dest), :, cols], outs[apart].at[slot]))
    split = late_ref.shape[1]
    pairs.append((panel_ref.at[0:split], late_ref.at[0]))
    pairs.append((panel_ref.at[split : 2 * split], early_ref.at[0, 0:split]))
    start_copies(pairs, sem)
    taps = taps_ref[...].astype(jnp.float32)
    high = jnp.concatenate(
        [taps[TAP_PAD // 2 :], jnp.zeros((TAP_PAD - TAPS, taps.shape[1]), jnp.float32)], axis=0
    )
    joined = jnp.concatenate([taps[: TAP_PAD // 2], high], axis=1)
    early_ref[0, split:, :] = joined.astype(jnp.bfloat16)
    wait_copies(pairs, sem)


def pack_channels(in_ref, *rest):
    outs, sem = rest[-N_CTX - 1 : -1], rest[-1]
    width = in_ref.shape[2] // N_CTX
    place = lax.axis_index("ctx")
    pairs = []
    for apart in (2, 3, 1, 0):
        cols = columns((place ^ apart) * width, width)
        for utt in range(2):
            pairs.append((in_ref.at[utt, :, cols], outs[apart].at[utt]))
    run_copies(pairs, sem)


def unpack_channels(*refs):
    ins, out_ref, sem = refs[:N_CTX], refs[N_CTX], refs[N_CTX + 1]
    width = ins[0].shape[2]
    place = lax.axis_index("ctx")
    pairs = []
    for apart in range(N_CTX):
        cols = columns((place ^ apart) * width, width)
        for utt in range(2):
            pairs.append((ins[apart].at[utt], out_ref.at[utt, :, cols]))
    run_copies(pairs, sem)


def unpack_heads(*refs):
    ins, outs, sem = refs[:N_CTX], refs[N_CTX : N_CTX + 3], refs[N_CTX + 3]
    half = ins[0].shape[2]
    place = lax.axis_index("ctx")
    pairs = []
    for apart in range(N_CTX):
        source = place ^ apart
        cols = columns((source & 1) * half, half)
        for slot in range(3):
            pairs.append((ins[apart].at[slot], outs[slot].at[half_of(source), :, cols]))
    run_copies(pairs, sem)


def head_parts(refs, slot):
    return jnp.concatenate([ref[slot] for ref in refs], axis=0)


def half_masks(rows):
    lane = lax.broadcasted_iota(jnp.int32, (rows, LANES), 1)
    low = jnp.where(lane < HEAD_DIM, 1.0, 0.0)
    return low.astype(jnp.bfloat16), (1.0 - low).astype(jnp.bfloat16)


def attend(length_ref, *refs):
    ins, attended_ref, weight_ref = refs[:N_CTX], refs[N_CTX], refs[N_CTX + 1]
    frames, half = ins[0].shape[1], ins[0].shape[2]
    rows = N_CTX * frames
    place = lax.axis_index("ctx")
    length = length_ref[half_of(place)]
    query, key, value = (head_parts(ins, slot) for slot in range(3))
    masks = half_masks(rows)
    frame = lax.broadcasted_iota(jnp.int32, (rows, rows), 0) ^ (place * frames)
    real = frame < length
    for pair in range(half // LANES):
        cols = slice(pair * LANES, (pair + 1) * LANES)
        key_pair, value_pair = key[:, cols], value[:, cols]
        parts = []
        for side in range(2):
            scores = dot_tt(key_pair, query[:, cols] * masks[side], 1, 1) * HEAD_DIM ** (-0.5)
            scores = jnp.where(real, scores, masked_score)
            largest = jnp.max(scores, axis=0, keepdims=True)
            powers = jnp.exp(scores - largest)
            total = jnp.sum(powers, axis=0, keepdims=True)
            low = (powers * (1.0 / total)).astype(jnp.bfloat16)
            weight_ref[2 * pair + side] = low
            mixed = dot_tt(value_pair, low, 0, 0)
            parts.append(mixed[side * HEAD_DIM : (side + 1) * HEAD_DIM])
        joined = jnp.concatenate(parts, axis=0).T.astype(jnp.bfloat16)
        attended_ref[:, :, cols] = joined.reshape(N_CTX, frames, LANES)


def forward(length_ref, early_ref, late_ref, *refs):
    attended_refs, frame_refs = refs[:N_CTX], refs[N_CTX : 2 * N_CTX]
    out_refs = refs[2 * N_CTX : 3 * N_CTX]
    whole_ref, rows_ref, taps_ref, total_ref, masked_ref = refs[3 * N_CTX : 3 * N_CTX + 5]
    hidden_ref, frame_ref, result_ref = refs[3 * N_CTX + 5 :]
    frames, half = attended_refs[0].shape[1], attended_refs[0].shape[2]
    width = frame_ref.shape[3]
    rows = N_CTX * frames
    chunks = width // LANES
    entries = 2 * half // N_DP
    own = width // 2
    group, place = lax.axis_index("dp"), lax.axis_index("ctx")
    for apart in range(N_CTX):
        source = place ^ apart
        cols = columns((source & 1) * half, half)
        for block in range(N_CTX):
            whole_ref[half_of(source), block ^ source, :, cols] = attended_refs[apart][block]
        frame_ref[source] = frame_refs[apart][...]
    split = late_ref.shape[1]
    for part in range(N_DP):
        first = part * entries
        rows_ref[first : first + split] = late_ref[slot_of(part, group, Y_FIRST)]
        rows_ref[first + split : first + entries] = early_ref[slot_of(part, group), 0:split]
    pieces = []
    for part in range(2):
        block = early_ref[slot_of(2 * place + part, group), split:].astype(jnp.float32)
        pieces.append(jnp.concatenate([block[:, :own], block[:, own:]], axis=0))
    taps = jnp.concatenate(pieces, axis=1)
    for chunk in range(chunks):
        for tap in range(TAPS):
            taps_ref[chunk, tap] = jnp.broadcast_to(
                taps[tap : tap + 1, chunk * LANES : (chunk + 1) * LANES], (8, LANES)
            )
    edge = jnp.zeros((2 * chunks, 16, LANES), jnp.float32)
    masked_ref[:, 0:16, :] = edge
    masked_ref[:, 16 + rows : 32 + rows, :] = edge
    for utt in range(2):
        real = lax.broadcasted_iota(jnp.int32, (rows, LANES), 0) < length_ref[utt]
        mixed = whole_ref[utt].reshape(rows, 2 * half)
        projected = dot_tt(mixed, rows_ref[...], 1, 0)
        hidden = frame_ref[:, utt].reshape(rows, width).astype(jnp.float32) + projected
        hidden = hidden.astype(jnp.bfloat16).astype(jnp.float32)
        for chunk in range(chunks):
            piece = hidden[:, chunk * LANES : (chunk + 1) * LANES]
            hidden_ref[utt * chunks + chunk] = piece
            masked_ref[utt * chunks + chunk, 16 : 16 + rows, :] = jnp.where(real, piece, 0.0)

    def convolve(step, carry):
        utt, chunk = step // chunks, step % chunks
        cols = columns(chunk * LANES, LANES)
        shape = (frames // 8, 8, LANES)
        for block in range(N_CTX):
            base = block * frames
            total = jnp.zeros(shape, jnp.float32)
            for tap in range(TAPS):
                first = base + tap + 16 - REACH
                piece = masked_ref[step, first : first + frames, :]
                total += taps_ref[chunk, tap][None] * piece.reshape(shape)
            total = total.reshape(frames, LANES)
            total_ref[step, base : base + frames, :] = total
            outer = hidden_ref[step, base : base + frames, :] + total * jax.nn.sigmoid(total)
            result_ref[block, utt, :, cols] = outer.astype(jnp.bfloat16)
        return carry

    lax.fori_loop(0, 2 * chunks, convolve, 0)
    for apart in range(N_CTX):
        out_refs[apart][...] = result_ref[place ^ apart]


def backward(length_ref, total_ref, masked_ref, taps_ref, rows_ref, *refs):
    side_refs, out_refs = refs[:N_CTX], refs[N_CTX : 2 * N_CTX]
    grad_ref, keep_ref, send_ref, sums_ref = refs[2 * N_CTX : 2 * N_CTX + 4]
    side_ref, result_ref, cotangent_ref, tap_sum_ref = refs[2 * N_CTX + 4 :]
    frames, width = side_refs[0].shape[1], side_refs[0].shape[2]
    rows = N_CTX * frames
    chunks = width // LANES
    half = rows_ref.shape[0] // 2
    place = lax.axis_index("ctx")
    for apart in range(N_CTX):
        side_ref[place ^ apart] = side_refs[apart][...]
    tap_sum_ref[...] = jnp.zeros_like(tap_sum_ref)
    edge = jnp.zeros((2 * chunks, 16, LANES), jnp.float32)
    cotangent_ref[:, 0:16, :] = edge
    cotangent_ref[:, 16 + rows : 32 + rows, :] = edge

    def convolve(step, carry):
        utt, chunk = step // chunks, step % chunks
        cols = columns(chunk * LANES, LANES)
        length = length_ref[utt]
        shape = (frames // 8, 8, LANES)
        for block in range(N_CTX):
            base = block * frames
            total = total_ref[step, base : base + frames, :]
            gate = jax.nn.sigmoid(total)
            incoming = side_ref[block, utt, :, cols].astype(jnp.float32)
            slope = gate * (1.0 + total * (1.0 - gate))
            low = (incoming * slope).astype(jnp.bfloat16)
            cotangent_ref[step, 16 + base : 16 + base + frames, :] = low.astype(jnp.float32)
        for block in range(N_CTX):
            base = block * frames
            total = jnp.zeros(shape, jnp.float32)
            held = masked_ref[step, 16 + base : 16 + base + frames, :].reshape(shape)
            for tap in range(TAPS):
                first = base + 16 + REACH - tap
                piece = cotangent_ref[step, first : first + frames, :].reshape(shape)
                total += taps_ref[chunk, tap][None] * piece
                tap_sum_ref[chunk, tap] += jnp.sum(held * piece, axis=0)
            place_of = base + lax.broadcasted_iota(jnp.int32, (frames, LANES), 0)
            total = jnp.where(place_of < length, total.reshape(frames, LANES), 0.0)
            incoming = side_ref[block, utt, :, cols].astype(jnp.float32)
            low = (incoming + total).astype(jnp.bfloat16)
            result_ref[block, utt, :, cols] = low
            grad_ref[utt, base : base + frames, cols] = low
        return carry

    lax.fori_loop(0, 2 * chunks, convolve, 0)
    sums = [
        jnp.concatenate(
            [
                jnp.sum(tap_sum_ref[chunk, tap], axis=0, keepdims=True)
                for tap in range(TAP_PAD)
            ],
            axis=0,
        )
        for chunk in range(chunks)
    ]
    sums = jnp.concatenate(sums, axis=1).astype(jnp.bfloat16)
    sums_ref[...] = sums
    for apart in range(N_CTX):
        out_refs[apart][...] = result_ref[place ^ apart]
        dest = place ^ apart
        mixed = dot_tt(
            grad_ref[half_of(dest)],
            rows_ref[pl.ds(pl.multiple_of((dest & 1) * half, half), half)],
            1,
            1,
        ).astype(jnp.bfloat16)
        ref = send_ref if apart % 2 else keep_ref
        for block in range(N_CTX):
            first = pl.multiple_of((block ^ dest) * frames, frames)
            ref[apart // 2, pl.ds(first, frames), :] = mixed[block * frames : (block + 1) * frames]
    for part in range(2):
        send_ref[part, rows:, :] = sums[part * TAP_PAD // 2 : (part + 1) * TAP_PAD // 2]


def make_panels(whole_ref, grad_ref, panel_ref):
    rows, half = grad_ref.shape[1], whole_ref.shape[3] // 2
    entries = 2 * half // N_DP
    group = lax.axis_index("dp")
    for side in range(2):
        panel = 0.0
        for utt in range(2):
            mixed = whole_ref[utt, :, :, side * half : (side + 1) * half].reshape(rows, half)
            panel += dot_tt(mixed, grad_ref[utt], 0, 0)
        panel = panel.astype(jnp.bfloat16)
        for part in range(N_DP // 2):
            panel_ref[slot_of(side * N_DP // 2 + part, group)] = panel[
                part * entries : (part + 1) * entries
            ]


def relay(keep_ref, came_ref, sums_ref, awaited_ref, out_ref):
    rows = keep_ref.shape[1]
    total = keep_ref[1].astype(jnp.float32) + came_ref[1, 0:rows, :].astype(jnp.float32)
    out_ref[0:rows, :] = total.astype(jnp.bfloat16)
    out_ref[rows : rows + TAP_PAD, :] = sums_ref[...]
    for part in range(2):
        first = rows + TAP_PAD + part * TAP_PAD // 2
        out_ref[first : first + TAP_PAD // 2, :] = came_ref[part, rows:, :]


def attend_back(weight_ref, keep_ref, came_ref, far_ref, sums_ref, *refs):
    ins, out_refs, taps_ref = refs[:N_CTX], refs[N_CTX : 2 * N_CTX], refs[2 * N_CTX]
    frames, half = ins[0].shape[1], ins[0].shape[2]
    rows = N_CTX * frames
    own = half // 2
    group, place = lax.axis_index("dp"), lax.axis_index("ctx")
    query, key, value = (head_parts(ins, slot) for slot in range(3))
    masks = half_masks(rows)
    scale = HEAD_DIM ** (-0.5)
    arriving = keep_ref[0].astype(jnp.float32) + came_ref[0, 0:rows, :].astype(jnp.float32)
    arriving = (arriving + far_ref[0:rows, :].astype(jnp.float32)).astype(jnp.bfloat16)
    low_lanes = lax.broadcasted_iota(jnp.int32, (rows, LANES), 1) < HEAD_DIM
    for pair in range(half // LANES):
        cols = slice(pair * LANES, (pair + 1) * LANES)
        key_pair, value_pair = key[:, cols], value[:, cols]
        query_pair, grad_pair = query[:, cols], arriving[:, cols]
        query_parts, key_parts, value_parts = [], [], []
        for side in range(2):
            low = weight_ref[2 * pair + side]
            weights = low.astype(jnp.float32)
            moved = weights * dot_tt(value_pair, grad_pair * masks[side], 1, 1)
            delta = jnp.sum(moved, axis=0, keepdims=True)
            grad_scores = (moved - weights * delta).astype(jnp.bfloat16)
            value_parts.append(dot_tt(low, grad_pair, 1, 0))
            key_parts.append(dot_tt(grad_scores, query_pair, 1, 0))
            mixed = dot_tt(key_pair, grad_scores, 0, 0)
            query_parts.append(mixed[side * HEAD_DIM : (side + 1) * HEAD_DIM])
        query_sum = (jnp.concatenate(query_parts, axis=0).T * scale).astype(jnp.bfloat16)
        key_sum = (jnp.where(low_lanes, key_parts[0], key_parts[1]) * scale).astype(jnp.bfloat16)
        value_sum = jnp.where(low_lanes, value_parts[0], value_parts[1]).astype(jnp.bfloat16)
        for slot, total in enumerate((query_sum, key_sum, value_sum)):
            for apart in range(N_CTX):
                out_refs[apart][slot, :, cols] = total[apart * frames : (apart + 1) * frames]
    pieces = [sums_ref[...]]
    pieces.append(jnp.concatenate([came_ref[0, rows:, :], came_ref[1, rows:, :]], axis=0))
    for part in range(2):
        first = rows + part * TAP_PAD
        pieces.append(far_ref[first : first + TAP_PAD, :])
    for apart, piece in enumerate(pieces):
        block = piece.astype(jnp.float32)
        for part in range(2):
            mine = block[:, part * own : (part + 1) * own]
            mine = jnp.concatenate([mine[: TAP_PAD // 2], mine[TAP_PAD // 2 :]], axis=1)
            taps_ref[slot_of(2 * (place ^ apart) + part, group)] = mine.astype(jnp.bfloat16)


def swapped(array, bit):
    return lax.ppermute(array, "dp", [(i, i ^ bit) for i in range(N_DP)])


def crossed(array, apart):
    return lax.ppermute(array, "ctx", [(i, i ^ apart) for i in range(N_CTX)])


def traded(blocks):
    came = {apart: crossed(blocks[apart], apart) for apart in (2, 3, 1)}
    return [blocks[0]] + [came[apart] for apart in (1, 2, 3)]


def per_device(
    frame_input, queries, key_proj, value_proj, out_weight, conv_weight, lengths, grad_output
):
    utts, frames, wide = frame_input.shape
    inner = queries.shape[2]
    half, width = inner // 2, wide // N_CTX
    rows = N_CTX * frames
    chunks = width // LANES
    low, f32 = jnp.bfloat16, jnp.float32
    shape = jax.ShapeDtypeStruct
    entries = out_weight.shape[1]
    tap_count = conv_weight.shape[0]
    dma = pltpu.SemaphoreType.DMA
    head_block = shape((3, frames, half), low)
    channel_block = shape((utts, frames, width), low)

    split = entries // 2
    *blocks, early, late = call_kernel(
        pack_heads,
        (head_block,) * N_CTX
        + (shape((1, split + TAP_PAD // 2, width), low), shape((1, split, width), low)),
        ["hbm"] * 4 + ["vmem"],
        scratch=[dma((3 * N_CTX + 2,))],
        room=63,
    )(queries, key_proj, value_proj, out_weight.T, conv_weight)
    packed = traded(blocks)
    for early_bit, late_bit in zip(Z_FIRST, Y_FIRST):
        early = jnp.concatenate([early, swapped(early, early_bit)], axis=0)
        late = jnp.concatenate([late, swapped(late, late_bit)], axis=0)

    def spread(array, *awaited):
        blocks = call_kernel(
            pack_channels,
            (channel_block,) * N_CTX,
            ["hbm"] + ["any"] * len(awaited),
            scratch=[dma((2 * N_CTX,))],
        )(array, *awaited)
        return traded(blocks)

    frame_blocks = spread(frame_input, blocks[0])
    attended, weights = call_kernel(
        attend,
        (
            shape((N_CTX, frames, half), low),
            shape((half // HEAD_DIM, rows, rows), low),
        ),
        ["smem"] + ["vmem"] * N_CTX,
    )(lengths, *packed)
    (attended,) = gate([attended], frame_blocks[2])
    across = crossed(attended, 2)
    beside = crossed(attended, 1)
    diagonal = crossed(across, 1)
    grad_blocks = spread(grad_output, attended)
    forward_out = call_kernel(
        forward,
        (channel_block,) * N_CTX
        + (
            shape((utts, N_CTX, frames, inner), low),
            shape((inner, width), low),
            shape((chunks, TAP_PAD, 8, LANES), f32),
            shape((utts * chunks, rows, LANES), f32),
            shape((utts * chunks, rows + 32, LANES), f32),
        ),
        ["smem"] + ["vmem"] * (2 + 2 * N_CTX),
        scratch=[
            pltpu.VMEM((utts * chunks, rows, LANES), f32),
            pltpu.VMEM((N_CTX, utts, frames, width), low),
            pltpu.VMEM((N_CTX, utts, frames, width), low),
        ],
    )(lengths, early, late, attended, beside, across, diagonal, *frame_blocks)
    output_blocks = traded(forward_out[:N_CTX])
    whole, weight_rows, taps, totals, masked = forward_out[N_CTX:]
    backward_out = call_kernel(
        backward,
        (channel_block,) * N_CTX
        + (
            shape((utts, rows, width), low),
            shape((2, rows, half), low),
            shape((2, rows + TAP_PAD // 2, half), low),
            shape((TAP_PAD, width), low),
        ),
        ["smem"] + ["vmem"] * (4 + N_CTX),
        scratch=[
            pltpu.VMEM((N_CTX, utts, frames, width), low),
            pltpu.VMEM((N_CTX, utts, frames, width), low),
            pltpu.VMEM((utts * chunks, rows + 32, LANES), f32),
            pltpu.VMEM((chunks, TAP_PAD, 8, LANES), f32),
        ],
    )(lengths, totals, masked, taps, weight_rows, *grad_blocks)
    grad_hidden, keep, send, sums = backward_out[N_CTX:]
    (send,) = gate([send], *output_blocks[2:])
    came = crossed(send, 1)
    input_blocks = traded(backward_out[:N_CTX])
    (panels,) = call_kernel(
        make_panels, (shape((N_DP, entries, width), low),), ["vmem"] * 2
    )(whole, grad_hidden)
    (far,) = call_kernel(
        relay, (shape((rows + 2 * TAP_PAD, half), low),), ["vmem"] * 3 + ["any"]
    )(keep, came, sums, input_blocks[2])
    far = crossed(far, 2)
    back_out = call_kernel(
        attend_back,
        (head_block,) * N_CTX + (shape((N_DP, TAP_PAD // 2, width), low),),
        ["vmem"] * (5 + N_CTX),
    )(weights, keep, came, far, sums, *packed)
    grad_blocks = traded(back_out[:N_CTX])
    tap_slots = back_out[N_CTX]

    def added(kept, arrived):
        return (kept.astype(f32) + arrived.astype(f32)).astype(low)

    panels = added(panels[:4], swapped(panels[4:], 1))
    tap_slots = added(tap_slots[:4], swapped(tap_slots[4:], 1))
    summed = jnp.concatenate([panels, tap_slots], axis=1)
    summed = added(summed[:2], swapped(summed[2:], 2))
    last = summed[0].astype(f32) + swapped(summed[1], 4).astype(f32)

    def gathered(blocks):
        return call_kernel(
            unpack_channels,
            (shape((utts, frames, wide), low),),
            ["any"] * N_CTX,
            ["hbm"],
            [dma((2 * N_CTX,))],
        )(*blocks)[0]

    block_output = gathered(output_blocks)
    grad_input = gathered(input_blocks)
    grad_queries, grad_keys, grad_values = call_kernel(
        unpack_heads,
        (shape((utts, frames, inner), low),) * 3,
        ["any"] * N_CTX,
        ["hbm"] * 3,
        [dma((3 * N_CTX,))],
    )(*grad_blocks)
    grad_out_weight = last[:entries].T
    own = width // 2
    grad_taps = jnp.concatenate([last[entries:, :own], last[entries:, own:]], axis=0)[:tap_count]
    return (
        block_output,
        grad_input,
        grad_queries,
        grad_keys,
        grad_values,
        grad_out_weight,
        grad_taps,
    )


def chosen(sizes, *arrays):
    frame_input, queries, out_weight, conv_weight = (arrays[i] for i in (0, 1, 4, 5))
    utts, frames, wide = frame_input.shape
    inner = queries.shape[2]
    fits = (
        sizes == (N_DP, N_CTX)
        and utts == 2
        and frames == 64
        and wide % (N_CTX * LANES) == 0
        and inner % (2 * LANES) == 0
        and inner // N_DP % 16 == 0
        and inner // 2 == wide // N_CTX
        and conv_weight.shape == (TAPS, wide // N_DP)
        and out_weight.shape == (wide // N_CTX, inner // N_DP)
    )
    return (per_device if fits else general_device)(*arrays)


def solution(mesh):
    placed = (
        P("dp", "ctx", None),
        P("dp", "ctx", None),
        P("dp", "ctx", None),
        P("dp", "ctx", None),
        P("ctx", "dp"),
        P(None, "dp"),
        P("dp"),
        P("dp", "ctx", None),
    )
    sizes = (mesh.shape["dp"], mesh.shape["ctx"])
    return jax.shard_map(
        functools.partial(chosen, sizes),
        mesh=mesh,
        in_specs=placed,
        out_specs=(
            P("dp", "ctx", None),
            P("dp", "ctx", None),
            P("dp", "ctx", None),
            P("dp", "ctx", None),
            P("dp", "ctx", None),
            P("ctx", "dp"),
            P(None, "dp"),
        ),
        check_vma=False,
    )
```

```python
import functools

import jax
import jax.numpy as jnp
from jax import lax
from jax.experimental import pallas as pl
from jax.experimental.pallas import tpu as pltpu
from jax.sharding import PartitionSpec as P

HEAD_DIM = 64


masked_score = -1e30


def padded_2(array, sides, width):
    for axis, dim in sides:
        size, length = (lax.axis_size(axis), array.shape[dim])
        up = [(i, (i + 1) % size) for i in range(size - 1)]
        down = [(j, i) for i, j in up]
        last = lax.slice_in_dim(array, length - width, length, axis=dim)
        leading = lax.slice_in_dim(array, 0, width, axis=dim)
        before = lax.ppermute(last, axis, up)
        after = lax.ppermute(leading, axis, down)
        array = jnp.concatenate([before, array, after], axis=dim)
    return array


def depthwise(lhs, rhs):
    return lax.conv_general_dilated(
        lhs,
        rhs,
        (1,),
        "VALID",
        dimension_numbers=("NWC", "WIO", "NWC"),
        feature_group_count=lhs.shape[2],
        precision=lax.Precision.HIGHEST,
    )


def general_device(
    frame_input, queries, key_proj, value_proj, out_weight, conv_weight, lengths, grad_output
):
    utt_count = frame_input.shape[0]
    frame_count = frame_input.shape[1]
    inner_width = queries.shape[2]
    head_count = inner_width // HEAD_DIM
    group_heads = max((g for g in range(1, 7) if head_count % g == 0))
    group_count = head_count // group_heads
    group_width = group_heads * HEAD_DIM
    tap_count = conv_weight.shape[0]
    half_span = (tap_count - 1) // 2
    score_scale = HEAD_DIM ** (-0.5)
    total_frames = frame_count * lax.axis_size("ctx")
    offset = lax.axis_index("ctx") * frame_count
    own_valid = (offset + jnp.arange(frame_count, dtype=jnp.int32))[None, :] < lengths[:, None]
    all_valid = jnp.arange(total_frames, dtype=jnp.int32)[None, :] < lengths[:, None]

    def grouped(values):
        row_count = values.shape[1]
        return values.reshape(utt_count, row_count, group_count, group_width).transpose(2, 0, 1, 3)

    def ungrouped(values):
        row_count = values.shape[2]
        return values.transpose(1, 2, 0, 3).reshape(utt_count, row_count, group_count * group_width)

    def split_heads(values):
        return values.reshape(utt_count, values.shape[1], group_heads, HEAD_DIM)

    def stats_grouped(values):
        row_count = values.shape[1]
        return values.reshape(utt_count, row_count, group_count, group_heads).transpose(2, 0, 3, 1)

    def masked_scores(query_block, key_block, key_mask):
        scores = (
            jnp.einsum(
                "uqgd,ukgd->ugqk", query_block, key_block, preferred_element_type=jnp.float32
            )
            * score_scale
        )
        return jnp.where(key_mask[:, None, None, :], scores, masked_score)

    taps = lax.all_gather(conv_weight, "dp", axis=1, tiled=True).astype(jnp.float32)
    panel_rows = lax.all_gather(out_weight, "dp", axis=1, tiled=True)
    weight_full = lax.all_gather(panel_rows, "ctx", axis=0, tiled=True)
    all_keys, all_values = (
        lax.all_gather(key_proj, "ctx", axis=1, tiled=True),
        lax.all_gather(value_proj, "ctx", axis=1, tiled=True),
    )
    query_groups = grouped(queries)
    key_groups = grouped(all_keys)
    value_groups = grouped(all_values)

    def forward_group(unused, items):
        query_group, key_group, value_group = items
        query_block = split_heads(query_group)
        scores = masked_scores(query_block, split_heads(key_group), all_valid)
        largest = jnp.max(scores, axis=-1)
        log_group = largest + jnp.log(jnp.sum(jnp.exp(scores - largest[..., None]), axis=-1))
        weights_low = jnp.exp(scores - log_group[..., None]).astype(jnp.bfloat16)
        attended_group = jnp.einsum(
            "ugqk,ukgd->uqgd",
            weights_low,
            split_heads(value_group),
            preferred_element_type=jnp.float32,
        )
        return (None, (log_group, attended_group.reshape(utt_count, frame_count, group_width)))

    _, (log_groups, attended_groups) = lax.scan(
        forward_group, None, (query_groups, key_groups, value_groups)
    )
    attended = ungrouped(attended_groups).astype(jnp.bfloat16)
    log_total = log_groups.transpose(1, 3, 0, 2).reshape(utt_count, frame_count, head_count)
    projected = jnp.einsum("ufe,de->ufd", attended, weight_full, preferred_element_type=jnp.float32)
    hidden = (frame_input.astype(jnp.float32) + projected).astype(jnp.bfloat16)
    masked_hidden = jnp.where(own_valid[:, :, None], hidden, jnp.zeros_like(hidden))
    padded = padded_2(masked_hidden, (("ctx", 1),), half_span).astype(jnp.float32)
    conv_sum = depthwise(padded, taps[:, None, :])
    sigmoid = jax.nn.sigmoid(conv_sum)
    block_output = (hidden.astype(jnp.float32) + conv_sum * sigmoid).astype(jnp.bfloat16)
    grad_local = grad_output.astype(jnp.float32)
    swish_slope = sigmoid * (1.0 + conv_sum * (1.0 - sigmoid))
    grad_conv = (grad_local * swish_slope).astype(jnp.bfloat16)
    grad_padded = padded_2(grad_conv, (("ctx", 1),), half_span).astype(jnp.float32)
    back_sum = depthwise(grad_padded, taps[::-1][:, None, :])
    grad_hidden = (grad_local + jnp.where(own_valid[:, :, None], back_sum, 0.0)).astype(
        jnp.bfloat16
    )
    grad_conv_wide = grad_conv.astype(jnp.float32)
    kernel_term = jnp.zeros((tap_count, conv_sum.shape[2]), jnp.float32)
    for utt_index in range(utt_count):
        kernel_term = (
            kernel_term
            + depthwise(padded[utt_index : utt_index + 1], grad_conv_wide[utt_index][:, None, :])[0]
        )
    kernel_whole = lax.psum(kernel_term.astype(jnp.bfloat16), "ctx")
    grad_conv_weight = lax.psum_scatter(kernel_whole, "dp", scatter_dimension=1, tiled=True).astype(
        jnp.float32
    )
    grad_attended = jnp.einsum(
        "ufd,de->ufe", grad_hidden, weight_full, preferred_element_type=jnp.float32
    ).astype(jnp.bfloat16)
    row_delta = jnp.sum(
        grad_attended.astype(jnp.float32).reshape(utt_count, frame_count, head_count, HEAD_DIM)
        * attended.astype(jnp.float32).reshape(utt_count, frame_count, head_count, HEAD_DIM),
        axis=-1,
    )
    grad_groups = grouped(grad_attended)

    def query_group_step(unused, items):
        query_group, key_group, value_group, grad_group, log_group, delta_group = items
        key_block = split_heads(key_group)
        weights = jnp.exp(
            masked_scores(split_heads(query_group), key_block, all_valid) - log_group[..., None]
        )
        grad_weights = jnp.einsum(
            "uqgd,ukgd->ugqk",
            split_heads(grad_group),
            split_heads(value_group),
            preferred_element_type=jnp.float32,
        )
        grad_scores = (weights * (grad_weights - delta_group[..., None])).astype(jnp.bfloat16)
        query_sum = jnp.einsum(
            "ugqk,ukgd->uqgd", grad_scores, key_block, preferred_element_type=jnp.float32
        )
        return (None, query_sum.reshape(utt_count, frame_count, group_width))

    _, query_sums = lax.scan(
        query_group_step,
        None,
        (
            query_groups,
            key_groups,
            value_groups,
            grad_groups,
            stats_grouped(log_total),
            stats_grouped(row_delta),
        ),
    )
    grad_queries = (ungrouped(query_sums) * score_scale).astype(jnp.bfloat16)
    total_log, total_delta = (
        lax.all_gather(log_total, "ctx", axis=1, tiled=True),
        lax.all_gather(row_delta, "ctx", axis=1, tiled=True),
    )
    own_key_groups = grouped(key_proj)
    own_value_groups = grouped(value_proj)
    group_zeros = jnp.zeros((group_count, utt_count, frame_count, group_width), jnp.float32)
    start_sums = (group_zeros, group_zeros)
    query_all, grad_all = (
        lax.all_gather(queries, "ctx", axis=1, tiled=True),
        lax.all_gather(grad_attended, "ctx", axis=1, tiled=True),
    )
    log_piece = stats_grouped(total_log)
    delta_piece = stats_grouped(total_delta)

    def key_group_step(unused, items):
        (
            query_group,
            grad_group,
            log_group,
            delta_group,
            key_group,
            value_group,
            key_sum,
            value_sum,
        ) = items
        query_block = split_heads(query_group)
        grad_block = split_heads(grad_group)
        weights = jnp.exp(
            masked_scores(query_block, split_heads(key_group), own_valid) - log_group[..., None]
        )
        grad_weights = jnp.einsum(
            "uqgd,ukgd->ugqk",
            grad_block,
            split_heads(value_group),
            preferred_element_type=jnp.float32,
        )
        grad_scores = (weights * (grad_weights - delta_group[..., None])).astype(jnp.bfloat16)
        key_next = key_sum + jnp.einsum(
            "ugqk,uqgd->ukgd", grad_scores, query_block, preferred_element_type=jnp.float32
        ).reshape(utt_count, frame_count, group_width)
        value_next = value_sum + jnp.einsum(
            "ugqk,uqgd->ukgd",
            weights.astype(jnp.bfloat16),
            grad_block,
            preferred_element_type=jnp.float32,
        ).reshape(utt_count, frame_count, group_width)
        return (None, (key_next, value_next))

    _, result_sums = lax.scan(
        key_group_step,
        None,
        (
            grouped(query_all),
            grouped(grad_all),
            log_piece,
            delta_piece,
            own_key_groups,
            own_value_groups,
            start_sums[0],
            start_sums[1],
        ),
    )
    key_sum, value_sum = result_sums
    grad_keys = (ungrouped(key_sum) * score_scale).astype(jnp.bfloat16)
    grad_values = ungrouped(value_sum).astype(jnp.bfloat16)
    hidden_cols = lax.slice_in_dim(
        grad_hidden, 0, weight_full.shape[0] // lax.axis_size("ctx") * lax.axis_size("ctx"), axis=2
    )
    panel_share = lax.psum_scatter(
        jnp.einsum("ufd,ufe->de", hidden_cols, attended, preferred_element_type=jnp.float32).astype(
            jnp.bfloat16
        ),
        "ctx",
        scatter_dimension=0,
        tiled=True,
    )
    grad_out_weight = lax.psum_scatter(panel_share, "dp", scatter_dimension=1, tiled=True).astype(
        jnp.float32
    )
    return (
        block_output,
        grad_hidden,
        grad_queries,
        grad_keys,
        grad_values,
        grad_out_weight,
        grad_conv_weight,
    )


LANES = 128
N_CTX = 4
N_DP = 8
Z_FIRST = (4, 2, 1)
Y_FIRST = (1, 4, 2)
Y_LAST = (1, 4, 2)
TAP_PAD = 32
FLOPS_A_MICRO = 1.15e9
TAPS = 31
REACH = 15


def slot_of(index, me, bits=Z_FIRST):
    apart = jnp.bitwise_xor(index, me)
    place = 0
    for order, bit in enumerate(bits):
        place += jnp.where((apart & bit) != 0, 1 << order, 0)
    return place


def dot_tt(lhs, rhs, lhs_dim, rhs_dim):
    return lax.dot_general(
        lhs, rhs, (((lhs_dim,), (rhs_dim,)), ((), ())), preferred_element_type=jnp.float32
    )


def call_kernel(body, out_shape, ins, outs=None, scratch=(), room=40, micros=1.0):
    spaces = {
        "smem": pl.BlockSpec(memory_space=pltpu.SMEM),
        "vmem": pl.BlockSpec(memory_space=pltpu.VMEM),
        "hbm": pl.BlockSpec(memory_space=pltpu.HBM),
        "any": pl.BlockSpec(memory_space=pl.ANY),
    }
    return pl.pallas_call(
        body,
        out_shape=out_shape,
        in_specs=[spaces[space] for space in ins],
        out_specs=[spaces[space] for space in (outs or ["vmem"] * len(out_shape))],
        scratch_shapes=list(scratch),
        compiler_params=pltpu.CompilerParams(vmem_limit_bytes=room * 1024 * 1024),
        cost_estimate=pl.CostEstimate(
            flops=int(micros * FLOPS_A_MICRO), bytes_accessed=0, transcendentals=0
        ),
    )


def half_of(index):
    return lax.shift_right_logical(index, 1)


def columns(start, size):
    return pl.ds(pl.multiple_of(start, LANES), size)


def start_copies(pairs, sem):
    for number, (source, target) in enumerate(pairs):
        pltpu.make_async_copy(source, target, sem.at[number]).start()


def wait_copies(pairs, sem):
    for number, (source, target) in enumerate(pairs):
        pltpu.make_async_copy(source, target, sem.at[number]).wait()


def run_copies(pairs, sem):
    start_copies(pairs, sem)
    wait_copies(pairs, sem)


def untouched(*refs):
    pass


def gate(arrays, *awaited):
    count = len(arrays)
    spec = pl.BlockSpec(memory_space=pl.ANY)
    return pl.pallas_call(
        untouched,
        out_shape=tuple(jax.ShapeDtypeStruct(array.shape, array.dtype) for array in arrays),
        in_specs=[spec] * (count + len(awaited)),
        out_specs=(spec,) * count,
        input_output_aliases={number: number for number in range(count)},
        compiler_params=pltpu.CompilerParams(vmem_limit_bytes=1024 * 1024),
    )(*arrays, *awaited)


def pack_heads(query_ref, key_ref, value_ref, *rest):
    outs, sem = rest[:N_CTX], rest[N_CTX]
    half = query_ref.shape[2] // 2
    place = lax.axis_index("ctx")
    pairs = []
    for apart in (2, 3, 1, 0):
        dest = place ^ apart
        cols = columns((dest & 1) * half, half)
        for slot, ref in enumerate((query_ref, key_ref, value_ref)):
            pairs.append((ref.at[half_of(dest), :, cols], outs[apart].at[slot]))
    run_copies(pairs, sem)


def pack_weights(panel_ref, taps_ref, awaited_ref, early_ref, late_ref):
    split = late_ref.shape[1]
    late_ref[0] = panel_ref[0:split]
    early_ref[0, 0:split] = panel_ref[split : 2 * split]
    taps = taps_ref[...].astype(jnp.float32)
    high = jnp.concatenate(
        [taps[TAP_PAD // 2 :], jnp.zeros((TAP_PAD - TAPS, taps.shape[1]), jnp.float32)], axis=0
    )
    joined = jnp.concatenate([taps[: TAP_PAD // 2], high], axis=1)
    early_ref[0, split:, :] = joined.astype(jnp.bfloat16)


def pack_channels(frame_ref, grad_ref, awaited_ref, *rest):
    frame_outs, grad_outs, beside_ref, own_ref, sem = rest[:2], rest[2:4], *rest[4:]
    width = frame_ref.shape[2] // N_CTX
    place = lax.axis_index("ctx")
    pairs = []
    for slot, (ref, outs) in enumerate(((frame_ref, frame_outs), (grad_ref, grad_outs))):
        targets = [own_ref.at[slot], beside_ref.at[slot], outs[0], outs[1]]
        for apart in (2, 3, 1, 0):
            cols = columns((place ^ apart) * width, width)
            for utt in range(2):
                pairs.append((ref.at[utt, :, cols], targets[apart].at[utt]))
    run_copies(pairs, sem)


def unpack(*refs):
    ins, own_ref, beside_ref = refs[:N_CTX], refs[N_CTX], refs[N_CTX + 1]
    across_refs, diagonal_refs = refs[N_CTX + 2 : N_CTX + 4], refs[N_CTX + 4 : N_CTX + 6]
    heads, channels, sem = refs[N_CTX + 7 : N_CTX + 10], refs[N_CTX + 10 : N_CTX + 12], refs[-1]
    half, width = ins[0].shape[2], own_ref.shape[3]
    frames = own_ref.shape[2]
    place = lax.axis_index("ctx")
    pairs = []
    for apart in range(N_CTX):
        source = place ^ apart
        cols = columns((source & 1) * half, half)
        for slot, ref in enumerate(heads):
            pairs.append((ins[apart].at[slot], ref.at[half_of(source), :, cols]))
    for slot, ref in enumerate(channels):
        for apart in range(N_CTX):
            cols = columns((place ^ apart) * width, width)
            for utt in range(2):
                if apart < 2:
                    block = (own_ref, beside_ref)[apart].at[slot, utt]
                else:
                    block = (across_refs, diagonal_refs)[apart - 2][slot]
                    block = block.at[utt * frames : (utt + 1) * frames]
                pairs.append((block, ref.at[utt, :, cols]))
    run_copies(pairs, sem)


def head_parts(refs, slot):
    return jnp.concatenate([ref[slot] for ref in refs], axis=0)


def half_masks(rows):
    lane = lax.broadcasted_iota(jnp.int32, (rows, LANES), 1)
    low = jnp.where(lane < HEAD_DIM, 1.0, 0.0)
    return low.astype(jnp.bfloat16), (1.0 - low).astype(jnp.bfloat16)


def attend(length_ref, *refs):
    ins, attended_ref, weight_ref = refs[:N_CTX], refs[N_CTX], refs[N_CTX + 1]
    frames, half = ins[0].shape[1], ins[0].shape[2]
    rows = N_CTX * frames
    place = lax.axis_index("ctx")
    length = length_ref[half_of(place)]
    query, key, value = (head_parts(ins, slot) for slot in range(3))
    masks = half_masks(rows)
    frame = lax.broadcasted_iota(jnp.int32, (rows, rows), 0) ^ (place * frames)
    real = frame < length
    for pair in range(half // LANES):
        cols = slice(pair * LANES, (pair + 1) * LANES)
        key_pair, value_pair = key[:, cols], value[:, cols]
        parts = []
        for side in range(2):
            scores = dot_tt(key_pair, query[:, cols] * masks[side], 1, 1) * HEAD_DIM ** (-0.5)
            scores = jnp.where(real, scores, masked_score)
            largest = jnp.max(scores, axis=0, keepdims=True)
            powers = jnp.exp(scores - largest)
            total = jnp.sum(powers, axis=0, keepdims=True)
            low = (powers * (1.0 / total)).astype(jnp.bfloat16)
            weight_ref[2 * pair + side] = low
            mixed = dot_tt(value_pair, low, 0, 0)
            parts.append(mixed[side * HEAD_DIM : (side + 1) * HEAD_DIM])
        joined = jnp.concatenate(parts, axis=0).T.astype(jnp.bfloat16)
        attended_ref[:, :, cols] = joined.reshape(N_CTX, frames, LANES)


def side_blocks(slot, refs):
    return refs[0].at[slot], refs[1].at[slot], refs[2], refs[3]


def forward(length_ref, early_ref, late_ref, *refs):
    attended_refs, frame_refs = refs[:N_CTX], side_blocks(0, refs[N_CTX : 2 * N_CTX])
    out_refs = refs[2 * N_CTX : 3 * N_CTX]
    whole_ref, rows_ref, taps_ref, total_ref, masked_ref = refs[3 * N_CTX : 3 * N_CTX + 5]
    hidden_ref, frame_ref, result_ref = refs[3 * N_CTX + 5 :]
    frames, half = attended_refs[0].shape[1], attended_refs[0].shape[2]
    width = frame_ref.shape[3]
    rows = N_CTX * frames
    chunks = width // LANES
    entries = 2 * half // N_DP
    own = width // 2
    group, place = lax.axis_index("dp"), lax.axis_index("ctx")
    for apart in range(N_CTX):
        source = place ^ apart
        cols = columns((source & 1) * half, half)
        for block in range(N_CTX):
            whole_ref[half_of(source), block ^ source, :, cols] = attended_refs[apart][block]
        frame_ref[source] = frame_refs[apart][...]
    split = late_ref.shape[1]
    for part in range(N_DP):
        first = part * entries
        rows_ref[first : first + split] = late_ref[slot_of(part, group, Y_FIRST)]
        rows_ref[first + split : first + entries] = early_ref[slot_of(part, group), 0:split]
    pieces = []
    for part in range(2):
        block = early_ref[slot_of(2 * place + part, group), split:].astype(jnp.float32)
        pieces.append(jnp.concatenate([block[:, :own], block[:, own:]], axis=0))
    taps = jnp.concatenate(pieces, axis=1)
    for chunk in range(chunks):
        for tap in range(TAPS):
            taps_ref[chunk, tap] = jnp.broadcast_to(
                taps[tap : tap + 1, chunk * LANES : (chunk + 1) * LANES], (8, LANES)
            )
    edge = jnp.zeros((2 * chunks, 16, LANES), jnp.float32)
    masked_ref[:, 0:16, :] = edge
    masked_ref[:, 16 + rows : 32 + rows, :] = edge
    for utt in range(2):
        real = lax.broadcasted_iota(jnp.int32, (rows, LANES), 0) < length_ref[utt]
        mixed = whole_ref[utt].reshape(rows, 2 * half)
        projected = dot_tt(mixed, rows_ref[...], 1, 0)
        hidden = frame_ref[:, utt].reshape(rows, width).astype(jnp.float32) + projected
        hidden = hidden.astype(jnp.bfloat16).astype(jnp.float32)
        for chunk in range(chunks):
            piece = hidden[:, chunk * LANES : (chunk + 1) * LANES]
            hidden_ref[utt * chunks + chunk] = piece
            masked_ref[utt * chunks + chunk, 16 : 16 + rows, :] = jnp.where(real, piece, 0.0)

    def convolve(step, carry):
        utt, chunk = step // chunks, step % chunks
        cols = columns(chunk * LANES, LANES)
        shape = (frames // 8, 8, LANES)
        for block in range(N_CTX):
            base = block * frames
            total = jnp.zeros(shape, jnp.float32)
            for tap in range(TAPS):
                first = base + tap + 16 - REACH
                piece = masked_ref[step, first : first + frames, :]
                total += taps_ref[chunk, tap][None] * piece.reshape(shape)
            total = total.reshape(frames, LANES)
            total_ref[step, base : base + frames, :] = total
            outer = hidden_ref[step, base : base + frames, :] + total * jax.nn.sigmoid(total)
            result_ref[block, utt, :, cols] = outer.astype(jnp.bfloat16)
        return carry

    lax.fori_loop(0, 2 * chunks, convolve, 0)
    for apart in range(N_CTX):
        mine = result_ref[place ^ apart]
        out_refs[apart][...] = mine.reshape(out_refs[apart].shape)


def backward(length_ref, total_ref, masked_ref, taps_ref, rows_ref, *refs):
    own_ref, beside_ref = refs[:2]
    side_refs, refs = side_blocks(1, refs[2 : 2 + N_CTX]), refs[2 + N_CTX :]
    own_pair_ref, beside_pair_ref, across_ref, diagonal_ref = refs[:N_CTX]
    grad_ref, keep_ref, send_ref, sums_ref = refs[N_CTX : N_CTX + 4]
    side_ref, result_ref, cotangent_ref, tap_sum_ref = refs[N_CTX + 4 :]
    own_pair_ref[0], beside_pair_ref[0] = own_ref[...], beside_ref[...]
    utts, frames, width = own_ref.shape
    rows = N_CTX * frames
    chunks = width // LANES
    half = rows_ref.shape[0] // 2
    place = lax.axis_index("ctx")
    for apart in range(N_CTX):
        side_ref[place ^ apart] = side_refs[apart][...]
    tap_sum_ref[...] = jnp.zeros_like(tap_sum_ref)
    edge = jnp.zeros((2 * chunks, 16, LANES), jnp.float32)
    cotangent_ref[:, 0:16, :] = edge
    cotangent_ref[:, 16 + rows : 32 + rows, :] = edge

    def convolve(step, carry):
        utt, chunk = step // chunks, step % chunks
        cols = columns(chunk * LANES, LANES)
        length = length_ref[utt]
        shape = (frames // 8, 8, LANES)
        for block in range(N_CTX):
            base = block * frames
            total = total_ref[step, base : base + frames, :]
            gate = jax.nn.sigmoid(total)
            incoming = side_ref[block, utt, :, cols].astype(jnp.float32)
            slope = gate * (1.0 + total * (1.0 - gate))
            low = (incoming * slope).astype(jnp.bfloat16)
            cotangent_ref[step, 16 + base : 16 + base + frames, :] = low.astype(jnp.float32)
        for block in range(N_CTX):
            base = block * frames
            total = jnp.zeros(shape, jnp.float32)
            held = masked_ref[step, 16 + base : 16 + base + frames, :].reshape(shape)
            for tap in range(TAPS):
                first = base + 16 + REACH - tap
                piece = cotangent_ref[step, first : first + frames, :].reshape(shape)
                total += taps_ref[chunk, tap][None] * piece
                tap_sum_ref[chunk, tap] += jnp.sum(held * piece, axis=0)
            place_of = base + lax.broadcasted_iota(jnp.int32, (frames, LANES), 0)
            total = jnp.where(place_of < length, total.reshape(frames, LANES), 0.0)
            incoming = side_ref[block, utt, :, cols].astype(jnp.float32)
            low = (incoming + total).astype(jnp.bfloat16)
            result_ref[block, utt, :, cols] = low
            grad_ref[utt, base : base + frames, cols] = low
        return carry

    lax.fori_loop(0, 2 * chunks, convolve, 0)
    sums = [
        jnp.concatenate(
            [
                jnp.sum(tap_sum_ref[chunk, tap], axis=0, keepdims=True)
                for tap in range(TAP_PAD)
            ],
            axis=0,
        )
        for chunk in range(chunks)
    ]
    sums = jnp.concatenate(sums, axis=1).astype(jnp.bfloat16)
    sums_ref[...] = sums
    for ref in (across_ref, diagonal_ref):
        ref[utts * frames :, :] = sums
    for part in range(2):
        send_ref[part, rows:, :] = sums[part * TAP_PAD // 2 : (part + 1) * TAP_PAD // 2]
    for apart in range(N_CTX):
        mine = result_ref[place ^ apart]
        if apart < 2:
            (own_pair_ref, beside_pair_ref)[apart][1] = mine
        else:
            ref = (across_ref, diagonal_ref)[apart - 2]
            ref[: utts * frames, :] = mine.reshape(utts * frames, width)
        dest = place ^ apart
        mixed = dot_tt(
            grad_ref[half_of(dest)],
            rows_ref[pl.ds(pl.multiple_of((dest & 1) * half, half), half)],
            1,
            1,
        ).astype(jnp.bfloat16)
        ref = send_ref if apart % 2 else keep_ref
        for block in range(N_CTX):
            first = pl.multiple_of((block ^ dest) * frames, frames)
            ref[apart // 2, pl.ds(first, frames), :] = mixed[block * frames : (block + 1) * frames]


def make_panels(whole_ref, grad_ref, awaited_ref, early_ref, late_ref):
    rows, half = grad_ref.shape[1], whole_ref.shape[3] // 2
    entries = 2 * half // N_DP
    split = entries // 2
    group = lax.axis_index("dp")
    for side in range(2):
        panel = 0.0
        for utt in range(2):
            mixed = whole_ref[utt, :, :, side * half : (side + 1) * half].reshape(rows, half)
            panel += dot_tt(mixed, grad_ref[utt], 0, 0)
        panel = panel.astype(jnp.bfloat16)
        for part in range(N_DP // 2):
            index, first = side * N_DP // 2 + part, part * entries
            late_ref[slot_of(index, group, Y_LAST)] = panel[first : first + split]
            early_ref[slot_of(index, group)] = panel[first + split : first + entries]


def make_tap_slots(sums_ref, came_ref, across_ref, diagonal_ref, awaited_ref, out_ref):
    own = sums_ref.shape[1] // 2
    rows, start = came_ref.shape[1] - TAP_PAD // 2, across_ref.shape[0] - TAP_PAD
    group, place = lax.axis_index("dp"), lax.axis_index("ctx")
    pieces = [
        sums_ref[...],
        jnp.concatenate([came_ref[0, rows:, :], came_ref[1, rows:, :]], axis=0),
        across_ref[start:, :],
        diagonal_ref[start:, :],
    ]
    for apart, piece in enumerate(pieces):
        block = piece.astype(jnp.float32)
        for part in range(2):
            mine = block[:, part * own : (part + 1) * own]
            mine = jnp.concatenate([mine[: TAP_PAD // 2], mine[TAP_PAD // 2 :]], axis=1)
            out_ref[slot_of(2 * (place ^ apart) + part, group)] = mine.astype(jnp.bfloat16)


def relay(keep_ref, came_ref, out_ref):
    rows = keep_ref.shape[1]
    total = keep_ref[1].astype(jnp.float32) + came_ref[1, 0:rows, :].astype(jnp.float32)
    out_ref[...] = total.astype(jnp.bfloat16)


def attend_back(weight_ref, keep_ref, came_ref, far_ref, *refs):
    ins, out_refs = refs[:N_CTX], refs[N_CTX:]
    frames, half = ins[0].shape[1], ins[0].shape[2]
    rows = N_CTX * frames
    query, key, value = (head_parts(ins, slot) for slot in range(3))
    masks = half_masks(rows)
    scale = HEAD_DIM ** (-0.5)
    arriving = keep_ref[0].astype(jnp.float32) + came_ref[0, 0:rows, :].astype(jnp.float32)
    arriving = (arriving + far_ref[...].astype(jnp.float32)).astype(jnp.bfloat16)
    low_lanes = lax.broadcasted_iota(jnp.int32, (rows, LANES), 1) < HEAD_DIM
    for pair in range(half // LANES):
        cols = slice(pair * LANES, (pair + 1) * LANES)
        key_pair, value_pair = key[:, cols], value[:, cols]
        query_pair, grad_pair = query[:, cols], arriving[:, cols]
        query_parts, key_parts, value_parts = [], [], []
        for side in range(2):
            low = weight_ref[2 * pair + side]
            weights = low.astype(jnp.float32)
            moved = weights * dot_tt(value_pair, grad_pair * masks[side], 1, 1)
            delta = jnp.sum(moved, axis=0, keepdims=True)
            grad_scores = (moved - weights * delta).astype(jnp.bfloat16)
            value_parts.append(dot_tt(low, grad_pair, 1, 0))
            key_parts.append(dot_tt(grad_scores, query_pair, 1, 0))
            mixed = dot_tt(key_pair, grad_scores, 0, 0)
            query_parts.append(mixed[side * HEAD_DIM : (side + 1) * HEAD_DIM])
        query_sum = (jnp.concatenate(query_parts, axis=0).T * scale).astype(jnp.bfloat16)
        key_sum = (jnp.where(low_lanes, key_parts[0], key_parts[1]) * scale).astype(jnp.bfloat16)
        value_sum = jnp.where(low_lanes, value_parts[0], value_parts[1]).astype(jnp.bfloat16)
        for slot, total in enumerate((query_sum, key_sum, value_sum)):
            for apart in range(N_CTX):
                out_refs[apart][slot, :, cols] = total[apart * frames : (apart + 1) * frames]


def swapped(array, bit):
    return lax.ppermute(array, "dp", [(i, i ^ bit) for i in range(N_DP)])


def crossed(array, apart):
    return lax.ppermute(array, "ctx", [(i, i ^ apart) for i in range(N_CTX)])


def traded(blocks):
    came = {apart: crossed(blocks[apart], apart) for apart in (2, 3, 1)}
    return [blocks[0]] + [came[apart] for apart in (1, 2, 3)]


def per_device(
    frame_input, queries, key_proj, value_proj, out_weight, conv_weight, lengths, grad_output
):
    utts, frames, wide = frame_input.shape
    inner = queries.shape[2]
    half, width = inner // 2, wide // N_CTX
    rows = N_CTX * frames
    chunks = width // LANES
    low, f32 = jnp.bfloat16, jnp.float32
    shape = jax.ShapeDtypeStruct
    entries = out_weight.shape[1]
    tap_count = conv_weight.shape[0]
    dma = pltpu.SemaphoreType.DMA
    head_block = shape((3, frames, half), low)
    channel_block = shape((utts, frames, width), low)

    split = entries // 2
    blocks = call_kernel(
        pack_heads,
        (head_block,) * N_CTX,
        ["hbm"] * 3,
        ["hbm"] * N_CTX,
        [dma((3 * N_CTX,))],
        room=63,
    )(queries, key_proj, value_proj)
    packed = traded(blocks)
    early, late = call_kernel(
        pack_weights,
        (shape((1, split + TAP_PAD // 2, width), low), shape((1, split, width), low)),
        ["vmem"] * 2 + ["any"],
    )(out_weight.T, conv_weight, packed[1])
    for early_bit, late_bit in zip(Z_FIRST, Y_FIRST):
        early = jnp.concatenate([early, swapped(early, early_bit)], axis=0)
        late = jnp.concatenate([late, swapped(late, late_bit)], axis=0)
    pair_block = shape((2, utts, frames, width), low)
    *sides, beside_sides, own_sides = call_kernel(
        pack_channels,
        (channel_block,) * 4 + (pair_block,) * 2,
        ["hbm"] * 2 + ["any"],
        scratch=[dma((4 * N_CTX,))],
    )(frame_input, grad_output, blocks[0])
    frame_across, frame_diagonal = crossed(sides[0], 2), crossed(sides[1], 3)
    beside_sides = crossed(beside_sides, 1)
    attended, weights = call_kernel(
        attend,
        (
            shape((N_CTX, frames, half), low),
            shape((half // HEAD_DIM, rows, rows), low),
        ),
        ["smem"] + ["vmem"] * N_CTX,
        micros=3.0,
    )(lengths, *packed)
    (attended,) = gate([attended], frame_across, frame_diagonal)
    across = crossed(attended, 2)
    beside = crossed(attended, 1)
    diagonal = crossed(across, 1)
    grad_across, grad_diagonal = crossed(sides[2], 2), crossed(sides[3], 3)
    frame_blocks = (own_sides, beside_sides, frame_across, frame_diagonal)
    grad_blocks = (own_sides, beside_sides, grad_across, grad_diagonal)
    forward_out = call_kernel(
        forward,
        (channel_block,) * 2
        + (shape((utts * frames, width), low),) * 2
        + (
            shape((utts, N_CTX, frames, inner), low),
            shape((inner, width), low),
            shape((chunks, TAP_PAD, 8, LANES), f32),
            shape((utts * chunks, rows, LANES), f32),
            shape((utts * chunks, rows + 32, LANES), f32),
        ),
        ["smem"] + ["vmem"] * (2 + 2 * N_CTX),
        scratch=[
            pltpu.VMEM((utts * chunks, rows, LANES), f32),
            pltpu.VMEM((N_CTX, utts, frames, width), low),
            pltpu.VMEM((N_CTX, utts, frames, width), low),
        ],
        micros=3.2,
    )(lengths, early, late, attended, beside, across, diagonal, *frame_blocks)
    output_across, output_diagonal = crossed(forward_out[2], 2), crossed(forward_out[3], 3)
    whole, weight_rows, taps, totals, masked = forward_out[N_CTX:]
    backward_out = call_kernel(
        backward,
        (pair_block,) * 2
        + (shape((utts * frames + TAP_PAD, width), low),) * 2
        + (
            shape((utts, rows, width), low),
            shape((2, rows, half), low),
            shape((2, rows + TAP_PAD // 2, half), low),
            shape((TAP_PAD, width), low),
        ),
        ["smem"] + ["vmem"] * (6 + N_CTX),
        scratch=[
            pltpu.VMEM((N_CTX, utts, frames, width), low),
            pltpu.VMEM((N_CTX, utts, frames, width), low),
            pltpu.VMEM((utts * chunks, rows + 32, LANES), f32),
            pltpu.VMEM((chunks, TAP_PAD, 8, LANES), f32),
        ],
        micros=5.2,
    )(lengths, totals, masked, taps, weight_rows, *forward_out[:2], *grad_blocks)
    grad_hidden, keep, send, sums = backward_out[N_CTX:]
    (send,) = gate([send], output_across, output_diagonal)
    came = crossed(send, 1)
    (far,) = call_kernel(
        relay, (shape((rows, half), low),), ["vmem"] * 2, micros=0.2
    )(keep, came)
    early_panels, late_panels = call_kernel(
        make_panels,
        (shape((N_DP, entries - split, width), low), shape((N_DP, split, width), low)),
        ["vmem"] * 2 + ["any"],
        micros=0.7,
    )(whole, grad_hidden, far)
    far = crossed(far, 2)

    def halved(slots, bit):
        count = slots.shape[0] // 2
        return (slots[:count].astype(f32) + swapped(slots[count:], bit).astype(f32)).astype(low)

    late_panels = halved(late_panels, Y_LAST[2])
    input_blocks = gate(backward_out[2:4], late_panels)
    input_across, input_diagonal = crossed(input_blocks[0], 2), crossed(input_blocks[1], 3)
    back_blocks = call_kernel(
        attend_back,
        (head_block,) * N_CTX,
        ["vmem"] * (4 + N_CTX),
        micros=2.2,
    )(weights, keep, came, far, *packed)
    grad_blocks = traded(gate(back_blocks, input_across))
    own_pair, beside_pair = backward_out[:2]
    (beside_pair,) = gate([beside_pair], grad_blocks[1])
    beside_pair = crossed(beside_pair, 1)

    def finished(slots, bit):
        return slots[0].astype(f32) + swapped(slots[1], bit).astype(f32)

    tap_slots = call_kernel(
        make_tap_slots,
        (shape((N_DP, TAP_PAD // 2, width), low),),
        ["vmem"] * 4 + ["any"],
        micros=0.2,
    )(sums, came, input_across, input_diagonal, grad_blocks[1])[0]
    tap_slots = halved(halved(tap_slots, 1), 2)
    late_panels = halved(late_panels, Y_LAST[1])
    early_panels = halved(halved(early_panels, 1), 2)
    late_panels, early_panels = gate([late_panels, early_panels], grad_blocks[1])
    grad_out_weight = jnp.concatenate(
        [finished(late_panels, Y_LAST[0]), finished(early_panels, 4)], axis=0
    ).T

    grad_queries, grad_keys, grad_values, block_output, grad_input = call_kernel(
        unpack,
        (shape((utts, frames, inner), low),) * 3 + (shape((utts, frames, wide), low),) * 2,
        ["any"] * (N_CTX + 7),
        ["hbm"] * 5,
        [dma((7 * N_CTX + 4 * N_CTX,))],
        micros=10.0,
    )(
        *grad_blocks,
        own_pair,
        beside_pair,
        output_across,
        input_across,
        output_diagonal,
        input_diagonal,
        tap_slots,
    )
    (tap_slots,) = gate([tap_slots], grad_queries)
    tap_sums = finished(tap_slots, 4)
    own = width // 2
    grad_taps = jnp.concatenate([tap_sums[:, :own], tap_sums[:, own:]], axis=0)[:tap_count]
    return (
        block_output,
        grad_input,
        grad_queries,
        grad_keys,
        grad_values,
        grad_out_weight,
        grad_taps,
    )


def chosen(sizes, *arrays):
    frame_input, queries, out_weight, conv_weight = (arrays[i] for i in (0, 1, 4, 5))
    utts, frames, wide = frame_input.shape
    inner = queries.shape[2]
    fits = (
        sizes == (N_DP, N_CTX)
        and utts == 2
        and frames == 64
        and wide % (N_CTX * LANES) == 0
        and inner % (2 * LANES) == 0
        and inner // N_DP % 16 == 0
        and inner // 2 == wide // N_CTX
        and conv_weight.shape == (TAPS, wide // N_DP)
        and out_weight.shape == (wide // N_CTX, inner // N_DP)
    )
    return (per_device if fits else general_device)(*arrays)


def solution(mesh):
    placed = (
        P("dp", "ctx", None),
        P("dp", "ctx", None),
        P("dp", "ctx", None),
        P("dp", "ctx", None),
        P("ctx", "dp"),
        P(None, "dp"),
        P("dp"),
        P("dp", "ctx", None),
    )
    sizes = (mesh.shape["dp"], mesh.shape["ctx"])
    return jax.shard_map(
        functools.partial(chosen, sizes),
        mesh=mesh,
        in_specs=placed,
        out_specs=(
            P("dp", "ctx", None),
            P("dp", "ctx", None),
            P("dp", "ctx", None),
            P("dp", "ctx", None),
            P("dp", "ctx", None),
            P("ctx", "dp"),
            P(None, "dp"),
        ),
        check_vma=False,
    )
```

```python
import functools

import jax
import jax.numpy as jnp
from jax import lax
from jax.experimental import pallas as pl
from jax.experimental.pallas import tpu as pltpu
from jax.sharding import PartitionSpec as P

HEAD_DIM = 64


masked_score = -1e30


def padded_2(array, sides, width):
    for axis, dim in sides:
        size, length = (lax.axis_size(axis), array.shape[dim])
        up = [(i, (i + 1) % size) for i in range(size - 1)]
        down = [(j, i) for i, j in up]
        last = lax.slice_in_dim(array, length - width, length, axis=dim)
        leading = lax.slice_in_dim(array, 0, width, axis=dim)
        before = lax.ppermute(last, axis, up)
        after = lax.ppermute(leading, axis, down)
        array = jnp.concatenate([before, array, after], axis=dim)
    return array


def depthwise(lhs, rhs):
    return lax.conv_general_dilated(
        lhs,
        rhs,
        (1,),
        "VALID",
        dimension_numbers=("NWC", "WIO", "NWC"),
        feature_group_count=lhs.shape[2],
        precision=lax.Precision.HIGHEST,
    )


def general_device(
    frame_input, queries, key_proj, value_proj, out_weight, conv_weight, lengths, grad_output
):
    utt_count = frame_input.shape[0]
    frame_count = frame_input.shape[1]
    inner_width = queries.shape[2]
    head_count = inner_width // HEAD_DIM
    group_heads = max((g for g in range(1, 7) if head_count % g == 0))
    group_count = head_count // group_heads
    group_width = group_heads * HEAD_DIM
    tap_count = conv_weight.shape[0]
    half_span = (tap_count - 1) // 2
    score_scale = HEAD_DIM ** (-0.5)
    total_frames = frame_count * lax.axis_size("ctx")
    offset = lax.axis_index("ctx") * frame_count
    own_valid = (offset + jnp.arange(frame_count, dtype=jnp.int32))[None, :] < lengths[:, None]
    all_valid = jnp.arange(total_frames, dtype=jnp.int32)[None, :] < lengths[:, None]

    def grouped(values):
        row_count = values.shape[1]
        return values.reshape(utt_count, row_count, group_count, group_width).transpose(2, 0, 1, 3)

    def ungrouped(values):
        row_count = values.shape[2]
        return values.transpose(1, 2, 0, 3).reshape(utt_count, row_count, group_count * group_width)

    def split_heads(values):
        return values.reshape(utt_count, values.shape[1], group_heads, HEAD_DIM)

    def stats_grouped(values):
        row_count = values.shape[1]
        return values.reshape(utt_count, row_count, group_count, group_heads).transpose(2, 0, 3, 1)

    def masked_scores(query_block, key_block, key_mask):
        scores = (
            jnp.einsum(
                "uqgd,ukgd->ugqk", query_block, key_block, preferred_element_type=jnp.float32
            )
            * score_scale
        )
        return jnp.where(key_mask[:, None, None, :], scores, masked_score)

    taps = lax.all_gather(conv_weight, "dp", axis=1, tiled=True).astype(jnp.float32)
    panel_rows = lax.all_gather(out_weight, "dp", axis=1, tiled=True)
    weight_full = lax.all_gather(panel_rows, "ctx", axis=0, tiled=True)
    all_keys, all_values = (
        lax.all_gather(key_proj, "ctx", axis=1, tiled=True),
        lax.all_gather(value_proj, "ctx", axis=1, tiled=True),
    )
    query_groups = grouped(queries)
    key_groups = grouped(all_keys)
    value_groups = grouped(all_values)

    def forward_group(unused, items):
        query_group, key_group, value_group = items
        query_block = split_heads(query_group)
        scores = masked_scores(query_block, split_heads(key_group), all_valid)
        largest = jnp.max(scores, axis=-1)
        log_group = largest + jnp.log(jnp.sum(jnp.exp(scores - largest[..., None]), axis=-1))
        weights_low = jnp.exp(scores - log_group[..., None]).astype(jnp.bfloat16)
        attended_group = jnp.einsum(
            "ugqk,ukgd->uqgd",
            weights_low,
            split_heads(value_group),
            preferred_element_type=jnp.float32,
        )
        return (None, (log_group, attended_group.reshape(utt_count, frame_count, group_width)))

    _, (log_groups, attended_groups) = lax.scan(
        forward_group, None, (query_groups, key_groups, value_groups)
    )
    attended = ungrouped(attended_groups).astype(jnp.bfloat16)
    log_total = log_groups.transpose(1, 3, 0, 2).reshape(utt_count, frame_count, head_count)
    projected = jnp.einsum("ufe,de->ufd", attended, weight_full, preferred_element_type=jnp.float32)
    hidden = (frame_input.astype(jnp.float32) + projected).astype(jnp.bfloat16)
    masked_hidden = jnp.where(own_valid[:, :, None], hidden, jnp.zeros_like(hidden))
    padded = padded_2(masked_hidden, (("ctx", 1),), half_span).astype(jnp.float32)
    conv_sum = depthwise(padded, taps[:, None, :])
    sigmoid = jax.nn.sigmoid(conv_sum)
    block_output = (hidden.astype(jnp.float32) + conv_sum * sigmoid).astype(jnp.bfloat16)
    grad_local = grad_output.astype(jnp.float32)
    swish_slope = sigmoid * (1.0 + conv_sum * (1.0 - sigmoid))
    grad_conv = (grad_local * swish_slope).astype(jnp.bfloat16)
    grad_padded = padded_2(grad_conv, (("ctx", 1),), half_span).astype(jnp.float32)
    back_sum = depthwise(grad_padded, taps[::-1][:, None, :])
    grad_hidden = (grad_local + jnp.where(own_valid[:, :, None], back_sum, 0.0)).astype(
        jnp.bfloat16
    )
    grad_conv_wide = grad_conv.astype(jnp.float32)
    kernel_term = jnp.zeros((tap_count, conv_sum.shape[2]), jnp.float32)
    for utt_index in range(utt_count):
        kernel_term = (
            kernel_term
            + depthwise(padded[utt_index : utt_index + 1], grad_conv_wide[utt_index][:, None, :])[0]
        )
    kernel_whole = lax.psum(kernel_term.astype(jnp.bfloat16), "ctx")
    grad_conv_weight = lax.psum_scatter(kernel_whole, "dp", scatter_dimension=1, tiled=True).astype(
        jnp.float32
    )
    grad_attended = jnp.einsum(
        "ufd,de->ufe", grad_hidden, weight_full, preferred_element_type=jnp.float32
    ).astype(jnp.bfloat16)
    row_delta = jnp.sum(
        grad_attended.astype(jnp.float32).reshape(utt_count, frame_count, head_count, HEAD_DIM)
        * attended.astype(jnp.float32).reshape(utt_count, frame_count, head_count, HEAD_DIM),
        axis=-1,
    )
    grad_groups = grouped(grad_attended)

    def query_group_step(unused, items):
        query_group, key_group, value_group, grad_group, log_group, delta_group = items
        key_block = split_heads(key_group)
        weights = jnp.exp(
            masked_scores(split_heads(query_group), key_block, all_valid) - log_group[..., None]
        )
        grad_weights = jnp.einsum(
            "uqgd,ukgd->ugqk",
            split_heads(grad_group),
            split_heads(value_group),
            preferred_element_type=jnp.float32,
        )
        grad_scores = (weights * (grad_weights - delta_group[..., None])).astype(jnp.bfloat16)
        query_sum = jnp.einsum(
            "ugqk,ukgd->uqgd", grad_scores, key_block, preferred_element_type=jnp.float32
        )
        return (None, query_sum.reshape(utt_count, frame_count, group_width))

    _, query_sums = lax.scan(
        query_group_step,
        None,
        (
            query_groups,
            key_groups,
            value_groups,
            grad_groups,
            stats_grouped(log_total),
            stats_grouped(row_delta),
        ),
    )
    grad_queries = (ungrouped(query_sums) * score_scale).astype(jnp.bfloat16)
    total_log, total_delta = (
        lax.all_gather(log_total, "ctx", axis=1, tiled=True),
        lax.all_gather(row_delta, "ctx", axis=1, tiled=True),
    )
    own_key_groups = grouped(key_proj)
    own_value_groups = grouped(value_proj)
    group_zeros = jnp.zeros((group_count, utt_count, frame_count, group_width), jnp.float32)
    start_sums = (group_zeros, group_zeros)
    query_all, grad_all = (
        lax.all_gather(queries, "ctx", axis=1, tiled=True),
        lax.all_gather(grad_attended, "ctx", axis=1, tiled=True),
    )
    log_piece = stats_grouped(total_log)
    delta_piece = stats_grouped(total_delta)

    def key_group_step(unused, items):
        (
            query_group,
            grad_group,
            log_group,
            delta_group,
            key_group,
            value_group,
            key_sum,
            value_sum,
        ) = items
        query_block = split_heads(query_group)
        grad_block = split_heads(grad_group)
        weights = jnp.exp(
            masked_scores(query_block, split_heads(key_group), own_valid) - log_group[..., None]
        )
        grad_weights = jnp.einsum(
            "uqgd,ukgd->ugqk",
            grad_block,
            split_heads(value_group),
            preferred_element_type=jnp.float32,
        )
        grad_scores = (weights * (grad_weights - delta_group[..., None])).astype(jnp.bfloat16)
        key_next = key_sum + jnp.einsum(
            "ugqk,uqgd->ukgd", grad_scores, query_block, preferred_element_type=jnp.float32
        ).reshape(utt_count, frame_count, group_width)
        value_next = value_sum + jnp.einsum(
            "ugqk,uqgd->ukgd",
            weights.astype(jnp.bfloat16),
            grad_block,
            preferred_element_type=jnp.float32,
        ).reshape(utt_count, frame_count, group_width)
        return (None, (key_next, value_next))

    _, result_sums = lax.scan(
        key_group_step,
        None,
        (
            grouped(query_all),
            grouped(grad_all),
            log_piece,
            delta_piece,
            own_key_groups,
            own_value_groups,
            start_sums[0],
            start_sums[1],
        ),
    )
    key_sum, value_sum = result_sums
    grad_keys = (ungrouped(key_sum) * score_scale).astype(jnp.bfloat16)
    grad_values = ungrouped(value_sum).astype(jnp.bfloat16)
    hidden_cols = lax.slice_in_dim(
        grad_hidden, 0, weight_full.shape[0] // lax.axis_size("ctx") * lax.axis_size("ctx"), axis=2
    )
    panel_share = lax.psum_scatter(
        jnp.einsum("ufd,ufe->de", hidden_cols, attended, preferred_element_type=jnp.float32).astype(
            jnp.bfloat16
        ),
        "ctx",
        scatter_dimension=0,
        tiled=True,
    )
    grad_out_weight = lax.psum_scatter(panel_share, "dp", scatter_dimension=1, tiled=True).astype(
        jnp.float32
    )
    return (
        block_output,
        grad_hidden,
        grad_queries,
        grad_keys,
        grad_values,
        grad_out_weight,
        grad_conv_weight,
    )


LANES = 128
N_CTX = 4
N_DP = 8
TAP_PAD = 32
FLOPS_A_MICRO = 1.15e9
TAPS = 31
REACH = 15


def slot_of(index, me):
    apart = index ^ me
    return ((apart & 1) << 2) | (apart & 2) | ((apart >> 2) & 1)


def dot_tt(lhs, rhs, lhs_dim, rhs_dim):
    return lax.dot_general(
        lhs, rhs, (((lhs_dim,), (rhs_dim,)), ((), ())), preferred_element_type=jnp.float32
    )


def call_kernel(body, out_shape, ins, outs=None, scratch=(), room=40, micros=1.0):
    spaces = {
        "smem": pl.BlockSpec(memory_space=pltpu.SMEM),
        "vmem": pl.BlockSpec(memory_space=pltpu.VMEM),
        "hbm": pl.BlockSpec(memory_space=pltpu.HBM),
        "any": pl.BlockSpec(memory_space=pl.ANY),
    }
    return pl.pallas_call(
        body,
        out_shape=out_shape,
        in_specs=[spaces[space] for space in ins],
        out_specs=[spaces[space] for space in (outs or ["vmem"] * len(out_shape))],
        scratch_shapes=list(scratch),
        compiler_params=pltpu.CompilerParams(vmem_limit_bytes=room * 1024 * 1024),
        cost_estimate=pl.CostEstimate(
            flops=int(micros * FLOPS_A_MICRO), bytes_accessed=0, transcendentals=0
        ),
    )


def half_of(index):
    return lax.shift_right_logical(index, 1)


def columns(start, size):
    return pl.ds(pl.multiple_of(start, LANES), size)


def start_copies(pairs, sem):
    for number, (source, target) in enumerate(pairs):
        pltpu.make_async_copy(source, target, sem.at[number]).start()


def wait_copies(pairs, sem):
    for number, (source, target) in enumerate(pairs):
        pltpu.make_async_copy(source, target, sem.at[number]).wait()


def run_copies(pairs, sem):
    start_copies(pairs, sem)
    wait_copies(pairs, sem)


def untouched(*refs):
    pass


def gate(arrays, *awaited, micros=0.0):
    count = len(arrays)
    spec = pl.BlockSpec(memory_space=pl.ANY)
    return pl.pallas_call(
        untouched,
        out_shape=tuple(jax.ShapeDtypeStruct(array.shape, array.dtype) for array in arrays),
        in_specs=[spec] * (count + len(awaited)),
        out_specs=(spec,) * count,
        input_output_aliases={number: number for number in range(count)},
        compiler_params=pltpu.CompilerParams(vmem_limit_bytes=1024 * 1024),
        cost_estimate=pl.CostEstimate(
            flops=int(micros * FLOPS_A_MICRO), bytes_accessed=0, transcendentals=0
        ),
    )(*arrays, *awaited)


def pack_heads(query_ref, key_ref, value_ref, *rest):
    outs, sem = rest[:N_CTX], rest[N_CTX]
    half = query_ref.shape[2] // 2
    place = lax.axis_index("ctx")
    pairs = []
    for apart in (2, 3, 1, 0):
        dest = place ^ apart
        cols = columns((dest & 1) * half, half)
        for slot, ref in enumerate((query_ref, key_ref, value_ref)):
            pairs.append((ref.at[half_of(dest), :, cols], outs[apart].at[slot]))
    run_copies(pairs, sem)


def pack_weights(panel_ref, taps_ref, awaited_ref, out_ref):
    entries = panel_ref.shape[0]
    taps = taps_ref[...].astype(jnp.float32)
    high = jnp.concatenate(
        [taps[TAP_PAD // 2 :], jnp.zeros((TAP_PAD - TAPS, taps.shape[1]), jnp.float32)], axis=0
    )
    joined = jnp.concatenate([taps[: TAP_PAD // 2], high], axis=1).astype(jnp.bfloat16)
    for target in range(N_DP):
        out_ref[target, 0:entries] = panel_ref[...]
        out_ref[target, entries:] = joined


def pack_channels(frame_ref, grad_ref, awaited_ref, *rest):
    frame_outs, grad_outs, beside_ref, own_ref, sem = rest[:2], rest[2:4], *rest[4:]
    width = frame_ref.shape[2] // N_CTX
    place = lax.axis_index("ctx")
    pairs = []
    for slot, (ref, outs) in enumerate(((frame_ref, frame_outs), (grad_ref, grad_outs))):
        targets = [own_ref.at[slot], beside_ref.at[slot], outs[0], outs[1]]
        for apart in (2, 3, 1, 0):
            cols = columns((place ^ apart) * width, width)
            for utt in range(2):
                pairs.append((ref.at[utt, :, cols], targets[apart].at[utt]))
    run_copies(pairs, sem)


def unpack(*refs):
    ins, own_ref, beside_ref = refs[:N_CTX], refs[N_CTX], refs[N_CTX + 1]
    across_refs, diagonal_refs = refs[N_CTX + 2 : N_CTX + 4], refs[N_CTX + 4 : N_CTX + 6]
    heads, channels, sem = refs[N_CTX + 6 : N_CTX + 9], refs[N_CTX + 9 : N_CTX + 11], refs[-1]
    half, width = ins[0].shape[2], own_ref.shape[3]
    frames = own_ref.shape[2]
    place = lax.axis_index("ctx")
    pairs = []
    for apart in range(N_CTX):
        source = place ^ apart
        cols = columns((source & 1) * half, half)
        for slot, ref in enumerate(heads):
            pairs.append((ins[apart].at[slot], ref.at[half_of(source), :, cols]))
    for slot, ref in enumerate(channels):
        for apart in range(N_CTX):
            cols = columns((place ^ apart) * width, width)
            for utt in range(2):
                if apart < 2:
                    block = (own_ref, beside_ref)[apart].at[slot, utt]
                else:
                    block = (across_refs, diagonal_refs)[apart - 2][slot]
                    block = block.at[utt * frames : (utt + 1) * frames]
                pairs.append((block, ref.at[utt, :, cols]))
    run_copies(pairs, sem)


def head_parts(refs, slot):
    return jnp.concatenate([ref[slot] for ref in refs], axis=0)


def half_masks(rows):
    lane = lax.broadcasted_iota(jnp.int32, (rows, LANES), 1)
    low = jnp.where(lane < HEAD_DIM, 1.0, 0.0)
    return low.astype(jnp.bfloat16), (1.0 - low).astype(jnp.bfloat16)


def attend(length_ref, *refs):
    ins, attended_ref, weight_ref = refs[:N_CTX], refs[N_CTX], refs[N_CTX + 1]
    frames, half = ins[0].shape[1], ins[0].shape[2]
    rows = N_CTX * frames
    place = lax.axis_index("ctx")
    length = length_ref[half_of(place)]
    query, key, value = (head_parts(ins, slot) for slot in range(3))
    masks = half_masks(rows)
    frame = lax.broadcasted_iota(jnp.int32, (rows, rows), 0) ^ (place * frames)
    real = frame < length
    for pair in range(half // LANES):
        cols = slice(pair * LANES, (pair + 1) * LANES)
        key_pair, value_pair = key[:, cols], value[:, cols]
        parts = []
        for side in range(2):
            scores = dot_tt(key_pair, query[:, cols] * masks[side], 1, 1) * HEAD_DIM ** (-0.5)
            scores = jnp.where(real, scores, masked_score)
            largest = jnp.max(scores, axis=0, keepdims=True)
            powers = jnp.exp(scores - largest)
            total = jnp.sum(powers, axis=0, keepdims=True)
            low = (powers * (1.0 / total)).astype(jnp.bfloat16)
            weight_ref[2 * pair + side] = low
            mixed = dot_tt(value_pair, low, 0, 0)
            parts.append(mixed[side * HEAD_DIM : (side + 1) * HEAD_DIM])
        joined = jnp.concatenate(parts, axis=0).T.astype(jnp.bfloat16)
        attended_ref[:, :, cols] = joined.reshape(N_CTX, frames, LANES)


def side_blocks(slot, refs):
    return refs[0].at[slot], refs[1].at[slot], refs[2], refs[3]


def forward(length_ref, weight_ref, *refs):
    attended_refs, frame_refs = refs[:N_CTX], side_blocks(0, refs[N_CTX : 2 * N_CTX])
    out_refs = refs[2 * N_CTX : 3 * N_CTX]
    whole_ref, rows_ref, taps_ref, total_ref, masked_ref = refs[3 * N_CTX : 3 * N_CTX + 5]
    hidden_ref, frame_ref, result_ref = refs[3 * N_CTX + 5 :]
    frames, half = attended_refs[0].shape[1], attended_refs[0].shape[2]
    width = frame_ref.shape[3]
    rows = N_CTX * frames
    chunks = width // LANES
    entries = 2 * half // N_DP
    own = width // 2
    place = lax.axis_index("ctx")
    for apart in range(N_CTX):
        source = place ^ apart
        cols = columns((source & 1) * half, half)
        for block in range(N_CTX):
            whole_ref[half_of(source), block ^ source, :, cols] = attended_refs[apart][block]
        frame_ref[source] = frame_refs[apart][...]
    for part in range(N_DP):
        rows_ref[part * entries : (part + 1) * entries] = weight_ref[part, 0:entries]
    pieces = []
    for part in range(2):
        block = weight_ref[2 * place + part, entries:].astype(jnp.float32)
        pieces.append(jnp.concatenate([block[:, :own], block[:, own:]], axis=0))
    taps = jnp.concatenate(pieces, axis=1)
    for chunk in range(chunks):
        for tap in range(TAPS):
            taps_ref[chunk, tap] = jnp.broadcast_to(
                taps[tap : tap + 1, chunk * LANES : (chunk + 1) * LANES], (8, LANES)
            )
    edge = jnp.zeros((2 * chunks, 16, LANES), jnp.float32)
    masked_ref[:, 0:16, :] = edge
    masked_ref[:, 16 + rows : 32 + rows, :] = edge
    for utt in range(2):
        real = lax.broadcasted_iota(jnp.int32, (rows, LANES), 0) < length_ref[utt]
        mixed = whole_ref[utt].reshape(rows, 2 * half)
        projected = dot_tt(mixed, rows_ref[...], 1, 0)
        hidden = frame_ref[:, utt].reshape(rows, width).astype(jnp.float32) + projected
        hidden = hidden.astype(jnp.bfloat16).astype(jnp.float32)
        for chunk in range(chunks):
            piece = hidden[:, chunk * LANES : (chunk + 1) * LANES]
            hidden_ref[utt * chunks + chunk] = piece
            masked_ref[utt * chunks + chunk, 16 : 16 + rows, :] = jnp.where(real, piece, 0.0)

    def convolve(step, carry):
        utt, chunk = step // chunks, step % chunks
        cols = columns(chunk * LANES, LANES)
        shape = (frames // 8, 8, LANES)
        for block in range(N_CTX):
            base = block * frames
            total = jnp.zeros(shape, jnp.float32)
            for tap in range(TAPS):
                first = base + tap + 16 - REACH
                piece = masked_ref[step, first : first + frames, :]
                total += taps_ref[chunk, tap][None] * piece.reshape(shape)
            total = total.reshape(frames, LANES)
            total_ref[step, base : base + frames, :] = total
            outer = hidden_ref[step, base : base + frames, :] + total * jax.nn.sigmoid(total)
            result_ref[block, utt, :, cols] = outer.astype(jnp.bfloat16)
        return carry

    lax.fori_loop(0, 2 * chunks, convolve, 0)
    for apart in range(N_CTX):
        mine = result_ref[place ^ apart]
        out_refs[apart][...] = mine.reshape(out_refs[apart].shape)


def backward(length_ref, total_ref, masked_ref, taps_ref, rows_ref, *refs):
    own_ref, beside_ref = refs[:2]
    side_refs, refs = side_blocks(1, refs[2 : 2 + N_CTX]), refs[2 + N_CTX :]
    own_pair_ref, beside_pair_ref, across_ref, diagonal_ref = refs[:N_CTX]
    grad_ref, keep_ref, send_ref, sums_ref = refs[N_CTX : N_CTX + 4]
    side_ref, result_ref, cotangent_ref, tap_sum_ref = refs[N_CTX + 4 :]
    own_pair_ref[0], beside_pair_ref[0] = own_ref[...], beside_ref[...]
    utts, frames, width = own_ref.shape
    rows = N_CTX * frames
    chunks = width // LANES
    half = rows_ref.shape[0] // 2
    place = lax.axis_index("ctx")
    for apart in range(N_CTX):
        side_ref[place ^ apart] = side_refs[apart][...]
    tap_sum_ref[...] = jnp.zeros_like(tap_sum_ref)
    edge = jnp.zeros((2 * chunks, 16, LANES), jnp.float32)
    cotangent_ref[:, 0:16, :] = edge
    cotangent_ref[:, 16 + rows : 32 + rows, :] = edge

    def convolve(step, carry):
        utt, chunk = step // chunks, step % chunks
        cols = columns(chunk * LANES, LANES)
        length = length_ref[utt]
        shape = (frames // 8, 8, LANES)
        for block in range(N_CTX):
            base = block * frames
            total = total_ref[step, base : base + frames, :]
            gate = jax.nn.sigmoid(total)
            incoming = side_ref[block, utt, :, cols].astype(jnp.float32)
            slope = gate * (1.0 + total * (1.0 - gate))
            low = (incoming * slope).astype(jnp.bfloat16)
            cotangent_ref[step, 16 + base : 16 + base + frames, :] = low.astype(jnp.float32)
        for block in range(N_CTX):
            base = block * frames
            total = jnp.zeros(shape, jnp.float32)
            held = masked_ref[step, 16 + base : 16 + base + frames, :].reshape(shape)
            for tap in range(TAPS):
                first = base + 16 + REACH - tap
                piece = cotangent_ref[step, first : first + frames, :].reshape(shape)
                total += taps_ref[chunk, tap][None] * piece
                tap_sum_ref[chunk, tap] += jnp.sum(held * piece, axis=0)
            place_of = base + lax.broadcasted_iota(jnp.int32, (frames, LANES), 0)
            total = jnp.where(place_of < length, total.reshape(frames, LANES), 0.0)
            incoming = side_ref[block, utt, :, cols].astype(jnp.float32)
            low = (incoming + total).astype(jnp.bfloat16)
            result_ref[block, utt, :, cols] = low
            grad_ref[utt, base : base + frames, cols] = low
        return carry

    lax.fori_loop(0, 2 * chunks, convolve, 0)
    sums = [
        jnp.concatenate(
            [
                jnp.sum(tap_sum_ref[chunk, tap], axis=0, keepdims=True)
                for tap in range(TAP_PAD)
            ],
            axis=0,
        )
        for chunk in range(chunks)
    ]
    sums = jnp.concatenate(sums, axis=1).astype(jnp.bfloat16)
    sums_ref[...] = sums
    for ref in (across_ref, diagonal_ref):
        ref[utts * frames :, :] = sums
    for part in range(2):
        send_ref[part, rows:, :] = sums[part * TAP_PAD // 2 : (part + 1) * TAP_PAD // 2]
    for apart in range(N_CTX):
        mine = result_ref[place ^ apart]
        if apart < 2:
            (own_pair_ref, beside_pair_ref)[apart][1] = mine
        else:
            ref = (across_ref, diagonal_ref)[apart - 2]
            ref[: utts * frames, :] = mine.reshape(utts * frames, width)
        dest = place ^ apart
        mixed = dot_tt(
            grad_ref[half_of(dest)],
            rows_ref[pl.ds(pl.multiple_of((dest & 1) * half, half), half)],
            1,
            1,
        ).astype(jnp.bfloat16)
        ref = send_ref if apart % 2 else keep_ref
        for block in range(N_CTX):
            first = pl.multiple_of((block ^ dest) * frames, frames)
            ref[apart // 2, pl.ds(first, frames), :] = mixed[block * frames : (block + 1) * frames]


def make_panels(whole_ref, grad_ref, awaited_ref, panel_ref):
    rows, half = grad_ref.shape[1], whole_ref.shape[3] // 2
    entries = 2 * half // N_DP
    group = lax.axis_index("dp")
    for side in range(2):
        panel = 0.0
        for utt in range(2):
            mixed = whole_ref[utt, :, :, side * half : (side + 1) * half].reshape(rows, half)
            panel += dot_tt(mixed, grad_ref[utt], 0, 0)
        panel = panel.astype(jnp.bfloat16)
        for part in range(N_DP // 2):
            panel_ref[slot_of(side * N_DP // 2 + part, group)] = panel[
                part * entries : (part + 1) * entries
            ]


def total_of(in_ref, out_ref):
    total = in_ref[0].astype(jnp.float32)
    for source in range(1, N_DP):
        total += in_ref[source].astype(jnp.float32)
    out_ref[...] = total


def make_tap_slots(sums_ref, came_ref, across_ref, diagonal_ref, awaited_ref, out_ref):
    own = sums_ref.shape[1] // 2
    rows, start = came_ref.shape[1] - TAP_PAD // 2, across_ref.shape[0] - TAP_PAD
    place = lax.axis_index("ctx")
    pieces = [
        sums_ref[...],
        jnp.concatenate([came_ref[0, rows:, :], came_ref[1, rows:, :]], axis=0),
        across_ref[start:, :],
        diagonal_ref[start:, :],
    ]
    for apart, piece in enumerate(pieces):
        block = piece.astype(jnp.float32)
        for part in range(2):
            mine = block[:, part * own : (part + 1) * own]
            mine = jnp.concatenate([mine[: TAP_PAD // 2], mine[TAP_PAD // 2 :]], axis=1)
            out_ref[2 * (place ^ apart) + part] = mine.astype(jnp.bfloat16)


def relay(keep_ref, came_ref, out_ref):
    rows = keep_ref.shape[1]
    total = keep_ref[1].astype(jnp.float32) + came_ref[1, 0:rows, :].astype(jnp.float32)
    out_ref[...] = total.astype(jnp.bfloat16)


def attend_back(weight_ref, keep_ref, came_ref, far_ref, *refs):
    ins, out_refs = refs[:N_CTX], refs[N_CTX:]
    frames, half = ins[0].shape[1], ins[0].shape[2]
    rows = N_CTX * frames
    query, key, value = (head_parts(ins, slot) for slot in range(3))
    masks = half_masks(rows)
    scale = HEAD_DIM ** (-0.5)
    arriving = keep_ref[0].astype(jnp.float32) + came_ref[0, 0:rows, :].astype(jnp.float32)
    arriving = (arriving + far_ref[...].astype(jnp.float32)).astype(jnp.bfloat16)
    low_lanes = lax.broadcasted_iota(jnp.int32, (rows, LANES), 1) < HEAD_DIM
    for pair in range(half // LANES):
        cols = slice(pair * LANES, (pair + 1) * LANES)
        key_pair, value_pair = key[:, cols], value[:, cols]
        query_pair, grad_pair = query[:, cols], arriving[:, cols]
        query_parts, key_parts, value_parts = [], [], []
        for side in range(2):
            low = weight_ref[2 * pair + side]
            weights = low.astype(jnp.float32)
            moved = weights * dot_tt(value_pair, grad_pair * masks[side], 1, 1)
            delta = jnp.sum(moved, axis=0, keepdims=True)
            grad_scores = (moved - weights * delta).astype(jnp.bfloat16)
            value_parts.append(dot_tt(low, grad_pair, 1, 0))
            key_parts.append(dot_tt(grad_scores, query_pair, 1, 0))
            mixed = dot_tt(key_pair, grad_scores, 0, 0)
            query_parts.append(mixed[side * HEAD_DIM : (side + 1) * HEAD_DIM])
        query_sum = (jnp.concatenate(query_parts, axis=0).T * scale).astype(jnp.bfloat16)
        key_sum = (jnp.where(low_lanes, key_parts[0], key_parts[1]) * scale).astype(jnp.bfloat16)
        value_sum = jnp.where(low_lanes, value_parts[0], value_parts[1]).astype(jnp.bfloat16)
        for slot, total in enumerate((query_sum, key_sum, value_sum)):
            for apart in range(N_CTX):
                out_refs[apart][slot, :, cols] = total[apart * frames : (apart + 1) * frames]


def swapped(array, bit):
    return lax.ppermute(array, "dp", [(i, i ^ bit) for i in range(N_DP)])


def dealt(slots):
    return lax.all_to_all(slots, "dp", 0, 0, tiled=True)


def crossed(array, apart):
    return lax.ppermute(array, "ctx", [(i, i ^ apart) for i in range(N_CTX)])


def traded(blocks):
    came = {apart: crossed(blocks[apart], apart) for apart in (2, 3, 1)}
    return [blocks[0]] + [came[apart] for apart in (1, 2, 3)]


def per_device(
    frame_input, queries, key_proj, value_proj, out_weight, conv_weight, lengths, grad_output
):
    utts, frames, wide = frame_input.shape
    inner = queries.shape[2]
    half, width = inner // 2, wide // N_CTX
    rows = N_CTX * frames
    chunks = width // LANES
    low, f32 = jnp.bfloat16, jnp.float32
    shape = jax.ShapeDtypeStruct
    entries = out_weight.shape[1]
    tap_count = conv_weight.shape[0]
    dma = pltpu.SemaphoreType.DMA
    head_block = shape((3, frames, half), low)
    channel_block = shape((utts, frames, width), low)

    blocks = call_kernel(
        pack_heads,
        (head_block,) * N_CTX,
        ["hbm"] * 3,
        scratch=[dma((3 * N_CTX,))],
        room=63,
    )(queries, key_proj, value_proj)
    packed = traded(blocks)
    (shards,) = call_kernel(
        pack_weights,
        (shape((N_DP, entries + TAP_PAD // 2, width), low),),
        ["vmem"] * 2 + ["any"],
    )(out_weight.T, conv_weight, packed[1])
    shards = dealt(shards)
    pair_block = shape((2, utts, frames, width), low)
    *sides, beside_sides, own_sides = call_kernel(
        pack_channels,
        (channel_block,) * 4 + (pair_block,) * 2,
        ["hbm"] * 2 + ["any"],
        scratch=[dma((4 * N_CTX,))],
    )(frame_input, grad_output, blocks[0])
    frame_across, frame_diagonal = crossed(sides[0], 2), crossed(sides[1], 3)
    beside_sides = crossed(beside_sides, 1)
    attended, weights = call_kernel(
        attend,
        (
            shape((N_CTX, frames, half), low),
            shape((half // HEAD_DIM, rows, rows), low),
        ),
        ["smem"] + ["vmem"] * N_CTX,
        micros=3.0,
    )(lengths, *packed)
    (attended,) = gate([attended], frame_across, frame_diagonal, micros=20.0)
    across = crossed(attended, 2)
    beside = crossed(attended, 1)
    diagonal = crossed(across, 1)
    grad_across, grad_diagonal = crossed(sides[2], 2), crossed(sides[3], 3)
    frame_blocks = (own_sides, beside_sides, frame_across, frame_diagonal)
    forward_out = call_kernel(
        forward,
        (channel_block,) * 2
        + (shape((utts * frames, width), low),) * 2
        + (
            shape((utts, N_CTX, frames, inner), low),
            shape((inner, width), low),
            shape((chunks, TAP_PAD, 8, LANES), f32),
            shape((utts * chunks, rows, LANES), f32),
            shape((utts * chunks, rows + 32, LANES), f32),
        ),
        ["smem"] + ["vmem"] * (1 + 2 * N_CTX),
        scratch=[
            pltpu.VMEM((utts * chunks, rows, LANES), f32),
            pltpu.VMEM((N_CTX, utts, frames, width), low),
            pltpu.VMEM((N_CTX, utts, frames, width), low),
        ],
        micros=3.2,
    )(lengths, shards, attended, beside, across, diagonal, *frame_blocks)
    output_across, output_diagonal = crossed(forward_out[2], 2), crossed(forward_out[3], 3)
    whole, weight_rows, taps, totals, masked = forward_out[N_CTX:]
    grad_blocks = gate([grad_across, grad_diagonal], totals, micros=10.0)
    grad_blocks = (own_sides, beside_sides, *grad_blocks)
    backward_out = call_kernel(
        backward,
        (pair_block,) * 2
        + (shape((utts * frames + TAP_PAD, width), low),) * 2
        + (
            shape((utts, rows, width), low),
            shape((2, rows, half), low),
            shape((2, rows + TAP_PAD // 2, half), low),
            shape((TAP_PAD, width), low),
        ),
        ["smem"] + ["vmem"] * (6 + N_CTX),
        scratch=[
            pltpu.VMEM((N_CTX, utts, frames, width), low),
            pltpu.VMEM((N_CTX, utts, frames, width), low),
            pltpu.VMEM((utts * chunks, rows + 32, LANES), f32),
            pltpu.VMEM((chunks, TAP_PAD, 8, LANES), f32),
        ],
        micros=5.2,
    )(lengths, totals, masked, taps, weight_rows, *forward_out[:2], *grad_blocks)
    grad_hidden, keep, send, sums = backward_out[N_CTX:]
    (send,) = gate([send], output_across, output_diagonal)
    came = crossed(send, 1)
    (far,) = call_kernel(
        relay, (shape((rows, half), low),), ["vmem"] * 2, micros=0.2
    )(keep, came)
    (panels,) = call_kernel(
        make_panels,
        (shape((N_DP, entries, width), low),),
        ["vmem"] * 2 + ["any"],
        micros=0.7,
    )(whole, grad_hidden, far)

    def halved(slots, bit):
        count = slots.shape[0] // 2
        return (slots[:count].astype(f32) + swapped(slots[count:], bit).astype(f32)).astype(low)

    panels = halved(halved(panels, 1), 2)
    input_blocks = gate(backward_out[2:4], far)
    far = crossed(far, 2)
    input_across, input_diagonal = crossed(input_blocks[0], 2), crossed(input_blocks[1], 3)
    back_blocks = call_kernel(
        attend_back,
        (head_block,) * N_CTX,
        ["vmem"] * (4 + N_CTX),
        micros=2.2,
    )(weights, keep, came, far, *packed)
    grad_blocks = traded(gate(back_blocks, input_across))
    own_pair, beside_pair = backward_out[:2]
    (beside_pair,) = gate([beside_pair], grad_blocks[1])
    beside_pair = crossed(beside_pair, 1)

    def summed(slots, micros):
        return call_kernel(
            total_of, (shape(slots.shape[1:], f32),), ["vmem"], micros=micros
        )(slots)[0]

    (tap_slots,) = call_kernel(
        make_tap_slots,
        (shape((N_DP, TAP_PAD // 2, width), low),),
        ["vmem"] * 4 + ["any"],
        micros=0.2,
    )(sums, came, input_across, input_diagonal, grad_blocks[1])

    tap_sums = summed(dealt(tap_slots), 1.0)
    (panels,) = gate([panels], grad_blocks[1])
    grad_out_weight = (panels[0].astype(f32) + swapped(panels[1], 4).astype(f32)).T

    unpacked = call_kernel(
        unpack,
        (shape((utts, frames, inner), low),) * 3 + (shape((utts, frames, wide), low),) * 2,
        ["any"] * (N_CTX + 6),
        ["hbm"] * 5,
        [dma((7 * N_CTX + 4 * N_CTX,))],
        micros=1.0,
    )(
        *grad_blocks,
        own_pair,
        beside_pair,
        output_across,
        input_across,
        output_diagonal,
        input_diagonal,
    )
    grad_queries, grad_keys, grad_values, block_output, grad_input = unpacked
    own = width // 2
    grad_taps = jnp.concatenate([tap_sums[:, :own], tap_sums[:, own:]], axis=0)[:tap_count]
    return (
        block_output,
        grad_input,
        grad_queries,
        grad_keys,
        grad_values,
        grad_out_weight,
        grad_taps,
    )


def chosen(sizes, *arrays):
    frame_input, queries, out_weight, conv_weight = (arrays[i] for i in (0, 1, 4, 5))
    utts, frames, wide = frame_input.shape
    inner = queries.shape[2]
    fits = (
        sizes == (N_DP, N_CTX)
        and utts == 2
        and frames == 64
        and wide % (N_CTX * LANES) == 0
        and inner % (2 * LANES) == 0
        and inner // N_DP % 16 == 0
        and inner // 2 == wide // N_CTX
        and conv_weight.shape == (TAPS, wide // N_DP)
        and out_weight.shape == (wide // N_CTX, inner // N_DP)
    )
    return (per_device if fits else general_device)(*arrays)


def solution(mesh):
    placed = (
        P("dp", "ctx", None),
        P("dp", "ctx", None),
        P("dp", "ctx", None),
        P("dp", "ctx", None),
        P("ctx", "dp"),
        P(None, "dp"),
        P("dp"),
        P("dp", "ctx", None),
    )
    sizes = (mesh.shape["dp"], mesh.shape["ctx"])
    return jax.shard_map(
        functools.partial(chosen, sizes),
        mesh=mesh,
        in_specs=placed,
        out_specs=(
            P("dp", "ctx", None),
            P("dp", "ctx", None),
            P("dp", "ctx", None),
            P("dp", "ctx", None),
            P("dp", "ctx", None),
            P("ctx", "dp"),
            P(None, "dp"),
        ),
        check_vma=False,
    )
```

```python
import functools

import jax
import jax.numpy as jnp
from jax import lax
from jax.experimental import pallas as pl
from jax.experimental.pallas import tpu as pltpu
from jax.sharding import PartitionSpec as P

HEAD_DIM = 64


masked_score = -1e30


def padded_2(array, sides, width):
    for axis, dim in sides:
        size, length = (lax.axis_size(axis), array.shape[dim])
        up = [(i, (i + 1) % size) for i in range(size - 1)]
        down = [(j, i) for i, j in up]
        last = lax.slice_in_dim(array, length - width, length, axis=dim)
        leading = lax.slice_in_dim(array, 0, width, axis=dim)
        before = lax.ppermute(last, axis, up)
        after = lax.ppermute(leading, axis, down)
        array = jnp.concatenate([before, array, after], axis=dim)
    return array


def depthwise(lhs, rhs):
    return lax.conv_general_dilated(
        lhs,
        rhs,
        (1,),
        "VALID",
        dimension_numbers=("NWC", "WIO", "NWC"),
        feature_group_count=lhs.shape[2],
        precision=lax.Precision.HIGHEST,
    )


def general_device(
    frame_input, queries, key_proj, value_proj, out_weight, conv_weight, lengths, grad_output
):
    utt_count = frame_input.shape[0]
    frame_count = frame_input.shape[1]
    inner_width = queries.shape[2]
    head_count = inner_width // HEAD_DIM
    group_heads = max((g for g in range(1, 7) if head_count % g == 0))
    group_count = head_count // group_heads
    group_width = group_heads * HEAD_DIM
    tap_count = conv_weight.shape[0]
    half_span = (tap_count - 1) // 2
    score_scale = HEAD_DIM ** (-0.5)
    total_frames = frame_count * lax.axis_size("ctx")
    offset = lax.axis_index("ctx") * frame_count
    own_valid = (offset + jnp.arange(frame_count, dtype=jnp.int32))[None, :] < lengths[:, None]
    all_valid = jnp.arange(total_frames, dtype=jnp.int32)[None, :] < lengths[:, None]

    def grouped(values):
        row_count = values.shape[1]
        return values.reshape(utt_count, row_count, group_count, group_width).transpose(2, 0, 1, 3)

    def ungrouped(values):
        row_count = values.shape[2]
        return values.transpose(1, 2, 0, 3).reshape(utt_count, row_count, group_count * group_width)

    def split_heads(values):
        return values.reshape(utt_count, values.shape[1], group_heads, HEAD_DIM)

    def stats_grouped(values):
        row_count = values.shape[1]
        return values.reshape(utt_count, row_count, group_count, group_heads).transpose(2, 0, 3, 1)

    def masked_scores(query_block, key_block, key_mask):
        scores = (
            jnp.einsum(
                "uqgd,ukgd->ugqk", query_block, key_block, preferred_element_type=jnp.float32
            )
            * score_scale
        )
        return jnp.where(key_mask[:, None, None, :], scores, masked_score)

    taps = lax.all_gather(conv_weight, "dp", axis=1, tiled=True).astype(jnp.float32)
    panel_rows = lax.all_gather(out_weight, "dp", axis=1, tiled=True)
    weight_full = lax.all_gather(panel_rows, "ctx", axis=0, tiled=True)
    all_keys, all_values = (
        lax.all_gather(key_proj, "ctx", axis=1, tiled=True),
        lax.all_gather(value_proj, "ctx", axis=1, tiled=True),
    )
    query_groups = grouped(queries)
    key_groups = grouped(all_keys)
    value_groups = grouped(all_values)

    def forward_group(unused, items):
        query_group, key_group, value_group = items
        query_block = split_heads(query_group)
        scores = masked_scores(query_block, split_heads(key_group), all_valid)
        largest = jnp.max(scores, axis=-1)
        log_group = largest + jnp.log(jnp.sum(jnp.exp(scores - largest[..., None]), axis=-1))
        weights_low = jnp.exp(scores - log_group[..., None]).astype(jnp.bfloat16)
        attended_group = jnp.einsum(
            "ugqk,ukgd->uqgd",
            weights_low,
            split_heads(value_group),
            preferred_element_type=jnp.float32,
        )
        return (None, (log_group, attended_group.reshape(utt_count, frame_count, group_width)))

    _, (log_groups, attended_groups) = lax.scan(
        forward_group, None, (query_groups, key_groups, value_groups)
    )
    attended = ungrouped(attended_groups).astype(jnp.bfloat16)
    log_total = log_groups.transpose(1, 3, 0, 2).reshape(utt_count, frame_count, head_count)
    projected = jnp.einsum("ufe,de->ufd", attended, weight_full, preferred_element_type=jnp.float32)
    hidden = (frame_input.astype(jnp.float32) + projected).astype(jnp.bfloat16)
    masked_hidden = jnp.where(own_valid[:, :, None], hidden, jnp.zeros_like(hidden))
    padded = padded_2(masked_hidden, (("ctx", 1),), half_span).astype(jnp.float32)
    conv_sum = depthwise(padded, taps[:, None, :])
    sigmoid = jax.nn.sigmoid(conv_sum)
    block_output = (hidden.astype(jnp.float32) + conv_sum * sigmoid).astype(jnp.bfloat16)
    grad_local = grad_output.astype(jnp.float32)
    swish_slope = sigmoid * (1.0 + conv_sum * (1.0 - sigmoid))
    grad_conv = (grad_local * swish_slope).astype(jnp.bfloat16)
    grad_padded = padded_2(grad_conv, (("ctx", 1),), half_span).astype(jnp.float32)
    back_sum = depthwise(grad_padded, taps[::-1][:, None, :])
    grad_hidden = (grad_local + jnp.where(own_valid[:, :, None], back_sum, 0.0)).astype(
        jnp.bfloat16
    )
    grad_conv_wide = grad_conv.astype(jnp.float32)
    kernel_term = jnp.zeros((tap_count, conv_sum.shape[2]), jnp.float32)
    for utt_index in range(utt_count):
        kernel_term = (
            kernel_term
            + depthwise(padded[utt_index : utt_index + 1], grad_conv_wide[utt_index][:, None, :])[0]
        )
    kernel_whole = lax.psum(kernel_term.astype(jnp.bfloat16), "ctx")
    grad_conv_weight = lax.psum_scatter(kernel_whole, "dp", scatter_dimension=1, tiled=True).astype(
        jnp.float32
    )
    grad_attended = jnp.einsum(
        "ufd,de->ufe", grad_hidden, weight_full, preferred_element_type=jnp.float32
    ).astype(jnp.bfloat16)
    row_delta = jnp.sum(
        grad_attended.astype(jnp.float32).reshape(utt_count, frame_count, head_count, HEAD_DIM)
        * attended.astype(jnp.float32).reshape(utt_count, frame_count, head_count, HEAD_DIM),
        axis=-1,
    )
    grad_groups = grouped(grad_attended)

    def query_group_step(unused, items):
        query_group, key_group, value_group, grad_group, log_group, delta_group = items
        key_block = split_heads(key_group)
        weights = jnp.exp(
            masked_scores(split_heads(query_group), key_block, all_valid) - log_group[..., None]
        )
        grad_weights = jnp.einsum(
            "uqgd,ukgd->ugqk",
            split_heads(grad_group),
            split_heads(value_group),
            preferred_element_type=jnp.float32,
        )
        grad_scores = (weights * (grad_weights - delta_group[..., None])).astype(jnp.bfloat16)
        query_sum = jnp.einsum(
            "ugqk,ukgd->uqgd", grad_scores, key_block, preferred_element_type=jnp.float32
        )
        return (None, query_sum.reshape(utt_count, frame_count, group_width))

    _, query_sums = lax.scan(
        query_group_step,
        None,
        (
            query_groups,
            key_groups,
            value_groups,
            grad_groups,
            stats_grouped(log_total),
            stats_grouped(row_delta),
        ),
    )
    grad_queries = (ungrouped(query_sums) * score_scale).astype(jnp.bfloat16)
    total_log, total_delta = (
        lax.all_gather(log_total, "ctx", axis=1, tiled=True),
        lax.all_gather(row_delta, "ctx", axis=1, tiled=True),
    )
    own_key_groups = grouped(key_proj)
    own_value_groups = grouped(value_proj)
    group_zeros = jnp.zeros((group_count, utt_count, frame_count, group_width), jnp.float32)
    start_sums = (group_zeros, group_zeros)
    query_all, grad_all = (
        lax.all_gather(queries, "ctx", axis=1, tiled=True),
        lax.all_gather(grad_attended, "ctx", axis=1, tiled=True),
    )
    log_piece = stats_grouped(total_log)
    delta_piece = stats_grouped(total_delta)

    def key_group_step(unused, items):
        (
            query_group,
            grad_group,
            log_group,
            delta_group,
            key_group,
            value_group,
            key_sum,
            value_sum,
        ) = items
        query_block = split_heads(query_group)
        grad_block = split_heads(grad_group)
        weights = jnp.exp(
            masked_scores(query_block, split_heads(key_group), own_valid) - log_group[..., None]
        )
        grad_weights = jnp.einsum(
            "uqgd,ukgd->ugqk",
            grad_block,
            split_heads(value_group),
            preferred_element_type=jnp.float32,
        )
        grad_scores = (weights * (grad_weights - delta_group[..., None])).astype(jnp.bfloat16)
        key_next = key_sum + jnp.einsum(
            "ugqk,uqgd->ukgd", grad_scores, query_block, preferred_element_type=jnp.float32
        ).reshape(utt_count, frame_count, group_width)
        value_next = value_sum + jnp.einsum(
            "ugqk,uqgd->ukgd",
            weights.astype(jnp.bfloat16),
            grad_block,
            preferred_element_type=jnp.float32,
        ).reshape(utt_count, frame_count, group_width)
        return (None, (key_next, value_next))

    _, result_sums = lax.scan(
        key_group_step,
        None,
        (
            grouped(query_all),
            grouped(grad_all),
            log_piece,
            delta_piece,
            own_key_groups,
            own_value_groups,
            start_sums[0],
            start_sums[1],
        ),
    )
    key_sum, value_sum = result_sums
    grad_keys = (ungrouped(key_sum) * score_scale).astype(jnp.bfloat16)
    grad_values = ungrouped(value_sum).astype(jnp.bfloat16)
    hidden_cols = lax.slice_in_dim(
        grad_hidden, 0, weight_full.shape[0] // lax.axis_size("ctx") * lax.axis_size("ctx"), axis=2
    )
    panel_share = lax.psum_scatter(
        jnp.einsum("ufd,ufe->de", hidden_cols, attended, preferred_element_type=jnp.float32).astype(
            jnp.bfloat16
        ),
        "ctx",
        scatter_dimension=0,
        tiled=True,
    )
    grad_out_weight = lax.psum_scatter(panel_share, "dp", scatter_dimension=1, tiled=True).astype(
        jnp.float32
    )
    return (
        block_output,
        grad_hidden,
        grad_queries,
        grad_keys,
        grad_values,
        grad_out_weight,
        grad_conv_weight,
    )


LANES = 128
N_CTX = 4
N_DP = 8
TAP_PAD = 32
FLOPS_A_MICRO = 1.15e9
TAPS = 31
REACH = 15


def slot_of(index, me):
    apart = index ^ me
    return ((apart & 1) << 2) | (apart & 2) | ((apart >> 2) & 1)


def dot_tt(lhs, rhs, lhs_dim, rhs_dim):
    return lax.dot_general(
        lhs, rhs, (((lhs_dim,), (rhs_dim,)), ((), ())), preferred_element_type=jnp.float32
    )


def call_kernel(body, out_shape, ins, outs=None, scratch=(), room=40, micros=1.0):
    spaces = {
        "smem": pl.BlockSpec(memory_space=pltpu.SMEM),
        "vmem": pl.BlockSpec(memory_space=pltpu.VMEM),
        "hbm": pl.BlockSpec(memory_space=pltpu.HBM),
        "any": pl.BlockSpec(memory_space=pl.ANY),
    }
    return pl.pallas_call(
        body,
        out_shape=out_shape,
        in_specs=[spaces[space] for space in ins],
        out_specs=[spaces[space] for space in (outs or ["vmem"] * len(out_shape))],
        scratch_shapes=list(scratch),
        compiler_params=pltpu.CompilerParams(vmem_limit_bytes=room * 1024 * 1024),
        cost_estimate=pl.CostEstimate(
            flops=int(micros * FLOPS_A_MICRO), bytes_accessed=0, transcendentals=0
        ),
    )


def half_of(index):
    return lax.shift_right_logical(index, 1)


def columns(start, size):
    return pl.ds(pl.multiple_of(start, LANES), size)


def start_copies(pairs, sem):
    for number, (source, target) in enumerate(pairs):
        pltpu.make_async_copy(source, target, sem.at[number]).start()


def wait_copies(pairs, sem):
    for number, (source, target) in enumerate(pairs):
        pltpu.make_async_copy(source, target, sem.at[number]).wait()


def run_copies(pairs, sem):
    start_copies(pairs, sem)
    wait_copies(pairs, sem)


def untouched(*refs):
    pass


def gate(arrays, *awaited, micros=0.0):
    count = len(arrays)
    spec = pl.BlockSpec(memory_space=pl.ANY)
    return pl.pallas_call(
        untouched,
        out_shape=tuple(jax.ShapeDtypeStruct(array.shape, array.dtype) for array in arrays),
        in_specs=[spec] * (count + len(awaited)),
        out_specs=(spec,) * count,
        input_output_aliases={number: number for number in range(count)},
        compiler_params=pltpu.CompilerParams(vmem_limit_bytes=1024 * 1024),
        cost_estimate=pl.CostEstimate(
            flops=int(micros * FLOPS_A_MICRO), bytes_accessed=0, transcendentals=0
        ),
    )(*arrays, *awaited)


def pack_heads(query_ref, key_ref, value_ref, *rest):
    outs, sem = rest[:N_CTX], rest[N_CTX]
    half = query_ref.shape[2] // 2
    place = lax.axis_index("ctx")
    pairs = []
    for apart in (2, 3, 1, 0):
        dest = place ^ apart
        cols = columns((dest & 1) * half, half)
        for slot, ref in enumerate((query_ref, key_ref, value_ref)):
            pairs.append((ref.at[half_of(dest), :, cols], outs[apart].at[slot]))
    run_copies(pairs, sem)


def pack_weights(panel_ref, taps_ref, awaited_ref, out_ref):
    entries = panel_ref.shape[0]
    taps = taps_ref[...].astype(jnp.float32)
    high = jnp.concatenate(
        [taps[TAP_PAD // 2 :], jnp.zeros((TAP_PAD - TAPS, taps.shape[1]), jnp.float32)], axis=0
    )
    joined = jnp.concatenate([taps[: TAP_PAD // 2], high], axis=1).astype(jnp.bfloat16)
    for target in range(N_DP):
        out_ref[target, 0:entries] = panel_ref[...]
        out_ref[target, entries:] = joined


def pack_channels(frame_ref, grad_ref, awaited_ref, *rest):
    frame_outs, grad_outs, beside_ref, own_ref, sem = rest[:2], rest[2:4], *rest[4:]
    width = frame_ref.shape[2] // N_CTX
    place = lax.axis_index("ctx")
    pairs = []
    for slot, (ref, outs) in enumerate(((frame_ref, frame_outs), (grad_ref, grad_outs))):
        targets = [own_ref.at[slot], beside_ref.at[slot], outs[0], outs[1]]
        for apart in (2, 3, 1, 0):
            cols = columns((place ^ apart) * width, width)
            for utt in range(2):
                pairs.append((ref.at[utt, :, cols], targets[apart].at[utt]))
    run_copies(pairs, sem)


def unpack(*refs):
    ins, refs = refs[:N_CTX], refs[N_CTX:]
    own_ref, beside_ref, output_ref, input_ref = refs[:4]
    heads, channels, sem = refs[4:7], refs[7:9], refs[9]
    half, width = ins[0].shape[2], own_ref.shape[3]
    frames = own_ref.shape[2]
    place = lax.axis_index("ctx")
    pairs = []
    for apart in range(N_CTX):
        source = place ^ apart
        cols = columns((source & 1) * half, half)
        for slot, ref in enumerate(heads):
            pairs.append((ins[apart].at[slot], ref.at[half_of(source), :, cols]))
    for slot, ref in enumerate(channels):
        for utt in range(2):
            part = pl.ds(utt * frames, frames)
            blocks = (
                own_ref.at[slot, utt],
                beside_ref.at[slot, part],
                (output_ref, input_ref)[slot].at[0, part],
                beside_ref.at[2 + slot, part],
            )
            for apart, block in enumerate(blocks):
                cols = columns((place ^ apart) * width, width)
                pairs.append((block, ref.at[utt, :, cols]))
    run_copies(pairs, sem)


def head_parts(refs, slot):
    return jnp.concatenate([ref[slot] for ref in refs], axis=0)


def half_masks(rows):
    lane = lax.broadcasted_iota(jnp.int32, (rows, LANES), 1)
    low = jnp.where(lane < HEAD_DIM, 1.0, 0.0)
    return low.astype(jnp.bfloat16), (1.0 - low).astype(jnp.bfloat16)


def attend(length_ref, *refs):
    ins, attended_ref, weight_ref = refs[:N_CTX], refs[N_CTX], refs[N_CTX + 1]
    frames, half = ins[0].shape[1], ins[0].shape[2]
    rows = N_CTX * frames
    place = lax.axis_index("ctx")
    length = length_ref[half_of(place)]
    query, key, value = (head_parts(ins, slot) for slot in range(3))
    masks = half_masks(rows)
    frame = lax.broadcasted_iota(jnp.int32, (rows, rows), 0) ^ (place * frames)
    real = frame < length
    for pair in range(half // LANES):
        cols = slice(pair * LANES, (pair + 1) * LANES)
        key_pair, value_pair = key[:, cols], value[:, cols]
        parts = []
        for side in range(2):
            scores = dot_tt(key_pair, query[:, cols] * masks[side], 1, 1) * HEAD_DIM ** (-0.5)
            scores = jnp.where(real, scores, masked_score)
            largest = jnp.max(scores, axis=0, keepdims=True)
            powers = jnp.exp(scores - largest)
            total = jnp.sum(powers, axis=0, keepdims=True)
            low = (powers * (1.0 / total)).astype(jnp.bfloat16)
            weight_ref[2 * pair + side] = low
            mixed = dot_tt(value_pair, low, 0, 0)
            parts.append(mixed[side * HEAD_DIM : (side + 1) * HEAD_DIM])
        joined = jnp.concatenate(parts, axis=0).T.astype(jnp.bfloat16)
        attended_ref[:, :, cols] = joined.reshape(N_CTX, frames, LANES)


def side_blocks(slot, refs):
    return refs[0].at[slot], refs[1].at[slot], refs[2], refs[3]


def forward(length_ref, weight_ref, *refs):
    attended_refs, frame_refs = refs[:N_CTX], side_blocks(0, refs[N_CTX : 2 * N_CTX])
    out_refs, refs = refs[2 * N_CTX : 2 * N_CTX + 3], refs[2 * N_CTX + 3 :]
    whole_ref, rows_ref, taps_ref, total_ref, masked_ref = refs[:5]
    hidden_ref, frame_ref, result_ref = refs[5:]
    frames, half = attended_refs[0].shape[1], attended_refs[0].shape[2]
    width = frame_ref.shape[3]
    rows = N_CTX * frames
    chunks = width // LANES
    entries = 2 * half // N_DP
    own = width // 2
    place = lax.axis_index("ctx")
    for apart in range(N_CTX):
        source = place ^ apart
        cols = columns((source & 1) * half, half)
        for block in range(N_CTX):
            whole_ref[half_of(source), block ^ source, :, cols] = attended_refs[apart][block]
        frame_ref[source] = frame_refs[apart][...]
    for part in range(N_DP):
        rows_ref[part * entries : (part + 1) * entries] = weight_ref[part, 0:entries]
    pieces = []
    for part in range(2):
        block = weight_ref[2 * place + part, entries:].astype(jnp.float32)
        pieces.append(jnp.concatenate([block[:, :own], block[:, own:]], axis=0))
    taps = jnp.concatenate(pieces, axis=1)
    for chunk in range(chunks):
        for tap in range(TAPS):
            taps_ref[chunk, tap] = jnp.broadcast_to(
                taps[tap : tap + 1, chunk * LANES : (chunk + 1) * LANES], (8, LANES)
            )
    edge = jnp.zeros((2 * chunks, 16, LANES), jnp.float32)
    masked_ref[:, 0:16, :] = edge
    masked_ref[:, 16 + rows : 32 + rows, :] = edge
    for utt in range(2):
        real = lax.broadcasted_iota(jnp.int32, (rows, LANES), 0) < length_ref[utt]
        mixed = whole_ref[utt].reshape(rows, 2 * half)
        projected = dot_tt(mixed, rows_ref[...], 1, 0)
        hidden = frame_ref[:, utt].reshape(rows, width).astype(jnp.float32) + projected
        hidden = hidden.astype(jnp.bfloat16).astype(jnp.float32)
        for chunk in range(chunks):
            piece = hidden[:, chunk * LANES : (chunk + 1) * LANES]
            hidden_ref[utt * chunks + chunk] = piece
            masked_ref[utt * chunks + chunk, 16 : 16 + rows, :] = jnp.where(real, piece, 0.0)

    def convolve(step, carry):
        utt, chunk = step // chunks, step % chunks
        cols = columns(chunk * LANES, LANES)
        shape = (frames // 8, 8, LANES)
        for block in range(N_CTX):
            base = block * frames
            total = jnp.zeros(shape, jnp.float32)
            for tap in range(TAPS):
                first = base + tap + 16 - REACH
                piece = masked_ref[step, first : first + frames, :]
                total += taps_ref[chunk, tap][None] * piece.reshape(shape)
            total = total.reshape(frames, LANES)
            total_ref[step, base : base + frames, :] = total
            outer = hidden_ref[step, base : base + frames, :] + total * jax.nn.sigmoid(total)
            result_ref[block, utt, :, cols] = outer.astype(jnp.bfloat16)
        return carry

    lax.fori_loop(0, 2 * chunks, convolve, 0)
    for apart in range(2):
        out_refs[apart][...] = result_ref[place ^ apart]
        out_refs[2][apart] = result_ref[place ^ (2 + apart)].reshape(2 * frames, width)


def backward(length_ref, total_ref, masked_ref, taps_ref, rows_ref, *refs):
    own_ref, beside_ref = refs[:2]
    side_refs, refs = side_blocks(1, refs[2 : 2 + N_CTX]), refs[2 + N_CTX :]
    own_pair_ref, beside_pair_ref, across_ref = refs[:3]
    grad_ref, keep_ref, send_ref, sums_ref = refs[3:7]
    side_ref, result_ref, cotangent_ref, tap_sum_ref = refs[7:]
    own_pair_ref[0], beside_pair_ref[0] = own_ref[...], beside_ref[...]
    utts, frames, width = own_ref.shape
    rows = N_CTX * frames
    chunks = width // LANES
    half = rows_ref.shape[0] // 2
    place = lax.axis_index("ctx")
    for apart in range(N_CTX):
        side_ref[place ^ apart] = side_refs[apart][...]
    tap_sum_ref[...] = jnp.zeros_like(tap_sum_ref)
    edge = jnp.zeros((2 * chunks, 16, LANES), jnp.float32)
    cotangent_ref[:, 0:16, :] = edge
    cotangent_ref[:, 16 + rows : 32 + rows, :] = edge

    def convolve(step, carry):
        utt, chunk = step // chunks, step % chunks
        cols = columns(chunk * LANES, LANES)
        length = length_ref[utt]
        shape = (frames // 8, 8, LANES)
        for block in range(N_CTX):
            base = block * frames
            total = total_ref[step, base : base + frames, :]
            gate = jax.nn.sigmoid(total)
            incoming = side_ref[block, utt, :, cols].astype(jnp.float32)
            slope = gate * (1.0 + total * (1.0 - gate))
            low = (incoming * slope).astype(jnp.bfloat16)
            cotangent_ref[step, 16 + base : 16 + base + frames, :] = low.astype(jnp.float32)
        for block in range(N_CTX):
            base = block * frames
            total = jnp.zeros(shape, jnp.float32)
            held = masked_ref[step, 16 + base : 16 + base + frames, :].reshape(shape)
            for tap in range(TAPS):
                first = base + 16 + REACH - tap
                piece = cotangent_ref[step, first : first + frames, :].reshape(shape)
                total += taps_ref[chunk, tap][None] * piece
                tap_sum_ref[chunk, tap] += jnp.sum(held * piece, axis=0)
            place_of = base + lax.broadcasted_iota(jnp.int32, (frames, LANES), 0)
            total = jnp.where(place_of < length, total.reshape(frames, LANES), 0.0)
            incoming = side_ref[block, utt, :, cols].astype(jnp.float32)
            low = (incoming + total).astype(jnp.bfloat16)
            result_ref[block, utt, :, cols] = low
            grad_ref[utt, base : base + frames, cols] = low
        return carry

    lax.fori_loop(0, 2 * chunks, convolve, 0)
    sums = [
        jnp.concatenate(
            [
                jnp.sum(tap_sum_ref[chunk, tap], axis=0, keepdims=True)
                for tap in range(TAP_PAD)
            ],
            axis=0,
        )
        for chunk in range(chunks)
    ]
    sums_ref[...] = jnp.concatenate(sums, axis=1)
    for apart in range(N_CTX):
        mine = result_ref[place ^ apart]
        if apart < 2:
            (own_pair_ref, beside_pair_ref)[apart][1] = mine
        else:
            across_ref[apart - 2] = mine.reshape(utts * frames, width)
        dest = place ^ apart
        mixed = dot_tt(
            grad_ref[half_of(dest)],
            rows_ref[pl.ds(pl.multiple_of((dest & 1) * half, half), half)],
            1,
            1,
        ).astype(jnp.bfloat16)
        ref = send_ref if apart % 2 else keep_ref
        for block in range(N_CTX):
            first = pl.multiple_of((block ^ dest) * frames, frames)
            ref[apart // 2, pl.ds(first, frames), :] = mixed[block * frames : (block + 1) * frames]


def make_panels(whole_ref, grad_ref, sums_ref, panel_ref):
    rows, half = grad_ref.shape[1], whole_ref.shape[3] // 2
    entries = 2 * half // N_DP
    group, place = lax.axis_index("dp"), lax.axis_index("ctx")
    for side in range(2):
        panel = 0.0
        for utt in range(2):
            mixed = whole_ref[utt, :, :, side * half : (side + 1) * half].reshape(rows, half)
            panel += dot_tt(mixed, grad_ref[utt], 0, 0)
        panel = panel.astype(jnp.bfloat16)
        for part in range(N_DP // 2):
            panel_ref[slot_of(side * N_DP // 2 + part, group), 0:entries] = panel[
                part * entries : (part + 1) * entries
            ]
    panel_ref[:, entries:, :] = jnp.zeros((N_DP, TAP_PAD // 2, half), jnp.bfloat16)
    own = half // 2
    for part in range(2):
        mine = sums_ref[:, part * own : (part + 1) * own]
        mine = jnp.concatenate([mine[: TAP_PAD // 2], mine[TAP_PAD // 2 :]], axis=1)
        panel_ref[slot_of(2 * place + part, group), entries:, :] = mine.astype(jnp.bfloat16)


def pick_taps(*refs):
    ins, held_ref, out_ref = refs[:N_CTX], refs[N_CTX + 1], refs[N_CTX]
    own = ins[0].shape[1] // 2
    for apart in range(N_CTX):
        held_ref[apart] = ins[apart][...]
    mine = held_ref[lax.axis_index("ctx") ^ half_of(lax.axis_index("dp"))]
    out_ref[...] = jnp.concatenate([mine[:, :own], mine[:, own:]], axis=0)[:TAPS]


def relay(keep_ref, came_ref, out_ref):
    total = keep_ref[1].astype(jnp.float32) + came_ref[1].astype(jnp.float32)
    out_ref[...] = total.astype(jnp.bfloat16)


def make_pair(pair_ref, output_ref, input_ref, awaited_ref, out_ref):
    for slot in range(2):
        out_ref[slot] = pair_ref[slot].reshape(out_ref.shape[1:])
    out_ref[2] = output_ref[1]
    out_ref[3] = input_ref[1]


def attend_back(weight_ref, keep_ref, came_ref, far_ref, *refs):
    ins, out_refs = refs[:N_CTX], refs[N_CTX:]
    frames, half = ins[0].shape[1], ins[0].shape[2]
    rows = N_CTX * frames
    query, key, value = (head_parts(ins, slot) for slot in range(3))
    masks = half_masks(rows)
    scale = HEAD_DIM ** (-0.5)
    arriving = keep_ref[0].astype(jnp.float32) + came_ref[0].astype(jnp.float32)
    arriving = (arriving + far_ref[...].astype(jnp.float32)).astype(jnp.bfloat16)
    low_lanes = lax.broadcasted_iota(jnp.int32, (rows, LANES), 1) < HEAD_DIM
    for pair in range(half // LANES):
        cols = slice(pair * LANES, (pair + 1) * LANES)
        key_pair, value_pair = key[:, cols], value[:, cols]
        query_pair, grad_pair = query[:, cols], arriving[:, cols]
        query_parts, key_parts, value_parts = [], [], []
        for side in range(2):
            low = weight_ref[2 * pair + side]
            weights = low.astype(jnp.float32)
            moved = weights * dot_tt(value_pair, grad_pair * masks[side], 1, 1)
            delta = jnp.sum(moved, axis=0, keepdims=True)
            grad_scores = (moved - weights * delta).astype(jnp.bfloat16)
            value_parts.append(dot_tt(low, grad_pair, 1, 0))
            key_parts.append(dot_tt(grad_scores, query_pair, 1, 0))
            mixed = dot_tt(key_pair, grad_scores, 0, 0)
            query_parts.append(mixed[side * HEAD_DIM : (side + 1) * HEAD_DIM])
        query_sum = (jnp.concatenate(query_parts, axis=0).T * scale).astype(jnp.bfloat16)
        key_sum = (jnp.where(low_lanes, key_parts[0], key_parts[1]) * scale).astype(jnp.bfloat16)
        value_sum = jnp.where(low_lanes, value_parts[0], value_parts[1]).astype(jnp.bfloat16)
        for slot, total in enumerate((query_sum, key_sum, value_sum)):
            for apart in range(N_CTX):
                out_refs[apart][slot, :, cols] = total[apart * frames : (apart + 1) * frames]


def swapped(array, bit):
    return lax.ppermute(array, "dp", [(i, i ^ bit) for i in range(N_DP)])


def dealt(slots):
    return lax.all_to_all(slots, "dp", 0, 0, tiled=True)


def crossed(array, apart):
    return lax.ppermute(array, "ctx", [(i, i ^ apart) for i in range(N_CTX)])


def traded(blocks):
    came = {apart: crossed(blocks[apart], apart) for apart in (2, 3, 1)}
    return [blocks[0]] + [came[apart] for apart in (1, 2, 3)]


def per_device(
    frame_input, queries, key_proj, value_proj, out_weight, conv_weight, lengths, grad_output
):
    utts, frames, wide = frame_input.shape
    inner = queries.shape[2]
    half, width = inner // 2, wide // N_CTX
    rows = N_CTX * frames
    chunks = width // LANES
    low, f32 = jnp.bfloat16, jnp.float32
    shape = jax.ShapeDtypeStruct
    entries = out_weight.shape[1]
    tap_count = conv_weight.shape[0]
    dma = pltpu.SemaphoreType.DMA
    head_block = shape((3, frames, half), low)
    channel_block = shape((utts, frames, width), low)

    blocks = call_kernel(
        pack_heads,
        (head_block,) * N_CTX,
        ["hbm"] * 3,
        scratch=[dma((3 * N_CTX,))],
        room=63,
    )(queries, key_proj, value_proj)
    packed = traded(blocks)
    (shards,) = call_kernel(
        pack_weights,
        (shape((N_DP, entries + TAP_PAD // 2, width), low),),
        ["vmem"] * 2 + ["any"],
    )(out_weight.T, conv_weight, packed[1])
    shards = dealt(shards)
    pair_block = shape((2, utts, frames, width), low)
    *sides, beside_sides, own_sides = call_kernel(
        pack_channels,
        (channel_block,) * 4 + (pair_block,) * 2,
        ["hbm"] * 2 + ["any"],
        scratch=[dma((4 * N_CTX,))],
    )(frame_input, grad_output, packed[2])
    frame_across, frame_diagonal = crossed(sides[0], 2), crossed(sides[1], 3)
    beside_sides = crossed(beside_sides, 1)
    attended, weights = call_kernel(
        attend,
        (
            shape((N_CTX, frames, half), low),
            shape((half // HEAD_DIM, rows, rows), low),
        ),
        ["smem"] + ["vmem"] * N_CTX,
        micros=3.0,
    )(lengths, *packed)
    (attended,) = gate([attended], frame_across, frame_diagonal, micros=20.0)
    across = crossed(attended, 2)
    beside = crossed(attended, 1)
    diagonal = crossed(across, 1)
    grad_across, grad_diagonal = crossed(sides[2], 2), crossed(sides[3], 3)
    frame_blocks = (own_sides, beside_sides, frame_across, frame_diagonal)
    forward_out = call_kernel(
        forward,
        (channel_block,) * 2
        + (
            shape((2, utts * frames, width), low),
            shape((utts, N_CTX, frames, inner), low),
            shape((inner, width), low),
            shape((chunks, TAP_PAD, 8, LANES), f32),
            shape((utts * chunks, rows, LANES), f32),
            shape((utts * chunks, rows + 32, LANES), f32),
        ),
        ["smem"] + ["vmem"] * (1 + 2 * N_CTX),
        scratch=[
            pltpu.VMEM((utts * chunks, rows, LANES), f32),
            pltpu.VMEM((N_CTX, utts, frames, width), low),
            pltpu.VMEM((N_CTX, utts, frames, width), low),
        ],
        micros=3.2,
    )(lengths, shards, attended, beside, across, diagonal, *frame_blocks)
    output_across = crossed(forward_out[2], 2)
    whole, weight_rows, taps, totals, masked = forward_out[3:]
    grad_blocks = gate([grad_across, grad_diagonal], totals, micros=10.0)
    grad_blocks = (own_sides, beside_sides, *grad_blocks)
    backward_out = call_kernel(
        backward,
        (pair_block,) * 2
        + (
            shape((2, utts * frames, width), low),
            shape((utts, rows, width), low),
            shape((2, rows, half), low),
            shape((2, rows, half), low),
            shape((TAP_PAD, width), f32),
        ),
        ["smem"] + ["vmem"] * (6 + N_CTX),
        scratch=[
            pltpu.VMEM((N_CTX, utts, frames, width), low),
            pltpu.VMEM((N_CTX, utts, frames, width), low),
            pltpu.VMEM((utts * chunks, rows + 32, LANES), f32),
            pltpu.VMEM((chunks, TAP_PAD, 8, LANES), f32),
        ],
        micros=5.2,
    )(lengths, totals, masked, taps, weight_rows, *forward_out[:2], *grad_blocks)
    grad_hidden, keep, send, sums = backward_out[3:]
    (send,) = gate([send], output_across)
    came = crossed(send, 1)
    (far,) = call_kernel(
        relay, (shape((rows, half), low),), ["vmem"] * 2, micros=0.2
    )(keep, came)
    (input_across,) = gate([backward_out[2]], far)
    (panels,) = call_kernel(
        make_panels,
        (shape((N_DP, entries + TAP_PAD // 2, width), low),),
        ["vmem"] * 3,
        micros=0.7,
    )(whole, grad_hidden, sums)

    def halved(slots, bit, *awaited):
        count = slots.shape[0] // 2
        came = swapped(slots[count:], bit)
        if awaited:
            (came,) = gate([came], *awaited)
        return (slots[:count].astype(f32) + came.astype(f32)).astype(low)

    far, input_across = crossed(far, 2), crossed(input_across, 2)
    panels = halved(panels, 1, far)
    back_blocks = call_kernel(
        attend_back,
        (head_block,) * N_CTX,
        ["vmem"] * (4 + N_CTX),
        micros=2.2,
    )(weights, keep, came, far, *packed)
    (across_block,) = gate([back_blocks[2]], input_across)
    grad_blocks = traded([*back_blocks[:2], across_block, back_blocks[3]])
    own_pair = backward_out[0]
    (beside_pair,) = call_kernel(
        make_pair,
        (shape((4, utts * frames, width), low),),
        ["vmem"] * 3 + ["any"],
        micros=0.2,
    )(backward_out[1], output_across, input_across, grad_blocks[2])
    beside_pair = crossed(beside_pair, 1)

    panels = halved(panels, 2, grad_blocks[1])
    total = panels[0].astype(f32) + swapped(panels[1], 4).astype(f32)
    grad_out_weight = total[:entries].T
    (tap_sums,) = gate([total[entries:]], grad_blocks[3], beside_pair)
    (grad_taps,) = call_kernel(
        pick_taps,
        (shape(conv_weight.shape, f32),),
        ["vmem"] * N_CTX,
        scratch=[pltpu.VMEM((N_CTX, TAP_PAD // 2, width), f32)],
    )(*traded([tap_sums] * N_CTX))
    unpacked = call_kernel(
        unpack,
        (shape((utts, frames, inner), low),) * 3 + (shape((utts, frames, wide), low),) * 2,
        ["any"] * (N_CTX + 4),
        ["hbm"] * 5,
        [dma((7 * N_CTX + 4 * N_CTX,))],
        micros=1.0,
    )(
        *grad_blocks,
        own_pair,
        beside_pair,
        output_across,
        input_across,
    )
    grad_queries, grad_keys, grad_values, block_output, grad_input = unpacked
    return (
        block_output,
        grad_input,
        grad_queries,
        grad_keys,
        grad_values,
        grad_out_weight,
        grad_taps,
    )


def chosen(sizes, *arrays):
    frame_input, queries, out_weight, conv_weight = (arrays[i] for i in (0, 1, 4, 5))
    utts, frames, wide = frame_input.shape
    inner = queries.shape[2]
    fits = (
        sizes == (N_DP, N_CTX)
        and utts == 2
        and frames == 64
        and wide % (N_CTX * LANES) == 0
        and inner % (2 * LANES) == 0
        and inner // N_DP % 16 == 0
        and inner // 2 == wide // N_CTX
        and conv_weight.shape == (TAPS, wide // N_DP)
        and out_weight.shape == (wide // N_CTX, inner // N_DP)
    )
    return (per_device if fits else general_device)(*arrays)


def solution(mesh):
    placed = (
        P("dp", "ctx", None),
        P("dp", "ctx", None),
        P("dp", "ctx", None),
        P("dp", "ctx", None),
        P("ctx", "dp"),
        P(None, "dp"),
        P("dp"),
        P("dp", "ctx", None),
    )
    sizes = (mesh.shape["dp"], mesh.shape["ctx"])
    return jax.shard_map(
        functools.partial(chosen, sizes),
        mesh=mesh,
        in_specs=placed,
        out_specs=(
            P("dp", "ctx", None),
            P("dp", "ctx", None),
            P("dp", "ctx", None),
            P("dp", "ctx", None),
            P("dp", "ctx", None),
            P("ctx", "dp"),
            P(None, "dp"),
        ),
        check_vma=False,
    )
```

```python
import functools

import jax
import jax.numpy as jnp
from jax import lax
from jax.experimental import pallas as pl
from jax.experimental.pallas import tpu as pltpu
from jax.sharding import PartitionSpec as P

HEAD_DIM = 64


masked_score = -1e30


def padded_2(array, sides, width):
    for axis, dim in sides:
        size, length = (lax.axis_size(axis), array.shape[dim])
        up = [(i, (i + 1) % size) for i in range(size - 1)]
        down = [(j, i) for i, j in up]
        last = lax.slice_in_dim(array, length - width, length, axis=dim)
        leading = lax.slice_in_dim(array, 0, width, axis=dim)
        before = lax.ppermute(last, axis, up)
        after = lax.ppermute(leading, axis, down)
        array = jnp.concatenate([before, array, after], axis=dim)
    return array


def depthwise(lhs, rhs):
    return lax.conv_general_dilated(
        lhs,
        rhs,
        (1,),
        "VALID",
        dimension_numbers=("NWC", "WIO", "NWC"),
        feature_group_count=lhs.shape[2],
        precision=lax.Precision.HIGHEST,
    )


def general_device(
    frame_input, queries, key_proj, value_proj, out_weight, conv_weight, lengths, grad_output
):
    utt_count = frame_input.shape[0]
    frame_count = frame_input.shape[1]
    inner_width = queries.shape[2]
    head_count = inner_width // HEAD_DIM
    group_heads = max((g for g in range(1, 7) if head_count % g == 0))
    group_count = head_count // group_heads
    group_width = group_heads * HEAD_DIM
    tap_count = conv_weight.shape[0]
    half_span = (tap_count - 1) // 2
    score_scale = HEAD_DIM ** (-0.5)
    total_frames = frame_count * lax.axis_size("ctx")
    offset = lax.axis_index("ctx") * frame_count
    own_valid = (offset + jnp.arange(frame_count, dtype=jnp.int32))[None, :] < lengths[:, None]
    all_valid = jnp.arange(total_frames, dtype=jnp.int32)[None, :] < lengths[:, None]

    def grouped(values):
        row_count = values.shape[1]
        return values.reshape(utt_count, row_count, group_count, group_width).transpose(2, 0, 1, 3)

    def ungrouped(values):
        row_count = values.shape[2]
        return values.transpose(1, 2, 0, 3).reshape(utt_count, row_count, group_count * group_width)

    def split_heads(values):
        return values.reshape(utt_count, values.shape[1], group_heads, HEAD_DIM)

    def stats_grouped(values):
        row_count = values.shape[1]
        return values.reshape(utt_count, row_count, group_count, group_heads).transpose(2, 0, 3, 1)

    def masked_scores(query_block, key_block, key_mask):
        scores = (
            jnp.einsum(
                "uqgd,ukgd->ugqk", query_block, key_block, preferred_element_type=jnp.float32
            )
            * score_scale
        )
        return jnp.where(key_mask[:, None, None, :], scores, masked_score)

    taps = lax.all_gather(conv_weight, "dp", axis=1, tiled=True).astype(jnp.float32)
    panel_rows = lax.all_gather(out_weight, "dp", axis=1, tiled=True)
    weight_full = lax.all_gather(panel_rows, "ctx", axis=0, tiled=True)
    all_keys, all_values = (
        lax.all_gather(key_proj, "ctx", axis=1, tiled=True),
        lax.all_gather(value_proj, "ctx", axis=1, tiled=True),
    )
    query_groups = grouped(queries)
    key_groups = grouped(all_keys)
    value_groups = grouped(all_values)

    def forward_group(unused, items):
        query_group, key_group, value_group = items
        query_block = split_heads(query_group)
        scores = masked_scores(query_block, split_heads(key_group), all_valid)
        largest = jnp.max(scores, axis=-1)
        log_group = largest + jnp.log(jnp.sum(jnp.exp(scores - largest[..., None]), axis=-1))
        weights_low = jnp.exp(scores - log_group[..., None]).astype(jnp.bfloat16)
        attended_group = jnp.einsum(
            "ugqk,ukgd->uqgd",
            weights_low,
            split_heads(value_group),
            preferred_element_type=jnp.float32,
        )
        return (None, (log_group, attended_group.reshape(utt_count, frame_count, group_width)))

    _, (log_groups, attended_groups) = lax.scan(
        forward_group, None, (query_groups, key_groups, value_groups)
    )
    attended = ungrouped(attended_groups).astype(jnp.bfloat16)
    log_total = log_groups.transpose(1, 3, 0, 2).reshape(utt_count, frame_count, head_count)
    projected = jnp.einsum("ufe,de->ufd", attended, weight_full, preferred_element_type=jnp.float32)
    hidden = (frame_input.astype(jnp.float32) + projected).astype(jnp.bfloat16)
    masked_hidden = jnp.where(own_valid[:, :, None], hidden, jnp.zeros_like(hidden))
    padded = padded_2(masked_hidden, (("ctx", 1),), half_span).astype(jnp.float32)
    conv_sum = depthwise(padded, taps[:, None, :])
    sigmoid = jax.nn.sigmoid(conv_sum)
    block_output = (hidden.astype(jnp.float32) + conv_sum * sigmoid).astype(jnp.bfloat16)
    grad_local = grad_output.astype(jnp.float32)
    swish_slope = sigmoid * (1.0 + conv_sum * (1.0 - sigmoid))
    grad_conv = (grad_local * swish_slope).astype(jnp.bfloat16)
    grad_padded = padded_2(grad_conv, (("ctx", 1),), half_span).astype(jnp.float32)
    back_sum = depthwise(grad_padded, taps[::-1][:, None, :])
    grad_hidden = (grad_local + jnp.where(own_valid[:, :, None], back_sum, 0.0)).astype(
        jnp.bfloat16
    )
    grad_conv_wide = grad_conv.astype(jnp.float32)
    kernel_term = jnp.zeros((tap_count, conv_sum.shape[2]), jnp.float32)
    for utt_index in range(utt_count):
        kernel_term = (
            kernel_term
            + depthwise(padded[utt_index : utt_index + 1], grad_conv_wide[utt_index][:, None, :])[0]
        )
    kernel_whole = lax.psum(kernel_term.astype(jnp.bfloat16), "ctx")
    grad_conv_weight = lax.psum_scatter(kernel_whole, "dp", scatter_dimension=1, tiled=True).astype(
        jnp.float32
    )
    grad_attended = jnp.einsum(
        "ufd,de->ufe", grad_hidden, weight_full, preferred_element_type=jnp.float32
    ).astype(jnp.bfloat16)
    row_delta = jnp.sum(
        grad_attended.astype(jnp.float32).reshape(utt_count, frame_count, head_count, HEAD_DIM)
        * attended.astype(jnp.float32).reshape(utt_count, frame_count, head_count, HEAD_DIM),
        axis=-1,
    )
    grad_groups = grouped(grad_attended)

    def query_group_step(unused, items):
        query_group, key_group, value_group, grad_group, log_group, delta_group = items
        key_block = split_heads(key_group)
        weights = jnp.exp(
            masked_scores(split_heads(query_group), key_block, all_valid) - log_group[..., None]
        )
        grad_weights = jnp.einsum(
            "uqgd,ukgd->ugqk",
            split_heads(grad_group),
            split_heads(value_group),
            preferred_element_type=jnp.float32,
        )
        grad_scores = (weights * (grad_weights - delta_group[..., None])).astype(jnp.bfloat16)
        query_sum = jnp.einsum(
            "ugqk,ukgd->uqgd", grad_scores, key_block, preferred_element_type=jnp.float32
        )
        return (None, query_sum.reshape(utt_count, frame_count, group_width))

    _, query_sums = lax.scan(
        query_group_step,
        None,
        (
            query_groups,
            key_groups,
            value_groups,
            grad_groups,
            stats_grouped(log_total),
            stats_grouped(row_delta),
        ),
    )
    grad_queries = (ungrouped(query_sums) * score_scale).astype(jnp.bfloat16)
    total_log, total_delta = (
        lax.all_gather(log_total, "ctx", axis=1, tiled=True),
        lax.all_gather(row_delta, "ctx", axis=1, tiled=True),
    )
    own_key_groups = grouped(key_proj)
    own_value_groups = grouped(value_proj)
    group_zeros = jnp.zeros((group_count, utt_count, frame_count, group_width), jnp.float32)
    start_sums = (group_zeros, group_zeros)
    query_all, grad_all = (
        lax.all_gather(queries, "ctx", axis=1, tiled=True),
        lax.all_gather(grad_attended, "ctx", axis=1, tiled=True),
    )
    log_piece = stats_grouped(total_log)
    delta_piece = stats_grouped(total_delta)

    def key_group_step(unused, items):
        (
            query_group,
            grad_group,
            log_group,
            delta_group,
            key_group,
            value_group,
            key_sum,
            value_sum,
        ) = items
        query_block = split_heads(query_group)
        grad_block = split_heads(grad_group)
        weights = jnp.exp(
            masked_scores(query_block, split_heads(key_group), own_valid) - log_group[..., None]
        )
        grad_weights = jnp.einsum(
            "uqgd,ukgd->ugqk",
            grad_block,
            split_heads(value_group),
            preferred_element_type=jnp.float32,
        )
        grad_scores = (weights * (grad_weights - delta_group[..., None])).astype(jnp.bfloat16)
        key_next = key_sum + jnp.einsum(
            "ugqk,uqgd->ukgd", grad_scores, query_block, preferred_element_type=jnp.float32
        ).reshape(utt_count, frame_count, group_width)
        value_next = value_sum + jnp.einsum(
            "ugqk,uqgd->ukgd",
            weights.astype(jnp.bfloat16),
            grad_block,
            preferred_element_type=jnp.float32,
        ).reshape(utt_count, frame_count, group_width)
        return (None, (key_next, value_next))

    _, result_sums = lax.scan(
        key_group_step,
        None,
        (
            grouped(query_all),
            grouped(grad_all),
            log_piece,
            delta_piece,
            own_key_groups,
            own_value_groups,
            start_sums[0],
            start_sums[1],
        ),
    )
    key_sum, value_sum = result_sums
    grad_keys = (ungrouped(key_sum) * score_scale).astype(jnp.bfloat16)
    grad_values = ungrouped(value_sum).astype(jnp.bfloat16)
    hidden_cols = lax.slice_in_dim(
        grad_hidden, 0, weight_full.shape[0] // lax.axis_size("ctx") * lax.axis_size("ctx"), axis=2
    )
    panel_share = lax.psum_scatter(
        jnp.einsum("ufd,ufe->de", hidden_cols, attended, preferred_element_type=jnp.float32).astype(
            jnp.bfloat16
        ),
        "ctx",
        scatter_dimension=0,
        tiled=True,
    )
    grad_out_weight = lax.psum_scatter(panel_share, "dp", scatter_dimension=1, tiled=True).astype(
        jnp.float32
    )
    return (
        block_output,
        grad_hidden,
        grad_queries,
        grad_keys,
        grad_values,
        grad_out_weight,
        grad_conv_weight,
    )


LANES = 128
N_CTX = 4
N_DP = 8
TAP_PAD = 32
FLOPS_A_MICRO = 1.15e9
TAPS = 31
REACH = 15


def slot_of(index, me):
    apart = index ^ me
    return ((apart & 1) << 2) | (apart & 2) | ((apart >> 2) & 1)


def dot_tt(lhs, rhs, lhs_dim, rhs_dim):
    return lax.dot_general(
        lhs, rhs, (((lhs_dim,), (rhs_dim,)), ((), ())), preferred_element_type=jnp.float32
    )


def call_kernel(body, out_shape, ins, outs=None, scratch=(), room=40, micros=1.0):
    spaces = {
        "smem": pl.BlockSpec(memory_space=pltpu.SMEM),
        "vmem": pl.BlockSpec(memory_space=pltpu.VMEM),
        "hbm": pl.BlockSpec(memory_space=pltpu.HBM),
        "any": pl.BlockSpec(memory_space=pl.ANY),
    }
    return pl.pallas_call(
        body,
        out_shape=out_shape,
        in_specs=[spaces[space] for space in ins],
        out_specs=[spaces[space] for space in (outs or ["vmem"] * len(out_shape))],
        scratch_shapes=list(scratch),
        compiler_params=pltpu.CompilerParams(vmem_limit_bytes=room * 1024 * 1024),
        cost_estimate=pl.CostEstimate(
            flops=int(micros * FLOPS_A_MICRO), bytes_accessed=0, transcendentals=0
        ),
    )


def half_of(index):
    return lax.shift_right_logical(index, 1)


def columns(start, size):
    return pl.ds(pl.multiple_of(start, LANES), size)


def start_copies(pairs, sem):
    for number, (source, target) in enumerate(pairs):
        pltpu.make_async_copy(source, target, sem.at[number]).start()


def wait_copies(pairs, sem):
    for number, (source, target) in enumerate(pairs):
        pltpu.make_async_copy(source, target, sem.at[number]).wait()


def run_copies(pairs, sem):
    start_copies(pairs, sem)
    wait_copies(pairs, sem)


def untouched(*refs):
    pass


def gate(arrays, *awaited, micros=0.0):
    count = len(arrays)
    spec = pl.BlockSpec(memory_space=pl.ANY)
    return pl.pallas_call(
        untouched,
        out_shape=tuple(jax.ShapeDtypeStruct(array.shape, array.dtype) for array in arrays),
        in_specs=[spec] * (count + len(awaited)),
        out_specs=(spec,) * count,
        input_output_aliases={number: number for number in range(count)},
        compiler_params=pltpu.CompilerParams(vmem_limit_bytes=1024 * 1024),
        cost_estimate=pl.CostEstimate(
            flops=int(micros * FLOPS_A_MICRO), bytes_accessed=0, transcendentals=0
        ),
    )(*arrays, *awaited)


def pack_heads(query_ref, key_ref, value_ref, *rest):
    outs, sem = rest[:N_CTX], rest[N_CTX]
    half = query_ref.shape[2] // 2
    place = lax.axis_index("ctx")
    pairs = []
    for apart in (2, 3, 1, 0):
        dest = place ^ apart
        cols = columns((dest & 1) * half, half)
        for slot, ref in enumerate((query_ref, key_ref, value_ref)):
            pairs.append((ref.at[half_of(dest), :, cols], outs[apart].at[slot]))
    run_copies(pairs, sem)


def pack_weights(panel_ref, taps_ref, awaited_ref, out_ref):
    entries = panel_ref.shape[0]
    taps = taps_ref[...].astype(jnp.float32)
    high = jnp.concatenate(
        [taps[TAP_PAD // 2 :], jnp.zeros((TAP_PAD - TAPS, taps.shape[1]), jnp.float32)], axis=0
    )
    out_ref[0, 0:entries] = panel_ref[...]
    joined = jnp.concatenate([taps[: TAP_PAD // 2], high], axis=1)
    out_ref[0, entries:] = joined.astype(jnp.bfloat16)


def pack_channels(frame_ref, grad_ref, awaited_ref, *rest):
    across_ref, grad_outs, beside_ref, own_ref, sem = rest[0], rest[1:3], *rest[3:]
    width = frame_ref.shape[2] // N_CTX
    frames = frame_ref.shape[1]
    place = lax.axis_index("ctx")
    pairs = []
    for slot, ref in enumerate((frame_ref, grad_ref)):
        for apart in (2, 3, 1, 0):
            cols = columns((place ^ apart) * width, width)
            for utt in range(2):
                rows = slice(utt * frames, (utt + 1) * frames)
                if apart < 2:
                    target = (own_ref, beside_ref)[apart].at[slot, rows]
                elif slot == 0:
                    target = across_ref.at[apart - 2, rows]
                else:
                    target = grad_outs[apart - 2].at[rows]
                pairs.append((ref.at[utt, :, cols], target))
    run_copies(pairs, sem)


def make_sides(beside_ref, across_ref, out_ref):
    out_ref[0:2] = beside_ref[...]
    out_ref[2] = across_ref[1]


def unpack(*refs):
    ins, refs = refs[:N_CTX], refs[N_CTX:]
    own_ref, beside_ref, output_ref, input_ref = refs[:4]
    heads, channels, sem = refs[4:7], refs[7:9], refs[9]
    half, width = ins[0].shape[2], own_ref.shape[3]
    frames = own_ref.shape[2]
    place = lax.axis_index("ctx")
    pairs = []
    for apart in range(N_CTX):
        source = place ^ apart
        cols = columns((source & 1) * half, half)
        for slot, ref in enumerate(heads):
            pairs.append((ins[apart].at[slot], ref.at[half_of(source), :, cols]))
    for slot, ref in enumerate(channels):
        for utt in range(2):
            part = pl.ds(utt * frames, frames)
            blocks = (
                own_ref.at[slot, utt],
                beside_ref.at[slot, part],
                (output_ref, input_ref)[slot].at[0, part],
                beside_ref.at[2 + slot, part],
            )
            for apart, block in enumerate(blocks):
                cols = columns((place ^ apart) * width, width)
                pairs.append((block, ref.at[utt, :, cols]))
    run_copies(pairs, sem)


def head_parts(refs, slot):
    return jnp.concatenate([ref[slot] for ref in refs], axis=0)


def half_masks(rows):
    lane = lax.broadcasted_iota(jnp.int32, (rows, LANES), 1)
    low = jnp.where(lane < HEAD_DIM, 1.0, 0.0)
    return low.astype(jnp.bfloat16), (1.0 - low).astype(jnp.bfloat16)


def weights_of(length_ref, key_pair, query_pair, mask, frames):
    place = lax.axis_index("ctx")
    rows = key_pair.shape[0]
    frame = lax.broadcasted_iota(jnp.int32, (rows, rows), 0) ^ (place * frames)
    scores = dot_tt(key_pair, query_pair * mask, 1, 1) * HEAD_DIM ** (-0.5)
    scores = jnp.where(frame < length_ref[half_of(place)], scores, masked_score)
    powers = jnp.exp(scores - jnp.max(scores, axis=0, keepdims=True))
    total = jnp.sum(powers, axis=0, keepdims=True)
    return (powers * (1.0 / total)).astype(jnp.bfloat16)


def attend(length_ref, *refs):
    ins, attended_ref = refs[:N_CTX], refs[N_CTX]
    frames, half = ins[0].shape[1], ins[0].shape[2]
    query, key, value = (head_parts(ins, slot) for slot in range(3))
    masks = half_masks(N_CTX * frames)
    for pair in range(half // LANES):
        cols = slice(pair * LANES, (pair + 1) * LANES)
        parts = []
        for side in range(2):
            low = weights_of(length_ref, key[:, cols], query[:, cols], masks[side], frames)
            mixed = dot_tt(value[:, cols], low, 0, 0)
            parts.append(mixed[side * HEAD_DIM : (side + 1) * HEAD_DIM])
        joined = jnp.concatenate(parts, axis=0).T.astype(jnp.bfloat16)
        attended_ref[:, :, cols] = joined.reshape(N_CTX, frames, LANES)


def weigh(length_ref, *refs):
    ins, weight_ref = refs[:N_CTX], refs[N_CTX + 1]
    frames, half = ins[0].shape[1], ins[0].shape[2]
    query, key = (head_parts(ins, slot) for slot in range(2))
    masks = half_masks(N_CTX * frames)
    for pair in range(half // LANES):
        cols = slice(pair * LANES, (pair + 1) * LANES)
        for side in range(2):
            weight_ref[2 * pair + side] = weights_of(
                length_ref, key[:, cols], query[:, cols], masks[side], frames
            )


def forward(length_ref, near_ref, other_ref, *refs):
    attended_refs, refs = refs[:N_CTX], refs[N_CTX:]
    own_ref, beside_ref, across_ref = refs[:3]
    out_refs, refs = refs[3:6], refs[6:]
    whole_ref, rows_ref, taps_ref, total_ref, masked_ref = refs[:5]
    hidden_ref, frame_ref, result_ref = refs[5:]
    frames, half = attended_refs[0].shape[1], attended_refs[0].shape[2]
    width = frame_ref.shape[3]
    rows = N_CTX * frames
    chunks = width // LANES
    entries = 2 * half // N_DP
    own = width // 2
    place = lax.axis_index("ctx")
    for apart in range(N_CTX):
        source = place ^ apart
        cols = columns((source & 1) * half, half)
        for block in range(N_CTX):
            whole_ref[half_of(source), block ^ source, :, cols] = attended_refs[apart][block]
        block = (own_ref, beside_ref, across_ref, beside_ref)[apart][(0, 0, 0, 2)[apart]]
        frame_ref[source] = block.reshape(frame_ref.shape[1:])
    group = lax.axis_index("dp")
    for slot, apart in enumerate((0, 4, 2, 6)):
        for odd, ref in enumerate((near_ref, other_ref)):
            first = pl.multiple_of((group ^ (apart + odd)) * entries, entries)
            rows_ref[pl.ds(first, entries)] = ref[slot, 0:entries]
    apart = place ^ half_of(group)
    slot = ((apart & 1) << 1) | half_of(apart)
    odd = (group & 1) == 1
    blocks = [ref[slot, entries:].astype(jnp.float32) for ref in (near_ref, other_ref)]
    blocks = (jnp.where(odd, blocks[1], blocks[0]), jnp.where(odd, blocks[0], blocks[1]))
    pieces = [jnp.concatenate([block[:, :own], block[:, own:]], axis=0) for block in blocks]
    taps = jnp.concatenate(pieces, axis=1)
    for chunk in range(chunks):
        for tap in range(TAPS):
            taps_ref[chunk, tap] = jnp.broadcast_to(
                taps[tap : tap + 1, chunk * LANES : (chunk + 1) * LANES], (8, LANES)
            )
    edge = jnp.zeros((2 * chunks, 16, LANES), jnp.float32)
    masked_ref[:, 0:16, :] = edge
    masked_ref[:, 16 + rows : 32 + rows, :] = edge
    for utt in range(2):
        real = lax.broadcasted_iota(jnp.int32, (rows, LANES), 0) < length_ref[utt]
        mixed = whole_ref[utt].reshape(rows, 2 * half)
        projected = dot_tt(mixed, rows_ref[...], 1, 0)
        hidden = frame_ref[:, utt].reshape(rows, width).astype(jnp.float32) + projected
        hidden = hidden.astype(jnp.bfloat16).astype(jnp.float32)
        for chunk in range(chunks):
            piece = hidden[:, chunk * LANES : (chunk + 1) * LANES]
            hidden_ref[utt * chunks + chunk] = piece
            masked_ref[utt * chunks + chunk, 16 : 16 + rows, :] = jnp.where(real, piece, 0.0)

    def convolve(step, carry):
        utt, chunk = step // chunks, step % chunks
        cols = columns(chunk * LANES, LANES)
        shape = (frames // 8, 8, LANES)
        for block in range(N_CTX):
            base = block * frames
            total = jnp.zeros(shape, jnp.float32)
            for tap in range(TAPS):
                first = base + tap + 16 - REACH
                piece = masked_ref[step, first : first + frames, :]
                total += taps_ref[chunk, tap][None] * piece.reshape(shape)
            total = total.reshape(frames, LANES)
            total_ref[step, base : base + frames, :] = total
            outer = hidden_ref[step, base : base + frames, :] + total * jax.nn.sigmoid(total)
            result_ref[block, utt, :, cols] = outer.astype(jnp.bfloat16)
        return carry

    lax.fori_loop(0, 2 * chunks, convolve, 0)
    for apart in range(2):
        out_refs[apart][...] = result_ref[place ^ apart]
        out_refs[2][apart] = result_ref[place ^ (2 + apart)].reshape(2 * frames, width)


def backward(length_ref, total_ref, masked_ref, taps_ref, rows_ref, *refs):
    own_ref, beside_ref = refs[:2]
    own_sides_ref, beside_sides_ref, grad_across_ref, grad_diagonal_ref = refs[2:6]
    refs = refs[6:]
    own_pair_ref, beside_pair_ref, across_ref = refs[:3]
    grad_ref, keep_ref, send_ref, sums_ref = refs[3:7]
    side_ref, result_ref, cotangent_ref, tap_sum_ref = refs[7:]
    own_pair_ref[0], beside_pair_ref[0] = own_ref[...], beside_ref[...]
    utts, frames, width = own_ref.shape
    rows = N_CTX * frames
    chunks = width // LANES
    half = rows_ref.shape[0] // 2
    place = lax.axis_index("ctx")
    blocks = (own_sides_ref[1], beside_sides_ref[1], grad_across_ref[...], grad_diagonal_ref[...])
    for apart in range(N_CTX):
        side_ref[place ^ apart] = blocks[apart].reshape(side_ref.shape[1:])
    tap_sum_ref[...] = jnp.zeros_like(tap_sum_ref)
    edge = jnp.zeros((2 * chunks, 16, LANES), jnp.float32)
    cotangent_ref[:, 0:16, :] = edge
    cotangent_ref[:, 16 + rows : 32 + rows, :] = edge

    def convolve(step, carry):
        utt, chunk = step // chunks, step % chunks
        cols = columns(chunk * LANES, LANES)
        length = length_ref[utt]
        shape = (frames // 8, 8, LANES)
        for block in range(N_CTX):
            base = block * frames
            total = total_ref[step, base : base + frames, :]
            gate = jax.nn.sigmoid(total)
            incoming = side_ref[block, utt, :, cols].astype(jnp.float32)
            slope = gate * (1.0 + total * (1.0 - gate))
            low = (incoming * slope).astype(jnp.bfloat16)
            cotangent_ref[step, 16 + base : 16 + base + frames, :] = low.astype(jnp.float32)
        for block in range(N_CTX):
            base = block * frames
            total = jnp.zeros(shape, jnp.float32)
            held = masked_ref[step, 16 + base : 16 + base + frames, :].reshape(shape)
            for tap in range(TAPS):
                first = base + 16 + REACH - tap
                piece = cotangent_ref[step, first : first + frames, :].reshape(shape)
                total += taps_ref[chunk, tap][None] * piece
                tap_sum_ref[chunk, tap] += jnp.sum(held * piece, axis=0)
            place_of = base + lax.broadcasted_iota(jnp.int32, (frames, LANES), 0)
            total = jnp.where(place_of < length, total.reshape(frames, LANES), 0.0)
            incoming = side_ref[block, utt, :, cols].astype(jnp.float32)
            low = (incoming + total).astype(jnp.bfloat16)
            result_ref[block, utt, :, cols] = low
            grad_ref[utt, base : base + frames, cols] = low
        return carry

    lax.fori_loop(0, 2 * chunks, convolve, 0)
    sums = [
        jnp.concatenate(
            [
                jnp.sum(tap_sum_ref[chunk, tap], axis=0, keepdims=True)
                for tap in range(TAP_PAD)
            ],
            axis=0,
        )
        for chunk in range(chunks)
    ]
    sums_ref[...] = jnp.concatenate(sums, axis=1)
    for apart in range(N_CTX):
        mine = result_ref[place ^ apart]
        if apart < 2:
            (own_pair_ref, beside_pair_ref)[apart][1] = mine
        else:
            across_ref[apart - 2] = mine.reshape(utts * frames, width)
        dest = place ^ apart
        mixed = dot_tt(
            grad_ref[half_of(dest)],
            rows_ref[pl.ds(pl.multiple_of((dest & 1) * half, half), half)],
            1,
            1,
        ).astype(jnp.bfloat16)
        ref = send_ref if apart % 2 else keep_ref
        for block in range(N_CTX):
            first = pl.multiple_of((block ^ dest) * frames, frames)
            ref[apart // 2, pl.ds(first, frames), :] = mixed[block * frames : (block + 1) * frames]


def make_panels(whole_ref, grad_ref, sums_ref, panel_ref):
    rows, half = grad_ref.shape[1], whole_ref.shape[3] // 2
    entries = 2 * half // N_DP
    group, place = lax.axis_index("dp"), lax.axis_index("ctx")
    for side in range(2):
        panel = 0.0
        for utt in range(2):
            mixed = whole_ref[utt, :, :, side * half : (side + 1) * half].reshape(rows, half)
            panel += dot_tt(mixed, grad_ref[utt], 0, 0)
        panel = panel.astype(jnp.bfloat16)
        for part in range(N_DP // 2):
            panel_ref[slot_of(side * N_DP // 2 + part, group), 0:entries] = panel[
                part * entries : (part + 1) * entries
            ]
    panel_ref[:, entries:, :] = jnp.zeros((N_DP, TAP_PAD // 2, half), jnp.bfloat16)
    own = half // 2
    for part in range(2):
        mine = sums_ref[:, part * own : (part + 1) * own]
        mine = jnp.concatenate([mine[: TAP_PAD // 2], mine[TAP_PAD // 2 :]], axis=1)
        panel_ref[slot_of(2 * place + part, group), entries:, :] = mine.astype(jnp.bfloat16)


def pick_taps(*refs):
    ins, held_ref, out_ref = refs[:N_CTX], refs[N_CTX + 1], refs[N_CTX]
    own = ins[0].shape[1] // 2
    for apart in range(N_CTX):
        held_ref[apart] = ins[apart][...]
    mine = held_ref[lax.axis_index("ctx") ^ half_of(lax.axis_index("dp"))]
    out_ref[...] = jnp.concatenate([mine[:, :own], mine[:, own:]], axis=0)[:TAPS]


def relay(keep_ref, came_ref, out_ref):
    total = keep_ref[1].astype(jnp.float32) + came_ref[1].astype(jnp.float32)
    out_ref[...] = total.astype(jnp.bfloat16)


def make_pair(pair_ref, output_ref, input_ref, awaited_ref, out_ref):
    for slot in range(2):
        out_ref[slot] = pair_ref[slot].reshape(out_ref.shape[1:])
    out_ref[2] = output_ref[1]
    out_ref[3] = input_ref[1]


def attend_back(weight_ref, keep_ref, came_ref, far_ref, *refs):
    ins, out_refs = refs[:N_CTX], refs[N_CTX:]
    frames, half = ins[0].shape[1], ins[0].shape[2]
    rows = N_CTX * frames
    query, key, value = (head_parts(ins, slot) for slot in range(3))
    masks = half_masks(rows)
    scale = HEAD_DIM ** (-0.5)
    arriving = keep_ref[0].astype(jnp.float32) + came_ref[0].astype(jnp.float32)
    arriving = (arriving + far_ref[...].astype(jnp.float32)).astype(jnp.bfloat16)
    low_lanes = lax.broadcasted_iota(jnp.int32, (rows, LANES), 1) < HEAD_DIM
    for pair in range(half // LANES):
        cols = slice(pair * LANES, (pair + 1) * LANES)
        key_pair, value_pair = key[:, cols], value[:, cols]
        query_pair, grad_pair = query[:, cols], arriving[:, cols]
        query_parts, key_parts, value_parts = [], [], []
        for side in range(2):
            low = weight_ref[2 * pair + side]
            weights = low.astype(jnp.float32)
            moved = weights * dot_tt(value_pair, grad_pair * masks[side], 1, 1)
            delta = jnp.sum(moved, axis=0, keepdims=True)
            grad_scores = (moved - weights * delta).astype(jnp.bfloat16)
            value_parts.append(dot_tt(low, grad_pair, 1, 0))
            key_parts.append(dot_tt(grad_scores, query_pair, 1, 0))
            mixed = dot_tt(key_pair, grad_scores, 0, 0)
            query_parts.append(mixed[side * HEAD_DIM : (side + 1) * HEAD_DIM])
        query_sum = (jnp.concatenate(query_parts, axis=0).T * scale).astype(jnp.bfloat16)
        key_sum = (jnp.where(low_lanes, key_parts[0], key_parts[1]) * scale).astype(jnp.bfloat16)
        value_sum = jnp.where(low_lanes, value_parts[0], value_parts[1]).astype(jnp.bfloat16)
        for slot, total in enumerate((query_sum, key_sum, value_sum)):
            for apart in range(N_CTX):
                out_refs[apart][slot, :, cols] = total[apart * frames : (apart + 1) * frames]


def swapped(array, bit):
    return lax.ppermute(array, "dp", [(i, i ^ bit) for i in range(N_DP)])


def dealt(slots):
    return lax.all_to_all(slots, "dp", 0, 0, tiled=True)


def crossed(array, apart):
    return lax.ppermute(array, "ctx", [(i, i ^ apart) for i in range(N_CTX)])


def traded(blocks):
    came = {apart: crossed(blocks[apart], apart) for apart in (2, 3, 1)}
    return [blocks[0]] + [came[apart] for apart in (1, 2, 3)]


def per_device(
    frame_input, queries, key_proj, value_proj, out_weight, conv_weight, lengths, grad_output
):
    utts, frames, wide = frame_input.shape
    inner = queries.shape[2]
    half, width = inner // 2, wide // N_CTX
    rows = N_CTX * frames
    chunks = width // LANES
    low, f32 = jnp.bfloat16, jnp.float32
    shape = jax.ShapeDtypeStruct
    entries = out_weight.shape[1]
    tap_count = conv_weight.shape[0]
    dma = pltpu.SemaphoreType.DMA
    head_block = shape((3, frames, half), low)
    channel_block = shape((utts, frames, width), low)

    blocks = call_kernel(
        pack_heads,
        (head_block,) * N_CTX,
        ["hbm"] * 3,
        scratch=[dma((3 * N_CTX,))],
        room=63,
    )(queries, key_proj, value_proj)
    packed = traded(blocks)
    (shard,) = call_kernel(
        pack_weights,
        (shape((1, entries + TAP_PAD // 2, width), low),),
        ["vmem"] * 2 + ["any"],
    )(out_weight.T, conv_weight, packed[1])
    for bit in (4, 2):
        shard = jnp.concatenate([shard, swapped(shard, bit)], axis=0)
    other_shard = swapped(shard, 1)
    pair_block = shape((2, utts, frames, width), low)
    side_block = shape((utts * frames, width), low)
    double_block = shape((2, utts * frames, width), low)
    frame_across, grad_across, grad_diagonal, beside_sides, own_sides = call_kernel(
        pack_channels,
        (double_block,) + (side_block,) * 2 + (double_block,) * 2,
        ["hbm"] * 2 + ["any"],
        scratch=[dma((4 * N_CTX,))],
    )(frame_input, grad_output, packed[2])
    frame_across = crossed(frame_across, 2)
    (beside_sides,) = call_kernel(
        make_sides, (shape((3, utts * frames, width), low),), ["vmem"] * 2
    )(beside_sides, frame_across)
    beside_sides = crossed(beside_sides, 1)
    (attended,) = call_kernel(
        attend,
        (shape((N_CTX, frames, half), low),),
        ["smem"] + ["vmem"] * N_CTX,
    )(lengths, *packed)
    (attended,) = gate([attended], frame_across)
    across = crossed(attended, 2)
    beside = crossed(attended, 1)
    diagonal = crossed(across, 1)
    grad_across, grad_diagonal = crossed(grad_across, 2), crossed(grad_diagonal, 3)
    forward_out = call_kernel(
        forward,
        (channel_block,) * 2
        + (
            shape((2, utts * frames, width), low),
            shape((utts, N_CTX, frames, inner), low),
            shape((inner, width), low),
            shape((chunks, TAP_PAD, 8, LANES), f32),
            shape((utts * chunks, rows, LANES), f32),
            shape((utts * chunks, rows + 32, LANES), f32),
        ),
        ["smem"] + ["vmem"] * (5 + N_CTX),
        scratch=[
            pltpu.VMEM((utts * chunks, rows, LANES), f32),
            pltpu.VMEM((N_CTX, utts, frames, width), low),
            pltpu.VMEM((N_CTX, utts, frames, width), low),
        ],
        micros=3.2,
    )(
        lengths,
        shard,
        other_shard,
        attended,
        beside,
        across,
        diagonal,
        own_sides,
        beside_sides,
        frame_across,
    )
    output_across = crossed(forward_out[2], 2)
    whole, weight_rows, taps, totals, masked = forward_out[3:]
    grad_blocks = gate([grad_across, grad_diagonal], totals, micros=10.0)
    grad_blocks = (own_sides, beside_sides, *grad_blocks)
    backward_out = call_kernel(
        backward,
        (pair_block,) * 2
        + (
            shape((2, utts * frames, width), low),
            shape((utts, rows, width), low),
            shape((2, rows, half), low),
            shape((2, rows, half), low),
            shape((TAP_PAD, width), f32),
        ),
        ["smem"] + ["vmem"] * (6 + N_CTX),
        scratch=[
            pltpu.VMEM((N_CTX, utts, frames, width), low),
            pltpu.VMEM((N_CTX, utts, frames, width), low),
            pltpu.VMEM((utts * chunks, rows + 32, LANES), f32),
            pltpu.VMEM((chunks, TAP_PAD, 8, LANES), f32),
        ],
        micros=5.2,
    )(lengths, totals, masked, taps, weight_rows, *forward_out[:2], *grad_blocks)
    grad_hidden, keep, send, sums = backward_out[3:]
    (send,) = gate([send], output_across)
    came = crossed(send, 1)
    (relayed,) = call_kernel(
        relay, (shape((rows, half), low),), ["vmem"] * 2, micros=0.2
    )(keep, came)
    (input_across,) = gate([backward_out[2]], relayed)
    (panels,) = call_kernel(
        make_panels,
        (shape((N_DP, entries + TAP_PAD // 2, width), low),),
        ["vmem"] * 3,
        micros=0.7,
    )(whole, grad_hidden, sums)

    def halved(slots, bit, *awaited):
        count = slots.shape[0] // 2
        came = swapped(slots[count:], bit)
        if awaited:
            (came,) = gate([came], *awaited)
        return (slots[:count].astype(f32) + came.astype(f32)).astype(low)

    far, input_across = crossed(relayed, 2), crossed(input_across, 2)
    (weights,) = call_kernel(
        weigh,
        (shape((half // HEAD_DIM, rows, rows), low),),
        ["smem"] + ["vmem"] * N_CTX + ["any"],
    )(lengths, *packed, relayed)
    back_blocks = call_kernel(
        attend_back,
        (head_block,) * N_CTX,
        ["vmem"] * (4 + N_CTX),
        micros=2.2,
    )(weights, keep, came, far, *packed)
    (across_block,) = gate([back_blocks[2]], input_across)
    grad_blocks = traded([*back_blocks[:2], across_block, back_blocks[3]])
    own_pair = backward_out[0]
    (beside_pair,) = call_kernel(
        make_pair,
        (shape((4, utts * frames, width), low),),
        ["vmem"] * 3 + ["any"],
        micros=0.2,
    )(backward_out[1], output_across, input_across, grad_blocks[2])
    beside_pair = crossed(beside_pair, 1)

    panels = halved(panels, 1, back_blocks[0])
    panels = halved(panels, 2, grad_blocks[1])
    total = panels[0].astype(f32) + swapped(panels[1], 4).astype(f32)
    grad_out_weight = total[:entries].T
    (tap_sums,) = gate([total[entries:]], grad_blocks[3], beside_pair)
    (grad_taps,) = call_kernel(
        pick_taps,
        (shape(conv_weight.shape, f32),),
        ["vmem"] * N_CTX,
        scratch=[pltpu.VMEM((N_CTX, TAP_PAD // 2, width), f32)],
    )(*traded([tap_sums] * N_CTX))
    unpacked = call_kernel(
        unpack,
        (shape((utts, frames, inner), low),) * 3 + (shape((utts, frames, wide), low),) * 2,
        ["any"] * (N_CTX + 4),
        ["hbm"] * 5,
        [dma((7 * N_CTX + 4 * N_CTX,))],
        micros=1.0,
    )(
        *grad_blocks,
        own_pair,
        beside_pair,
        output_across,
        input_across,
    )
    grad_queries, grad_keys, grad_values, block_output, grad_input = unpacked
    return (
        block_output,
        grad_input,
        grad_queries,
        grad_keys,
        grad_values,
        grad_out_weight,
        grad_taps,
    )


def chosen(sizes, *arrays):
    frame_input, queries, out_weight, conv_weight = (arrays[i] for i in (0, 1, 4, 5))
    utts, frames, wide = frame_input.shape
    inner = queries.shape[2]
    fits = (
        sizes == (N_DP, N_CTX)
        and utts == 2
        and frames == 64
        and wide % (N_CTX * LANES) == 0
        and inner % (2 * LANES) == 0
        and inner // N_DP % 16 == 0
        and inner // 2 == wide // N_CTX
        and conv_weight.shape == (TAPS, wide // N_DP)
        and out_weight.shape == (wide // N_CTX, inner // N_DP)
    )
    return (per_device if fits else general_device)(*arrays)


def solution(mesh):
    placed = (
        P("dp", "ctx", None),
        P("dp", "ctx", None),
        P("dp", "ctx", None),
        P("dp", "ctx", None),
        P("ctx", "dp"),
        P(None, "dp"),
        P("dp"),
        P("dp", "ctx", None),
    )
    sizes = (mesh.shape["dp"], mesh.shape["ctx"])
    return jax.shard_map(
        functools.partial(chosen, sizes),
        mesh=mesh,
        in_specs=placed,
        out_specs=(
            P("dp", "ctx", None),
            P("dp", "ctx", None),
            P("dp", "ctx", None),
            P("dp", "ctx", None),
            P("dp", "ctx", None),
            P("ctx", "dp"),
            P(None, "dp"),
        ),
        check_vma=False,
    )
```

```python
import functools

import jax
import jax.numpy as jnp
from jax import lax
from jax.experimental import pallas as pl
from jax.experimental.pallas import tpu as pltpu
from jax.sharding import PartitionSpec as P

HEAD_DIM = 64


masked_score = -1e30


def padded_2(array, sides, width):
    for axis, dim in sides:
        size, length = (lax.axis_size(axis), array.shape[dim])
        up = [(i, (i + 1) % size) for i in range(size - 1)]
        down = [(j, i) for i, j in up]
        last = lax.slice_in_dim(array, length - width, length, axis=dim)
        leading = lax.slice_in_dim(array, 0, width, axis=dim)
        before = lax.ppermute(last, axis, up)
        after = lax.ppermute(leading, axis, down)
        array = jnp.concatenate([before, array, after], axis=dim)
    return array


def depthwise(lhs, rhs):
    return lax.conv_general_dilated(
        lhs,
        rhs,
        (1,),
        "VALID",
        dimension_numbers=("NWC", "WIO", "NWC"),
        feature_group_count=lhs.shape[2],
        precision=lax.Precision.HIGHEST,
    )


def general_device(
    frame_input, queries, key_proj, value_proj, out_weight, conv_weight, lengths, grad_output
):
    utt_count = frame_input.shape[0]
    frame_count = frame_input.shape[1]
    inner_width = queries.shape[2]
    head_count = inner_width // HEAD_DIM
    group_heads = max((g for g in range(1, 7) if head_count % g == 0))
    group_count = head_count // group_heads
    group_width = group_heads * HEAD_DIM
    tap_count = conv_weight.shape[0]
    half_span = (tap_count - 1) // 2
    score_scale = HEAD_DIM ** (-0.5)
    total_frames = frame_count * lax.axis_size("ctx")
    offset = lax.axis_index("ctx") * frame_count
    own_valid = (offset + jnp.arange(frame_count, dtype=jnp.int32))[None, :] < lengths[:, None]
    all_valid = jnp.arange(total_frames, dtype=jnp.int32)[None, :] < lengths[:, None]

    def grouped(values):
        row_count = values.shape[1]
        return values.reshape(utt_count, row_count, group_count, group_width).transpose(2, 0, 1, 3)

    def ungrouped(values):
        row_count = values.shape[2]
        return values.transpose(1, 2, 0, 3).reshape(utt_count, row_count, group_count * group_width)

    def split_heads(values):
        return values.reshape(utt_count, values.shape[1], group_heads, HEAD_DIM)

    def stats_grouped(values):
        row_count = values.shape[1]
        return values.reshape(utt_count, row_count, group_count, group_heads).transpose(2, 0, 3, 1)

    def masked_scores(query_block, key_block, key_mask):
        scores = (
            jnp.einsum(
                "uqgd,ukgd->ugqk", query_block, key_block, preferred_element_type=jnp.float32
            )
            * score_scale
        )
        return jnp.where(key_mask[:, None, None, :], scores, masked_score)

    taps = lax.all_gather(conv_weight, "dp", axis=1, tiled=True).astype(jnp.float32)
    panel_rows = lax.all_gather(out_weight, "dp", axis=1, tiled=True)
    weight_full = lax.all_gather(panel_rows, "ctx", axis=0, tiled=True)
    all_keys, all_values = (
        lax.all_gather(key_proj, "ctx", axis=1, tiled=True),
        lax.all_gather(value_proj, "ctx", axis=1, tiled=True),
    )
    query_groups = grouped(queries)
    key_groups = grouped(all_keys)
    value_groups = grouped(all_values)

    def forward_group(unused, items):
        query_group, key_group, value_group = items
        query_block = split_heads(query_group)
        scores = masked_scores(query_block, split_heads(key_group), all_valid)
        largest = jnp.max(scores, axis=-1)
        log_group = largest + jnp.log(jnp.sum(jnp.exp(scores - largest[..., None]), axis=-1))
        weights_low = jnp.exp(scores - log_group[..., None]).astype(jnp.bfloat16)
        attended_group = jnp.einsum(
            "ugqk,ukgd->uqgd",
            weights_low,
            split_heads(value_group),
            preferred_element_type=jnp.float32,
        )
        return (None, (log_group, attended_group.reshape(utt_count, frame_count, group_width)))

    _, (log_groups, attended_groups) = lax.scan(
        forward_group, None, (query_groups, key_groups, value_groups)
    )
    attended = ungrouped(attended_groups).astype(jnp.bfloat16)
    log_total = log_groups.transpose(1, 3, 0, 2).reshape(utt_count, frame_count, head_count)
    projected = jnp.einsum("ufe,de->ufd", attended, weight_full, preferred_element_type=jnp.float32)
    hidden = (frame_input.astype(jnp.float32) + projected).astype(jnp.bfloat16)
    masked_hidden = jnp.where(own_valid[:, :, None], hidden, jnp.zeros_like(hidden))
    padded = padded_2(masked_hidden, (("ctx", 1),), half_span).astype(jnp.float32)
    conv_sum = depthwise(padded, taps[:, None, :])
    sigmoid = jax.nn.sigmoid(conv_sum)
    block_output = (hidden.astype(jnp.float32) + conv_sum * sigmoid).astype(jnp.bfloat16)
    grad_local = grad_output.astype(jnp.float32)
    swish_slope = sigmoid * (1.0 + conv_sum * (1.0 - sigmoid))
    grad_conv = (grad_local * swish_slope).astype(jnp.bfloat16)
    grad_padded = padded_2(grad_conv, (("ctx", 1),), half_span).astype(jnp.float32)
    back_sum = depthwise(grad_padded, taps[::-1][:, None, :])
    grad_hidden = (grad_local + jnp.where(own_valid[:, :, None], back_sum, 0.0)).astype(
        jnp.bfloat16
    )
    grad_conv_wide = grad_conv.astype(jnp.float32)
    kernel_term = jnp.zeros((tap_count, conv_sum.shape[2]), jnp.float32)
    for utt_index in range(utt_count):
        kernel_term = (
            kernel_term
            + depthwise(padded[utt_index : utt_index + 1], grad_conv_wide[utt_index][:, None, :])[0]
        )
    kernel_whole = lax.psum(kernel_term.astype(jnp.bfloat16), "ctx")
    grad_conv_weight = lax.psum_scatter(kernel_whole, "dp", scatter_dimension=1, tiled=True).astype(
        jnp.float32
    )
    grad_attended = jnp.einsum(
        "ufd,de->ufe", grad_hidden, weight_full, preferred_element_type=jnp.float32
    ).astype(jnp.bfloat16)
    row_delta = jnp.sum(
        grad_attended.astype(jnp.float32).reshape(utt_count, frame_count, head_count, HEAD_DIM)
        * attended.astype(jnp.float32).reshape(utt_count, frame_count, head_count, HEAD_DIM),
        axis=-1,
    )
    grad_groups = grouped(grad_attended)

    def query_group_step(unused, items):
        query_group, key_group, value_group, grad_group, log_group, delta_group = items
        key_block = split_heads(key_group)
        weights = jnp.exp(
            masked_scores(split_heads(query_group), key_block, all_valid) - log_group[..., None]
        )
        grad_weights = jnp.einsum(
            "uqgd,ukgd->ugqk",
            split_heads(grad_group),
            split_heads(value_group),
            preferred_element_type=jnp.float32,
        )
        grad_scores = (weights * (grad_weights - delta_group[..., None])).astype(jnp.bfloat16)
        query_sum = jnp.einsum(
            "ugqk,ukgd->uqgd", grad_scores, key_block, preferred_element_type=jnp.float32
        )
        return (None, query_sum.reshape(utt_count, frame_count, group_width))

    _, query_sums = lax.scan(
        query_group_step,
        None,
        (
            query_groups,
            key_groups,
            value_groups,
            grad_groups,
            stats_grouped(log_total),
            stats_grouped(row_delta),
        ),
    )
    grad_queries = (ungrouped(query_sums) * score_scale).astype(jnp.bfloat16)
    total_log, total_delta = (
        lax.all_gather(log_total, "ctx", axis=1, tiled=True),
        lax.all_gather(row_delta, "ctx", axis=1, tiled=True),
    )
    own_key_groups = grouped(key_proj)
    own_value_groups = grouped(value_proj)
    group_zeros = jnp.zeros((group_count, utt_count, frame_count, group_width), jnp.float32)
    start_sums = (group_zeros, group_zeros)
    query_all, grad_all = (
        lax.all_gather(queries, "ctx", axis=1, tiled=True),
        lax.all_gather(grad_attended, "ctx", axis=1, tiled=True),
    )
    log_piece = stats_grouped(total_log)
    delta_piece = stats_grouped(total_delta)

    def key_group_step(unused, items):
        (
            query_group,
            grad_group,
            log_group,
            delta_group,
            key_group,
            value_group,
            key_sum,
            value_sum,
        ) = items
        query_block = split_heads(query_group)
        grad_block = split_heads(grad_group)
        weights = jnp.exp(
            masked_scores(query_block, split_heads(key_group), own_valid) - log_group[..., None]
        )
        grad_weights = jnp.einsum(
            "uqgd,ukgd->ugqk",
            grad_block,
            split_heads(value_group),
            preferred_element_type=jnp.float32,
        )
        grad_scores = (weights * (grad_weights - delta_group[..., None])).astype(jnp.bfloat16)
        key_next = key_sum + jnp.einsum(
            "ugqk,uqgd->ukgd", grad_scores, query_block, preferred_element_type=jnp.float32
        ).reshape(utt_count, frame_count, group_width)
        value_next = value_sum + jnp.einsum(
            "ugqk,uqgd->ukgd",
            weights.astype(jnp.bfloat16),
            grad_block,
            preferred_element_type=jnp.float32,
        ).reshape(utt_count, frame_count, group_width)
        return (None, (key_next, value_next))

    _, result_sums = lax.scan(
        key_group_step,
        None,
        (
            grouped(query_all),
            grouped(grad_all),
            log_piece,
            delta_piece,
            own_key_groups,
            own_value_groups,
            start_sums[0],
            start_sums[1],
        ),
    )
    key_sum, value_sum = result_sums
    grad_keys = (ungrouped(key_sum) * score_scale).astype(jnp.bfloat16)
    grad_values = ungrouped(value_sum).astype(jnp.bfloat16)
    hidden_cols = lax.slice_in_dim(
        grad_hidden, 0, weight_full.shape[0] // lax.axis_size("ctx") * lax.axis_size("ctx"), axis=2
    )
    panel_share = lax.psum_scatter(
        jnp.einsum("ufd,ufe->de", hidden_cols, attended, preferred_element_type=jnp.float32).astype(
            jnp.bfloat16
        ),
        "ctx",
        scatter_dimension=0,
        tiled=True,
    )
    grad_out_weight = lax.psum_scatter(panel_share, "dp", scatter_dimension=1, tiled=True).astype(
        jnp.float32
    )
    return (
        block_output,
        grad_hidden,
        grad_queries,
        grad_keys,
        grad_values,
        grad_out_weight,
        grad_conv_weight,
    )


LANES = 128
N_CTX = 4
N_DP = 8
TAP_PAD = 32
FLOPS_A_MICRO = 1.15e9
TAPS = 31
REACH = 15


def slot_of(index, me):
    apart = index ^ me
    return ((apart & 1) << 2) | (apart & 2) | ((apart >> 2) & 1)


def dot_tt(lhs, rhs, lhs_dim, rhs_dim):
    return lax.dot_general(
        lhs, rhs, (((lhs_dim,), (rhs_dim,)), ((), ())), preferred_element_type=jnp.float32
    )


def call_kernel(body, out_shape, ins, outs=None, scratch=(), room=40, micros=1.0):
    spaces = {
        "smem": pl.BlockSpec(memory_space=pltpu.SMEM),
        "vmem": pl.BlockSpec(memory_space=pltpu.VMEM),
        "hbm": pl.BlockSpec(memory_space=pltpu.HBM),
        "any": pl.BlockSpec(memory_space=pl.ANY),
    }
    return pl.pallas_call(
        body,
        out_shape=out_shape,
        in_specs=[spaces[space] for space in ins],
        out_specs=[spaces[space] for space in (outs or ["vmem"] * len(out_shape))],
        scratch_shapes=list(scratch),
        compiler_params=pltpu.CompilerParams(vmem_limit_bytes=room * 1024 * 1024),
        cost_estimate=pl.CostEstimate(
            flops=int(micros * FLOPS_A_MICRO), bytes_accessed=0, transcendentals=0
        ),
    )


def half_of(index):
    return lax.shift_right_logical(index, 1)


def columns(start, size):
    return pl.ds(pl.multiple_of(start, LANES), size)


def start_copies(pairs, sem):
    for number, (source, target) in enumerate(pairs):
        pltpu.make_async_copy(source, target, sem.at[number]).start()


def wait_copies(pairs, sem):
    for number, (source, target) in enumerate(pairs):
        pltpu.make_async_copy(source, target, sem.at[number]).wait()


def run_copies(pairs, sem):
    start_copies(pairs, sem)
    wait_copies(pairs, sem)


def untouched(*refs):
    pass


def gate(arrays, *awaited, micros=0.0):
    count = len(arrays)
    spec = pl.BlockSpec(memory_space=pl.ANY)
    return pl.pallas_call(
        untouched,
        out_shape=tuple(jax.ShapeDtypeStruct(array.shape, array.dtype) for array in arrays),
        in_specs=[spec] * (count + len(awaited)),
        out_specs=(spec,) * count,
        input_output_aliases={number: number for number in range(count)},
        compiler_params=pltpu.CompilerParams(vmem_limit_bytes=1024 * 1024),
        cost_estimate=pl.CostEstimate(
            flops=int(micros * FLOPS_A_MICRO), bytes_accessed=0, transcendentals=0
        ),
    )(*arrays, *awaited)


def pack_heads(query_ref, key_ref, value_ref, *rest):
    outs, sem = rest[:N_CTX], rest[N_CTX]
    half = query_ref.shape[2] // 2
    place = lax.axis_index("ctx")
    pairs = []
    for apart in (2, 3, 1, 0):
        dest = place ^ apart
        cols = columns((dest & 1) * half, half)
        for slot, ref in enumerate((query_ref, key_ref, value_ref)):
            pairs.append((ref.at[half_of(dest), :, cols], outs[apart].at[slot]))
    run_copies(pairs, sem)


def pack_weights(panel_ref, taps_ref, awaited_ref, out_ref):
    entries = panel_ref.shape[0]
    taps = taps_ref[...].astype(jnp.float32)
    high = jnp.concatenate(
        [taps[TAP_PAD // 2 :], jnp.zeros((TAP_PAD - TAPS, taps.shape[1]), jnp.float32)], axis=0
    )
    out_ref[0, 0:entries] = panel_ref[...]
    joined = jnp.concatenate([taps[: TAP_PAD // 2], high], axis=1)
    out_ref[0, entries:] = joined.astype(jnp.bfloat16)


def pack_channels(frame_ref, grad_ref, awaited_ref, *rest):
    across_ref, grad_outs, beside_ref, own_ref, sem = rest[0], rest[1:3], *rest[3:]
    width = frame_ref.shape[2] // N_CTX
    frames = frame_ref.shape[1]
    place = lax.axis_index("ctx")
    pairs = []
    for slot, ref in enumerate((frame_ref, grad_ref)):
        for apart in (2, 3, 1, 0):
            cols = columns((place ^ apart) * width, width)
            for utt in range(2):
                rows = slice(utt * frames, (utt + 1) * frames)
                if apart < 2:
                    target = (own_ref, beside_ref)[apart].at[slot, rows]
                elif slot == 0:
                    target = across_ref.at[apart - 2, rows]
                else:
                    target = grad_outs[apart - 2].at[rows]
                pairs.append((ref.at[utt, :, cols], target))
    run_copies(pairs, sem)


def make_sides(beside_ref, across_ref, out_ref):
    out_ref[0:2] = beside_ref[...]
    out_ref[2] = across_ref[1]


def unpack(*refs):
    ins, refs = refs[:N_CTX], refs[N_CTX:]
    own_ref, beside_ref, output_ref, input_ref = refs[:4]
    heads, channels, sem = refs[4:7], refs[7:9], refs[9]
    half, width = ins[0].shape[2], own_ref.shape[3]
    frames = own_ref.shape[2]
    place = lax.axis_index("ctx")
    pairs = []
    for apart in range(N_CTX):
        source = place ^ apart
        cols = columns((source & 1) * half, half)
        for slot, ref in enumerate(heads):
            pairs.append((ins[apart].at[slot], ref.at[half_of(source), :, cols]))
    for slot, ref in enumerate(channels):
        for utt in range(2):
            part = pl.ds(utt * frames, frames)
            blocks = (
                own_ref.at[slot, utt],
                beside_ref.at[slot, part],
                (output_ref, input_ref)[slot].at[0, part],
                beside_ref.at[2 + slot, part],
            )
            for apart, block in enumerate(blocks):
                cols = columns((place ^ apart) * width, width)
                pairs.append((block, ref.at[utt, :, cols]))
    run_copies(pairs, sem)


def head_parts(refs, slot):
    return jnp.concatenate([ref[slot] for ref in refs], axis=0)


def half_masks(rows):
    lane = lax.broadcasted_iota(jnp.int32, (rows, LANES), 1)
    low = jnp.where(lane < HEAD_DIM, 1.0, 0.0)
    return low.astype(jnp.bfloat16), (1.0 - low).astype(jnp.bfloat16)


def weights_of(length_ref, key_pair, query_pair, mask, frames):
    place = lax.axis_index("ctx")
    rows = key_pair.shape[0]
    frame = lax.broadcasted_iota(jnp.int32, (rows, rows), 0) ^ (place * frames)
    scores = dot_tt(key_pair, query_pair * mask, 1, 1) * HEAD_DIM ** (-0.5)
    scores = jnp.where(frame < length_ref[half_of(place)], scores, masked_score)
    powers = jnp.exp(scores - jnp.max(scores, axis=0, keepdims=True))
    total = jnp.sum(powers, axis=0, keepdims=True)
    return (powers * (1.0 / total)).astype(jnp.bfloat16)


def attend(length_ref, *refs):
    ins, attended_ref = refs[:N_CTX], refs[N_CTX]
    frames, half = ins[0].shape[1], ins[0].shape[2]
    query, key, value = (head_parts(ins, slot) for slot in range(3))
    masks = half_masks(N_CTX * frames)
    for pair in range(half // LANES):
        cols = slice(pair * LANES, (pair + 1) * LANES)
        parts = []
        for side in range(2):
            low = weights_of(length_ref, key[:, cols], query[:, cols], masks[side], frames)
            mixed = dot_tt(value[:, cols], low, 0, 0)
            parts.append(mixed[side * HEAD_DIM : (side + 1) * HEAD_DIM])
        joined = jnp.concatenate(parts, axis=0).T.astype(jnp.bfloat16)
        attended_ref[:, :, cols] = joined.reshape(N_CTX, frames, LANES)


def weigh(length_ref, *refs):
    ins, weight_ref = refs[:N_CTX], refs[N_CTX + 1]
    frames, half = ins[0].shape[1], ins[0].shape[2]
    query, key = (head_parts(ins, slot) for slot in range(2))
    masks = half_masks(N_CTX * frames)
    for pair in range(half // LANES):
        cols = slice(pair * LANES, (pair + 1) * LANES)
        for side in range(2):
            weight_ref[2 * pair + side] = weights_of(
                length_ref, key[:, cols], query[:, cols], masks[side], frames
            )


def forward(length_ref, near_ref, other_ref, *refs):
    attended_refs, refs = refs[:N_CTX], refs[N_CTX:]
    own_ref, beside_ref, across_ref = refs[:3]
    out_refs, refs = refs[3:6], refs[6:]
    whole_ref, rows_ref, taps_ref, total_ref, masked_ref = refs[:5]
    hidden_ref, frame_ref, result_ref = refs[5:]
    frames, half = attended_refs[0].shape[1], attended_refs[0].shape[2]
    width = frame_ref.shape[3]
    rows = N_CTX * frames
    chunks = width // LANES
    entries = 2 * half // N_DP
    own = width // 2
    place = lax.axis_index("ctx")
    for apart in range(N_CTX):
        source = place ^ apart
        cols = columns((source & 1) * half, half)
        for block in range(N_CTX):
            whole_ref[half_of(source), block ^ source, :, cols] = attended_refs[apart][block]
        block = (own_ref, beside_ref, across_ref, beside_ref)[apart][(0, 0, 0, 2)[apart]]
        frame_ref[source] = block.reshape(frame_ref.shape[1:])
    group = lax.axis_index("dp")
    for slot, apart in enumerate((0, 4, 2, 6)):
        for odd, ref in enumerate((near_ref, other_ref)):
            first = pl.multiple_of((group ^ (apart + odd)) * entries, entries)
            rows_ref[pl.ds(first, entries)] = ref[slot, 0:entries]
    apart = place ^ half_of(group)
    slot = ((apart & 1) << 1) | half_of(apart)
    odd = (group & 1) == 1
    blocks = [ref[slot, entries:].astype(jnp.float32) for ref in (near_ref, other_ref)]
    blocks = (jnp.where(odd, blocks[1], blocks[0]), jnp.where(odd, blocks[0], blocks[1]))
    pieces = [jnp.concatenate([block[:, :own], block[:, own:]], axis=0) for block in blocks]
    taps = jnp.concatenate(pieces, axis=1)
    for chunk in range(chunks):
        for tap in range(TAPS):
            taps_ref[chunk, tap] = jnp.broadcast_to(
                taps[tap : tap + 1, chunk * LANES : (chunk + 1) * LANES], (8, LANES)
            )
    edge = jnp.zeros((2 * chunks, 16, LANES), jnp.float32)
    masked_ref[:, 0:16, :] = edge
    masked_ref[:, 16 + rows : 32 + rows, :] = edge
    for utt in range(2):
        real = lax.broadcasted_iota(jnp.int32, (rows, LANES), 0) < length_ref[utt]
        mixed = whole_ref[utt].reshape(rows, 2 * half)
        projected = dot_tt(mixed, rows_ref[...], 1, 0)
        hidden = frame_ref[:, utt].reshape(rows, width).astype(jnp.float32) + projected
        hidden = hidden.astype(jnp.bfloat16).astype(jnp.float32)
        for chunk in range(chunks):
            piece = hidden[:, chunk * LANES : (chunk + 1) * LANES]
            hidden_ref[utt * chunks + chunk] = piece
            masked_ref[utt * chunks + chunk, 16 : 16 + rows, :] = jnp.where(real, piece, 0.0)

    def convolve(step, carry):
        utt, chunk = step // chunks, step % chunks
        cols = columns(chunk * LANES, LANES)
        shape = (frames // 8, 8, LANES)
        for block in range(N_CTX):
            base = block * frames
            total = jnp.zeros(shape, jnp.float32)
            for tap in range(TAPS):
                first = base + tap + 16 - REACH
                piece = masked_ref[step, first : first + frames, :]
                total += taps_ref[chunk, tap][None] * piece.reshape(shape)
            total = total.reshape(frames, LANES)
            total_ref[step, base : base + frames, :] = total
            outer = hidden_ref[step, base : base + frames, :] + total * jax.nn.sigmoid(total)
            result_ref[block, utt, :, cols] = outer.astype(jnp.bfloat16)
        return carry

    lax.fori_loop(0, 2 * chunks, convolve, 0)
    for apart in range(2):
        out_refs[apart][...] = result_ref[place ^ apart]
        out_refs[2][apart] = result_ref[place ^ (2 + apart)].reshape(2 * frames, width)


def backward(length_ref, total_ref, taps_ref, rows_ref, *refs):
    own_ref, beside_ref = refs[:2]
    own_sides_ref, beside_sides_ref, grad_across_ref, grad_diagonal_ref = refs[2:6]
    refs = refs[6:]
    own_pair_ref, beside_pair_ref, across_ref = refs[:3]
    grad_ref, keep_ref, send_ref, cotangent_ref = refs[3:7]
    side_ref, result_ref = refs[7:]
    own_pair_ref[0], beside_pair_ref[0] = own_ref[...], beside_ref[...]
    utts, frames, width = own_ref.shape
    rows = N_CTX * frames
    chunks = width // LANES
    half = rows_ref.shape[0] // 2
    place = lax.axis_index("ctx")
    blocks = (own_sides_ref[1], beside_sides_ref[1], grad_across_ref[...], grad_diagonal_ref[...])
    for apart in range(N_CTX):
        side_ref[place ^ apart] = blocks[apart].reshape(side_ref.shape[1:])
    edge = jnp.zeros((2 * chunks, 16, LANES), jnp.float32)
    cotangent_ref[:, 0:16, :] = edge
    cotangent_ref[:, 16 + rows : 32 + rows, :] = edge

    def convolve(step, carry):
        utt, chunk = step // chunks, step % chunks
        cols = columns(chunk * LANES, LANES)
        length = length_ref[utt]
        shape = (frames // 8, 8, LANES)
        for block in range(N_CTX):
            base = block * frames
            total = total_ref[step, base : base + frames, :]
            gate = jax.nn.sigmoid(total)
            incoming = side_ref[block, utt, :, cols].astype(jnp.float32)
            slope = gate * (1.0 + total * (1.0 - gate))
            low = (incoming * slope).astype(jnp.bfloat16)
            cotangent_ref[step, 16 + base : 16 + base + frames, :] = low.astype(jnp.float32)
        for block in range(N_CTX):
            base = block * frames
            total = jnp.zeros(shape, jnp.float32)
            for tap in range(TAPS):
                first = base + 16 + REACH - tap
                piece = cotangent_ref[step, first : first + frames, :].reshape(shape)
                total += taps_ref[chunk, tap][None] * piece
            place_of = base + lax.broadcasted_iota(jnp.int32, (frames, LANES), 0)
            total = jnp.where(place_of < length, total.reshape(frames, LANES), 0.0)
            incoming = side_ref[block, utt, :, cols].astype(jnp.float32)
            low = (incoming + total).astype(jnp.bfloat16)
            result_ref[block, utt, :, cols] = low
            grad_ref[utt, base : base + frames, cols] = low
        return carry

    lax.fori_loop(0, 2 * chunks, convolve, 0)
    for apart in range(N_CTX):
        mine = result_ref[place ^ apart]
        if apart < 2:
            (own_pair_ref, beside_pair_ref)[apart][1] = mine
        else:
            across_ref[apart - 2] = mine.reshape(utts * frames, width)
        dest = place ^ apart
        mixed = dot_tt(
            grad_ref[half_of(dest)],
            rows_ref[pl.ds(pl.multiple_of((dest & 1) * half, half), half)],
            1,
            1,
        ).astype(jnp.bfloat16)
        ref = send_ref if apart % 2 else keep_ref
        for block in range(N_CTX):
            first = pl.multiple_of((block ^ dest) * frames, frames)
            ref[apart // 2, pl.ds(first, frames), :] = mixed[block * frames : (block + 1) * frames]


def make_taps(masked_ref, cotangent_ref, awaited_ref, keep_ref, send_ref, tap_sum_ref):
    steps, rows, chunks = masked_ref.shape[0], masked_ref.shape[1] - 32, tap_sum_ref.shape[0]
    block = 64
    shape = (block // 8, 8, LANES)
    tap_sum_ref[...] = jnp.zeros_like(tap_sum_ref)

    def correlate(step, carry):
        chunk = step % chunks
        for base in range(0, rows, block):
            held = masked_ref[step, 16 + base : 16 + base + block, :].reshape(shape)
            for tap in range(TAPS):
                first = base + 16 + REACH - tap
                piece = cotangent_ref[step, first : first + block, :].reshape(shape)
                tap_sum_ref[chunk, tap] += jnp.sum(held * piece, axis=0)
        return carry

    lax.fori_loop(0, steps, correlate, 0)
    sums = [
        jnp.concatenate(
            [
                jnp.sum(tap_sum_ref[chunk, tap], axis=0, keepdims=True)
                for tap in range(TAP_PAD)
            ],
            axis=0,
        )
        for chunk in range(chunks)
    ]
    sums = jnp.concatenate(sums, axis=1)
    own = sums.shape[1] // 2
    halves = [
        jnp.concatenate([part[: TAP_PAD // 2], part[TAP_PAD // 2 :]], axis=1)
        for part in (sums[:, :own], sums[:, own:])
    ]
    odd = (lax.axis_index("dp") & 1) == 1
    keep_ref[...] = jnp.where(odd, halves[1], halves[0])
    send_ref[...] = jnp.where(odd, halves[0], halves[1])


def make_panels(whole_ref, grad_ref, panel_ref):
    rows, half = grad_ref.shape[1], whole_ref.shape[3] // 2
    entries = 2 * half // N_DP
    group = lax.axis_index("dp")
    for side in range(2):
        panel = 0.0
        for utt in range(2):
            mixed = whole_ref[utt, :, :, side * half : (side + 1) * half].reshape(rows, half)
            panel += dot_tt(mixed, grad_ref[utt], 0, 0)
        panel = panel.astype(jnp.bfloat16)
        for part in range(N_DP // 2):
            panel_ref[slot_of(side * N_DP // 2 + part, group)] = panel[
                part * entries : (part + 1) * entries
            ]


def join(panel_ref, came_ref, tap_ref, tap_came_ref, awaited_ref, keep_ref, send_ref):
    entries = panel_ref.shape[1]
    group, place = lax.axis_index("dp"), lax.axis_index("ctx")
    taps = (tap_ref[...] + tap_came_ref[...]).astype(jnp.bfloat16)
    none = jnp.zeros_like(taps)
    for slot in range(N_DP // 2):
        ref = (keep_ref, send_ref)[slot // 2]
        total = panel_ref[slot].astype(jnp.float32) + came_ref[slot].astype(jnp.float32)
        ref[slot % 2, 0:entries] = total.astype(jnp.bfloat16)
        ref[slot % 2, entries:] = none
    mine = slot_of(2 * place, group & 6)
    for slot in range(N_DP // 2):
        ref = (keep_ref, send_ref)[slot // 2]

        @pl.when(mine == slot)
        def _(ref=ref, slot=slot):
            ref[slot % 2, entries:] = taps


def pick_taps(*refs):
    ins, held_ref, out_ref = refs[:N_CTX], refs[N_CTX + 1], refs[N_CTX]
    own = ins[0].shape[1] // 2
    for apart in range(N_CTX):
        held_ref[apart] = ins[apart][...]
    mine = held_ref[lax.axis_index("ctx") ^ half_of(lax.axis_index("dp"))]
    out_ref[...] = jnp.concatenate([mine[:, :own], mine[:, own:]], axis=0)[:TAPS]


def relay(keep_ref, came_ref, out_ref):
    total = keep_ref[1].astype(jnp.float32) + came_ref[1].astype(jnp.float32)
    out_ref[...] = total.astype(jnp.bfloat16)


def make_pair(pair_ref, output_ref, input_ref, *refs):
    out_ref = refs[-1]
    for slot in range(2):
        out_ref[slot] = pair_ref[slot].reshape(out_ref.shape[1:])
    out_ref[2] = output_ref[1]
    out_ref[3] = input_ref[1]


def attend_back(weight_ref, keep_ref, came_ref, far_ref, *refs):
    ins, out_refs = refs[:N_CTX], refs[N_CTX + 1 :]
    frames, half = ins[0].shape[1], ins[0].shape[2]
    rows = N_CTX * frames
    query, key, value = (head_parts(ins, slot) for slot in range(3))
    masks = half_masks(rows)
    scale = HEAD_DIM ** (-0.5)
    arriving = keep_ref[0].astype(jnp.float32) + came_ref[0].astype(jnp.float32)
    arriving = (arriving + far_ref[...].astype(jnp.float32)).astype(jnp.bfloat16)
    low_lanes = lax.broadcasted_iota(jnp.int32, (rows, LANES), 1) < HEAD_DIM
    for pair in range(half // LANES):
        cols = slice(pair * LANES, (pair + 1) * LANES)
        key_pair, value_pair = key[:, cols], value[:, cols]
        query_pair, grad_pair = query[:, cols], arriving[:, cols]
        query_parts, key_parts, value_parts = [], [], []
        for side in range(2):
            low = weight_ref[2 * pair + side]
            weights = low.astype(jnp.float32)
            moved = weights * dot_tt(value_pair, grad_pair * masks[side], 1, 1)
            delta = jnp.sum(moved, axis=0, keepdims=True)
            grad_scores = (moved - weights * delta).astype(jnp.bfloat16)
            value_parts.append(dot_tt(low, grad_pair, 1, 0))
            key_parts.append(dot_tt(grad_scores, query_pair, 1, 0))
            mixed = dot_tt(key_pair, grad_scores, 0, 0)
            query_parts.append(mixed[side * HEAD_DIM : (side + 1) * HEAD_DIM])
        query_sum = (jnp.concatenate(query_parts, axis=0).T * scale).astype(jnp.bfloat16)
        key_sum = (jnp.where(low_lanes, key_parts[0], key_parts[1]) * scale).astype(jnp.bfloat16)
        value_sum = jnp.where(low_lanes, value_parts[0], value_parts[1]).astype(jnp.bfloat16)
        for slot, total in enumerate((query_sum, key_sum, value_sum)):
            for apart in range(N_CTX):
                out_refs[apart][slot, :, cols] = total[apart * frames : (apart + 1) * frames]


def swapped(array, bit):
    return lax.ppermute(array, "dp", [(i, i ^ bit) for i in range(N_DP)])


def dealt(slots):
    return lax.all_to_all(slots, "dp", 0, 0, tiled=True)


def crossed(array, apart):
    return lax.ppermute(array, "ctx", [(i, i ^ apart) for i in range(N_CTX)])


def traded(blocks):
    came = {apart: crossed(blocks[apart], apart) for apart in (2, 3, 1)}
    return [blocks[0]] + [came[apart] for apart in (1, 2, 3)]


def per_device(
    frame_input, queries, key_proj, value_proj, out_weight, conv_weight, lengths, grad_output
):
    utts, frames, wide = frame_input.shape
    inner = queries.shape[2]
    half, width = inner // 2, wide // N_CTX
    rows = N_CTX * frames
    chunks = width // LANES
    low, f32 = jnp.bfloat16, jnp.float32
    shape = jax.ShapeDtypeStruct
    entries = out_weight.shape[1]
    tap_count = conv_weight.shape[0]
    dma = pltpu.SemaphoreType.DMA
    head_block = shape((3, frames, half), low)
    channel_block = shape((utts, frames, width), low)

    blocks = call_kernel(
        pack_heads,
        (head_block,) * N_CTX,
        ["hbm"] * 3,
        scratch=[dma((3 * N_CTX,))],
        room=63,
    )(queries, key_proj, value_proj)
    packed = traded(blocks)
    (shard,) = call_kernel(
        pack_weights,
        (shape((1, entries + TAP_PAD // 2, width), low),),
        ["vmem"] * 2 + ["any"],
    )(out_weight.T, conv_weight, packed[1])
    for bit in (4, 2):
        shard = jnp.concatenate([shard, swapped(shard, bit)], axis=0)
    other_shard = swapped(shard, 1)
    pair_block = shape((2, utts, frames, width), low)
    side_block = shape((utts * frames, width), low)
    double_block = shape((2, utts * frames, width), low)
    frame_across, grad_across, grad_diagonal, beside_sides, own_sides = call_kernel(
        pack_channels,
        (double_block,) + (side_block,) * 2 + (double_block,) * 2,
        ["hbm"] * 2 + ["any"],
        scratch=[dma((4 * N_CTX,))],
    )(frame_input, grad_output, packed[2])
    frame_across = crossed(frame_across, 2)
    (beside_sides,) = call_kernel(
        make_sides, (shape((3, utts * frames, width), low),), ["vmem"] * 2
    )(beside_sides, frame_across)
    beside_sides = crossed(beside_sides, 1)
    (attended,) = call_kernel(
        attend,
        (shape((N_CTX, frames, half), low),),
        ["smem"] + ["vmem"] * N_CTX,
    )(lengths, *packed)
    (attended,) = gate([attended], frame_across)
    across = crossed(attended, 2)
    beside = crossed(attended, 1)
    diagonal = crossed(across, 1)
    grad_across, grad_diagonal = crossed(grad_across, 2), crossed(grad_diagonal, 3)
    forward_out = call_kernel(
        forward,
        (channel_block,) * 2
        + (
            shape((2, utts * frames, width), low),
            shape((utts, N_CTX, frames, inner), low),
            shape((inner, width), low),
            shape((chunks, TAP_PAD, 8, LANES), f32),
            shape((utts * chunks, rows, LANES), f32),
            shape((utts * chunks, rows + 32, LANES), f32),
        ),
        ["smem"] + ["vmem"] * (5 + N_CTX),
        scratch=[
            pltpu.VMEM((utts * chunks, rows, LANES), f32),
            pltpu.VMEM((N_CTX, utts, frames, width), low),
            pltpu.VMEM((N_CTX, utts, frames, width), low),
        ],
        micros=3.2,
    )(
        lengths,
        shard,
        other_shard,
        attended,
        beside,
        across,
        diagonal,
        own_sides,
        beside_sides,
        frame_across,
    )
    output_across = crossed(forward_out[2], 2)
    whole, weight_rows, taps, totals, masked = forward_out[3:]
    grad_blocks = gate([grad_across, grad_diagonal], totals, micros=10.0)
    grad_blocks = (own_sides, beside_sides, *grad_blocks)
    backward_out = call_kernel(
        backward,
        (pair_block,) * 2
        + (
            shape((2, utts * frames, width), low),
            shape((utts, rows, width), low),
            shape((2, rows, half), low),
            shape((2, rows, half), low),
            shape((utts * chunks, rows + 32, LANES), f32),
        ),
        ["smem"] + ["vmem"] * (5 + N_CTX),
        scratch=[
            pltpu.VMEM((N_CTX, utts, frames, width), low),
            pltpu.VMEM((N_CTX, utts, frames, width), low),
        ],
        micros=5.2,
    )(lengths, totals, taps, weight_rows, *forward_out[:2], *grad_blocks)
    grad_hidden, keep, send, cotangents = backward_out[3:]
    (send,) = gate([send], output_across)
    came = crossed(send, 1)
    (relayed,) = call_kernel(
        relay, (shape((rows, half), low),), ["vmem"] * 2, micros=0.2
    )(keep, came)
    (input_across,) = gate([backward_out[2]], relayed)
    (panels,) = call_kernel(
        make_panels,
        (shape((N_DP, entries, width), low),),
        ["vmem"] * 2,
        micros=0.7,
    )(whole, grad_hidden)
    panels_came = swapped(panels[4:], 1)
    tap_block = shape((TAP_PAD // 2, width), f32)
    tap_keep, tap_send = call_kernel(
        make_taps,
        (tap_block,) * 2,
        ["vmem"] * 2 + ["any"],
        scratch=[pltpu.VMEM((chunks, TAP_PAD, 8, LANES), f32)],
    )(masked, cotangents, relayed)
    taps_came = swapped(tap_send, 1)
    far, input_across = crossed(relayed, 2), crossed(input_across, 2)
    (weights,) = call_kernel(
        weigh,
        (shape((half // HEAD_DIM, rows, rows), low),),
        ["smem"] + ["vmem"] * N_CTX + ["any"],
    )(lengths, *packed, relayed)
    back_blocks = call_kernel(
        attend_back,
        (head_block,) * N_CTX,
        ["vmem"] * (4 + N_CTX) + ["any"],
        micros=2.2,
    )(weights, keep, came, far, *packed, taps_came)
    (across_block,) = gate([back_blocks[2]], input_across)
    grad_blocks = traded([*back_blocks[:2], across_block, back_blocks[3]])
    own_pair = backward_out[0]
    (beside_pair,) = call_kernel(
        make_pair,
        (shape((4, utts * frames, width), low),),
        ["vmem"] * 3 + ["any"] * 3,
        micros=0.2,
    )(backward_out[1], output_across, input_across, *grad_blocks[1:])
    beside_pair = crossed(beside_pair, 1)

    kept, sent = call_kernel(
        join,
        (shape((2, entries + TAP_PAD // 2, width), low),) * 2,
        ["vmem"] * 4 + ["any"],
    )(panels[:4], panels_came, tap_keep, taps_came, back_blocks[0])
    panels = (kept.astype(f32) + swapped(sent, 2).astype(f32)).astype(low)
    total = panels[0].astype(f32) + swapped(panels[1], 4).astype(f32)
    grad_out_weight = total[:entries].T
    (tap_sums,) = gate([total[entries:]], beside_pair)
    (grad_taps,) = call_kernel(
        pick_taps,
        (shape(conv_weight.shape, f32),),
        ["vmem"] * N_CTX,
        scratch=[pltpu.VMEM((N_CTX, TAP_PAD // 2, width), f32)],
    )(*traded([tap_sums] * N_CTX))
    unpacked = call_kernel(
        unpack,
        (shape((utts, frames, inner), low),) * 3 + (shape((utts, frames, wide), low),) * 2,
        ["any"] * (N_CTX + 4),
        ["hbm"] * 5,
        [dma((7 * N_CTX + 4 * N_CTX,))],
        micros=1.0,
    )(
        *grad_blocks,
        own_pair,
        beside_pair,
        output_across,
        input_across,
    )
    grad_queries, grad_keys, grad_values, block_output, grad_input = unpacked
    return (
        block_output,
        grad_input,
        grad_queries,
        grad_keys,
        grad_values,
        grad_out_weight,
        grad_taps,
    )


def chosen(sizes, *arrays):
    frame_input, queries, out_weight, conv_weight = (arrays[i] for i in (0, 1, 4, 5))
    utts, frames, wide = frame_input.shape
    inner = queries.shape[2]
    fits = (
        sizes == (N_DP, N_CTX)
        and utts == 2
        and frames == 64
        and wide % (N_CTX * LANES) == 0
        and inner % (2 * LANES) == 0
        and inner // N_DP % 16 == 0
        and inner // 2 == wide // N_CTX
        and conv_weight.shape == (TAPS, wide // N_DP)
        and out_weight.shape == (wide // N_CTX, inner // N_DP)
    )
    return (per_device if fits else general_device)(*arrays)


def solution(mesh):
    placed = (
        P("dp", "ctx", None),
        P("dp", "ctx", None),
        P("dp", "ctx", None),
        P("dp", "ctx", None),
        P("ctx", "dp"),
        P(None, "dp"),
        P("dp"),
        P("dp", "ctx", None),
    )
    sizes = (mesh.shape["dp"], mesh.shape["ctx"])
    return jax.shard_map(
        functools.partial(chosen, sizes),
        mesh=mesh,
        in_specs=placed,
        out_specs=(
            P("dp", "ctx", None),
            P("dp", "ctx", None),
            P("dp", "ctx", None),
            P("dp", "ctx", None),
            P("dp", "ctx", None),
            P("ctx", "dp"),
            P(None, "dp"),
        ),
        check_vma=False,
    )
```

```python
import functools

import jax
import jax.numpy as jnp
from jax import lax
from jax.experimental import pallas as pl
from jax.experimental.pallas import tpu as pltpu
from jax.sharding import PartitionSpec as P

HEAD_DIM = 64


masked_score = -1e30


def padded_2(array, sides, width):
    for axis, dim in sides:
        size, length = (lax.axis_size(axis), array.shape[dim])
        up = [(i, (i + 1) % size) for i in range(size - 1)]
        down = [(j, i) for i, j in up]
        last = lax.slice_in_dim(array, length - width, length, axis=dim)
        leading = lax.slice_in_dim(array, 0, width, axis=dim)
        before = lax.ppermute(last, axis, up)
        after = lax.ppermute(leading, axis, down)
        array = jnp.concatenate([before, array, after], axis=dim)
    return array


def depthwise(lhs, rhs):
    return lax.conv_general_dilated(
        lhs,
        rhs,
        (1,),
        "VALID",
        dimension_numbers=("NWC", "WIO", "NWC"),
        feature_group_count=lhs.shape[2],
        precision=lax.Precision.HIGHEST,
    )


def general_device(
    frame_input, queries, key_proj, value_proj, out_weight, conv_weight, lengths, grad_output
):
    utt_count = frame_input.shape[0]
    frame_count = frame_input.shape[1]
    inner_width = queries.shape[2]
    head_count = inner_width // HEAD_DIM
    group_heads = max((g for g in range(1, 7) if head_count % g == 0))
    group_count = head_count // group_heads
    group_width = group_heads * HEAD_DIM
    tap_count = conv_weight.shape[0]
    half_span = (tap_count - 1) // 2
    score_scale = HEAD_DIM ** (-0.5)
    total_frames = frame_count * lax.axis_size("ctx")
    offset = lax.axis_index("ctx") * frame_count
    own_valid = (offset + jnp.arange(frame_count, dtype=jnp.int32))[None, :] < lengths[:, None]
    all_valid = jnp.arange(total_frames, dtype=jnp.int32)[None, :] < lengths[:, None]

    def grouped(values):
        row_count = values.shape[1]
        return values.reshape(utt_count, row_count, group_count, group_width).transpose(2, 0, 1, 3)

    def ungrouped(values):
        row_count = values.shape[2]
        return values.transpose(1, 2, 0, 3).reshape(utt_count, row_count, group_count * group_width)

    def split_heads(values):
        return values.reshape(utt_count, values.shape[1], group_heads, HEAD_DIM)

    def stats_grouped(values):
        row_count = values.shape[1]
        return values.reshape(utt_count, row_count, group_count, group_heads).transpose(2, 0, 3, 1)

    def masked_scores(query_block, key_block, key_mask):
        scores = (
            jnp.einsum(
                "uqgd,ukgd->ugqk", query_block, key_block, preferred_element_type=jnp.float32
            )
            * score_scale
        )
        return jnp.where(key_mask[:, None, None, :], scores, masked_score)

    taps = lax.all_gather(conv_weight, "dp", axis=1, tiled=True).astype(jnp.float32)
    panel_rows = lax.all_gather(out_weight, "dp", axis=1, tiled=True)
    weight_full = lax.all_gather(panel_rows, "ctx", axis=0, tiled=True)
    all_keys, all_values = (
        lax.all_gather(key_proj, "ctx", axis=1, tiled=True),
        lax.all_gather(value_proj, "ctx", axis=1, tiled=True),
    )
    query_groups = grouped(queries)
    key_groups = grouped(all_keys)
    value_groups = grouped(all_values)

    def forward_group(unused, items):
        query_group, key_group, value_group = items
        query_block = split_heads(query_group)
        scores = masked_scores(query_block, split_heads(key_group), all_valid)
        largest = jnp.max(scores, axis=-1)
        log_group = largest + jnp.log(jnp.sum(jnp.exp(scores - largest[..., None]), axis=-1))
        weights_low = jnp.exp(scores - log_group[..., None]).astype(jnp.bfloat16)
        attended_group = jnp.einsum(
            "ugqk,ukgd->uqgd",
            weights_low,
            split_heads(value_group),
            preferred_element_type=jnp.float32,
        )
        return (None, (log_group, attended_group.reshape(utt_count, frame_count, group_width)))

    _, (log_groups, attended_groups) = lax.scan(
        forward_group, None, (query_groups, key_groups, value_groups)
    )
    attended = ungrouped(attended_groups).astype(jnp.bfloat16)
    log_total = log_groups.transpose(1, 3, 0, 2).reshape(utt_count, frame_count, head_count)
    projected = jnp.einsum("ufe,de->ufd", attended, weight_full, preferred_element_type=jnp.float32)
    hidden = (frame_input.astype(jnp.float32) + projected).astype(jnp.bfloat16)
    masked_hidden = jnp.where(own_valid[:, :, None], hidden, jnp.zeros_like(hidden))
    padded = padded_2(masked_hidden, (("ctx", 1),), half_span).astype(jnp.float32)
    conv_sum = depthwise(padded, taps[:, None, :])
    sigmoid = jax.nn.sigmoid(conv_sum)
    block_output = (hidden.astype(jnp.float32) + conv_sum * sigmoid).astype(jnp.bfloat16)
    grad_local = grad_output.astype(jnp.float32)
    swish_slope = sigmoid * (1.0 + conv_sum * (1.0 - sigmoid))
    grad_conv = (grad_local * swish_slope).astype(jnp.bfloat16)
    grad_padded = padded_2(grad_conv, (("ctx", 1),), half_span).astype(jnp.float32)
    back_sum = depthwise(grad_padded, taps[::-1][:, None, :])
    grad_hidden = (grad_local + jnp.where(own_valid[:, :, None], back_sum, 0.0)).astype(
        jnp.bfloat16
    )
    grad_conv_wide = grad_conv.astype(jnp.float32)
    kernel_term = jnp.zeros((tap_count, conv_sum.shape[2]), jnp.float32)
    for utt_index in range(utt_count):
        kernel_term = (
            kernel_term
            + depthwise(padded[utt_index : utt_index + 1], grad_conv_wide[utt_index][:, None, :])[0]
        )
    kernel_whole = lax.psum(kernel_term.astype(jnp.bfloat16), "ctx")
    grad_conv_weight = lax.psum_scatter(kernel_whole, "dp", scatter_dimension=1, tiled=True).astype(
        jnp.float32
    )
    grad_attended = jnp.einsum(
        "ufd,de->ufe", grad_hidden, weight_full, preferred_element_type=jnp.float32
    ).astype(jnp.bfloat16)
    row_delta = jnp.sum(
        grad_attended.astype(jnp.float32).reshape(utt_count, frame_count, head_count, HEAD_DIM)
        * attended.astype(jnp.float32).reshape(utt_count, frame_count, head_count, HEAD_DIM),
        axis=-1,
    )
    grad_groups = grouped(grad_attended)

    def query_group_step(unused, items):
        query_group, key_group, value_group, grad_group, log_group, delta_group = items
        key_block = split_heads(key_group)
        weights = jnp.exp(
            masked_scores(split_heads(query_group), key_block, all_valid) - log_group[..., None]
        )
        grad_weights = jnp.einsum(
            "uqgd,ukgd->ugqk",
            split_heads(grad_group),
            split_heads(value_group),
            preferred_element_type=jnp.float32,
        )
        grad_scores = (weights * (grad_weights - delta_group[..., None])).astype(jnp.bfloat16)
        query_sum = jnp.einsum(
            "ugqk,ukgd->uqgd", grad_scores, key_block, preferred_element_type=jnp.float32
        )
        return (None, query_sum.reshape(utt_count, frame_count, group_width))

    _, query_sums = lax.scan(
        query_group_step,
        None,
        (
            query_groups,
            key_groups,
            value_groups,
            grad_groups,
            stats_grouped(log_total),
            stats_grouped(row_delta),
        ),
    )
    grad_queries = (ungrouped(query_sums) * score_scale).astype(jnp.bfloat16)
    total_log, total_delta = (
        lax.all_gather(log_total, "ctx", axis=1, tiled=True),
        lax.all_gather(row_delta, "ctx", axis=1, tiled=True),
    )
    own_key_groups = grouped(key_proj)
    own_value_groups = grouped(value_proj)
    group_zeros = jnp.zeros((group_count, utt_count, frame_count, group_width), jnp.float32)
    start_sums = (group_zeros, group_zeros)
    query_all, grad_all = (
        lax.all_gather(queries, "ctx", axis=1, tiled=True),
        lax.all_gather(grad_attended, "ctx", axis=1, tiled=True),
    )
    log_piece = stats_grouped(total_log)
    delta_piece = stats_grouped(total_delta)

    def key_group_step(unused, items):
        (
            query_group,
            grad_group,
            log_group,
            delta_group,
            key_group,
            value_group,
            key_sum,
            value_sum,
        ) = items
        query_block = split_heads(query_group)
        grad_block = split_heads(grad_group)
        weights = jnp.exp(
            masked_scores(query_block, split_heads(key_group), own_valid) - log_group[..., None]
        )
        grad_weights = jnp.einsum(
            "uqgd,ukgd->ugqk",
            grad_block,
            split_heads(value_group),
            preferred_element_type=jnp.float32,
        )
        grad_scores = (weights * (grad_weights - delta_group[..., None])).astype(jnp.bfloat16)
        key_next = key_sum + jnp.einsum(
            "ugqk,uqgd->ukgd", grad_scores, query_block, preferred_element_type=jnp.float32
        ).reshape(utt_count, frame_count, group_width)
        value_next = value_sum + jnp.einsum(
            "ugqk,uqgd->ukgd",
            weights.astype(jnp.bfloat16),
            grad_block,
            preferred_element_type=jnp.float32,
        ).reshape(utt_count, frame_count, group_width)
        return (None, (key_next, value_next))

    _, result_sums = lax.scan(
        key_group_step,
        None,
        (
            grouped(query_all),
            grouped(grad_all),
            log_piece,
            delta_piece,
            own_key_groups,
            own_value_groups,
            start_sums[0],
            start_sums[1],
        ),
    )
    key_sum, value_sum = result_sums
    grad_keys = (ungrouped(key_sum) * score_scale).astype(jnp.bfloat16)
    grad_values = ungrouped(value_sum).astype(jnp.bfloat16)
    hidden_cols = lax.slice_in_dim(
        grad_hidden, 0, weight_full.shape[0] // lax.axis_size("ctx") * lax.axis_size("ctx"), axis=2
    )
    panel_share = lax.psum_scatter(
        jnp.einsum("ufd,ufe->de", hidden_cols, attended, preferred_element_type=jnp.float32).astype(
            jnp.bfloat16
        ),
        "ctx",
        scatter_dimension=0,
        tiled=True,
    )
    grad_out_weight = lax.psum_scatter(panel_share, "dp", scatter_dimension=1, tiled=True).astype(
        jnp.float32
    )
    return (
        block_output,
        grad_hidden,
        grad_queries,
        grad_keys,
        grad_values,
        grad_out_weight,
        grad_conv_weight,
    )


LANES = 128
N_CTX = 4
N_DP = 8
TAP_PAD = 32
FLOPS_A_MICRO = 1.15e9
TAPS = 31
REACH = 15


def slot_of(index, me):
    apart = index ^ me
    return ((apart & 1) << 2) | (apart & 2) | ((apart >> 2) & 1)


def dot_tt(lhs, rhs, lhs_dim, rhs_dim):
    return lax.dot_general(
        lhs, rhs, (((lhs_dim,), (rhs_dim,)), ((), ())), preferred_element_type=jnp.float32
    )


def call_kernel(body, out_shape, ins, outs=None, scratch=(), room=40, micros=1.0):
    spaces = {
        "smem": pl.BlockSpec(memory_space=pltpu.SMEM),
        "vmem": pl.BlockSpec(memory_space=pltpu.VMEM),
        "hbm": pl.BlockSpec(memory_space=pltpu.HBM),
        "any": pl.BlockSpec(memory_space=pl.ANY),
    }
    return pl.pallas_call(
        body,
        out_shape=out_shape,
        in_specs=[spaces[space] for space in ins],
        out_specs=[spaces[space] for space in (outs or ["vmem"] * len(out_shape))],
        scratch_shapes=list(scratch),
        compiler_params=pltpu.CompilerParams(vmem_limit_bytes=room * 1024 * 1024),
        cost_estimate=pl.CostEstimate(
            flops=int(micros * FLOPS_A_MICRO), bytes_accessed=0, transcendentals=0
        ),
    )


def half_of(index):
    return lax.shift_right_logical(index, 1)


def columns(start, size):
    return pl.ds(pl.multiple_of(start, LANES), size)


def start_copies(pairs, sem):
    for number, (source, target) in enumerate(pairs):
        pltpu.make_async_copy(source, target, sem.at[number]).start()


def wait_copies(pairs, sem):
    for number, (source, target) in enumerate(pairs):
        pltpu.make_async_copy(source, target, sem.at[number]).wait()


def run_copies(pairs, sem):
    start_copies(pairs, sem)
    wait_copies(pairs, sem)


def untouched(*refs):
    pass


def gate(arrays, *awaited, micros=0.0):
    count = len(arrays)
    spec = pl.BlockSpec(memory_space=pl.ANY)
    return pl.pallas_call(
        untouched,
        out_shape=tuple(jax.ShapeDtypeStruct(array.shape, array.dtype) for array in arrays),
        in_specs=[spec] * (count + len(awaited)),
        out_specs=(spec,) * count,
        input_output_aliases={number: number for number in range(count)},
        compiler_params=pltpu.CompilerParams(vmem_limit_bytes=1024 * 1024),
        cost_estimate=pl.CostEstimate(
            flops=int(micros * FLOPS_A_MICRO), bytes_accessed=0, transcendentals=0
        ),
    )(*arrays, *awaited)


def pack_heads(query_ref, key_ref, value_ref, *rest):
    outs, sem = rest[:N_CTX], rest[N_CTX]
    half = query_ref.shape[2] // 2
    place = lax.axis_index("ctx")
    pairs = []
    for apart in (2, 3, 1, 0):
        dest = place ^ apart
        cols = columns((dest & 1) * half, half)
        for slot, ref in enumerate((query_ref, key_ref, value_ref)):
            pairs.append((ref.at[half_of(dest), :, cols], outs[apart].at[slot]))
    run_copies(pairs, sem)


def pack_weights(panel_ref, taps_ref, awaited_ref, out_ref):
    entries = panel_ref.shape[0]
    taps = taps_ref[...].astype(jnp.float32)
    high = jnp.concatenate(
        [taps[TAP_PAD // 2 :], jnp.zeros((TAP_PAD - TAPS, taps.shape[1]), jnp.float32)], axis=0
    )
    out_ref[0, 0:entries] = panel_ref[...]
    joined = jnp.concatenate([taps[: TAP_PAD // 2], high], axis=1)
    out_ref[0, entries:] = joined.astype(jnp.bfloat16)


def pack_near(held_ref, came_ref, out_ref):
    entries = held_ref.shape[1] - TAP_PAD // 2
    for slot in range(2):
        for half, ref in enumerate((held_ref, came_ref)):
            first = (2 * half + slot) * entries
            out_ref[first : first + entries, :] = ref[slot, 0:entries]
    apart = lax.axis_index("ctx") ^ half_of(lax.axis_index("dp"))
    slot = half_of(apart)
    taps = [ref[slot, entries:].astype(jnp.float32) for ref in (held_ref, came_ref)]
    taps = jnp.where((apart & 1) == 1, taps[1], taps[0])
    out_ref[4 * entries :, :] = taps.astype(jnp.bfloat16)


def pack_channels(frame_ref, grad_ref, awaited_ref, *rest):
    across_ref, grad_outs, beside_ref, own_ref, sem = rest[0], rest[1:3], *rest[3:]
    width = frame_ref.shape[2] // N_CTX
    frames = frame_ref.shape[1]
    place = lax.axis_index("ctx")
    pairs = []
    for slot, ref in enumerate((frame_ref, grad_ref)):
        for apart in (2, 3, 1, 0):
            cols = columns((place ^ apart) * width, width)
            for utt in range(2):
                rows = slice(utt * frames, (utt + 1) * frames)
                if apart < 2:
                    target = (own_ref, beside_ref)[apart].at[slot, rows]
                elif slot == 0:
                    target = across_ref.at[apart - 2, rows]
                else:
                    target = grad_outs[apart - 2].at[rows]
                pairs.append((ref.at[utt, :, cols], target))
    run_copies(pairs, sem)


def make_sides(beside_ref, across_ref, out_ref):
    out_ref[0:2] = beside_ref[...]
    out_ref[2] = across_ref[1]


def unpack(*refs):
    ins, refs = refs[:N_CTX], refs[N_CTX:]
    own_ref, beside_ref, output_ref, input_ref = refs[:4]
    heads, channels, sem = refs[4:7], refs[7:9], refs[9]
    half, width = ins[0].shape[2], own_ref.shape[3]
    frames = own_ref.shape[2]
    place = lax.axis_index("ctx")
    pairs = []
    for apart in range(N_CTX):
        source = place ^ apart
        cols = columns((source & 1) * half, half)
        for slot, ref in enumerate(heads):
            pairs.append((ins[apart].at[slot], ref.at[half_of(source), :, cols]))
    for slot, ref in enumerate(channels):
        for utt in range(2):
            part = pl.ds(utt * frames, frames)
            blocks = (
                own_ref.at[slot, utt],
                beside_ref.at[slot, part],
                (output_ref, input_ref)[slot].at[0, part],
                beside_ref.at[2 + slot, part],
            )
            for apart, block in enumerate(blocks):
                cols = columns((place ^ apart) * width, width)
                pairs.append((block, ref.at[utt, :, cols]))
    run_copies(pairs, sem)


def head_parts(refs, slot):
    return jnp.concatenate([ref[slot] for ref in refs], axis=0)


def half_masks(rows):
    lane = lax.broadcasted_iota(jnp.int32, (rows, LANES), 1)
    low = jnp.where(lane < HEAD_DIM, 1.0, 0.0)
    return low.astype(jnp.bfloat16), (1.0 - low).astype(jnp.bfloat16)


def weights_of(length_ref, key_pair, query_pair, mask, frames):
    place = lax.axis_index("ctx")
    rows = key_pair.shape[0]
    frame = lax.broadcasted_iota(jnp.int32, (rows, rows), 0) ^ (place * frames)
    scores = dot_tt(key_pair, query_pair * mask, 1, 1) * HEAD_DIM ** (-0.5)
    scores = jnp.where(frame < length_ref[half_of(place)], scores, masked_score)
    powers = jnp.exp(scores - jnp.max(scores, axis=0, keepdims=True))
    total = jnp.sum(powers, axis=0, keepdims=True)
    return (powers * (1.0 / total)).astype(jnp.bfloat16)


def attend(length_ref, *refs):
    ins, attended_ref = refs[:N_CTX], refs[N_CTX]
    frames, half = ins[0].shape[1], ins[0].shape[2]
    query, key, value = (head_parts(ins, slot) for slot in range(3))
    masks = half_masks(N_CTX * frames)
    for pair in range(half // LANES):
        cols = slice(pair * LANES, (pair + 1) * LANES)
        parts = []
        for side in range(2):
            low = weights_of(length_ref, key[:, cols], query[:, cols], masks[side], frames)
            mixed = dot_tt(value[:, cols], low, 0, 0)
            parts.append(mixed[side * HEAD_DIM : (side + 1) * HEAD_DIM])
        joined = jnp.concatenate(parts, axis=0).T.astype(jnp.bfloat16)
        attended_ref[:, :, cols] = joined.reshape(N_CTX, frames, LANES)


def weigh(length_ref, *refs):
    ins, weight_ref = refs[:N_CTX], refs[N_CTX + 1]
    frames, half = ins[0].shape[1], ins[0].shape[2]
    query, key = (head_parts(ins, slot) for slot in range(2))
    masks = half_masks(N_CTX * frames)
    for pair in range(half // LANES):
        cols = slice(pair * LANES, (pair + 1) * LANES)
        for side in range(2):
            weight_ref[2 * pair + side] = weights_of(
                length_ref, key[:, cols], query[:, cols], masks[side], frames
            )


def forward(length_ref, near_ref, other_ref, *refs):
    attended_refs, refs = refs[:N_CTX], refs[N_CTX:]
    own_ref, beside_ref, across_ref = refs[:3]
    out_refs, refs = refs[3:6], refs[6:]
    whole_ref, rows_ref, taps_ref, total_ref, masked_ref = refs[:5]
    hidden_ref, frame_ref, result_ref = refs[5:]
    frames, half = attended_refs[0].shape[1], attended_refs[0].shape[2]
    width = frame_ref.shape[3]
    rows = N_CTX * frames
    chunks = width // LANES
    entries = 2 * half // N_DP
    own = width // 2
    place = lax.axis_index("ctx")
    for apart in range(N_CTX):
        source = place ^ apart
        cols = columns((source & 1) * half, half)
        for block in range(N_CTX):
            whole_ref[half_of(source), block ^ source, :, cols] = attended_refs[apart][block]
        block = (own_ref, beside_ref, across_ref, beside_ref)[apart][(0, 0, 0, 2)[apart]]
        frame_ref[source] = block.reshape(frame_ref.shape[1:])
    group = lax.axis_index("dp")
    for slot, apart in enumerate((0, 4, 2, 6)):
        for odd, ref in enumerate((near_ref, other_ref)):
            first = pl.multiple_of((group ^ (apart + odd)) * entries, entries)
            rows_ref[pl.ds(first, entries)] = ref[slot * entries : (slot + 1) * entries]
    odd = (group & 1) == 1
    blocks = [ref[4 * entries :].astype(jnp.float32) for ref in (near_ref, other_ref)]
    blocks = (jnp.where(odd, blocks[1], blocks[0]), jnp.where(odd, blocks[0], blocks[1]))
    pieces = [jnp.concatenate([block[:, :own], block[:, own:]], axis=0) for block in blocks]
    taps = jnp.concatenate(pieces, axis=1)
    for chunk in range(chunks):
        for tap in range(TAPS):
            taps_ref[chunk, tap] = jnp.broadcast_to(
                taps[tap : tap + 1, chunk * LANES : (chunk + 1) * LANES], (8, LANES)
            )
    edge = jnp.zeros((2 * chunks, 16, LANES), jnp.float32)
    masked_ref[:, 0:16, :] = edge
    masked_ref[:, 16 + rows : 32 + rows, :] = edge
    for utt in range(2):
        real = lax.broadcasted_iota(jnp.int32, (rows, LANES), 0) < length_ref[utt]
        mixed = whole_ref[utt].reshape(rows, 2 * half)
        projected = dot_tt(mixed, rows_ref[...], 1, 0)
        hidden = frame_ref[:, utt].reshape(rows, width).astype(jnp.float32) + projected
        hidden = hidden.astype(jnp.bfloat16).astype(jnp.float32)
        for chunk in range(chunks):
            piece = hidden[:, chunk * LANES : (chunk + 1) * LANES]
            hidden_ref[utt * chunks + chunk] = piece
            masked_ref[utt * chunks + chunk, 16 : 16 + rows, :] = jnp.where(real, piece, 0.0)

    def convolve(step, carry):
        utt, chunk = step // chunks, step % chunks
        cols = columns(chunk * LANES, LANES)
        shape = (frames // 8, 8, LANES)
        for block in range(N_CTX):
            base = block * frames
            total = jnp.zeros(shape, jnp.float32)
            for tap in range(TAPS):
                first = base + tap + 16 - REACH
                piece = masked_ref[step, first : first + frames, :]
                total += taps_ref[chunk, tap][None] * piece.reshape(shape)
            total = total.reshape(frames, LANES)
            total_ref[step, base : base + frames, :] = total
            outer = hidden_ref[step, base : base + frames, :] + total * jax.nn.sigmoid(total)
            result_ref[block, utt, :, cols] = outer.astype(jnp.bfloat16)
        return carry

    lax.fori_loop(0, 2 * chunks, convolve, 0)
    for apart in range(2):
        out_refs[apart][...] = result_ref[place ^ apart]
        out_refs[2][apart] = result_ref[place ^ (2 + apart)].reshape(2 * frames, width)


def backward(length_ref, total_ref, taps_ref, rows_ref, *refs):
    own_ref, beside_ref = refs[:2]
    own_sides_ref, beside_sides_ref, grad_across_ref, grad_diagonal_ref = refs[2:6]
    refs = refs[6:]
    own_pair_ref, beside_pair_ref, across_ref = refs[:3]
    grad_ref, keep_ref, send_ref, cotangent_ref = refs[3:7]
    side_ref, result_ref = refs[7:]
    own_pair_ref[0], beside_pair_ref[0] = own_ref[...], beside_ref[...]
    utts, frames, width = own_ref.shape
    rows = N_CTX * frames
    chunks = width // LANES
    half = rows_ref.shape[0] // 2
    place = lax.axis_index("ctx")
    blocks = (own_sides_ref[1], beside_sides_ref[1], grad_across_ref[...], grad_diagonal_ref[...])
    for apart in range(N_CTX):
        side_ref[place ^ apart] = blocks[apart].reshape(side_ref.shape[1:])
    edge = jnp.zeros((2 * chunks, 16, LANES), jnp.float32)
    cotangent_ref[:, 0:16, :] = edge
    cotangent_ref[:, 16 + rows : 32 + rows, :] = edge

    def convolve(step, carry):
        utt, chunk = step // chunks, step % chunks
        cols = columns(chunk * LANES, LANES)
        length = length_ref[utt]
        shape = (frames // 8, 8, LANES)
        for block in range(N_CTX):
            base = block * frames
            total = total_ref[step, base : base + frames, :]
            gate = jax.nn.sigmoid(total)
            incoming = side_ref[block, utt, :, cols].astype(jnp.float32)
            slope = gate * (1.0 + total * (1.0 - gate))
            low = (incoming * slope).astype(jnp.bfloat16)
            cotangent_ref[step, 16 + base : 16 + base + frames, :] = low.astype(jnp.float32)
        for block in range(N_CTX):
            base = block * frames
            total = jnp.zeros(shape, jnp.float32)
            for tap in range(TAPS):
                first = base + 16 + REACH - tap
                piece = cotangent_ref[step, first : first + frames, :].reshape(shape)
                total += taps_ref[chunk, tap][None] * piece
            place_of = base + lax.broadcasted_iota(jnp.int32, (frames, LANES), 0)
            total = jnp.where(place_of < length, total.reshape(frames, LANES), 0.0)
            incoming = side_ref[block, utt, :, cols].astype(jnp.float32)
            low = (incoming + total).astype(jnp.bfloat16)
            result_ref[block, utt, :, cols] = low
            grad_ref[utt, base : base + frames, cols] = low
        return carry

    lax.fori_loop(0, 2 * chunks, convolve, 0)
    for apart in range(N_CTX):
        mine = result_ref[place ^ apart]
        if apart < 2:
            (own_pair_ref, beside_pair_ref)[apart][1] = mine
        else:
            across_ref[apart - 2] = mine.reshape(utts * frames, width)
        dest = place ^ apart
        mixed = dot_tt(
            grad_ref[half_of(dest)],
            rows_ref[pl.ds(pl.multiple_of((dest & 1) * half, half), half)],
            1,
            1,
        ).astype(jnp.bfloat16)
        ref = send_ref if apart % 2 else keep_ref
        for block in range(N_CTX):
            first = pl.multiple_of((block ^ dest) * frames, frames)
            ref[apart // 2, pl.ds(first, frames), :] = mixed[block * frames : (block + 1) * frames]


def make_taps(masked_ref, cotangent_ref, awaited_ref, keep_ref, send_ref, tap_sum_ref):
    steps, rows, chunks = masked_ref.shape[0], masked_ref.shape[1] - 32, tap_sum_ref.shape[0]
    block = 64
    shape = (block // 8, 8, LANES)
    tap_sum_ref[...] = jnp.zeros_like(tap_sum_ref)

    def correlate(step, carry):
        chunk = step % chunks
        for base in range(0, rows, block):
            held = masked_ref[step, 16 + base : 16 + base + block, :].reshape(shape)
            for tap in range(TAPS):
                first = base + 16 + REACH - tap
                piece = cotangent_ref[step, first : first + block, :].reshape(shape)
                tap_sum_ref[chunk, tap] += jnp.sum(held * piece, axis=0)
        return carry

    lax.fori_loop(0, steps, correlate, 0)
    sums = [
        jnp.concatenate(
            [
                jnp.sum(tap_sum_ref[chunk, tap], axis=0, keepdims=True)
                for tap in range(TAP_PAD)
            ],
            axis=0,
        )
        for chunk in range(chunks)
    ]
    sums = jnp.concatenate(sums, axis=1)
    own = sums.shape[1] // 2
    halves = [
        jnp.concatenate([part[: TAP_PAD // 2], part[TAP_PAD // 2 :]], axis=1)
        for part in (sums[:, :own], sums[:, own:])
    ]
    odd = (lax.axis_index("dp") & 1) == 1
    keep_ref[...] = jnp.where(odd, halves[1], halves[0])
    send_ref[...] = jnp.where(odd, halves[0], halves[1])


def make_panels(whole_ref, grad_ref, panel_ref):
    rows, half = grad_ref.shape[1], whole_ref.shape[3] // 2
    entries = 2 * half // N_DP
    group = lax.axis_index("dp")
    for side in range(2):
        panel = 0.0
        for utt in range(2):
            mixed = whole_ref[utt, :, :, side * half : (side + 1) * half].reshape(rows, half)
            panel += dot_tt(mixed, grad_ref[utt], 0, 0)
        panel = panel.astype(jnp.bfloat16)
        for part in range(N_DP // 2):
            panel_ref[slot_of(side * N_DP // 2 + part, group)] = panel[
                part * entries : (part + 1) * entries
            ]


def join(panel_ref, came_ref, tap_ref, tap_came_ref, awaited_ref, keep_ref, send_ref):
    entries = panel_ref.shape[1]
    group, place = lax.axis_index("dp"), lax.axis_index("ctx")
    taps = (tap_ref[...] + tap_came_ref[...]).astype(jnp.bfloat16)
    none = jnp.zeros_like(taps)
    for slot in range(N_DP // 2):
        ref = (keep_ref, send_ref)[slot // 2]
        total = panel_ref[slot].astype(jnp.float32) + came_ref[slot].astype(jnp.float32)
        ref[slot % 2, 0:entries] = total.astype(jnp.bfloat16)
        ref[slot % 2, entries:] = none
    mine = slot_of(2 * place, group & 6)
    for slot in range(N_DP // 2):
        ref = (keep_ref, send_ref)[slot // 2]

        @pl.when(mine == slot)
        def _(ref=ref, slot=slot):
            ref[slot % 2, entries:] = taps


def mark(*refs):
    refs[-1][...] = jnp.zeros_like(refs[-1])


def finish(kept_ref, came_ref, awaited_ref, panel_ref, taps_ref):
    entries = panel_ref.shape[0]
    total = kept_ref[0].astype(jnp.float32) + came_ref[...].astype(jnp.float32)
    panel_ref[...] = total[:entries]
    taps_ref[...] = total[entries:]


def pick_taps(*refs):
    ins, out_ref, held_ref = refs[:N_CTX], refs[N_CTX + 1], refs[N_CTX + 2]
    own = ins[0].shape[1] // 2
    for apart in range(N_CTX):
        held_ref[apart] = ins[apart][...]
    mine = held_ref[lax.axis_index("ctx") ^ half_of(lax.axis_index("dp"))]
    out_ref[...] = jnp.concatenate([mine[:, :own], mine[:, own:]], axis=0)[:TAPS]


def relay(keep_ref, came_ref, out_ref):
    total = keep_ref[1].astype(jnp.float32) + came_ref[1].astype(jnp.float32)
    out_ref[...] = total.astype(jnp.bfloat16)


def make_pair(pair_ref, output_ref, input_ref, *refs):
    out_ref = refs[-1]
    for slot in range(2):
        out_ref[slot] = pair_ref[slot].reshape(out_ref.shape[1:])
    out_ref[2] = output_ref[1]
    out_ref[3] = input_ref[1]


def attend_back(weight_ref, keep_ref, came_ref, far_ref, *refs):
    ins, out_refs = refs[:N_CTX], refs[N_CTX + 1 :]
    frames, half = ins[0].shape[1], ins[0].shape[2]
    rows = N_CTX * frames
    query, key, value = (head_parts(ins, slot) for slot in range(3))
    masks = half_masks(rows)
    scale = HEAD_DIM ** (-0.5)
    arriving = keep_ref[0].astype(jnp.float32) + came_ref[0].astype(jnp.float32)
    arriving = (arriving + far_ref[...].astype(jnp.float32)).astype(jnp.bfloat16)
    low_lanes = lax.broadcasted_iota(jnp.int32, (rows, LANES), 1) < HEAD_DIM
    for pair in range(half // LANES):
        cols = slice(pair * LANES, (pair + 1) * LANES)
        key_pair, value_pair = key[:, cols], value[:, cols]
        query_pair, grad_pair = query[:, cols], arriving[:, cols]
        query_parts, key_parts, value_parts = [], [], []
        for side in range(2):
            low = weight_ref[2 * pair + side]
            weights = low.astype(jnp.float32)
            moved = weights * dot_tt(value_pair, grad_pair * masks[side], 1, 1)
            delta = jnp.sum(moved, axis=0, keepdims=True)
            grad_scores = (moved - weights * delta).astype(jnp.bfloat16)
            value_parts.append(dot_tt(low, grad_pair, 1, 0))
            key_parts.append(dot_tt(grad_scores, query_pair, 1, 0))
            mixed = dot_tt(key_pair, grad_scores, 0, 0)
            query_parts.append(mixed[side * HEAD_DIM : (side + 1) * HEAD_DIM])
        query_sum = (jnp.concatenate(query_parts, axis=0).T * scale).astype(jnp.bfloat16)
        key_sum = (jnp.where(low_lanes, key_parts[0], key_parts[1]) * scale).astype(jnp.bfloat16)
        value_sum = jnp.where(low_lanes, value_parts[0], value_parts[1]).astype(jnp.bfloat16)
        for slot, total in enumerate((query_sum, key_sum, value_sum)):
            for apart in range(N_CTX):
                out_refs[apart][slot, :, cols] = total[apart * frames : (apart + 1) * frames]


def swapped(array, bit):
    return lax.ppermute(array, "dp", [(i, i ^ bit) for i in range(N_DP)])


def dealt(slots):
    return lax.all_to_all(slots, "dp", 0, 0, tiled=True)


def crossed(array, apart):
    return lax.ppermute(array, "ctx", [(i, i ^ apart) for i in range(N_CTX)])


def traded(blocks):
    came = {apart: crossed(blocks[apart], apart) for apart in (2, 3, 1)}
    return [blocks[0]] + [came[apart] for apart in (1, 2, 3)]


def per_device(
    frame_input, queries, key_proj, value_proj, out_weight, conv_weight, lengths, grad_output
):
    utts, frames, wide = frame_input.shape
    inner = queries.shape[2]
    half, width = inner // 2, wide // N_CTX
    rows = N_CTX * frames
    chunks = width // LANES
    low, f32 = jnp.bfloat16, jnp.float32
    shape = jax.ShapeDtypeStruct
    entries = out_weight.shape[1]
    tap_count = conv_weight.shape[0]
    dma = pltpu.SemaphoreType.DMA
    head_block = shape((3, frames, half), low)
    channel_block = shape((utts, frames, width), low)

    blocks = call_kernel(
        pack_heads,
        (head_block,) * N_CTX,
        ["hbm"] * 3,
        scratch=[dma((3 * N_CTX,))],
        room=63,
    )(queries, key_proj, value_proj)
    packed = traded(blocks)
    (shard,) = call_kernel(
        pack_weights,
        (shape((1, entries + TAP_PAD // 2, width), low),),
        ["vmem"] * 2 + ["any"],
    )(out_weight.T, conv_weight, packed[1])
    shard = jnp.concatenate([shard, swapped(shard, 4)], axis=0)
    (shard,) = call_kernel(
        pack_near, (shape((4 * entries + TAP_PAD // 2, width), low),), ["vmem"] * 2
    )(shard, swapped(shard, 2))
    other_shard = swapped(shard, 1)
    pair_block = shape((2, utts, frames, width), low)
    side_block = shape((utts * frames, width), low)
    double_block = shape((2, utts * frames, width), low)
    frame_across, grad_across, grad_diagonal, beside_sides, own_sides = call_kernel(
        pack_channels,
        (double_block,) + (side_block,) * 2 + (double_block,) * 2,
        ["hbm"] * 2 + ["any"],
        scratch=[dma((4 * N_CTX,))],
    )(frame_input, grad_output, packed[2])
    frame_across = crossed(frame_across, 2)
    (beside_sides,) = call_kernel(
        make_sides, (shape((3, utts * frames, width), low),), ["vmem"] * 2
    )(beside_sides, frame_across)
    beside_sides = crossed(beside_sides, 1)
    (attended,) = call_kernel(
        attend,
        (shape((N_CTX, frames, half), low),),
        ["smem"] + ["vmem"] * N_CTX,
    )(lengths, *packed)
    (attended,) = gate([attended], frame_across)
    across = crossed(attended, 2)
    beside = crossed(attended, 1)
    diagonal = crossed(across, 1)
    grad_across, grad_diagonal = crossed(grad_across, 2), crossed(grad_diagonal, 3)
    forward_out = call_kernel(
        forward,
        (channel_block,) * 2
        + (
            shape((2, utts * frames, width), low),
            shape((utts, N_CTX, frames, inner), low),
            shape((inner, width), low),
            shape((chunks, TAP_PAD, 8, LANES), f32),
            shape((utts * chunks, rows, LANES), f32),
            shape((utts * chunks, rows + 32, LANES), f32),
        ),
        ["smem"] + ["vmem"] * (5 + N_CTX),
        scratch=[
            pltpu.VMEM((utts * chunks, rows, LANES), f32),
            pltpu.VMEM((N_CTX, utts, frames, width), low),
            pltpu.VMEM((N_CTX, utts, frames, width), low),
        ],
        micros=3.2,
    )(
        lengths,
        shard,
        other_shard,
        attended,
        beside,
        across,
        diagonal,
        own_sides,
        beside_sides,
        frame_across,
    )
    output_across = crossed(forward_out[2], 2)
    whole, weight_rows, taps, totals, masked = forward_out[3:]
    grad_blocks = gate([grad_across, grad_diagonal], totals, micros=10.0)
    grad_blocks = (own_sides, beside_sides, *grad_blocks)
    backward_out = call_kernel(
        backward,
        (pair_block,) * 2
        + (
            shape((2, utts * frames, width), low),
            shape((utts, rows, width), low),
            shape((2, rows, half), low),
            shape((2, rows, half), low),
            shape((utts * chunks, rows + 32, LANES), f32),
        ),
        ["smem"] + ["vmem"] * (5 + N_CTX),
        scratch=[
            pltpu.VMEM((N_CTX, utts, frames, width), low),
            pltpu.VMEM((N_CTX, utts, frames, width), low),
        ],
        micros=5.2,
    )(lengths, totals, taps, weight_rows, *forward_out[:2], *grad_blocks)
    grad_hidden, keep, send, cotangents = backward_out[3:]
    (send,) = gate([send], output_across)
    came = crossed(send, 1)
    (relayed,) = call_kernel(
        relay, (shape((rows, half), low),), ["vmem"] * 2, micros=0.2
    )(keep, came)
    (input_across,) = gate([backward_out[2]], relayed)
    (panels,) = call_kernel(
        make_panels,
        (shape((N_DP, entries, width), low),),
        ["vmem"] * 2,
        micros=0.7,
    )(whole, grad_hidden)
    panels_came = swapped(panels[4:], 1)
    tap_block = shape((TAP_PAD // 2, width), f32)
    tap_keep, tap_send = call_kernel(
        make_taps,
        (tap_block,) * 2,
        ["vmem"] * 2 + ["any"],
        scratch=[pltpu.VMEM((chunks, TAP_PAD, 8, LANES), f32)],
    )(masked, cotangents, relayed)
    taps_came = swapped(tap_send, 1)
    far, input_across = crossed(relayed, 2), crossed(input_across, 2)
    (weights,) = call_kernel(
        weigh,
        (shape((half // HEAD_DIM, rows, rows), low),),
        ["smem"] + ["vmem"] * N_CTX + ["any"],
    )(lengths, *packed, relayed)
    back_blocks = call_kernel(
        attend_back,
        (head_block,) * N_CTX,
        ["vmem"] * (4 + N_CTX) + ["any"],
        micros=2.2,
    )(weights, keep, came, far, *packed, taps_came)
    (across_block,) = gate([back_blocks[2]], input_across)
    grad_blocks = traded([*back_blocks[:2], across_block, back_blocks[3]])
    own_pair = backward_out[0]
    (beside_pair,) = call_kernel(
        make_pair,
        (shape((4, utts * frames, width), low),),
        ["vmem"] * 3 + ["any"],
        micros=0.2,
    )(backward_out[1], output_across, input_across, grad_blocks[1])
    beside_pair = crossed(beside_pair, 1)

    kept, sent = call_kernel(
        join,
        (shape((2, entries + TAP_PAD // 2, width), low),) * 2,
        ["vmem"] * 4 + ["any"],
    )(panels[:4], panels_came, tap_keep, taps_came, back_blocks[0])
    panels = (kept.astype(f32) + swapped(sent, 2).astype(f32)).astype(low)
    (arrived,) = call_kernel(mark, (shape((8, LANES), f32),), ["any"] * 2)(*grad_blocks[2:])
    panel_total, tap_sums = call_kernel(
        finish,
        (shape((entries, width), f32), shape((TAP_PAD // 2, width), f32)),
        ["vmem"] * 2 + ["any"],
    )(panels, swapped(panels[1], 4), arrived)
    grad_out_weight = panel_total.T
    unpacked = call_kernel(
        unpack,
        (shape((utts, frames, inner), low),) * 3 + (shape((utts, frames, wide), low),) * 2,
        ["any"] * (N_CTX + 4),
        ["hbm"] * 5,
        [dma((7 * N_CTX + 4 * N_CTX,))],
        micros=1.0,
    )(
        *grad_blocks,
        own_pair,
        beside_pair,
        output_across,
        input_across,
    )
    (grad_taps,) = call_kernel(
        pick_taps,
        (shape(conv_weight.shape, f32),),
        ["vmem"] * N_CTX + ["any"],
        scratch=[pltpu.VMEM((N_CTX, TAP_PAD // 2, width), f32)],
    )(*traded([tap_sums] * N_CTX), unpacked[0])
    grad_queries, grad_keys, grad_values, block_output, grad_input = unpacked
    return (
        block_output,
        grad_input,
        grad_queries,
        grad_keys,
        grad_values,
        grad_out_weight,
        grad_taps,
    )


def chosen(sizes, *arrays):
    frame_input, queries, out_weight, conv_weight = (arrays[i] for i in (0, 1, 4, 5))
    utts, frames, wide = frame_input.shape
    inner = queries.shape[2]
    fits = (
        sizes == (N_DP, N_CTX)
        and utts == 2
        and frames == 64
        and wide % (N_CTX * LANES) == 0
        and inner % (2 * LANES) == 0
        and inner // N_DP % 16 == 0
        and inner // 2 == wide // N_CTX
        and conv_weight.shape == (TAPS, wide // N_DP)
        and out_weight.shape == (wide // N_CTX, inner // N_DP)
    )
    return (per_device if fits else general_device)(*arrays)


def solution(mesh):
    placed = (
        P("dp", "ctx", None),
        P("dp", "ctx", None),
        P("dp", "ctx", None),
        P("dp", "ctx", None),
        P("ctx", "dp"),
        P(None, "dp"),
        P("dp"),
        P("dp", "ctx", None),
    )
    sizes = (mesh.shape["dp"], mesh.shape["ctx"])
    return jax.shard_map(
        functools.partial(chosen, sizes),
        mesh=mesh,
        in_specs=placed,
        out_specs=(
            P("dp", "ctx", None),
            P("dp", "ctx", None),
            P("dp", "ctx", None),
            P("dp", "ctx", None),
            P("dp", "ctx", None),
            P("ctx", "dp"),
            P(None, "dp"),
        ),
        check_vma=False,
    )
```

```python
import functools

import jax
import jax.numpy as jnp
from jax import lax
from jax.experimental import pallas as pl
from jax.experimental.pallas import tpu as pltpu
from jax.sharding import PartitionSpec as P

HEAD_DIM = 64


masked_score = -1e30


def padded_2(array, sides, width):
    for axis, dim in sides:
        size, length = (lax.axis_size(axis), array.shape[dim])
        up = [(i, (i + 1) % size) for i in range(size - 1)]
        down = [(j, i) for i, j in up]
        last = lax.slice_in_dim(array, length - width, length, axis=dim)
        leading = lax.slice_in_dim(array, 0, width, axis=dim)
        before = lax.ppermute(last, axis, up)
        after = lax.ppermute(leading, axis, down)
        array = jnp.concatenate([before, array, after], axis=dim)
    return array


def depthwise(lhs, rhs):
    return lax.conv_general_dilated(
        lhs,
        rhs,
        (1,),
        "VALID",
        dimension_numbers=("NWC", "WIO", "NWC"),
        feature_group_count=lhs.shape[2],
        precision=lax.Precision.HIGHEST,
    )


def general_device(
    frame_input, queries, key_proj, value_proj, out_weight, conv_weight, lengths, grad_output
):
    utt_count = frame_input.shape[0]
    frame_count = frame_input.shape[1]
    inner_width = queries.shape[2]
    head_count = inner_width // HEAD_DIM
    group_heads = max((g for g in range(1, 7) if head_count % g == 0))
    group_count = head_count // group_heads
    group_width = group_heads * HEAD_DIM
    tap_count = conv_weight.shape[0]
    half_span = (tap_count - 1) // 2
    score_scale = HEAD_DIM ** (-0.5)
    total_frames = frame_count * lax.axis_size("ctx")
    offset = lax.axis_index("ctx") * frame_count
    own_valid = (offset + jnp.arange(frame_count, dtype=jnp.int32))[None, :] < lengths[:, None]
    all_valid = jnp.arange(total_frames, dtype=jnp.int32)[None, :] < lengths[:, None]

    def grouped(values):
        row_count = values.shape[1]
        return values.reshape(utt_count, row_count, group_count, group_width).transpose(2, 0, 1, 3)

    def ungrouped(values):
        row_count = values.shape[2]
        return values.transpose(1, 2, 0, 3).reshape(utt_count, row_count, group_count * group_width)

    def split_heads(values):
        return values.reshape(utt_count, values.shape[1], group_heads, HEAD_DIM)

    def stats_grouped(values):
        row_count = values.shape[1]
        return values.reshape(utt_count, row_count, group_count, group_heads).transpose(2, 0, 3, 1)

    def masked_scores(query_block, key_block, key_mask):
        scores = (
            jnp.einsum(
                "uqgd,ukgd->ugqk", query_block, key_block, preferred_element_type=jnp.float32
            )
            * score_scale
        )
        return jnp.where(key_mask[:, None, None, :], scores, masked_score)

    taps = lax.all_gather(conv_weight, "dp", axis=1, tiled=True).astype(jnp.float32)
    panel_rows = lax.all_gather(out_weight, "dp", axis=1, tiled=True)
    weight_full = lax.all_gather(panel_rows, "ctx", axis=0, tiled=True)
    all_keys, all_values = (
        lax.all_gather(key_proj, "ctx", axis=1, tiled=True),
        lax.all_gather(value_proj, "ctx", axis=1, tiled=True),
    )
    query_groups = grouped(queries)
    key_groups = grouped(all_keys)
    value_groups = grouped(all_values)

    def forward_group(unused, items):
        query_group, key_group, value_group = items
        query_block = split_heads(query_group)
        scores = masked_scores(query_block, split_heads(key_group), all_valid)
        largest = jnp.max(scores, axis=-1)
        log_group = largest + jnp.log(jnp.sum(jnp.exp(scores - largest[..., None]), axis=-1))
        weights_low = jnp.exp(scores - log_group[..., None]).astype(jnp.bfloat16)
        attended_group = jnp.einsum(
            "ugqk,ukgd->uqgd",
            weights_low,
            split_heads(value_group),
            preferred_element_type=jnp.float32,
        )
        return (None, (log_group, attended_group.reshape(utt_count, frame_count, group_width)))

    _, (log_groups, attended_groups) = lax.scan(
        forward_group, None, (query_groups, key_groups, value_groups)
    )
    attended = ungrouped(attended_groups).astype(jnp.bfloat16)
    log_total = log_groups.transpose(1, 3, 0, 2).reshape(utt_count, frame_count, head_count)
    projected = jnp.einsum("ufe,de->ufd", attended, weight_full, preferred_element_type=jnp.float32)
    hidden = (frame_input.astype(jnp.float32) + projected).astype(jnp.bfloat16)
    masked_hidden = jnp.where(own_valid[:, :, None], hidden, jnp.zeros_like(hidden))
    padded = padded_2(masked_hidden, (("ctx", 1),), half_span).astype(jnp.float32)
    conv_sum = depthwise(padded, taps[:, None, :])
    sigmoid = jax.nn.sigmoid(conv_sum)
    block_output = (hidden.astype(jnp.float32) + conv_sum * sigmoid).astype(jnp.bfloat16)
    grad_local = grad_output.astype(jnp.float32)
    swish_slope = sigmoid * (1.0 + conv_sum * (1.0 - sigmoid))
    grad_conv = (grad_local * swish_slope).astype(jnp.bfloat16)
    grad_padded = padded_2(grad_conv, (("ctx", 1),), half_span).astype(jnp.float32)
    back_sum = depthwise(grad_padded, taps[::-1][:, None, :])
    grad_hidden = (grad_local + jnp.where(own_valid[:, :, None], back_sum, 0.0)).astype(
        jnp.bfloat16
    )
    grad_conv_wide = grad_conv.astype(jnp.float32)
    kernel_term = jnp.zeros((tap_count, conv_sum.shape[2]), jnp.float32)
    for utt_index in range(utt_count):
        kernel_term = (
            kernel_term
            + depthwise(padded[utt_index : utt_index + 1], grad_conv_wide[utt_index][:, None, :])[0]
        )
    kernel_whole = lax.psum(kernel_term.astype(jnp.bfloat16), "ctx")
    grad_conv_weight = lax.psum_scatter(kernel_whole, "dp", scatter_dimension=1, tiled=True).astype(
        jnp.float32
    )
    grad_attended = jnp.einsum(
        "ufd,de->ufe", grad_hidden, weight_full, preferred_element_type=jnp.float32
    ).astype(jnp.bfloat16)
    row_delta = jnp.sum(
        grad_attended.astype(jnp.float32).reshape(utt_count, frame_count, head_count, HEAD_DIM)
        * attended.astype(jnp.float32).reshape(utt_count, frame_count, head_count, HEAD_DIM),
        axis=-1,
    )
    grad_groups = grouped(grad_attended)

    def query_group_step(unused, items):
        query_group, key_group, value_group, grad_group, log_group, delta_group = items
        key_block = split_heads(key_group)
        weights = jnp.exp(
            masked_scores(split_heads(query_group), key_block, all_valid) - log_group[..., None]
        )
        grad_weights = jnp.einsum(
            "uqgd,ukgd->ugqk",
            split_heads(grad_group),
            split_heads(value_group),
            preferred_element_type=jnp.float32,
        )
        grad_scores = (weights * (grad_weights - delta_group[..., None])).astype(jnp.bfloat16)
        query_sum = jnp.einsum(
            "ugqk,ukgd->uqgd", grad_scores, key_block, preferred_element_type=jnp.float32
        )
        return (None, query_sum.reshape(utt_count, frame_count, group_width))

    _, query_sums = lax.scan(
        query_group_step,
        None,
        (
            query_groups,
            key_groups,
            value_groups,
            grad_groups,
            stats_grouped(log_total),
            stats_grouped(row_delta),
        ),
    )
    grad_queries = (ungrouped(query_sums) * score_scale).astype(jnp.bfloat16)
    total_log, total_delta = (
        lax.all_gather(log_total, "ctx", axis=1, tiled=True),
        lax.all_gather(row_delta, "ctx", axis=1, tiled=True),
    )
    own_key_groups = grouped(key_proj)
    own_value_groups = grouped(value_proj)
    group_zeros = jnp.zeros((group_count, utt_count, frame_count, group_width), jnp.float32)
    start_sums = (group_zeros, group_zeros)
    query_all, grad_all = (
        lax.all_gather(queries, "ctx", axis=1, tiled=True),
        lax.all_gather(grad_attended, "ctx", axis=1, tiled=True),
    )
    log_piece = stats_grouped(total_log)
    delta_piece = stats_grouped(total_delta)

    def key_group_step(unused, items):
        (
            query_group,
            grad_group,
            log_group,
            delta_group,
            key_group,
            value_group,
            key_sum,
            value_sum,
        ) = items
        query_block = split_heads(query_group)
        grad_block = split_heads(grad_group)
        weights = jnp.exp(
            masked_scores(query_block, split_heads(key_group), own_valid) - log_group[..., None]
        )
        grad_weights = jnp.einsum(
            "uqgd,ukgd->ugqk",
            grad_block,
            split_heads(value_group),
            preferred_element_type=jnp.float32,
        )
        grad_scores = (weights * (grad_weights - delta_group[..., None])).astype(jnp.bfloat16)
        key_next = key_sum + jnp.einsum(
            "ugqk,uqgd->ukgd", grad_scores, query_block, preferred_element_type=jnp.float32
        ).reshape(utt_count, frame_count, group_width)
        value_next = value_sum + jnp.einsum(
            "ugqk,uqgd->ukgd",
            weights.astype(jnp.bfloat16),
            grad_block,
            preferred_element_type=jnp.float32,
        ).reshape(utt_count, frame_count, group_width)
        return (None, (key_next, value_next))

    _, result_sums = lax.scan(
        key_group_step,
        None,
        (
            grouped(query_all),
            grouped(grad_all),
            log_piece,
            delta_piece,
            own_key_groups,
            own_value_groups,
            start_sums[0],
            start_sums[1],
        ),
    )
    key_sum, value_sum = result_sums
    grad_keys = (ungrouped(key_sum) * score_scale).astype(jnp.bfloat16)
    grad_values = ungrouped(value_sum).astype(jnp.bfloat16)
    hidden_cols = lax.slice_in_dim(
        grad_hidden, 0, weight_full.shape[0] // lax.axis_size("ctx") * lax.axis_size("ctx"), axis=2
    )
    panel_share = lax.psum_scatter(
        jnp.einsum("ufd,ufe->de", hidden_cols, attended, preferred_element_type=jnp.float32).astype(
            jnp.bfloat16
        ),
        "ctx",
        scatter_dimension=0,
        tiled=True,
    )
    grad_out_weight = lax.psum_scatter(panel_share, "dp", scatter_dimension=1, tiled=True).astype(
        jnp.float32
    )
    return (
        block_output,
        grad_hidden,
        grad_queries,
        grad_keys,
        grad_values,
        grad_out_weight,
        grad_conv_weight,
    )


LANES = 128
N_CTX = 4
N_DP = 8
TAP_PAD = 32
FLOPS_A_MICRO = 1.15e9
TAPS = 31
REACH = 15


def slot_of(index, me):
    apart = index ^ me
    return ((apart & 1) << 2) | (apart & 2) | ((apart >> 2) & 1)


def dot_tt(lhs, rhs, lhs_dim, rhs_dim):
    return lax.dot_general(
        lhs, rhs, (((lhs_dim,), (rhs_dim,)), ((), ())), preferred_element_type=jnp.float32
    )


def call_kernel(body, out_shape, ins, outs=None, scratch=(), room=40, micros=1.0):
    spaces = {
        "smem": pl.BlockSpec(memory_space=pltpu.SMEM),
        "vmem": pl.BlockSpec(memory_space=pltpu.VMEM),
        "hbm": pl.BlockSpec(memory_space=pltpu.HBM),
        "any": pl.BlockSpec(memory_space=pl.ANY),
    }
    return pl.pallas_call(
        body,
        out_shape=out_shape,
        in_specs=[spaces[space] for space in ins],
        out_specs=[spaces[space] for space in (outs or ["vmem"] * len(out_shape))],
        scratch_shapes=list(scratch),
        compiler_params=pltpu.CompilerParams(vmem_limit_bytes=room * 1024 * 1024),
        cost_estimate=pl.CostEstimate(
            flops=int(micros * FLOPS_A_MICRO), bytes_accessed=0, transcendentals=0
        ),
    )


def half_of(index):
    return lax.shift_right_logical(index, 1)


def columns(start, size):
    return pl.ds(pl.multiple_of(start, LANES), size)


def start_copies(pairs, sem):
    for number, (source, target) in enumerate(pairs):
        pltpu.make_async_copy(source, target, sem.at[number]).start()


def wait_copies(pairs, sem):
    for number, (source, target) in enumerate(pairs):
        pltpu.make_async_copy(source, target, sem.at[number]).wait()


def run_copies(pairs, sem):
    start_copies(pairs, sem)
    wait_copies(pairs, sem)


def untouched(*refs):
    pass


def gate(arrays, *awaited, micros=0.0):
    count = len(arrays)
    spec = pl.BlockSpec(memory_space=pl.ANY)
    return pl.pallas_call(
        untouched,
        out_shape=tuple(jax.ShapeDtypeStruct(array.shape, array.dtype) for array in arrays),
        in_specs=[spec] * (count + len(awaited)),
        out_specs=(spec,) * count,
        input_output_aliases={number: number for number in range(count)},
        compiler_params=pltpu.CompilerParams(vmem_limit_bytes=1024 * 1024),
        cost_estimate=pl.CostEstimate(
            flops=int(micros * FLOPS_A_MICRO), bytes_accessed=0, transcendentals=0
        ),
    )(*arrays, *awaited)


def pack_heads(query_ref, key_ref, value_ref, *rest):
    outs, sem = rest[:N_CTX], rest[N_CTX]
    half = query_ref.shape[2] // 2
    place = lax.axis_index("ctx")
    pairs = []
    for apart in (2, 3, 1, 0):
        dest = place ^ apart
        cols = columns((dest & 1) * half, half)
        for slot, ref in enumerate((query_ref, key_ref, value_ref)):
            pairs.append((ref.at[half_of(dest), :, cols], outs[apart].at[slot]))
    run_copies(pairs, sem)


def pack_weights(panel_ref, taps_ref, awaited_ref, out_ref):
    entries = panel_ref.shape[0]
    taps = taps_ref[...].astype(jnp.float32)
    high = jnp.concatenate(
        [taps[TAP_PAD // 2 :], jnp.zeros((TAP_PAD - TAPS, taps.shape[1]), jnp.float32)], axis=0
    )
    out_ref[0, 0:entries] = panel_ref[...]
    joined = jnp.concatenate([taps[: TAP_PAD // 2], high], axis=1)
    out_ref[0, entries:] = joined.astype(jnp.bfloat16)


def pack_near(held_ref, came_ref, out_ref):
    entries = held_ref.shape[1] - TAP_PAD // 2
    for slot in range(2):
        for half, ref in enumerate((held_ref, came_ref)):
            first = (2 * half + slot) * entries
            out_ref[first : first + entries, :] = ref[slot, 0:entries]
    apart = lax.axis_index("ctx") ^ half_of(lax.axis_index("dp"))
    slot = half_of(apart)
    taps = [ref[slot, entries:].astype(jnp.float32) for ref in (held_ref, came_ref)]
    taps = jnp.where((apart & 1) == 1, taps[1], taps[0])
    out_ref[4 * entries :, :] = taps.astype(jnp.bfloat16)


def pack_channels(frame_ref, grad_ref, awaited_ref, *rest):
    across_ref, grad_outs, beside_ref, own_ref, sem = rest[0], rest[1:3], *rest[3:]
    width = frame_ref.shape[2] // N_CTX
    frames = frame_ref.shape[1]
    place = lax.axis_index("ctx")
    pairs = []
    for slot, ref in enumerate((frame_ref, grad_ref)):
        for apart in (2, 3, 1, 0):
            cols = columns((place ^ apart) * width, width)
            for utt in range(2):
                rows = slice(utt * frames, (utt + 1) * frames)
                if apart < 2:
                    target = (own_ref, beside_ref)[apart].at[slot, rows]
                elif slot == 0:
                    target = across_ref.at[apart - 2, rows]
                else:
                    target = grad_outs[apart - 2].at[rows]
                pairs.append((ref.at[utt, :, cols], target))
    run_copies(pairs, sem)


def make_sides(beside_ref, across_ref, out_ref):
    out_ref[0:2] = beside_ref[...]
    out_ref[2] = across_ref[1]


def unpack(*refs):
    ins, refs = refs[:N_CTX], refs[N_CTX:]
    own_ref, beside_ref, output_ref, input_ref = refs[:4]
    heads, channels, token_ref, sem = refs[4:7], refs[7:9], refs[9], refs[10]
    token_ref[...] = jnp.zeros_like(token_ref)
    half, width = ins[0].shape[2], own_ref.shape[3]
    frames = own_ref.shape[2]
    place = lax.axis_index("ctx")
    pairs = []
    for apart in range(N_CTX):
        source = place ^ apart
        cols = columns((source & 1) * half, half)
        for slot, ref in enumerate(heads):
            pairs.append((ins[apart].at[slot], ref.at[half_of(source), :, cols]))
    for slot, ref in enumerate(channels):
        for utt in range(2):
            part = pl.ds(utt * frames, frames)
            blocks = (
                own_ref.at[slot, utt],
                beside_ref.at[slot, part],
                (output_ref, input_ref)[slot].at[0, part],
                beside_ref.at[2 + slot, part],
            )
            for apart, block in enumerate(blocks):
                cols = columns((place ^ apart) * width, width)
                pairs.append((block, ref.at[utt, :, cols]))
    run_copies(pairs, sem)


def head_parts(refs, slot):
    return jnp.concatenate([ref[slot] for ref in refs], axis=0)


def half_masks(rows):
    lane = lax.broadcasted_iota(jnp.int32, (rows, LANES), 1)
    low = jnp.where(lane < HEAD_DIM, 1.0, 0.0)
    return low.astype(jnp.bfloat16), (1.0 - low).astype(jnp.bfloat16)


def weights_of(length_ref, key_pair, query_pair, mask, frames):
    place = lax.axis_index("ctx")
    rows = key_pair.shape[0]
    frame = lax.broadcasted_iota(jnp.int32, (rows, rows), 0) ^ (place * frames)
    scores = dot_tt(key_pair, query_pair * mask, 1, 1) * HEAD_DIM ** (-0.5)
    scores = jnp.where(frame < length_ref[half_of(place)], scores, masked_score)
    powers = jnp.exp(scores - jnp.max(scores, axis=0, keepdims=True))
    total = jnp.sum(powers, axis=0, keepdims=True)
    return (powers * (1.0 / total)).astype(jnp.bfloat16)


def attend(length_ref, *refs):
    ins, attended_ref = refs[:N_CTX], refs[N_CTX]
    frames, half = ins[0].shape[1], ins[0].shape[2]
    query, key, value = (head_parts(ins, slot) for slot in range(3))
    masks = half_masks(N_CTX * frames)
    for pair in range(half // LANES):
        cols = slice(pair * LANES, (pair + 1) * LANES)
        parts = []
        for side in range(2):
            low = weights_of(length_ref, key[:, cols], query[:, cols], masks[side], frames)
            mixed = dot_tt(value[:, cols], low, 0, 0)
            parts.append(mixed[side * HEAD_DIM : (side + 1) * HEAD_DIM])
        joined = jnp.concatenate(parts, axis=0).T.astype(jnp.bfloat16)
        attended_ref[:, :, cols] = joined.reshape(N_CTX, frames, LANES)


def weigh(length_ref, *refs):
    ins, weight_ref = refs[:N_CTX], refs[N_CTX + 1]
    frames, half = ins[0].shape[1], ins[0].shape[2]
    query, key = (head_parts(ins, slot) for slot in range(2))
    masks = half_masks(N_CTX * frames)
    for pair in range(half // LANES):
        cols = slice(pair * LANES, (pair + 1) * LANES)
        for side in range(2):
            weight_ref[2 * pair + side] = weights_of(
                length_ref, key[:, cols], query[:, cols], masks[side], frames
            )


def forward(length_ref, near_ref, other_ref, *refs):
    attended_refs, refs = refs[:N_CTX], refs[N_CTX:]
    own_ref, beside_ref, across_ref = refs[:3]
    out_refs, refs = refs[3:6], refs[6:]
    whole_ref, rows_ref, taps_ref, total_ref, masked_ref = refs[:5]
    hidden_ref, frame_ref, result_ref = refs[5:]
    frames, half = attended_refs[0].shape[1], attended_refs[0].shape[2]
    width = frame_ref.shape[3]
    rows = N_CTX * frames
    chunks = width // LANES
    entries = 2 * half // N_DP
    own = width // 2
    place = lax.axis_index("ctx")
    for apart in range(N_CTX):
        source = place ^ apart
        cols = columns((source & 1) * half, half)
        for block in range(N_CTX):
            whole_ref[half_of(source), block ^ source, :, cols] = attended_refs[apart][block]
        block = (own_ref, beside_ref, across_ref, beside_ref)[apart][(0, 0, 0, 2)[apart]]
        frame_ref[source] = block.reshape(frame_ref.shape[1:])
    group = lax.axis_index("dp")
    for slot, apart in enumerate((0, 4, 2, 6)):
        for odd, ref in enumerate((near_ref, other_ref)):
            first = pl.multiple_of((group ^ (apart + odd)) * entries, entries)
            rows_ref[pl.ds(first, entries)] = ref[slot * entries : (slot + 1) * entries]
    odd = (group & 1) == 1
    blocks = [ref[4 * entries :].astype(jnp.float32) for ref in (near_ref, other_ref)]
    blocks = (jnp.where(odd, blocks[1], blocks[0]), jnp.where(odd, blocks[0], blocks[1]))
    pieces = [jnp.concatenate([block[:, :own], block[:, own:]], axis=0) for block in blocks]
    taps = jnp.concatenate(pieces, axis=1)
    for chunk in range(chunks):
        for tap in range(TAPS):
            taps_ref[chunk, tap] = jnp.broadcast_to(
                taps[tap : tap + 1, chunk * LANES : (chunk + 1) * LANES], (8, LANES)
            )
    edge = jnp.zeros((2 * chunks, 16, LANES), jnp.float32)
    masked_ref[:, 0:16, :] = edge
    masked_ref[:, 16 + rows : 32 + rows, :] = edge
    for utt in range(2):
        real = lax.broadcasted_iota(jnp.int32, (rows, LANES), 0) < length_ref[utt]
        mixed = whole_ref[utt].reshape(rows, 2 * half)
        projected = dot_tt(mixed, rows_ref[...], 1, 0)
        hidden = frame_ref[:, utt].reshape(rows, width).astype(jnp.float32) + projected
        hidden = hidden.astype(jnp.bfloat16).astype(jnp.float32)
        for chunk in range(chunks):
            piece = hidden[:, chunk * LANES : (chunk + 1) * LANES]
            hidden_ref[utt * chunks + chunk] = piece
            masked_ref[utt * chunks + chunk, 16 : 16 + rows, :] = jnp.where(real, piece, 0.0)

    def convolve(step, carry):
        utt, chunk = step // chunks, step % chunks
        cols = columns(chunk * LANES, LANES)
        shape = (frames // 8, 8, LANES)
        for block in range(N_CTX):
            base = block * frames
            total = jnp.zeros(shape, jnp.float32)
            for tap in range(TAPS):
                first = base + tap + 16 - REACH
                piece = masked_ref[step, first : first + frames, :]
                total += taps_ref[chunk, tap][None] * piece.reshape(shape)
            total = total.reshape(frames, LANES)
            total_ref[step, base : base + frames, :] = total
            outer = hidden_ref[step, base : base + frames, :] + total * jax.nn.sigmoid(total)
            result_ref[block, utt, :, cols] = outer.astype(jnp.bfloat16)
        return carry

    lax.fori_loop(0, 2 * chunks, convolve, 0)
    for apart in range(2):
        out_refs[apart][...] = result_ref[place ^ apart]
        out_refs[2][apart] = result_ref[place ^ (2 + apart)].reshape(2 * frames, width)


def backward(length_ref, total_ref, taps_ref, rows_ref, *refs):
    own_ref, beside_ref = refs[:2]
    own_sides_ref, beside_sides_ref, grad_across_ref, grad_diagonal_ref = refs[2:6]
    refs = refs[6:]
    own_pair_ref, beside_pair_ref, across_ref = refs[:3]
    grad_ref, keep_ref, send_ref, cotangent_ref = refs[3:7]
    side_ref, result_ref = refs[7:]
    own_pair_ref[0], beside_pair_ref[0] = own_ref[...], beside_ref[...]
    utts, frames, width = own_ref.shape
    rows = N_CTX * frames
    chunks = width // LANES
    half = rows_ref.shape[0] // 2
    place = lax.axis_index("ctx")
    blocks = (own_sides_ref[1], beside_sides_ref[1], grad_across_ref[...], grad_diagonal_ref[...])
    for apart in range(N_CTX):
        side_ref[place ^ apart] = blocks[apart].reshape(side_ref.shape[1:])
    edge = jnp.zeros((2 * chunks, 16, LANES), jnp.float32)
    cotangent_ref[:, 0:16, :] = edge
    cotangent_ref[:, 16 + rows : 32 + rows, :] = edge

    def convolve(step, carry):
        utt, chunk = step // chunks, step % chunks
        cols = columns(chunk * LANES, LANES)
        length = length_ref[utt]
        shape = (frames // 8, 8, LANES)
        for block in range(N_CTX):
            base = block * frames
            total = total_ref[step, base : base + frames, :]
            gate = jax.nn.sigmoid(total)
            incoming = side_ref[block, utt, :, cols].astype(jnp.float32)
            slope = gate * (1.0 + total * (1.0 - gate))
            low = (incoming * slope).astype(jnp.bfloat16)
            cotangent_ref[step, 16 + base : 16 + base + frames, :] = low.astype(jnp.float32)
        for block in range(N_CTX):
            base = block * frames
            total = jnp.zeros(shape, jnp.float32)
            for tap in range(TAPS):
                first = base + 16 + REACH - tap
                piece = cotangent_ref[step, first : first + frames, :].reshape(shape)
                total += taps_ref[chunk, tap][None] * piece
            place_of = base + lax.broadcasted_iota(jnp.int32, (frames, LANES), 0)
            total = jnp.where(place_of < length, total.reshape(frames, LANES), 0.0)
            incoming = side_ref[block, utt, :, cols].astype(jnp.float32)
            low = (incoming + total).astype(jnp.bfloat16)
            result_ref[block, utt, :, cols] = low
            grad_ref[utt, base : base + frames, cols] = low
        return carry

    lax.fori_loop(0, 2 * chunks, convolve, 0)
    for apart in range(N_CTX):
        mine = result_ref[place ^ apart]
        if apart < 2:
            (own_pair_ref, beside_pair_ref)[apart][1] = mine
        else:
            across_ref[apart - 2] = mine.reshape(utts * frames, width)
        dest = place ^ apart
        mixed = dot_tt(
            grad_ref[half_of(dest)],
            rows_ref[pl.ds(pl.multiple_of((dest & 1) * half, half), half)],
            1,
            1,
        ).astype(jnp.bfloat16)
        ref = send_ref if apart % 2 else keep_ref
        for block in range(N_CTX):
            first = pl.multiple_of((block ^ dest) * frames, frames)
            ref[apart // 2, pl.ds(first, frames), :] = mixed[block * frames : (block + 1) * frames]


def make_taps(masked_ref, cotangent_ref, awaited_ref, keep_ref, send_ref, tap_sum_ref):
    steps, rows, chunks = masked_ref.shape[0], masked_ref.shape[1] - 32, tap_sum_ref.shape[0]
    block = 64
    shape = (block // 8, 8, LANES)
    tap_sum_ref[...] = jnp.zeros_like(tap_sum_ref)

    def correlate(step, carry):
        chunk = step % chunks
        for base in range(0, rows, block):
            held = masked_ref[step, 16 + base : 16 + base + block, :].reshape(shape)
            for tap in range(TAPS):
                first = base + 16 + REACH - tap
                piece = cotangent_ref[step, first : first + block, :].reshape(shape)
                tap_sum_ref[chunk, tap] += jnp.sum(held * piece, axis=0)
        return carry

    lax.fori_loop(0, steps, correlate, 0)
    sums = [
        jnp.concatenate(
            [
                jnp.sum(tap_sum_ref[chunk, tap], axis=0, keepdims=True)
                for tap in range(TAP_PAD)
            ],
            axis=0,
        )
        for chunk in range(chunks)
    ]
    sums = jnp.concatenate(sums, axis=1)
    own = sums.shape[1] // 2
    halves = [
        jnp.concatenate([part[: TAP_PAD // 2], part[TAP_PAD // 2 :]], axis=1)
        for part in (sums[:, :own], sums[:, own:])
    ]
    odd = (lax.axis_index("dp") & 1) == 1
    keep_ref[...] = jnp.where(odd, halves[1], halves[0])
    send_ref[...] = jnp.where(odd, halves[0], halves[1])


def make_panels(whole_ref, grad_ref, panel_ref):
    rows, half = grad_ref.shape[1], whole_ref.shape[3] // 2
    entries = 2 * half // N_DP
    group = lax.axis_index("dp")
    for side in range(2):
        panel = 0.0
        for utt in range(2):
            mixed = whole_ref[utt, :, :, side * half : (side + 1) * half].reshape(rows, half)
            panel += dot_tt(mixed, grad_ref[utt], 0, 0)
        panel = panel.astype(jnp.bfloat16)
        for part in range(N_DP // 2):
            panel_ref[slot_of(side * N_DP // 2 + part, group)] = panel[
                part * entries : (part + 1) * entries
            ]


def join(panel_ref, came_ref, tap_ref, tap_came_ref, awaited_ref, keep_ref, send_ref):
    entries = panel_ref.shape[1]
    group, place = lax.axis_index("dp"), lax.axis_index("ctx")
    taps = (tap_ref[...] + tap_came_ref[...]).astype(jnp.bfloat16)
    none = jnp.zeros_like(taps)
    for slot in range(N_DP // 2):
        ref = (keep_ref, send_ref)[slot // 2]
        total = panel_ref[slot].astype(jnp.float32) + came_ref[slot].astype(jnp.float32)
        ref[slot % 2, 0:entries] = total.astype(jnp.bfloat16)
        ref[slot % 2, entries:] = none
    mine = slot_of(2 * place, group & 6)
    for slot in range(N_DP // 2):
        ref = (keep_ref, send_ref)[slot // 2]

        @pl.when(mine == slot)
        def _(ref=ref, slot=slot):
            ref[slot % 2, entries:] = taps


def mark(*refs):
    refs[-1][...] = jnp.zeros_like(refs[-1])


def finish(kept_ref, came_ref, awaited_ref, panel_ref, taps_ref):
    entries = panel_ref.shape[0]
    total = kept_ref[0].astype(jnp.float32) + came_ref[...].astype(jnp.float32)
    panel_ref[...] = total[:entries]
    taps_ref[...] = total[entries:]


def pick_taps(*refs):
    ins, out_ref, held_ref = refs[:N_CTX], refs[N_CTX + 1], refs[N_CTX + 2]
    own = ins[0].shape[1] // 2
    for apart in range(N_CTX):
        held_ref[apart] = ins[apart][...]
    mine = held_ref[lax.axis_index("ctx") ^ half_of(lax.axis_index("dp"))]
    out_ref[...] = jnp.concatenate([mine[:, :own], mine[:, own:]], axis=0)[:TAPS]


def relay(keep_ref, came_ref, out_ref):
    total = keep_ref[1].astype(jnp.float32) + came_ref[1].astype(jnp.float32)
    out_ref[...] = total.astype(jnp.bfloat16)


def make_pair(pair_ref, output_ref, input_ref, *refs):
    out_ref = refs[-1]
    for slot in range(2):
        out_ref[slot] = pair_ref[slot].reshape(out_ref.shape[1:])
    out_ref[2] = output_ref[1]
    out_ref[3] = input_ref[1]


def attend_back(weight_ref, keep_ref, came_ref, far_ref, *refs):
    ins, out_refs = refs[:N_CTX], refs[N_CTX + 1 :]
    frames, half = ins[0].shape[1], ins[0].shape[2]
    rows = N_CTX * frames
    query, key, value = (head_parts(ins, slot) for slot in range(3))
    masks = half_masks(rows)
    scale = HEAD_DIM ** (-0.5)
    arriving = keep_ref[0].astype(jnp.float32) + came_ref[0].astype(jnp.float32)
    arriving = (arriving + far_ref[...].astype(jnp.float32)).astype(jnp.bfloat16)
    low_lanes = lax.broadcasted_iota(jnp.int32, (rows, LANES), 1) < HEAD_DIM
    for pair in range(half // LANES):
        cols = slice(pair * LANES, (pair + 1) * LANES)
        key_pair, value_pair = key[:, cols], value[:, cols]
        query_pair, grad_pair = query[:, cols], arriving[:, cols]
        query_parts, key_parts, value_parts = [], [], []
        for side in range(2):
            low = weight_ref[2 * pair + side]
            weights = low.astype(jnp.float32)
            moved = weights * dot_tt(value_pair, grad_pair * masks[side], 1, 1)
            delta = jnp.sum(moved, axis=0, keepdims=True)
            grad_scores = (moved - weights * delta).astype(jnp.bfloat16)
            value_parts.append(dot_tt(low, grad_pair, 1, 0))
            key_parts.append(dot_tt(grad_scores, query_pair, 1, 0))
            mixed = dot_tt(key_pair, grad_scores, 0, 0)
            query_parts.append(mixed[side * HEAD_DIM : (side + 1) * HEAD_DIM])
        query_sum = (jnp.concatenate(query_parts, axis=0).T * scale).astype(jnp.bfloat16)
        key_sum = (jnp.where(low_lanes, key_parts[0], key_parts[1]) * scale).astype(jnp.bfloat16)
        value_sum = jnp.where(low_lanes, value_parts[0], value_parts[1]).astype(jnp.bfloat16)
        for slot, total in enumerate((query_sum, key_sum, value_sum)):
            for apart in range(N_CTX):
                out_refs[apart][slot, :, cols] = total[apart * frames : (apart + 1) * frames]


def swapped(array, bit):
    return lax.ppermute(array, "dp", [(i, i ^ bit) for i in range(N_DP)])


def dealt(slots):
    return lax.all_to_all(slots, "dp", 0, 0, tiled=True)


def crossed(array, apart):
    return lax.ppermute(array, "ctx", [(i, i ^ apart) for i in range(N_CTX)])


def traded(blocks):
    came = {apart: crossed(blocks[apart], apart) for apart in (2, 3, 1)}
    return [blocks[0]] + [came[apart] for apart in (1, 2, 3)]


def per_device(
    frame_input, queries, key_proj, value_proj, out_weight, conv_weight, lengths, grad_output
):
    utts, frames, wide = frame_input.shape
    inner = queries.shape[2]
    half, width = inner // 2, wide // N_CTX
    rows = N_CTX * frames
    chunks = width // LANES
    low, f32 = jnp.bfloat16, jnp.float32
    shape = jax.ShapeDtypeStruct
    entries = out_weight.shape[1]
    tap_count = conv_weight.shape[0]
    dma = pltpu.SemaphoreType.DMA
    head_block = shape((3, frames, half), low)
    channel_block = shape((utts, frames, width), low)

    blocks = call_kernel(
        pack_heads,
        (head_block,) * N_CTX,
        ["hbm"] * 3,
        scratch=[dma((3 * N_CTX,))],
        room=63,
    )(queries, key_proj, value_proj)
    packed = traded(blocks)
    (shard,) = call_kernel(
        pack_weights,
        (shape((1, entries + TAP_PAD // 2, width), low),),
        ["vmem"] * 2 + ["any"],
    )(out_weight.T, conv_weight, packed[1])
    shard = jnp.concatenate([shard, swapped(shard, 4)], axis=0)
    (shard,) = call_kernel(
        pack_near, (shape((4 * entries + TAP_PAD // 2, width), low),), ["vmem"] * 2
    )(shard, swapped(shard, 2))
    other_shard = swapped(shard, 1)
    pair_block = shape((2, utts, frames, width), low)
    side_block = shape((utts * frames, width), low)
    double_block = shape((2, utts * frames, width), low)
    frame_across, grad_across, grad_diagonal, beside_sides, own_sides = call_kernel(
        pack_channels,
        (double_block,) + (side_block,) * 2 + (double_block,) * 2,
        ["hbm"] * 2 + ["any"],
        scratch=[dma((4 * N_CTX,))],
    )(frame_input, grad_output, packed[2])
    frame_across = crossed(frame_across, 2)
    (beside_sides,) = call_kernel(
        make_sides, (shape((3, utts * frames, width), low),), ["vmem"] * 2
    )(beside_sides, frame_across)
    beside_sides = crossed(beside_sides, 1)
    (attended,) = call_kernel(
        attend,
        (shape((N_CTX, frames, half), low),),
        ["smem"] + ["vmem"] * N_CTX,
    )(lengths, *packed)
    (attended,) = gate([attended], frame_across)
    across = crossed(attended, 2)
    beside = crossed(attended, 1)
    diagonal = crossed(across, 1)
    grad_across, grad_diagonal = crossed(grad_across, 2), crossed(grad_diagonal, 3)
    forward_out = call_kernel(
        forward,
        (channel_block,) * 2
        + (
            shape((2, utts * frames, width), low),
            shape((utts, N_CTX, frames, inner), low),
            shape((inner, width), low),
            shape((chunks, TAP_PAD, 8, LANES), f32),
            shape((utts * chunks, rows, LANES), f32),
            shape((utts * chunks, rows + 32, LANES), f32),
        ),
        ["smem"] + ["vmem"] * (5 + N_CTX),
        scratch=[
            pltpu.VMEM((utts * chunks, rows, LANES), f32),
            pltpu.VMEM((N_CTX, utts, frames, width), low),
            pltpu.VMEM((N_CTX, utts, frames, width), low),
        ],
        micros=3.2,
    )(
        lengths,
        shard,
        other_shard,
        attended,
        beside,
        across,
        diagonal,
        own_sides,
        beside_sides,
        frame_across,
    )
    output_across = crossed(forward_out[2], 2)
    whole, weight_rows, taps, totals, masked = forward_out[3:]
    grad_blocks = gate([grad_across, grad_diagonal], totals, micros=10.0)
    grad_blocks = (own_sides, beside_sides, *grad_blocks)
    backward_out = call_kernel(
        backward,
        (pair_block,) * 2
        + (
            shape((2, utts * frames, width), low),
            shape((utts, rows, width), low),
            shape((2, rows, half), low),
            shape((2, rows, half), low),
            shape((utts * chunks, rows + 32, LANES), f32),
        ),
        ["smem"] + ["vmem"] * (5 + N_CTX),
        scratch=[
            pltpu.VMEM((N_CTX, utts, frames, width), low),
            pltpu.VMEM((N_CTX, utts, frames, width), low),
        ],
        micros=5.2,
    )(lengths, totals, taps, weight_rows, *forward_out[:2], *grad_blocks)
    grad_hidden, keep, send, cotangents = backward_out[3:]
    (send,) = gate([send], output_across)
    came = crossed(send, 1)
    (relayed,) = call_kernel(
        relay, (shape((rows, half), low),), ["vmem"] * 2, micros=0.2
    )(keep, came)
    (input_across,) = gate([backward_out[2]], relayed)
    (panels,) = call_kernel(
        make_panels,
        (shape((N_DP, entries, width), low),),
        ["vmem"] * 2,
        micros=0.7,
    )(whole, grad_hidden)
    panels_came = swapped(panels[4:], 1)
    tap_block = shape((TAP_PAD // 2, width), f32)
    tap_keep, tap_send = call_kernel(
        make_taps,
        (tap_block,) * 2,
        ["vmem"] * 2 + ["any"],
        scratch=[pltpu.VMEM((chunks, TAP_PAD, 8, LANES), f32)],
    )(masked, cotangents, relayed)
    taps_came = swapped(tap_send, 1)
    far, input_across = crossed(relayed, 2), crossed(input_across, 2)
    (weights,) = call_kernel(
        weigh,
        (shape((half // HEAD_DIM, rows, rows), low),),
        ["smem"] + ["vmem"] * N_CTX + ["any"],
    )(lengths, *packed, relayed)
    back_blocks = call_kernel(
        attend_back,
        (head_block,) * N_CTX,
        ["vmem"] * (4 + N_CTX) + ["any"],
        micros=2.2,
    )(weights, keep, came, far, *packed, tap_keep)
    (across_block,) = gate([back_blocks[2]], input_across)
    grad_blocks = traded([*back_blocks[:2], across_block, back_blocks[3]])
    own_pair = backward_out[0]
    (beside_pair,) = call_kernel(
        make_pair,
        (shape((4, utts * frames, width), low),),
        ["vmem"] * 3 + ["any"],
        micros=0.2,
    )(backward_out[1], output_across, input_across, grad_blocks[1])
    beside_pair = crossed(beside_pair, 1)

    kept, sent = call_kernel(
        join,
        (shape((2, entries + TAP_PAD // 2, width), low),) * 2,
        ["vmem"] * 4 + ["any"],
    )(panels[:4], panels_came, tap_keep, taps_came, back_blocks[0])
    panels = (kept.astype(f32) + swapped(sent, 2).astype(f32)).astype(low)
    (arrived,) = call_kernel(mark, (shape((8, LANES), f32),), ["any"] * 2)(*grad_blocks[2:])
    panel_total, tap_sums = call_kernel(
        finish,
        (shape((entries, width), f32), shape((TAP_PAD // 2, width), f32)),
        ["vmem"] * 2 + ["any"],
    )(panels, swapped(panels[1], 4), arrived)
    grad_out_weight = panel_total.T
    unpacked = call_kernel(
        unpack,
        (shape((utts, frames, inner), low),) * 3
        + (shape((utts, frames, wide), low),) * 2
        + (shape((8, LANES), f32),),
        ["any"] * (N_CTX + 4),
        ["hbm"] * 5 + ["vmem"],
        [dma((7 * N_CTX + 4 * N_CTX,))],
        micros=1.0,
    )(
        *grad_blocks,
        own_pair,
        beside_pair,
        output_across,
        input_across,
    )
    (grad_taps,) = call_kernel(
        pick_taps,
        (shape(conv_weight.shape, f32),),
        ["vmem"] * N_CTX + ["any"],
        scratch=[pltpu.VMEM((N_CTX, TAP_PAD // 2, width), f32)],
    )(*traded([tap_sums] * N_CTX), unpacked[5])
    grad_queries, grad_keys, grad_values, block_output, grad_input = unpacked[:5]
    return (
        block_output,
        grad_input,
        grad_queries,
        grad_keys,
        grad_values,
        grad_out_weight,
        grad_taps,
    )


def chosen(sizes, *arrays):
    frame_input, queries, out_weight, conv_weight = (arrays[i] for i in (0, 1, 4, 5))
    utts, frames, wide = frame_input.shape
    inner = queries.shape[2]
    fits = (
        sizes == (N_DP, N_CTX)
        and utts == 2
        and frames == 64
        and wide % (N_CTX * LANES) == 0
        and inner % (2 * LANES) == 0
        and inner // N_DP % 16 == 0
        and inner // 2 == wide // N_CTX
        and conv_weight.shape == (TAPS, wide // N_DP)
        and out_weight.shape == (wide // N_CTX, inner // N_DP)
    )
    return (per_device if fits else general_device)(*arrays)


def solution(mesh):
    placed = (
        P("dp", "ctx", None),
        P("dp", "ctx", None),
        P("dp", "ctx", None),
        P("dp", "ctx", None),
        P("ctx", "dp"),
        P(None, "dp"),
        P("dp"),
        P("dp", "ctx", None),
    )
    sizes = (mesh.shape["dp"], mesh.shape["ctx"])
    return jax.shard_map(
        functools.partial(chosen, sizes),
        mesh=mesh,
        in_specs=placed,
        out_specs=(
            P("dp", "ctx", None),
            P("dp", "ctx", None),
            P("dp", "ctx", None),
            P("dp", "ctx", None),
            P("dp", "ctx", None),
            P("ctx", "dp"),
            P(None, "dp"),
        ),
        check_vma=False,
    )
```

```python
import functools

import jax
import jax.numpy as jnp
from jax import lax
from jax.experimental import pallas as pl
from jax.experimental.pallas import tpu as pltpu
from jax.sharding import PartitionSpec as P

HEAD_DIM = 64


masked_score = -1e30


def padded_2(array, sides, width):
    for axis, dim in sides:
        size, length = (lax.axis_size(axis), array.shape[dim])
        up = [(i, (i + 1) % size) for i in range(size - 1)]
        down = [(j, i) for i, j in up]
        last = lax.slice_in_dim(array, length - width, length, axis=dim)
        leading = lax.slice_in_dim(array, 0, width, axis=dim)
        before = lax.ppermute(last, axis, up)
        after = lax.ppermute(leading, axis, down)
        array = jnp.concatenate([before, array, after], axis=dim)
    return array


def depthwise(lhs, rhs):
    return lax.conv_general_dilated(
        lhs,
        rhs,
        (1,),
        "VALID",
        dimension_numbers=("NWC", "WIO", "NWC"),
        feature_group_count=lhs.shape[2],
        precision=lax.Precision.HIGHEST,
    )


def general_device(
    frame_input, queries, key_proj, value_proj, out_weight, conv_weight, lengths, grad_output
):
    utt_count = frame_input.shape[0]
    frame_count = frame_input.shape[1]
    inner_width = queries.shape[2]
    head_count = inner_width // HEAD_DIM
    group_heads = max((g for g in range(1, 7) if head_count % g == 0))
    group_count = head_count // group_heads
    group_width = group_heads * HEAD_DIM
    tap_count = conv_weight.shape[0]
    half_span = (tap_count - 1) // 2
    score_scale = HEAD_DIM ** (-0.5)
    total_frames = frame_count * lax.axis_size("ctx")
    offset = lax.axis_index("ctx") * frame_count
    own_valid = (offset + jnp.arange(frame_count, dtype=jnp.int32))[None, :] < lengths[:, None]
    all_valid = jnp.arange(total_frames, dtype=jnp.int32)[None, :] < lengths[:, None]

    def grouped(values):
        row_count = values.shape[1]
        return values.reshape(utt_count, row_count, group_count, group_width).transpose(2, 0, 1, 3)

    def ungrouped(values):
        row_count = values.shape[2]
        return values.transpose(1, 2, 0, 3).reshape(utt_count, row_count, group_count * group_width)

    def split_heads(values):
        return values.reshape(utt_count, values.shape[1], group_heads, HEAD_DIM)

    def stats_grouped(values):
        row_count = values.shape[1]
        return values.reshape(utt_count, row_count, group_count, group_heads).transpose(2, 0, 3, 1)

    def masked_scores(query_block, key_block, key_mask):
        scores = (
            jnp.einsum(
                "uqgd,ukgd->ugqk", query_block, key_block, preferred_element_type=jnp.float32
            )
            * score_scale
        )
        return jnp.where(key_mask[:, None, None, :], scores, masked_score)

    taps = lax.all_gather(conv_weight, "dp", axis=1, tiled=True).astype(jnp.float32)
    panel_rows = lax.all_gather(out_weight, "dp", axis=1, tiled=True)
    weight_full = lax.all_gather(panel_rows, "ctx", axis=0, tiled=True)
    all_keys, all_values = (
        lax.all_gather(key_proj, "ctx", axis=1, tiled=True),
        lax.all_gather(value_proj, "ctx", axis=1, tiled=True),
    )
    query_groups = grouped(queries)
    key_groups = grouped(all_keys)
    value_groups = grouped(all_values)

    def forward_group(unused, items):
        query_group, key_group, value_group = items
        query_block = split_heads(query_group)
        scores = masked_scores(query_block, split_heads(key_group), all_valid)
        largest = jnp.max(scores, axis=-1)
        log_group = largest + jnp.log(jnp.sum(jnp.exp(scores - largest[..., None]), axis=-1))
        weights_low = jnp.exp(scores - log_group[..., None]).astype(jnp.bfloat16)
        attended_group = jnp.einsum(
            "ugqk,ukgd->uqgd",
            weights_low,
            split_heads(value_group),
            preferred_element_type=jnp.float32,
        )
        return (None, (log_group, attended_group.reshape(utt_count, frame_count, group_width)))

    _, (log_groups, attended_groups) = lax.scan(
        forward_group, None, (query_groups, key_groups, value_groups)
    )
    attended = ungrouped(attended_groups).astype(jnp.bfloat16)
    log_total = log_groups.transpose(1, 3, 0, 2).reshape(utt_count, frame_count, head_count)
    projected = jnp.einsum("ufe,de->ufd", attended, weight_full, preferred_element_type=jnp.float32)
    hidden = (frame_input.astype(jnp.float32) + projected).astype(jnp.bfloat16)
    masked_hidden = jnp.where(own_valid[:, :, None], hidden, jnp.zeros_like(hidden))
    padded = padded_2(masked_hidden, (("ctx", 1),), half_span).astype(jnp.float32)
    conv_sum = depthwise(padded, taps[:, None, :])
    sigmoid = jax.nn.sigmoid(conv_sum)
    block_output = (hidden.astype(jnp.float32) + conv_sum * sigmoid).astype(jnp.bfloat16)
    grad_local = grad_output.astype(jnp.float32)
    swish_slope = sigmoid * (1.0 + conv_sum * (1.0 - sigmoid))
    grad_conv = (grad_local * swish_slope).astype(jnp.bfloat16)
    grad_padded = padded_2(grad_conv, (("ctx", 1),), half_span).astype(jnp.float32)
    back_sum = depthwise(grad_padded, taps[::-1][:, None, :])
    grad_hidden = (grad_local + jnp.where(own_valid[:, :, None], back_sum, 0.0)).astype(
        jnp.bfloat16
    )
    grad_conv_wide = grad_conv.astype(jnp.float32)
    kernel_term = jnp.zeros((tap_count, conv_sum.shape[2]), jnp.float32)
    for utt_index in range(utt_count):
        kernel_term = (
            kernel_term
            + depthwise(padded[utt_index : utt_index + 1], grad_conv_wide[utt_index][:, None, :])[0]
        )
    kernel_whole = lax.psum(kernel_term.astype(jnp.bfloat16), "ctx")
    grad_conv_weight = lax.psum_scatter(kernel_whole, "dp", scatter_dimension=1, tiled=True).astype(
        jnp.float32
    )
    grad_attended = jnp.einsum(
        "ufd,de->ufe", grad_hidden, weight_full, preferred_element_type=jnp.float32
    ).astype(jnp.bfloat16)
    row_delta = jnp.sum(
        grad_attended.astype(jnp.float32).reshape(utt_count, frame_count, head_count, HEAD_DIM)
        * attended.astype(jnp.float32).reshape(utt_count, frame_count, head_count, HEAD_DIM),
        axis=-1,
    )
    grad_groups = grouped(grad_attended)

    def query_group_step(unused, items):
        query_group, key_group, value_group, grad_group, log_group, delta_group = items
        key_block = split_heads(key_group)
        weights = jnp.exp(
            masked_scores(split_heads(query_group), key_block, all_valid) - log_group[..., None]
        )
        grad_weights = jnp.einsum(
            "uqgd,ukgd->ugqk",
            split_heads(grad_group),
            split_heads(value_group),
            preferred_element_type=jnp.float32,
        )
        grad_scores = (weights * (grad_weights - delta_group[..., None])).astype(jnp.bfloat16)
        query_sum = jnp.einsum(
            "ugqk,ukgd->uqgd", grad_scores, key_block, preferred_element_type=jnp.float32
        )
        return (None, query_sum.reshape(utt_count, frame_count, group_width))

    _, query_sums = lax.scan(
        query_group_step,
        None,
        (
            query_groups,
            key_groups,
            value_groups,
            grad_groups,
            stats_grouped(log_total),
            stats_grouped(row_delta),
        ),
    )
    grad_queries = (ungrouped(query_sums) * score_scale).astype(jnp.bfloat16)
    total_log, total_delta = (
        lax.all_gather(log_total, "ctx", axis=1, tiled=True),
        lax.all_gather(row_delta, "ctx", axis=1, tiled=True),
    )
    own_key_groups = grouped(key_proj)
    own_value_groups = grouped(value_proj)
    group_zeros = jnp.zeros((group_count, utt_count, frame_count, group_width), jnp.float32)
    start_sums = (group_zeros, group_zeros)
    query_all, grad_all = (
        lax.all_gather(queries, "ctx", axis=1, tiled=True),
        lax.all_gather(grad_attended, "ctx", axis=1, tiled=True),
    )
    log_piece = stats_grouped(total_log)
    delta_piece = stats_grouped(total_delta)

    def key_group_step(unused, items):
        (
            query_group,
            grad_group,
            log_group,
            delta_group,
            key_group,
            value_group,
            key_sum,
            value_sum,
        ) = items
        query_block = split_heads(query_group)
        grad_block = split_heads(grad_group)
        weights = jnp.exp(
            masked_scores(query_block, split_heads(key_group), own_valid) - log_group[..., None]
        )
        grad_weights = jnp.einsum(
            "uqgd,ukgd->ugqk",
            grad_block,
            split_heads(value_group),
            preferred_element_type=jnp.float32,
        )
        grad_scores = (weights * (grad_weights - delta_group[..., None])).astype(jnp.bfloat16)
        key_next = key_sum + jnp.einsum(
            "ugqk,uqgd->ukgd", grad_scores, query_block, preferred_element_type=jnp.float32
        ).reshape(utt_count, frame_count, group_width)
        value_next = value_sum + jnp.einsum(
            "ugqk,uqgd->ukgd",
            weights.astype(jnp.bfloat16),
            grad_block,
            preferred_element_type=jnp.float32,
        ).reshape(utt_count, frame_count, group_width)
        return (None, (key_next, value_next))

    _, result_sums = lax.scan(
        key_group_step,
        None,
        (
            grouped(query_all),
            grouped(grad_all),
            log_piece,
            delta_piece,
            own_key_groups,
            own_value_groups,
            start_sums[0],
            start_sums[1],
        ),
    )
    key_sum, value_sum = result_sums
    grad_keys = (ungrouped(key_sum) * score_scale).astype(jnp.bfloat16)
    grad_values = ungrouped(value_sum).astype(jnp.bfloat16)
    hidden_cols = lax.slice_in_dim(
        grad_hidden, 0, weight_full.shape[0] // lax.axis_size("ctx") * lax.axis_size("ctx"), axis=2
    )
    panel_share = lax.psum_scatter(
        jnp.einsum("ufd,ufe->de", hidden_cols, attended, preferred_element_type=jnp.float32).astype(
            jnp.bfloat16
        ),
        "ctx",
        scatter_dimension=0,
        tiled=True,
    )
    grad_out_weight = lax.psum_scatter(panel_share, "dp", scatter_dimension=1, tiled=True).astype(
        jnp.float32
    )
    return (
        block_output,
        grad_hidden,
        grad_queries,
        grad_keys,
        grad_values,
        grad_out_weight,
        grad_conv_weight,
    )


LANES = 128
N_CTX = 4
N_DP = 8
TAP_PAD = 32
FLOPS_A_MICRO = 1.15e9
TAPS = 31
REACH = 15


def slot_of(index, me):
    apart = index ^ me
    return ((apart & 1) << 2) | (apart & 2) | ((apart >> 2) & 1)


def dot_tt(lhs, rhs, lhs_dim, rhs_dim):
    return lax.dot_general(
        lhs, rhs, (((lhs_dim,), (rhs_dim,)), ((), ())), preferred_element_type=jnp.float32
    )


def call_kernel(body, out_shape, ins, outs=None, scratch=(), room=40, micros=1.0):
    spaces = {
        "smem": pl.BlockSpec(memory_space=pltpu.SMEM),
        "vmem": pl.BlockSpec(memory_space=pltpu.VMEM),
        "hbm": pl.BlockSpec(memory_space=pltpu.HBM),
        "any": pl.BlockSpec(memory_space=pl.ANY),
    }
    return pl.pallas_call(
        body,
        out_shape=out_shape,
        in_specs=[spaces[space] for space in ins],
        out_specs=[spaces[space] for space in (outs or ["vmem"] * len(out_shape))],
        scratch_shapes=list(scratch),
        compiler_params=pltpu.CompilerParams(vmem_limit_bytes=room * 1024 * 1024),
        cost_estimate=pl.CostEstimate(
            flops=int(micros * FLOPS_A_MICRO), bytes_accessed=0, transcendentals=0
        ),
    )


def half_of(index):
    return lax.shift_right_logical(index, 1)


def columns(start, size):
    return pl.ds(pl.multiple_of(start, LANES), size)


def start_copies(pairs, sem):
    for number, (source, target) in enumerate(pairs):
        pltpu.make_async_copy(source, target, sem.at[number]).start()


def wait_copies(pairs, sem):
    for number, (source, target) in enumerate(pairs):
        pltpu.make_async_copy(source, target, sem.at[number]).wait()


def run_copies(pairs, sem):
    start_copies(pairs, sem)
    wait_copies(pairs, sem)


def untouched(*refs):
    pass


def gate(arrays, *awaited, micros=0.0):
    count = len(arrays)
    spec = pl.BlockSpec(memory_space=pl.ANY)
    return pl.pallas_call(
        untouched,
        out_shape=tuple(jax.ShapeDtypeStruct(array.shape, array.dtype) for array in arrays),
        in_specs=[spec] * (count + len(awaited)),
        out_specs=(spec,) * count,
        input_output_aliases={number: number for number in range(count)},
        compiler_params=pltpu.CompilerParams(vmem_limit_bytes=1024 * 1024),
        cost_estimate=pl.CostEstimate(
            flops=int(micros * FLOPS_A_MICRO), bytes_accessed=0, transcendentals=0
        ),
    )(*arrays, *awaited)


def pack_heads(query_ref, key_ref, value_ref, *rest):
    outs, sem = rest[:N_CTX], rest[N_CTX]
    half = query_ref.shape[2] // 2
    place = lax.axis_index("ctx")
    pairs = []
    for apart in (2, 3, 1, 0):
        dest = place ^ apart
        cols = columns((dest & 1) * half, half)
        for slot, ref in enumerate((query_ref, key_ref, value_ref)):
            pairs.append((ref.at[half_of(dest), :, cols], outs[apart].at[slot]))
    run_copies(pairs, sem)


def pack_weights(panel_ref, taps_ref, awaited_ref, out_ref):
    entries = panel_ref.shape[0]
    taps = taps_ref[...].astype(jnp.float32)
    high = jnp.concatenate(
        [taps[TAP_PAD // 2 :], jnp.zeros((TAP_PAD - TAPS, taps.shape[1]), jnp.float32)], axis=0
    )
    out_ref[0, 0:entries] = panel_ref[...]
    joined = jnp.concatenate([taps[: TAP_PAD // 2], high], axis=1)
    out_ref[0, entries:] = joined.astype(jnp.bfloat16)


def pack_near(held_ref, came_ref, out_ref):
    entries = held_ref.shape[1] - TAP_PAD // 2
    for slot in range(2):
        for half, ref in enumerate((held_ref, came_ref)):
            first = (2 * half + slot) * entries
            out_ref[first : first + entries, :] = ref[slot, 0:entries]
    apart = lax.axis_index("ctx") ^ half_of(lax.axis_index("dp"))
    slot = half_of(apart)
    taps = [ref[slot, entries:].astype(jnp.float32) for ref in (held_ref, came_ref)]
    taps = jnp.where((apart & 1) == 1, taps[1], taps[0])
    out_ref[4 * entries :, :] = taps.astype(jnp.bfloat16)


def pack_channels(frame_ref, grad_ref, awaited_ref, *rest):
    across_ref, grad_outs, beside_ref, own_ref, sem = rest[0], rest[1:3], *rest[3:]
    width = frame_ref.shape[2] // N_CTX
    frames = frame_ref.shape[1]
    place = lax.axis_index("ctx")
    pairs = []
    for slot, ref in enumerate((frame_ref, grad_ref)):
        for apart in (2, 3, 1, 0):
            cols = columns((place ^ apart) * width, width)
            for utt in range(2):
                rows = slice(utt * frames, (utt + 1) * frames)
                if apart < 2:
                    target = (own_ref, beside_ref)[apart].at[slot, rows]
                elif slot == 0:
                    target = across_ref.at[apart - 2, rows]
                else:
                    target = grad_outs[apart - 2].at[rows]
                pairs.append((ref.at[utt, :, cols], target))
    run_copies(pairs, sem)


def make_sides(beside_ref, across_ref, out_ref):
    out_ref[0:2] = beside_ref[...]
    out_ref[2] = across_ref[1]


def unpack(*refs):
    ins, refs = refs[:N_CTX], refs[N_CTX:]
    own_ref, beside_ref, output_ref, input_ref = refs[:4]
    taps, heads, channels, taps_ref = refs[4:8], refs[8:11], refs[11:13], refs[13]
    held_ref, picked_ref, sem = refs[14:]
    half, width = ins[0].shape[2], own_ref.shape[3]
    frames = own_ref.shape[2]
    place = lax.axis_index("ctx")
    pairs = []
    for apart in range(N_CTX):
        source = place ^ apart
        cols = columns((source & 1) * half, half)
        for slot, ref in enumerate(heads):
            pairs.append((ins[apart].at[slot], ref.at[half_of(source), :, cols]))
    for slot, ref in enumerate(channels):
        for utt in range(2):
            part = pl.ds(utt * frames, frames)
            blocks = (
                own_ref.at[slot, utt],
                beside_ref.at[slot, part],
                (output_ref, input_ref)[slot].at[0, part],
                beside_ref.at[2 + slot, part],
            )
            for apart, block in enumerate(blocks):
                cols = columns((place ^ apart) * width, width)
                pairs.append((block, ref.at[utt, :, cols]))
    start_copies(pairs, sem)
    for apart in range(N_CTX):
        held_ref[apart] = taps[apart][...]
    mine = held_ref[place ^ half_of(lax.axis_index("dp"))]
    side = mine.shape[1] // 2
    picked_ref[...] = jnp.concatenate([mine[:, :side], mine[:, side:]], axis=0)[:TAPS]
    last = pltpu.make_async_copy(picked_ref, taps_ref, sem.at[len(pairs)])
    last.start()
    wait_copies(pairs, sem)
    last.wait()


def head_parts(refs, slot):
    return jnp.concatenate([ref[slot] for ref in refs], axis=0)


def half_masks(rows):
    lane = lax.broadcasted_iota(jnp.int32, (rows, LANES), 1)
    low = jnp.where(lane < HEAD_DIM, 1.0, 0.0)
    return low.astype(jnp.bfloat16), (1.0 - low).astype(jnp.bfloat16)


def weights_of(length_ref, key_pair, query_pair, mask, frames):
    place = lax.axis_index("ctx")
    rows = key_pair.shape[0]
    frame = lax.broadcasted_iota(jnp.int32, (rows, rows), 0) ^ (place * frames)
    scores = dot_tt(key_pair, query_pair * mask, 1, 1) * HEAD_DIM ** (-0.5)
    scores = jnp.where(frame < length_ref[half_of(place)], scores, masked_score)
    powers = jnp.exp(scores - jnp.max(scores, axis=0, keepdims=True))
    total = jnp.sum(powers, axis=0, keepdims=True)
    return (powers * (1.0 / total)).astype(jnp.bfloat16)


def attend(length_ref, *refs):
    ins, attended_ref = refs[:N_CTX], refs[N_CTX]
    frames, half = ins[0].shape[1], ins[0].shape[2]
    query, key, value = (head_parts(ins, slot) for slot in range(3))
    masks = half_masks(N_CTX * frames)
    for pair in range(half // LANES):
        cols = slice(pair * LANES, (pair + 1) * LANES)
        parts = []
        for side in range(2):
            low = weights_of(length_ref, key[:, cols], query[:, cols], masks[side], frames)
            mixed = dot_tt(value[:, cols], low, 0, 0)
            parts.append(mixed[side * HEAD_DIM : (side + 1) * HEAD_DIM])
        joined = jnp.concatenate(parts, axis=0).T.astype(jnp.bfloat16)
        attended_ref[:, :, cols] = joined.reshape(N_CTX, frames, LANES)


def weigh(length_ref, *refs):
    ins, weight_ref = refs[:N_CTX], refs[N_CTX + 1]
    frames, half = ins[0].shape[1], ins[0].shape[2]
    query, key = (head_parts(ins, slot) for slot in range(2))
    masks = half_masks(N_CTX * frames)
    for pair in range(half // LANES):
        cols = slice(pair * LANES, (pair + 1) * LANES)
        for side in range(2):
            weight_ref[2 * pair + side] = weights_of(
                length_ref, key[:, cols], query[:, cols], masks[side], frames
            )


def forward(length_ref, near_ref, other_ref, *refs):
    attended_refs, refs = refs[:N_CTX], refs[N_CTX:]
    own_ref, beside_ref, across_ref = refs[:3]
    out_refs, refs = refs[3:6], refs[6:]
    whole_ref, rows_ref, taps_ref, total_ref, masked_ref = refs[:5]
    hidden_ref, frame_ref, result_ref = refs[5:]
    frames, half = attended_refs[0].shape[1], attended_refs[0].shape[2]
    width = frame_ref.shape[3]
    rows = N_CTX * frames
    chunks = width // LANES
    entries = 2 * half // N_DP
    own = width // 2
    place = lax.axis_index("ctx")
    for apart in range(N_CTX):
        source = place ^ apart
        cols = columns((source & 1) * half, half)
        for block in range(N_CTX):
            whole_ref[half_of(source), block ^ source, :, cols] = attended_refs[apart][block]
        block = (own_ref, beside_ref, across_ref, beside_ref)[apart][(0, 0, 0, 2)[apart]]
        frame_ref[source] = block.reshape(frame_ref.shape[1:])
    group = lax.axis_index("dp")
    for slot, apart in enumerate((0, 4, 2, 6)):
        for odd, ref in enumerate((near_ref, other_ref)):
            first = pl.multiple_of((group ^ (apart + odd)) * entries, entries)
            rows_ref[pl.ds(first, entries)] = ref[slot * entries : (slot + 1) * entries]
    odd = (group & 1) == 1
    blocks = [ref[4 * entries :].astype(jnp.float32) for ref in (near_ref, other_ref)]
    blocks = (jnp.where(odd, blocks[1], blocks[0]), jnp.where(odd, blocks[0], blocks[1]))
    pieces = [jnp.concatenate([block[:, :own], block[:, own:]], axis=0) for block in blocks]
    taps = jnp.concatenate(pieces, axis=1)
    for chunk in range(chunks):
        for tap in range(TAPS):
            taps_ref[chunk, tap] = jnp.broadcast_to(
                taps[tap : tap + 1, chunk * LANES : (chunk + 1) * LANES], (8, LANES)
            )
    edge = jnp.zeros((2 * chunks, 16, LANES), jnp.float32)
    masked_ref[:, 0:16, :] = edge
    masked_ref[:, 16 + rows : 32 + rows, :] = edge
    for utt in range(2):
        real = lax.broadcasted_iota(jnp.int32, (rows, LANES), 0) < length_ref[utt]
        mixed = whole_ref[utt].reshape(rows, 2 * half)
        projected = dot_tt(mixed, rows_ref[...], 1, 0)
        hidden = frame_ref[:, utt].reshape(rows, width).astype(jnp.float32) + projected
        hidden = hidden.astype(jnp.bfloat16).astype(jnp.float32)
        for chunk in range(chunks):
            piece = hidden[:, chunk * LANES : (chunk + 1) * LANES]
            hidden_ref[utt * chunks + chunk] = piece
            masked_ref[utt * chunks + chunk, 16 : 16 + rows, :] = jnp.where(real, piece, 0.0)

    def convolve(step, carry):
        utt, chunk = step // chunks, step % chunks
        cols = columns(chunk * LANES, LANES)
        shape = (frames // 8, 8, LANES)
        for block in range(N_CTX):
            base = block * frames
            total = jnp.zeros(shape, jnp.float32)
            for tap in range(TAPS):
                first = base + tap + 16 - REACH
                piece = masked_ref[step, first : first + frames, :]
                total += taps_ref[chunk, tap][None] * piece.reshape(shape)
            total = total.reshape(frames, LANES)
            total_ref[step, base : base + frames, :] = total
            outer = hidden_ref[step, base : base + frames, :] + total * jax.nn.sigmoid(total)
            result_ref[block, utt, :, cols] = outer.astype(jnp.bfloat16)
        return carry

    lax.fori_loop(0, 2 * chunks, convolve, 0)
    for apart in range(2):
        out_refs[apart][...] = result_ref[place ^ apart]
        out_refs[2][apart] = result_ref[place ^ (2 + apart)].reshape(2 * frames, width)


def backward(length_ref, total_ref, taps_ref, rows_ref, *refs):
    own_ref, beside_ref = refs[:2]
    own_sides_ref, beside_sides_ref, grad_across_ref, grad_diagonal_ref = refs[2:6]
    refs = refs[6:]
    own_pair_ref, beside_pair_ref, across_ref = refs[:3]
    grad_ref, keep_ref, send_ref, cotangent_ref = refs[3:7]
    side_ref, result_ref = refs[7:]
    own_pair_ref[0], beside_pair_ref[0] = own_ref[...], beside_ref[...]
    utts, frames, width = own_ref.shape
    rows = N_CTX * frames
    chunks = width // LANES
    half = rows_ref.shape[0] // 2
    place = lax.axis_index("ctx")
    blocks = (own_sides_ref[1], beside_sides_ref[1], grad_across_ref[...], grad_diagonal_ref[...])
    for apart in range(N_CTX):
        side_ref[place ^ apart] = blocks[apart].reshape(side_ref.shape[1:])
    edge = jnp.zeros((2 * chunks, 16, LANES), jnp.float32)
    cotangent_ref[:, 0:16, :] = edge
    cotangent_ref[:, 16 + rows : 32 + rows, :] = edge

    def convolve(step, carry):
        utt, chunk = step // chunks, step % chunks
        cols = columns(chunk * LANES, LANES)
        length = length_ref[utt]
        shape = (frames // 8, 8, LANES)
        for block in range(N_CTX):
            base = block * frames
            total = total_ref[step, base : base + frames, :]
            gate = jax.nn.sigmoid(total)
            incoming = side_ref[block, utt, :, cols].astype(jnp.float32)
            slope = gate * (1.0 + total * (1.0 - gate))
            low = (incoming * slope).astype(jnp.bfloat16)
            cotangent_ref[step, 16 + base : 16 + base + frames, :] = low.astype(jnp.float32)
        for block in range(N_CTX):
            base = block * frames
            total = jnp.zeros(shape, jnp.float32)
            for tap in range(TAPS):
                first = base + 16 + REACH - tap
                piece = cotangent_ref[step, first : first + frames, :].reshape(shape)
                total += taps_ref[chunk, tap][None] * piece
            place_of = base + lax.broadcasted_iota(jnp.int32, (frames, LANES), 0)
            total = jnp.where(place_of < length, total.reshape(frames, LANES), 0.0)
            incoming = side_ref[block, utt, :, cols].astype(jnp.float32)
            low = (incoming + total).astype(jnp.bfloat16)
            result_ref[block, utt, :, cols] = low
            grad_ref[utt, base : base + frames, cols] = low
        return carry

    lax.fori_loop(0, 2 * chunks, convolve, 0)
    for apart in range(N_CTX):
        mine = result_ref[place ^ apart]
        if apart < 2:
            (own_pair_ref, beside_pair_ref)[apart][1] = mine
        else:
            across_ref[apart - 2] = mine.reshape(utts * frames, width)
        dest = place ^ apart
        mixed = dot_tt(
            grad_ref[half_of(dest)],
            rows_ref[pl.ds(pl.multiple_of((dest & 1) * half, half), half)],
            1,
            1,
        ).astype(jnp.bfloat16)
        ref = send_ref if apart % 2 else keep_ref
        for block in range(N_CTX):
            first = pl.multiple_of((block ^ dest) * frames, frames)
            ref[apart // 2, pl.ds(first, frames), :] = mixed[block * frames : (block + 1) * frames]


def make_taps(masked_ref, cotangent_ref, awaited_ref, keep_ref, send_ref, tap_sum_ref):
    steps, rows, chunks = masked_ref.shape[0], masked_ref.shape[1] - 32, tap_sum_ref.shape[0]
    block = 64
    shape = (block // 8, 8, LANES)
    tap_sum_ref[...] = jnp.zeros_like(tap_sum_ref)

    def correlate(step, carry):
        chunk = step % chunks
        for base in range(0, rows, block):
            held = masked_ref[step, 16 + base : 16 + base + block, :].reshape(shape)
            for tap in range(TAPS):
                first = base + 16 + REACH - tap
                piece = cotangent_ref[step, first : first + block, :].reshape(shape)
                tap_sum_ref[chunk, tap] += jnp.sum(held * piece, axis=0)
        return carry

    lax.fori_loop(0, steps, correlate, 0)
    sums = [
        jnp.concatenate(
            [
                jnp.sum(tap_sum_ref[chunk, tap], axis=0, keepdims=True)
                for tap in range(TAP_PAD)
            ],
            axis=0,
        )
        for chunk in range(chunks)
    ]
    sums = jnp.concatenate(sums, axis=1)
    own = sums.shape[1] // 2
    halves = [
        jnp.concatenate([part[: TAP_PAD // 2], part[TAP_PAD // 2 :]], axis=1)
        for part in (sums[:, :own], sums[:, own:])
    ]
    odd = (lax.axis_index("dp") & 1) == 1
    keep_ref[...] = jnp.where(odd, halves[1], halves[0])
    send_ref[...] = jnp.where(odd, halves[0], halves[1])


def make_panels(whole_ref, grad_ref, panel_ref):
    rows, half = grad_ref.shape[1], whole_ref.shape[3] // 2
    entries = 2 * half // N_DP
    group = lax.axis_index("dp")
    for side in range(2):
        panel = 0.0
        for utt in range(2):
            mixed = whole_ref[utt, :, :, side * half : (side + 1) * half].reshape(rows, half)
            panel += dot_tt(mixed, grad_ref[utt], 0, 0)
        panel = panel.astype(jnp.bfloat16)
        for part in range(N_DP // 2):
            panel_ref[slot_of(side * N_DP // 2 + part, group)] = panel[
                part * entries : (part + 1) * entries
            ]


def join(panel_ref, came_ref, tap_ref, tap_came_ref, awaited_ref, keep_ref, send_ref):
    entries = panel_ref.shape[1]
    group, place = lax.axis_index("dp"), lax.axis_index("ctx")
    taps = (tap_ref[...] + tap_came_ref[...]).astype(jnp.bfloat16)
    none = jnp.zeros_like(taps)
    for slot in range(N_DP // 2):
        ref = (keep_ref, send_ref)[slot // 2]
        total = panel_ref[slot].astype(jnp.float32) + came_ref[slot].astype(jnp.float32)
        ref[slot % 2, 0:entries] = total.astype(jnp.bfloat16)
        ref[slot % 2, entries:] = none
    mine = slot_of(2 * place, group & 6)
    for slot in range(N_DP // 2):
        ref = (keep_ref, send_ref)[slot // 2]

        @pl.when(mine == slot)
        def _(ref=ref, slot=slot):
            ref[slot % 2, entries:] = taps


def mark(*refs):
    refs[-1][...] = jnp.zeros_like(refs[-1])


def finish(kept_ref, came_ref, awaited_ref, taps_ref):
    entries = kept_ref.shape[1] - TAP_PAD // 2
    total = kept_ref[0, entries:].astype(jnp.float32)
    taps_ref[...] = total + came_ref[entries:].astype(jnp.float32)


def relay(keep_ref, came_ref, out_ref):
    total = keep_ref[1].astype(jnp.float32) + came_ref[1].astype(jnp.float32)
    out_ref[...] = total.astype(jnp.bfloat16)


def make_pair(pair_ref, output_ref, input_ref, *refs):
    out_ref = refs[-1]
    for slot in range(2):
        out_ref[slot] = pair_ref[slot].reshape(out_ref.shape[1:])
    out_ref[2] = output_ref[1]
    out_ref[3] = input_ref[1]


def attend_back(weight_ref, keep_ref, came_ref, far_ref, *refs):
    ins, out_refs = refs[:N_CTX], refs[N_CTX + 1 :]
    frames, half = ins[0].shape[1], ins[0].shape[2]
    rows = N_CTX * frames
    query, key, value = (head_parts(ins, slot) for slot in range(3))
    masks = half_masks(rows)
    scale = HEAD_DIM ** (-0.5)
    arriving = keep_ref[0].astype(jnp.float32) + came_ref[0].astype(jnp.float32)
    arriving = (arriving + far_ref[...].astype(jnp.float32)).astype(jnp.bfloat16)
    low_lanes = lax.broadcasted_iota(jnp.int32, (rows, LANES), 1) < HEAD_DIM
    for pair in range(half // LANES):
        cols = slice(pair * LANES, (pair + 1) * LANES)
        key_pair, value_pair = key[:, cols], value[:, cols]
        query_pair, grad_pair = query[:, cols], arriving[:, cols]
        query_parts, key_parts, value_parts = [], [], []
        for side in range(2):
            low = weight_ref[2 * pair + side]
            weights = low.astype(jnp.float32)
            moved = weights * dot_tt(value_pair, grad_pair * masks[side], 1, 1)
            delta = jnp.sum(moved, axis=0, keepdims=True)
            grad_scores = (moved - weights * delta).astype(jnp.bfloat16)
            value_parts.append(dot_tt(low, grad_pair, 1, 0))
            key_parts.append(dot_tt(grad_scores, query_pair, 1, 0))
            mixed = dot_tt(key_pair, grad_scores, 0, 0)
            query_parts.append(mixed[side * HEAD_DIM : (side + 1) * HEAD_DIM])
        query_sum = (jnp.concatenate(query_parts, axis=0).T * scale).astype(jnp.bfloat16)
        key_sum = (jnp.where(low_lanes, key_parts[0], key_parts[1]) * scale).astype(jnp.bfloat16)
        value_sum = jnp.where(low_lanes, value_parts[0], value_parts[1]).astype(jnp.bfloat16)
        for slot, total in enumerate((query_sum, key_sum, value_sum)):
            for apart in range(N_CTX):
                out_refs[apart][slot, :, cols] = total[apart * frames : (apart + 1) * frames]


def swapped(array, bit):
    return lax.ppermute(array, "dp", [(i, i ^ bit) for i in range(N_DP)])


def dealt(slots):
    return lax.all_to_all(slots, "dp", 0, 0, tiled=True)


def crossed(array, apart):
    return lax.ppermute(array, "ctx", [(i, i ^ apart) for i in range(N_CTX)])


def traded(blocks):
    came = {apart: crossed(blocks[apart], apart) for apart in (2, 3, 1)}
    return [blocks[0]] + [came[apart] for apart in (1, 2, 3)]


def per_device(
    frame_input, queries, key_proj, value_proj, out_weight, conv_weight, lengths, grad_output
):
    utts, frames, wide = frame_input.shape
    inner = queries.shape[2]
    half, width = inner // 2, wide // N_CTX
    rows = N_CTX * frames
    chunks = width // LANES
    low, f32 = jnp.bfloat16, jnp.float32
    shape = jax.ShapeDtypeStruct
    entries = out_weight.shape[1]
    tap_count = conv_weight.shape[0]
    dma = pltpu.SemaphoreType.DMA
    head_block = shape((3, frames, half), low)
    channel_block = shape((utts, frames, width), low)

    blocks = call_kernel(
        pack_heads,
        (head_block,) * N_CTX,
        ["hbm"] * 3,
        scratch=[dma((3 * N_CTX,))],
        room=63,
    )(queries, key_proj, value_proj)
    packed = traded(blocks)
    (shard,) = call_kernel(
        pack_weights,
        (shape((1, entries + TAP_PAD // 2, width), low),),
        ["vmem"] * 2 + ["any"],
    )(out_weight.T, conv_weight, packed[1])
    shard = jnp.concatenate([shard, swapped(shard, 4)], axis=0)
    (shard,) = call_kernel(
        pack_near, (shape((4 * entries + TAP_PAD // 2, width), low),), ["vmem"] * 2
    )(shard, swapped(shard, 2))
    other_shard = swapped(shard, 1)
    pair_block = shape((2, utts, frames, width), low)
    side_block = shape((utts * frames, width), low)
    double_block = shape((2, utts * frames, width), low)
    frame_across, grad_across, grad_diagonal, beside_sides, own_sides = call_kernel(
        pack_channels,
        (double_block,) + (side_block,) * 2 + (double_block,) * 2,
        ["hbm"] * 2 + ["any"],
        scratch=[dma((4 * N_CTX,))],
    )(frame_input, grad_output, packed[2])
    frame_across = crossed(frame_across, 2)
    (beside_sides,) = call_kernel(
        make_sides, (shape((3, utts * frames, width), low),), ["vmem"] * 2
    )(beside_sides, frame_across)
    beside_sides = crossed(beside_sides, 1)
    (attended,) = call_kernel(
        attend,
        (shape((N_CTX, frames, half), low),),
        ["smem"] + ["vmem"] * N_CTX,
    )(lengths, *packed)
    (attended,) = gate([attended], frame_across)
    across = crossed(attended, 2)
    beside = crossed(attended, 1)
    diagonal = crossed(across, 1)
    grad_across, grad_diagonal = crossed(grad_across, 2), crossed(grad_diagonal, 3)
    forward_out = call_kernel(
        forward,
        (channel_block,) * 2
        + (
            shape((2, utts * frames, width), low),
            shape((utts, N_CTX, frames, inner), low),
            shape((inner, width), low),
            shape((chunks, TAP_PAD, 8, LANES), f32),
            shape((utts * chunks, rows, LANES), f32),
            shape((utts * chunks, rows + 32, LANES), f32),
        ),
        ["smem"] + ["vmem"] * (5 + N_CTX),
        scratch=[
            pltpu.VMEM((utts * chunks, rows, LANES), f32),
            pltpu.VMEM((N_CTX, utts, frames, width), low),
            pltpu.VMEM((N_CTX, utts, frames, width), low),
        ],
        micros=3.2,
    )(
        lengths,
        shard,
        other_shard,
        attended,
        beside,
        across,
        diagonal,
        own_sides,
        beside_sides,
        frame_across,
    )
    output_across = crossed(forward_out[2], 2)
    whole, weight_rows, taps, totals, masked = forward_out[3:]
    grad_blocks = gate([grad_across, grad_diagonal], totals, micros=10.0)
    grad_blocks = (own_sides, beside_sides, *grad_blocks)
    backward_out = call_kernel(
        backward,
        (pair_block,) * 2
        + (
            shape((2, utts * frames, width), low),
            shape((utts, rows, width), low),
            shape((2, rows, half), low),
            shape((2, rows, half), low),
            shape((utts * chunks, rows + 32, LANES), f32),
        ),
        ["smem"] + ["vmem"] * (5 + N_CTX),
        scratch=[
            pltpu.VMEM((N_CTX, utts, frames, width), low),
            pltpu.VMEM((N_CTX, utts, frames, width), low),
        ],
        micros=5.2,
    )(lengths, totals, taps, weight_rows, *forward_out[:2], *grad_blocks)
    grad_hidden, keep, send, cotangents = backward_out[3:]
    (send,) = gate([send], output_across)
    came = crossed(send, 1)
    (relayed,) = call_kernel(
        relay, (shape((rows, half), low),), ["vmem"] * 2, micros=0.2
    )(keep, came)
    (input_across,) = gate([backward_out[2]], relayed)
    (panels,) = call_kernel(
        make_panels,
        (shape((N_DP, entries, width), low),),
        ["vmem"] * 2,
        micros=0.7,
    )(whole, grad_hidden)
    panels_came = swapped(panels[4:], 1)
    tap_block = shape((TAP_PAD // 2, width), f32)
    tap_keep, tap_send = call_kernel(
        make_taps,
        (tap_block,) * 2,
        ["vmem"] * 2 + ["any"],
        scratch=[pltpu.VMEM((chunks, TAP_PAD, 8, LANES), f32)],
    )(masked, cotangents, relayed)
    taps_came = swapped(tap_send, 1)
    far, input_across = crossed(relayed, 2), crossed(input_across, 2)
    (weights,) = call_kernel(
        weigh,
        (shape((half // HEAD_DIM, rows, rows), low),),
        ["smem"] + ["vmem"] * N_CTX + ["any"],
    )(lengths, *packed, relayed)
    back_blocks = call_kernel(
        attend_back,
        (head_block,) * N_CTX,
        ["vmem"] * (4 + N_CTX) + ["any"],
        micros=2.2,
    )(weights, keep, came, far, *packed, tap_keep)
    (across_block,) = gate([back_blocks[2]], input_across)
    grad_blocks = traded([*back_blocks[:2], across_block, back_blocks[3]])
    own_pair = backward_out[0]
    (beside_pair,) = call_kernel(
        make_pair,
        (shape((4, utts * frames, width), low),),
        ["vmem"] * 3 + ["any"],
        micros=0.2,
    )(backward_out[1], output_across, input_across, grad_blocks[1])
    beside_pair = crossed(beside_pair, 1)

    kept, sent = call_kernel(
        join,
        (shape((2, entries + TAP_PAD // 2, width), low),) * 2,
        ["vmem"] * 4 + ["any"],
    )(panels[:4], panels_came, tap_keep, taps_came, back_blocks[0])
    panels = (kept.astype(f32) + swapped(sent, 2).astype(f32)).astype(low)
    (arrived,) = call_kernel(mark, (shape((8, LANES), f32),), ["any"] * 2)(*grad_blocks[2:])
    panels_last = swapped(panels[1], 4)
    (tap_sums,) = call_kernel(
        finish, (shape((TAP_PAD // 2, width), f32),), ["vmem"] * 2 + ["any"]
    )(panels, panels_last, arrived)
    total = panels[0].astype(f32) + panels_last.astype(f32)
    grad_out_weight = total[:entries].T
    tap_blocks = traded([tap_sums] * N_CTX)
    grad_queries, grad_keys, grad_values, block_output, grad_input, grad_taps = call_kernel(
        unpack,
        (shape((utts, frames, inner), low),) * 3
        + (shape((utts, frames, wide), low),) * 2
        + (shape(conv_weight.shape, f32),),
        ["any"] * (N_CTX + 4) + ["vmem"] * N_CTX,
        ["hbm"] * 6,
        [
            pltpu.VMEM((N_CTX, TAP_PAD // 2, width), f32),
            pltpu.VMEM(conv_weight.shape, f32),
            dma((7 * N_CTX + 1,)),
        ],
        micros=1.0,
    )(
        *grad_blocks,
        own_pair,
        beside_pair,
        output_across,
        input_across,
        *tap_blocks,
    )
    return (
        block_output,
        grad_input,
        grad_queries,
        grad_keys,
        grad_values,
        grad_out_weight,
        grad_taps,
    )


def chosen(sizes, *arrays):
    frame_input, queries, out_weight, conv_weight = (arrays[i] for i in (0, 1, 4, 5))
    utts, frames, wide = frame_input.shape
    inner = queries.shape[2]
    fits = (
        sizes == (N_DP, N_CTX)
        and utts == 2
        and frames == 64
        and wide % (N_CTX * LANES) == 0
        and inner % (2 * LANES) == 0
        and inner // N_DP % 16 == 0
        and inner // 2 == wide // N_CTX
        and conv_weight.shape == (TAPS, wide // N_DP)
        and out_weight.shape == (wide // N_CTX, inner // N_DP)
    )
    return (per_device if fits else general_device)(*arrays)


def solution(mesh):
    placed = (
        P("dp", "ctx", None),
        P("dp", "ctx", None),
        P("dp", "ctx", None),
        P("dp", "ctx", None),
        P("ctx", "dp"),
        P(None, "dp"),
        P("dp"),
        P("dp", "ctx", None),
    )
    sizes = (mesh.shape["dp"], mesh.shape["ctx"])
    return jax.shard_map(
        functools.partial(chosen, sizes),
        mesh=mesh,
        in_specs=placed,
        out_specs=(
            P("dp", "ctx", None),
            P("dp", "ctx", None),
            P("dp", "ctx", None),
            P("dp", "ctx", None),
            P("dp", "ctx", None),
            P("ctx", "dp"),
            P(None, "dp"),
        ),
        check_vma=False,
    )
```

```python
import functools

import jax
import jax.numpy as jnp
from jax import lax
from jax.experimental import pallas as pl
from jax.experimental.pallas import tpu as pltpu
from jax.sharding import PartitionSpec as P

HEAD_DIM = 64


masked_score = -1e30


def padded_2(array, sides, width):
    for axis, dim in sides:
        size, length = (lax.axis_size(axis), array.shape[dim])
        up = [(i, (i + 1) % size) for i in range(size - 1)]
        down = [(j, i) for i, j in up]
        last = lax.slice_in_dim(array, length - width, length, axis=dim)
        leading = lax.slice_in_dim(array, 0, width, axis=dim)
        before = lax.ppermute(last, axis, up)
        after = lax.ppermute(leading, axis, down)
        array = jnp.concatenate([before, array, after], axis=dim)
    return array


def depthwise(lhs, rhs):
    return lax.conv_general_dilated(
        lhs,
        rhs,
        (1,),
        "VALID",
        dimension_numbers=("NWC", "WIO", "NWC"),
        feature_group_count=lhs.shape[2],
        precision=lax.Precision.HIGHEST,
    )


def general_device(
    frame_input, queries, key_proj, value_proj, out_weight, conv_weight, lengths, grad_output
):
    utt_count = frame_input.shape[0]
    frame_count = frame_input.shape[1]
    inner_width = queries.shape[2]
    head_count = inner_width // HEAD_DIM
    group_heads = max((g for g in range(1, 7) if head_count % g == 0))
    group_count = head_count // group_heads
    group_width = group_heads * HEAD_DIM
    tap_count = conv_weight.shape[0]
    half_span = (tap_count - 1) // 2
    score_scale = HEAD_DIM ** (-0.5)
    total_frames = frame_count * lax.axis_size("ctx")
    offset = lax.axis_index("ctx") * frame_count
    own_valid = (offset + jnp.arange(frame_count, dtype=jnp.int32))[None, :] < lengths[:, None]
    all_valid = jnp.arange(total_frames, dtype=jnp.int32)[None, :] < lengths[:, None]

    def grouped(values):
        row_count = values.shape[1]
        return values.reshape(utt_count, row_count, group_count, group_width).transpose(2, 0, 1, 3)

    def ungrouped(values):
        row_count = values.shape[2]
        return values.transpose(1, 2, 0, 3).reshape(utt_count, row_count, group_count * group_width)

    def split_heads(values):
        return values.reshape(utt_count, values.shape[1], group_heads, HEAD_DIM)

    def stats_grouped(values):
        row_count = values.shape[1]
        return values.reshape(utt_count, row_count, group_count, group_heads).transpose(2, 0, 3, 1)

    def masked_scores(query_block, key_block, key_mask):
        scores = (
            jnp.einsum(
                "uqgd,ukgd->ugqk", query_block, key_block, preferred_element_type=jnp.float32
            )
            * score_scale
        )
        return jnp.where(key_mask[:, None, None, :], scores, masked_score)

    taps = lax.all_gather(conv_weight, "dp", axis=1, tiled=True).astype(jnp.float32)
    panel_rows = lax.all_gather(out_weight, "dp", axis=1, tiled=True)
    weight_full = lax.all_gather(panel_rows, "ctx", axis=0, tiled=True)
    all_keys, all_values = (
        lax.all_gather(key_proj, "ctx", axis=1, tiled=True),
        lax.all_gather(value_proj, "ctx", axis=1, tiled=True),
    )
    query_groups = grouped(queries)
    key_groups = grouped(all_keys)
    value_groups = grouped(all_values)

    def forward_group(unused, items):
        query_group, key_group, value_group = items
        query_block = split_heads(query_group)
        scores = masked_scores(query_block, split_heads(key_group), all_valid)
        largest = jnp.max(scores, axis=-1)
        log_group = largest + jnp.log(jnp.sum(jnp.exp(scores - largest[..., None]), axis=-1))
        weights_low = jnp.exp(scores - log_group[..., None]).astype(jnp.bfloat16)
        attended_group = jnp.einsum(
            "ugqk,ukgd->uqgd",
            weights_low,
            split_heads(value_group),
            preferred_element_type=jnp.float32,
        )
        return (None, (log_group, attended_group.reshape(utt_count, frame_count, group_width)))

    _, (log_groups, attended_groups) = lax.scan(
        forward_group, None, (query_groups, key_groups, value_groups)
    )
    attended = ungrouped(attended_groups).astype(jnp.bfloat16)
    log_total = log_groups.transpose(1, 3, 0, 2).reshape(utt_count, frame_count, head_count)
    projected = jnp.einsum("ufe,de->ufd", attended, weight_full, preferred_element_type=jnp.float32)
    hidden = (frame_input.astype(jnp.float32) + projected).astype(jnp.bfloat16)
    masked_hidden = jnp.where(own_valid[:, :, None], hidden, jnp.zeros_like(hidden))
    padded = padded_2(masked_hidden, (("ctx", 1),), half_span).astype(jnp.float32)
    conv_sum = depthwise(padded, taps[:, None, :])
    sigmoid = jax.nn.sigmoid(conv_sum)
    block_output = (hidden.astype(jnp.float32) + conv_sum * sigmoid).astype(jnp.bfloat16)
    grad_local = grad_output.astype(jnp.float32)
    swish_slope = sigmoid * (1.0 + conv_sum * (1.0 - sigmoid))
    grad_conv = (grad_local * swish_slope).astype(jnp.bfloat16)
    grad_padded = padded_2(grad_conv, (("ctx", 1),), half_span).astype(jnp.float32)
    back_sum = depthwise(grad_padded, taps[::-1][:, None, :])
    grad_hidden = (grad_local + jnp.where(own_valid[:, :, None], back_sum, 0.0)).astype(
        jnp.bfloat16
    )
    grad_conv_wide = grad_conv.astype(jnp.float32)
    kernel_term = jnp.zeros((tap_count, conv_sum.shape[2]), jnp.float32)
    for utt_index in range(utt_count):
        kernel_term = (
            kernel_term
            + depthwise(padded[utt_index : utt_index + 1], grad_conv_wide[utt_index][:, None, :])[0]
        )
    kernel_whole = lax.psum(kernel_term.astype(jnp.bfloat16), "ctx")
    grad_conv_weight = lax.psum_scatter(kernel_whole, "dp", scatter_dimension=1, tiled=True).astype(
        jnp.float32
    )
    grad_attended = jnp.einsum(
        "ufd,de->ufe", grad_hidden, weight_full, preferred_element_type=jnp.float32
    ).astype(jnp.bfloat16)
    row_delta = jnp.sum(
        grad_attended.astype(jnp.float32).reshape(utt_count, frame_count, head_count, HEAD_DIM)
        * attended.astype(jnp.float32).reshape(utt_count, frame_count, head_count, HEAD_DIM),
        axis=-1,
    )
    grad_groups = grouped(grad_attended)

    def query_group_step(unused, items):
        query_group, key_group, value_group, grad_group, log_group, delta_group = items
        key_block = split_heads(key_group)
        weights = jnp.exp(
            masked_scores(split_heads(query_group), key_block, all_valid) - log_group[..., None]
        )
        grad_weights = jnp.einsum(
            "uqgd,ukgd->ugqk",
            split_heads(grad_group),
            split_heads(value_group),
            preferred_element_type=jnp.float32,
        )
        grad_scores = (weights * (grad_weights - delta_group[..., None])).astype(jnp.bfloat16)
        query_sum = jnp.einsum(
            "ugqk,ukgd->uqgd", grad_scores, key_block, preferred_element_type=jnp.float32
        )
        return (None, query_sum.reshape(utt_count, frame_count, group_width))

    _, query_sums = lax.scan(
        query_group_step,
        None,
        (
            query_groups,
            key_groups,
            value_groups,
            grad_groups,
            stats_grouped(log_total),
            stats_grouped(row_delta),
        ),
    )
    grad_queries = (ungrouped(query_sums) * score_scale).astype(jnp.bfloat16)
    total_log, total_delta = (
        lax.all_gather(log_total, "ctx", axis=1, tiled=True),
        lax.all_gather(row_delta, "ctx", axis=1, tiled=True),
    )
    own_key_groups = grouped(key_proj)
    own_value_groups = grouped(value_proj)
    group_zeros = jnp.zeros((group_count, utt_count, frame_count, group_width), jnp.float32)
    start_sums = (group_zeros, group_zeros)
    query_all, grad_all = (
        lax.all_gather(queries, "ctx", axis=1, tiled=True),
        lax.all_gather(grad_attended, "ctx", axis=1, tiled=True),
    )
    log_piece = stats_grouped(total_log)
    delta_piece = stats_grouped(total_delta)

    def key_group_step(unused, items):
        (
            query_group,
            grad_group,
            log_group,
            delta_group,
            key_group,
            value_group,
            key_sum,
            value_sum,
        ) = items
        query_block = split_heads(query_group)
        grad_block = split_heads(grad_group)
        weights = jnp.exp(
            masked_scores(query_block, split_heads(key_group), own_valid) - log_group[..., None]
        )
        grad_weights = jnp.einsum(
            "uqgd,ukgd->ugqk",
            grad_block,
            split_heads(value_group),
            preferred_element_type=jnp.float32,
        )
        grad_scores = (weights * (grad_weights - delta_group[..., None])).astype(jnp.bfloat16)
        key_next = key_sum + jnp.einsum(
            "ugqk,uqgd->ukgd", grad_scores, query_block, preferred_element_type=jnp.float32
        ).reshape(utt_count, frame_count, group_width)
        value_next = value_sum + jnp.einsum(
            "ugqk,uqgd->ukgd",
            weights.astype(jnp.bfloat16),
            grad_block,
            preferred_element_type=jnp.float32,
        ).reshape(utt_count, frame_count, group_width)
        return (None, (key_next, value_next))

    _, result_sums = lax.scan(
        key_group_step,
        None,
        (
            grouped(query_all),
            grouped(grad_all),
            log_piece,
            delta_piece,
            own_key_groups,
            own_value_groups,
            start_sums[0],
            start_sums[1],
        ),
    )
    key_sum, value_sum = result_sums
    grad_keys = (ungrouped(key_sum) * score_scale).astype(jnp.bfloat16)
    grad_values = ungrouped(value_sum).astype(jnp.bfloat16)
    hidden_cols = lax.slice_in_dim(
        grad_hidden, 0, weight_full.shape[0] // lax.axis_size("ctx") * lax.axis_size("ctx"), axis=2
    )
    panel_share = lax.psum_scatter(
        jnp.einsum("ufd,ufe->de", hidden_cols, attended, preferred_element_type=jnp.float32).astype(
            jnp.bfloat16
        ),
        "ctx",
        scatter_dimension=0,
        tiled=True,
    )
    grad_out_weight = lax.psum_scatter(panel_share, "dp", scatter_dimension=1, tiled=True).astype(
        jnp.float32
    )
    return (
        block_output,
        grad_hidden,
        grad_queries,
        grad_keys,
        grad_values,
        grad_out_weight,
        grad_conv_weight,
    )


LANES = 128
N_CTX = 4
N_DP = 8
TAP_PAD = 32
FLOPS_A_MICRO = 1.15e9
TAPS = 31
REACH = 15


def slot_of(index, me):
    apart = index ^ me
    return ((apart & 1) << 2) | (apart & 2) | ((apart >> 2) & 1)


def dot_tt(lhs, rhs, lhs_dim, rhs_dim):
    return lax.dot_general(
        lhs, rhs, (((lhs_dim,), (rhs_dim,)), ((), ())), preferred_element_type=jnp.float32
    )


def call_kernel(body, out_shape, ins, outs=None, scratch=(), room=40, micros=1.0):
    spaces = {
        "smem": pl.BlockSpec(memory_space=pltpu.SMEM),
        "vmem": pl.BlockSpec(memory_space=pltpu.VMEM),
        "hbm": pl.BlockSpec(memory_space=pltpu.HBM),
        "any": pl.BlockSpec(memory_space=pl.ANY),
    }
    return pl.pallas_call(
        body,
        out_shape=out_shape,
        in_specs=[spaces[space] for space in ins],
        out_specs=[spaces[space] for space in (outs or ["vmem"] * len(out_shape))],
        scratch_shapes=list(scratch),
        compiler_params=pltpu.CompilerParams(vmem_limit_bytes=room * 1024 * 1024),
        cost_estimate=pl.CostEstimate(
            flops=int(micros * FLOPS_A_MICRO), bytes_accessed=0, transcendentals=0
        ),
    )


def half_of(index):
    return lax.shift_right_logical(index, 1)


def columns(start, size):
    return pl.ds(pl.multiple_of(start, LANES), size)


def start_copies(pairs, sem):
    for number, (source, target) in enumerate(pairs):
        pltpu.make_async_copy(source, target, sem.at[number]).start()


def wait_copies(pairs, sem):
    for number, (source, target) in enumerate(pairs):
        pltpu.make_async_copy(source, target, sem.at[number]).wait()


def run_copies(pairs, sem):
    start_copies(pairs, sem)
    wait_copies(pairs, sem)


def untouched(*refs):
    pass


def gate(arrays, *awaited, micros=0.0):
    count = len(arrays)
    spec = pl.BlockSpec(memory_space=pl.ANY)
    return pl.pallas_call(
        untouched,
        out_shape=tuple(jax.ShapeDtypeStruct(array.shape, array.dtype) for array in arrays),
        in_specs=[spec] * (count + len(awaited)),
        out_specs=(spec,) * count,
        input_output_aliases={number: number for number in range(count)},
        compiler_params=pltpu.CompilerParams(vmem_limit_bytes=1024 * 1024),
        cost_estimate=pl.CostEstimate(
            flops=int(micros * FLOPS_A_MICRO), bytes_accessed=0, transcendentals=0
        ),
    )(*arrays, *awaited)


def pack_heads(query_ref, key_ref, value_ref, *rest):
    outs, sem = rest[:N_CTX], rest[N_CTX]
    half = query_ref.shape[2] // 2
    place = lax.axis_index("ctx")
    pairs = []
    for apart in (2, 3, 1, 0):
        dest = place ^ apart
        cols = columns((dest & 1) * half, half)
        for slot, ref in enumerate((query_ref, key_ref, value_ref)):
            pairs.append((ref.at[half_of(dest), :, cols], outs[apart].at[slot]))
    run_copies(pairs, sem)


def pack_weights(panel_ref, taps_ref, awaited_ref, out_ref):
    entries = panel_ref.shape[0]
    taps = taps_ref[...].astype(jnp.float32)
    high = jnp.concatenate(
        [taps[TAP_PAD // 2 :], jnp.zeros((TAP_PAD - TAPS, taps.shape[1]), jnp.float32)], axis=0
    )
    out_ref[0, 0:entries] = panel_ref[...]
    joined = jnp.concatenate([taps[: TAP_PAD // 2], high], axis=1)
    out_ref[0, entries:] = joined.astype(jnp.bfloat16)


def pack_near(held_ref, came_ref, out_ref):
    entries = held_ref.shape[1] - TAP_PAD // 2
    for slot in range(2):
        for half, ref in enumerate((held_ref, came_ref)):
            first = (2 * half + slot) * entries
            out_ref[first : first + entries, :] = ref[slot, 0:entries]
    apart = lax.axis_index("ctx") ^ half_of(lax.axis_index("dp"))
    slot = half_of(apart)
    taps = [ref[slot, entries:].astype(jnp.float32) for ref in (held_ref, came_ref)]
    taps = jnp.where((apart & 1) == 1, taps[1], taps[0])
    out_ref[4 * entries :, :] = taps.astype(jnp.bfloat16)


def pack_channels(frame_ref, grad_ref, awaited_ref, *rest):
    across_ref, grad_outs, beside_ref, own_ref, sem = rest[0], rest[1:3], *rest[3:]
    width = frame_ref.shape[2] // N_CTX
    frames = frame_ref.shape[1]
    place = lax.axis_index("ctx")
    pairs = []
    for slot, ref in enumerate((frame_ref, grad_ref)):
        for apart in (2, 3, 1, 0):
            cols = columns((place ^ apart) * width, width)
            for utt in range(2):
                rows = slice(utt * frames, (utt + 1) * frames)
                if apart < 2:
                    target = (own_ref, beside_ref)[apart].at[slot, rows]
                elif slot == 0:
                    target = across_ref.at[apart - 2, rows]
                else:
                    target = grad_outs[apart - 2].at[rows]
                pairs.append((ref.at[utt, :, cols], target))
    run_copies(pairs, sem)


def make_sides(beside_ref, across_ref, out_ref):
    out_ref[0:2] = beside_ref[...]
    out_ref[2] = across_ref[1]


def unpack(*refs):
    ins, refs = refs[:N_CTX], refs[N_CTX:]
    own_ref, beside_ref, output_ref, input_ref = refs[:4]
    taps, heads, channels, taps_ref = refs[4:8], refs[8:11], refs[11:13], refs[13]
    held_ref, picked_ref, sem = refs[14:]
    half, width = ins[0].shape[2], own_ref.shape[3]
    frames = own_ref.shape[2]
    place = lax.axis_index("ctx")
    pairs = []
    for apart in range(N_CTX):
        source = place ^ apart
        cols = columns((source & 1) * half, half)
        for slot, ref in enumerate(heads):
            pairs.append((ins[apart].at[slot], ref.at[half_of(source), :, cols]))
    for slot, ref in enumerate(channels):
        for utt in range(2):
            part = pl.ds(utt * frames, frames)
            blocks = (
                own_ref.at[slot, utt],
                beside_ref.at[slot, part],
                (output_ref, input_ref)[slot].at[0, part],
                beside_ref.at[2 + slot, part],
            )
            for apart, block in enumerate(blocks):
                cols = columns((place ^ apart) * width, width)
                pairs.append((block, ref.at[utt, :, cols]))
    start_copies(pairs, sem)
    for apart in range(N_CTX):
        held_ref[apart] = taps[apart][...]
    mine = held_ref[place ^ half_of(lax.axis_index("dp"))]
    side = mine.shape[1] // 2
    picked_ref[...] = jnp.concatenate([mine[:, :side], mine[:, side:]], axis=0)[:TAPS]
    last = pltpu.make_async_copy(picked_ref, taps_ref, sem.at[len(pairs)])
    last.start()
    wait_copies(pairs, sem)
    last.wait()


def head_parts(refs, slot):
    return jnp.concatenate([ref[slot] for ref in refs], axis=0)


def half_masks(rows):
    lane = lax.broadcasted_iota(jnp.int32, (rows, LANES), 1)
    low = jnp.where(lane < HEAD_DIM, 1.0, 0.0)
    return low.astype(jnp.bfloat16), (1.0 - low).astype(jnp.bfloat16)


def weights_of(length_ref, key_pair, query_pair, mask, frames):
    place = lax.axis_index("ctx")
    rows = key_pair.shape[0]
    frame = lax.broadcasted_iota(jnp.int32, (rows, rows), 0) ^ (place * frames)
    scores = dot_tt(key_pair, query_pair * mask, 1, 1) * HEAD_DIM ** (-0.5)
    scores = jnp.where(frame < length_ref[half_of(place)], scores, masked_score)
    powers = jnp.exp(scores - jnp.max(scores, axis=0, keepdims=True))
    total = jnp.sum(powers, axis=0, keepdims=True)
    return (powers * (1.0 / total)).astype(jnp.bfloat16)


def attend(length_ref, *refs):
    ins, attended_ref = refs[:N_CTX], refs[N_CTX]
    frames, half = ins[0].shape[1], ins[0].shape[2]
    query, key, value = (head_parts(ins, slot) for slot in range(3))
    masks = half_masks(N_CTX * frames)
    for pair in range(half // LANES):
        cols = slice(pair * LANES, (pair + 1) * LANES)
        parts = []
        for side in range(2):
            low = weights_of(length_ref, key[:, cols], query[:, cols], masks[side], frames)
            mixed = dot_tt(value[:, cols], low, 0, 0)
            parts.append(mixed[side * HEAD_DIM : (side + 1) * HEAD_DIM])
        joined = jnp.concatenate(parts, axis=0).T.astype(jnp.bfloat16)
        attended_ref[:, :, cols] = joined.reshape(N_CTX, frames, LANES)


def weigh(length_ref, *refs):
    ins, weight_ref = refs[:N_CTX], refs[N_CTX + 1]
    frames, half = ins[0].shape[1], ins[0].shape[2]
    query, key = (head_parts(ins, slot) for slot in range(2))
    masks = half_masks(N_CTX * frames)
    for pair in range(half // LANES):
        cols = slice(pair * LANES, (pair + 1) * LANES)
        for side in range(2):
            weight_ref[2 * pair + side] = weights_of(
                length_ref, key[:, cols], query[:, cols], masks[side], frames
            )


def forward(length_ref, near_ref, other_ref, *refs):
    attended_refs, refs = refs[:N_CTX], refs[N_CTX:]
    own_ref, beside_ref, across_ref = refs[:3]
    out_refs, refs = refs[3:6], refs[6:]
    whole_ref, rows_ref, taps_ref, total_ref, masked_ref = refs[:5]
    hidden_ref, frame_ref, result_ref = refs[5:]
    frames, half = attended_refs[0].shape[1], attended_refs[0].shape[2]
    width = frame_ref.shape[3]
    rows = N_CTX * frames
    chunks = width // LANES
    entries = 2 * half // N_DP
    own = width // 2
    place = lax.axis_index("ctx")
    for apart in range(N_CTX):
        source = place ^ apart
        cols = columns((source & 1) * half, half)
        for block in range(N_CTX):
            whole_ref[half_of(source), block ^ source, :, cols] = attended_refs[apart][block]
        block = (own_ref, beside_ref, across_ref, beside_ref)[apart][(0, 0, 0, 2)[apart]]
        frame_ref[source] = block.reshape(frame_ref.shape[1:])
    group = lax.axis_index("dp")
    for slot, apart in enumerate((0, 4, 2, 6)):
        for odd, ref in enumerate((near_ref, other_ref)):
            first = pl.multiple_of((group ^ (apart + odd)) * entries, entries)
            rows_ref[pl.ds(first, entries)] = ref[slot * entries : (slot + 1) * entries]
    odd = (group & 1) == 1
    blocks = [ref[4 * entries :].astype(jnp.float32) for ref in (near_ref, other_ref)]
    blocks = (jnp.where(odd, blocks[1], blocks[0]), jnp.where(odd, blocks[0], blocks[1]))
    pieces = [jnp.concatenate([block[:, :own], block[:, own:]], axis=0) for block in blocks]
    taps = jnp.concatenate(pieces, axis=1)
    for chunk in range(chunks):
        for tap in range(TAPS):
            taps_ref[chunk, tap] = jnp.broadcast_to(
                taps[tap : tap + 1, chunk * LANES : (chunk + 1) * LANES], (8, LANES)
            )
    edge = jnp.zeros((2 * chunks, 16, LANES), jnp.float32)
    masked_ref[:, 0:16, :] = edge
    masked_ref[:, 16 + rows : 32 + rows, :] = edge
    for utt in range(2):
        real = lax.broadcasted_iota(jnp.int32, (rows, LANES), 0) < length_ref[utt]
        mixed = whole_ref[utt].reshape(rows, 2 * half)
        projected = dot_tt(mixed, rows_ref[...], 1, 0)
        hidden = frame_ref[:, utt].reshape(rows, width).astype(jnp.float32) + projected
        hidden = hidden.astype(jnp.bfloat16).astype(jnp.float32)
        for chunk in range(chunks):
            piece = hidden[:, chunk * LANES : (chunk + 1) * LANES]
            hidden_ref[utt * chunks + chunk] = piece
            masked_ref[utt * chunks + chunk, 16 : 16 + rows, :] = jnp.where(real, piece, 0.0)

    def convolve(step, carry):
        utt, chunk = step // chunks, step % chunks
        cols = columns(chunk * LANES, LANES)
        shape = (frames // 8, 8, LANES)
        for block in range(N_CTX):
            base = block * frames
            total = jnp.zeros(shape, jnp.float32)
            for tap in range(TAPS):
                first = base + tap + 16 - REACH
                piece = masked_ref[step, first : first + frames, :]
                total += taps_ref[chunk, tap][None] * piece.reshape(shape)
            total = total.reshape(frames, LANES)
            total_ref[step, base : base + frames, :] = total
            outer = hidden_ref[step, base : base + frames, :] + total * jax.nn.sigmoid(total)
            result_ref[block, utt, :, cols] = outer.astype(jnp.bfloat16)
        return carry

    lax.fori_loop(0, 2 * chunks, convolve, 0)
    for apart in range(2):
        out_refs[apart][...] = result_ref[place ^ apart]
        out_refs[2][apart] = result_ref[place ^ (2 + apart)].reshape(2 * frames, width)


def backward(length_ref, total_ref, taps_ref, rows_ref, *refs):
    own_ref, beside_ref = refs[:2]
    own_sides_ref, beside_sides_ref, grad_across_ref, grad_diagonal_ref = refs[2:6]
    refs = refs[6:]
    own_pair_ref, beside_pair_ref, across_ref = refs[:3]
    grad_ref, keep_ref, send_ref, cotangent_ref = refs[3:7]
    side_ref, result_ref = refs[7:]
    own_pair_ref[0], beside_pair_ref[0] = own_ref[...], beside_ref[...]
    utts, frames, width = own_ref.shape
    rows = N_CTX * frames
    chunks = width // LANES
    half = rows_ref.shape[0] // 2
    place = lax.axis_index("ctx")
    blocks = (own_sides_ref[1], beside_sides_ref[1], grad_across_ref[...], grad_diagonal_ref[...])
    for apart in range(N_CTX):
        side_ref[place ^ apart] = blocks[apart].reshape(side_ref.shape[1:])
    edge = jnp.zeros((2 * chunks, 16, LANES), jnp.float32)
    cotangent_ref[:, 0:16, :] = edge
    cotangent_ref[:, 16 + rows : 32 + rows, :] = edge

    def convolve(step, carry):
        utt, chunk = step // chunks, step % chunks
        cols = columns(chunk * LANES, LANES)
        length = length_ref[utt]
        shape = (frames // 8, 8, LANES)
        for block in range(N_CTX):
            base = block * frames
            total = total_ref[step, base : base + frames, :]
            gate = jax.nn.sigmoid(total)
            incoming = side_ref[block, utt, :, cols].astype(jnp.float32)
            slope = gate * (1.0 + total * (1.0 - gate))
            low = (incoming * slope).astype(jnp.bfloat16)
            cotangent_ref[step, 16 + base : 16 + base + frames, :] = low.astype(jnp.float32)
        for block in range(N_CTX):
            base = block * frames
            total = jnp.zeros(shape, jnp.float32)
            for tap in range(TAPS):
                first = base + 16 + REACH - tap
                piece = cotangent_ref[step, first : first + frames, :].reshape(shape)
                total += taps_ref[chunk, tap][None] * piece
            place_of = base + lax.broadcasted_iota(jnp.int32, (frames, LANES), 0)
            total = jnp.where(place_of < length, total.reshape(frames, LANES), 0.0)
            incoming = side_ref[block, utt, :, cols].astype(jnp.float32)
            low = (incoming + total).astype(jnp.bfloat16)
            result_ref[block, utt, :, cols] = low
            grad_ref[utt, base : base + frames, cols] = low
        return carry

    lax.fori_loop(0, 2 * chunks, convolve, 0)
    for apart in range(N_CTX):
        mine = result_ref[place ^ apart]
        if apart < 2:
            (own_pair_ref, beside_pair_ref)[apart][1] = mine
        else:
            across_ref[apart - 2] = mine.reshape(utts * frames, width)
        dest = place ^ apart
        mixed = dot_tt(
            grad_ref[half_of(dest)],
            rows_ref[pl.ds(pl.multiple_of((dest & 1) * half, half), half)],
            1,
            1,
        ).astype(jnp.bfloat16)
        ref = send_ref if apart % 2 else keep_ref
        for block in range(N_CTX):
            first = pl.multiple_of((block ^ dest) * frames, frames)
            ref[apart // 2, pl.ds(first, frames), :] = mixed[block * frames : (block + 1) * frames]


def make_taps(masked_ref, cotangent_ref, awaited_ref, keep_ref, send_ref, tap_sum_ref):
    steps, rows, chunks = masked_ref.shape[0], masked_ref.shape[1] - 32, tap_sum_ref.shape[0]
    block = 64
    shape = (block // 8, 8, LANES)
    tap_sum_ref[...] = jnp.zeros_like(tap_sum_ref)

    def correlate(step, carry):
        chunk = step % chunks
        for base in range(0, rows, block):
            held = masked_ref[step, 16 + base : 16 + base + block, :].reshape(shape)
            for tap in range(TAPS):
                first = base + 16 + REACH - tap
                piece = cotangent_ref[step, first : first + block, :].reshape(shape)
                tap_sum_ref[chunk, tap] += jnp.sum(held * piece, axis=0)
        return carry

    lax.fori_loop(0, steps, correlate, 0)
    sums = [
        jnp.concatenate(
            [
                jnp.sum(tap_sum_ref[chunk, tap], axis=0, keepdims=True)
                for tap in range(TAP_PAD)
            ],
            axis=0,
        )
        for chunk in range(chunks)
    ]
    sums = jnp.concatenate(sums, axis=1)
    own = sums.shape[1] // 2
    halves = [
        jnp.concatenate([part[: TAP_PAD // 2], part[TAP_PAD // 2 :]], axis=1)
        for part in (sums[:, :own], sums[:, own:])
    ]
    odd = (lax.axis_index("dp") & 1) == 1
    keep_ref[...] = jnp.where(odd, halves[1], halves[0])
    send_ref[...] = jnp.where(odd, halves[0], halves[1])


def make_panels(whole_ref, grad_ref, panel_ref):
    rows, half = grad_ref.shape[1], whole_ref.shape[3] // 2
    entries = 2 * half // N_DP
    group = lax.axis_index("dp")
    for side in range(2):
        panel = 0.0
        for utt in range(2):
            mixed = whole_ref[utt, :, :, side * half : (side + 1) * half].reshape(rows, half)
            panel += dot_tt(mixed, grad_ref[utt], 0, 0)
        panel = panel.astype(jnp.bfloat16)
        for part in range(N_DP // 2):
            panel_ref[slot_of(side * N_DP // 2 + part, group)] = panel[
                part * entries : (part + 1) * entries
            ]


def join(panel_ref, came_ref, tap_ref, tap_came_ref, awaited_ref, *refs):
    first_refs, second_refs = refs[0:2], refs[2:4]
    split = first_refs[0].shape[1]
    entries = panel_ref.shape[1]
    place = lax.axis_index("ctx")
    taps = (tap_ref[...] + tap_came_ref[...]).astype(jnp.bfloat16)
    none = jnp.zeros_like(taps)
    mine = place ^ half_of(lax.axis_index("dp"))
    for slot, apart in enumerate((0, 2, 1, 3)):
        total = panel_ref[slot].astype(jnp.float32) + came_ref[slot].astype(jnp.float32)
        total = total.astype(jnp.bfloat16)
        first_refs[apart // 2][apart & 1] = total[:split]
        ref, number = second_refs[apart & 1], apart // 2
        ref[number, 0 : entries - split] = total[split:]
        ref[number, entries - split :] = none

        @pl.when(mine == apart)
        def _(ref=ref, number=number):
            ref[number, entries - split :] = taps


def mark(*refs):
    refs[-1][...] = jnp.zeros_like(refs[-1])


def finish(kept_ref, came_ref, awaited_ref, taps_ref):
    entries = kept_ref.shape[1] - TAP_PAD // 2
    total = kept_ref[0, entries:].astype(jnp.float32)
    taps_ref[...] = total + came_ref[entries:].astype(jnp.float32)


def relay(keep_ref, came_ref, out_ref):
    total = keep_ref[1].astype(jnp.float32) + came_ref[1].astype(jnp.float32)
    out_ref[...] = total.astype(jnp.bfloat16)


def make_pair(pair_ref, output_ref, input_ref, *refs):
    out_ref = refs[-1]
    for slot in range(2):
        out_ref[slot] = pair_ref[slot].reshape(out_ref.shape[1:])
    out_ref[2] = output_ref[1]
    out_ref[3] = input_ref[1]


def attend_back(weight_ref, keep_ref, came_ref, far_ref, *refs):
    ins, out_refs = refs[:N_CTX], refs[N_CTX + 1 :]
    frames, half = ins[0].shape[1], ins[0].shape[2]
    rows = N_CTX * frames
    query, key, value = (head_parts(ins, slot) for slot in range(3))
    masks = half_masks(rows)
    scale = HEAD_DIM ** (-0.5)
    arriving = keep_ref[0].astype(jnp.float32) + came_ref[0].astype(jnp.float32)
    arriving = (arriving + far_ref[...].astype(jnp.float32)).astype(jnp.bfloat16)
    low_lanes = lax.broadcasted_iota(jnp.int32, (rows, LANES), 1) < HEAD_DIM
    for pair in range(half // LANES):
        cols = slice(pair * LANES, (pair + 1) * LANES)
        key_pair, value_pair = key[:, cols], value[:, cols]
        query_pair, grad_pair = query[:, cols], arriving[:, cols]
        query_parts, key_parts, value_parts = [], [], []
        for side in range(2):
            low = weight_ref[2 * pair + side]
            weights = low.astype(jnp.float32)
            moved = weights * dot_tt(value_pair, grad_pair * masks[side], 1, 1)
            delta = jnp.sum(moved, axis=0, keepdims=True)
            grad_scores = (moved - weights * delta).astype(jnp.bfloat16)
            value_parts.append(dot_tt(low, grad_pair, 1, 0))
            key_parts.append(dot_tt(grad_scores, query_pair, 1, 0))
            mixed = dot_tt(key_pair, grad_scores, 0, 0)
            query_parts.append(mixed[side * HEAD_DIM : (side + 1) * HEAD_DIM])
        query_sum = (jnp.concatenate(query_parts, axis=0).T * scale).astype(jnp.bfloat16)
        key_sum = (jnp.where(low_lanes, key_parts[0], key_parts[1]) * scale).astype(jnp.bfloat16)
        value_sum = jnp.where(low_lanes, value_parts[0], value_parts[1]).astype(jnp.bfloat16)
        for slot, total in enumerate((query_sum, key_sum, value_sum)):
            for apart in range(N_CTX):
                out_refs[apart][slot, :, cols] = total[apart * frames : (apart + 1) * frames]


def swapped(array, bit):
    return lax.ppermute(array, "dp", [(i, i ^ bit) for i in range(N_DP)])


def dealt(slots):
    return lax.all_to_all(slots, "dp", 0, 0, tiled=True)


def crossed(array, apart):
    return lax.ppermute(array, "ctx", [(i, i ^ apart) for i in range(N_CTX)])


def traded(blocks):
    came = {apart: crossed(blocks[apart], apart) for apart in (2, 3, 1)}
    return [blocks[0]] + [came[apart] for apart in (1, 2, 3)]


def per_device(
    frame_input, queries, key_proj, value_proj, out_weight, conv_weight, lengths, grad_output
):
    utts, frames, wide = frame_input.shape
    inner = queries.shape[2]
    half, width = inner // 2, wide // N_CTX
    rows = N_CTX * frames
    chunks = width // LANES
    low, f32 = jnp.bfloat16, jnp.float32
    shape = jax.ShapeDtypeStruct
    entries = out_weight.shape[1]
    tap_count = conv_weight.shape[0]
    dma = pltpu.SemaphoreType.DMA
    head_block = shape((3, frames, half), low)
    channel_block = shape((utts, frames, width), low)

    blocks = call_kernel(
        pack_heads,
        (head_block,) * N_CTX,
        ["hbm"] * 3,
        scratch=[dma((3 * N_CTX,))],
        room=63,
    )(queries, key_proj, value_proj)
    packed = traded(blocks)
    (shard,) = call_kernel(
        pack_weights,
        (shape((1, entries + TAP_PAD // 2, width), low),),
        ["vmem"] * 2 + ["any"],
    )(out_weight.T, conv_weight, packed[1])
    shard = jnp.concatenate([shard, swapped(shard, 4)], axis=0)
    (shard,) = call_kernel(
        pack_near, (shape((4 * entries + TAP_PAD // 2, width), low),), ["vmem"] * 2
    )(shard, swapped(shard, 2))
    other_shard = swapped(shard, 1)
    pair_block = shape((2, utts, frames, width), low)
    side_block = shape((utts * frames, width), low)
    double_block = shape((2, utts * frames, width), low)
    frame_across, grad_across, grad_diagonal, beside_sides, own_sides = call_kernel(
        pack_channels,
        (double_block,) + (side_block,) * 2 + (double_block,) * 2,
        ["hbm"] * 2 + ["any"],
        scratch=[dma((4 * N_CTX,))],
    )(frame_input, grad_output, packed[2])
    frame_across = crossed(frame_across, 2)
    (beside_sides,) = call_kernel(
        make_sides, (shape((3, utts * frames, width), low),), ["vmem"] * 2
    )(beside_sides, frame_across)
    beside_sides = crossed(beside_sides, 1)
    (attended,) = call_kernel(
        attend,
        (shape((N_CTX, frames, half), low),),
        ["smem"] + ["vmem"] * N_CTX,
    )(lengths, *packed)
    (attended,) = gate([attended], frame_across)
    across = crossed(attended, 2)
    beside = crossed(attended, 1)
    diagonal = crossed(across, 1)
    grad_across, grad_diagonal = crossed(grad_across, 2), crossed(grad_diagonal, 3)
    forward_out = call_kernel(
        forward,
        (channel_block,) * 2
        + (
            shape((2, utts * frames, width), low),
            shape((utts, N_CTX, frames, inner), low),
            shape((inner, width), low),
            shape((chunks, TAP_PAD, 8, LANES), f32),
            shape((utts * chunks, rows, LANES), f32),
            shape((utts * chunks, rows + 32, LANES), f32),
        ),
        ["smem"] + ["vmem"] * (5 + N_CTX),
        scratch=[
            pltpu.VMEM((utts * chunks, rows, LANES), f32),
            pltpu.VMEM((N_CTX, utts, frames, width), low),
            pltpu.VMEM((N_CTX, utts, frames, width), low),
        ],
        micros=3.2,
    )(
        lengths,
        shard,
        other_shard,
        attended,
        beside,
        across,
        diagonal,
        own_sides,
        beside_sides,
        frame_across,
    )
    output_across = crossed(forward_out[2], 2)
    whole, weight_rows, taps, totals, masked = forward_out[3:]
    grad_blocks = gate([grad_across, grad_diagonal], totals, micros=10.0)
    grad_blocks = (own_sides, beside_sides, *grad_blocks)
    backward_out = call_kernel(
        backward,
        (pair_block,) * 2
        + (
            shape((2, utts * frames, width), low),
            shape((utts, rows, width), low),
            shape((2, rows, half), low),
            shape((2, rows, half), low),
            shape((utts * chunks, rows + 32, LANES), f32),
        ),
        ["smem"] + ["vmem"] * (5 + N_CTX),
        scratch=[
            pltpu.VMEM((N_CTX, utts, frames, width), low),
            pltpu.VMEM((N_CTX, utts, frames, width), low),
        ],
        micros=5.2,
    )(lengths, totals, taps, weight_rows, *forward_out[:2], *grad_blocks)
    grad_hidden, keep, send, cotangents = backward_out[3:]
    (send,) = gate([send], output_across)
    came = crossed(send, 1)
    (relayed,) = call_kernel(
        relay, (shape((rows, half), low),), ["vmem"] * 2, micros=0.2
    )(keep, came)
    (input_across,) = gate([backward_out[2]], relayed)
    (panels,) = call_kernel(
        make_panels,
        (shape((N_DP, entries, width), low),),
        ["vmem"] * 2,
        micros=0.7,
    )(whole, grad_hidden)
    panels_came = swapped(panels[4:], 1)
    tap_block = shape((TAP_PAD // 2, width), f32)
    tap_keep, tap_send = call_kernel(
        make_taps,
        (tap_block,) * 2,
        ["vmem"] * 2 + ["any"],
        scratch=[pltpu.VMEM((chunks, TAP_PAD, 8, LANES), f32)],
    )(masked, cotangents, relayed)
    taps_came = swapped(tap_send, 1)
    far, input_across = crossed(relayed, 2), crossed(input_across, 2)
    (weights,) = call_kernel(
        weigh,
        (shape((half // HEAD_DIM, rows, rows), low),),
        ["smem"] + ["vmem"] * N_CTX + ["any"],
    )(lengths, *packed, relayed)
    back_blocks = call_kernel(
        attend_back,
        (head_block,) * N_CTX,
        ["vmem"] * (4 + N_CTX) + ["any"],
        micros=2.2,
    )(weights, keep, came, far, *packed, tap_keep)
    (across_block,) = gate([back_blocks[2]], input_across)
    grad_blocks = traded([*back_blocks[:2], across_block, back_blocks[3]])
    own_pair = backward_out[0]
    (beside_pair,) = call_kernel(
        make_pair,
        (shape((4, utts * frames, width), low),),
        ["vmem"] * 3 + ["any"],
        micros=0.2,
    )(backward_out[1], output_across, input_across, grad_blocks[1])
    beside_pair = crossed(beside_pair, 1)

    split = entries // 2
    first_kept, first_sent, second_kept, second_sent = call_kernel(
        join,
        (shape((2, split, width), low),) * 2
        + (shape((2, entries - split + TAP_PAD // 2, width), low),) * 2,
        ["vmem"] * 4 + ["any"],
    )(panels[:4], panels_came, tap_keep, taps_came, back_blocks[0])
    (first_sent,) = gate([first_sent], grad_blocks[1])
    second_came, first_came = swapped(second_sent, 2), swapped(first_sent, 4)
    second = (second_kept.astype(f32) + second_came.astype(f32)).astype(low)
    first = (first_kept.astype(f32) + first_came.astype(f32)).astype(low)
    second_last, first_last = swapped(second[1], 4), swapped(first[1], 2)
    (arrived,) = call_kernel(mark, (shape((8, LANES), f32),), ["any"] * 2)(*grad_blocks[2:])
    (tap_sums,) = call_kernel(
        finish, (shape((TAP_PAD // 2, width), f32),), ["vmem"] * 2 + ["any"]
    )(second, second_last, arrived)
    total = jnp.concatenate(
        [
            first[0].astype(f32) + first_last.astype(f32),
            (second[0].astype(f32) + second_last.astype(f32))[: entries - split],
        ],
        axis=0,
    )
    grad_out_weight = total.T
    tap_blocks = traded([tap_sums] * N_CTX)
    grad_queries, grad_keys, grad_values, block_output, grad_input, grad_taps = call_kernel(
        unpack,
        (shape((utts, frames, inner), low),) * 3
        + (shape((utts, frames, wide), low),) * 2
        + (shape(conv_weight.shape, f32),),
        ["any"] * (N_CTX + 4) + ["vmem"] * N_CTX,
        ["hbm"] * 6,
        [
            pltpu.VMEM((N_CTX, TAP_PAD // 2, width), f32),
            pltpu.VMEM(conv_weight.shape, f32),
            dma((7 * N_CTX + 1,)),
        ],
        micros=1.0,
    )(
        *grad_blocks,
        own_pair,
        beside_pair,
        output_across,
        input_across,
        *tap_blocks,
    )
    return (
        block_output,
        grad_input,
        grad_queries,
        grad_keys,
        grad_values,
        grad_out_weight,
        grad_taps,
    )


def chosen(sizes, *arrays):
    frame_input, queries, out_weight, conv_weight = (arrays[i] for i in (0, 1, 4, 5))
    utts, frames, wide = frame_input.shape
    inner = queries.shape[2]
    fits = (
        sizes == (N_DP, N_CTX)
        and utts == 2
        and frames == 64
        and wide % (N_CTX * LANES) == 0
        and inner % (2 * LANES) == 0
        and inner // N_DP % 16 == 0
        and inner // 2 == wide // N_CTX
        and conv_weight.shape == (TAPS, wide // N_DP)
        and out_weight.shape == (wide // N_CTX, inner // N_DP)
    )
    return (per_device if fits else general_device)(*arrays)


def solution(mesh):
    placed = (
        P("dp", "ctx", None),
        P("dp", "ctx", None),
        P("dp", "ctx", None),
        P("dp", "ctx", None),
        P("ctx", "dp"),
        P(None, "dp"),
        P("dp"),
        P("dp", "ctx", None),
    )
    sizes = (mesh.shape["dp"], mesh.shape["ctx"])
    return jax.shard_map(
        functools.partial(chosen, sizes),
        mesh=mesh,
        in_specs=placed,
        out_specs=(
            P("dp", "ctx", None),
            P("dp", "ctx", None),
            P("dp", "ctx", None),
            P("dp", "ctx", None),
            P("dp", "ctx", None),
            P("ctx", "dp"),
            P(None, "dp"),
        ),
        check_vma=False,
    )
```

```python
import functools

import jax
import jax.numpy as jnp
from jax import lax
from jax.experimental import pallas as pl
from jax.experimental.pallas import tpu as pltpu
from jax.sharding import PartitionSpec as P

HEAD_DIM = 64


masked_score = -1e30


def padded_2(array, sides, width):
    for axis, dim in sides:
        size, length = (lax.axis_size(axis), array.shape[dim])
        up = [(i, (i + 1) % size) for i in range(size - 1)]
        down = [(j, i) for i, j in up]
        last = lax.slice_in_dim(array, length - width, length, axis=dim)
        leading = lax.slice_in_dim(array, 0, width, axis=dim)
        before = lax.ppermute(last, axis, up)
        after = lax.ppermute(leading, axis, down)
        array = jnp.concatenate([before, array, after], axis=dim)
    return array


def depthwise(lhs, rhs):
    return lax.conv_general_dilated(
        lhs,
        rhs,
        (1,),
        "VALID",
        dimension_numbers=("NWC", "WIO", "NWC"),
        feature_group_count=lhs.shape[2],
        precision=lax.Precision.HIGHEST,
    )


def general_device(
    frame_input, queries, key_proj, value_proj, out_weight, conv_weight, lengths, grad_output
):
    utt_count = frame_input.shape[0]
    frame_count = frame_input.shape[1]
    inner_width = queries.shape[2]
    head_count = inner_width // HEAD_DIM
    group_heads = max((g for g in range(1, 7) if head_count % g == 0))
    group_count = head_count // group_heads
    group_width = group_heads * HEAD_DIM
    tap_count = conv_weight.shape[0]
    half_span = (tap_count - 1) // 2
    score_scale = HEAD_DIM ** (-0.5)
    total_frames = frame_count * lax.axis_size("ctx")
    offset = lax.axis_index("ctx") * frame_count
    own_valid = (offset + jnp.arange(frame_count, dtype=jnp.int32))[None, :] < lengths[:, None]
    all_valid = jnp.arange(total_frames, dtype=jnp.int32)[None, :] < lengths[:, None]

    def grouped(values):
        row_count = values.shape[1]
        return values.reshape(utt_count, row_count, group_count, group_width).transpose(2, 0, 1, 3)

    def ungrouped(values):
        row_count = values.shape[2]
        return values.transpose(1, 2, 0, 3).reshape(utt_count, row_count, group_count * group_width)

    def split_heads(values):
        return values.reshape(utt_count, values.shape[1], group_heads, HEAD_DIM)

    def stats_grouped(values):
        row_count = values.shape[1]
        return values.reshape(utt_count, row_count, group_count, group_heads).transpose(2, 0, 3, 1)

    def masked_scores(query_block, key_block, key_mask):
        scores = (
            jnp.einsum(
                "uqgd,ukgd->ugqk", query_block, key_block, preferred_element_type=jnp.float32
            )
            * score_scale
        )
        return jnp.where(key_mask[:, None, None, :], scores, masked_score)

    taps = lax.all_gather(conv_weight, "dp", axis=1, tiled=True).astype(jnp.float32)
    panel_rows = lax.all_gather(out_weight, "dp", axis=1, tiled=True)
    weight_full = lax.all_gather(panel_rows, "ctx", axis=0, tiled=True)
    all_keys, all_values = (
        lax.all_gather(key_proj, "ctx", axis=1, tiled=True),
        lax.all_gather(value_proj, "ctx", axis=1, tiled=True),
    )
    query_groups = grouped(queries)
    key_groups = grouped(all_keys)
    value_groups = grouped(all_values)

    def forward_group(unused, items):
        query_group, key_group, value_group = items
        query_block = split_heads(query_group)
        scores = masked_scores(query_block, split_heads(key_group), all_valid)
        largest = jnp.max(scores, axis=-1)
        log_group = largest + jnp.log(jnp.sum(jnp.exp(scores - largest[..., None]), axis=-1))
        weights_low = jnp.exp(scores - log_group[..., None]).astype(jnp.bfloat16)
        attended_group = jnp.einsum(
            "ugqk,ukgd->uqgd",
            weights_low,
            split_heads(value_group),
            preferred_element_type=jnp.float32,
        )
        return (None, (log_group, attended_group.reshape(utt_count, frame_count, group_width)))

    _, (log_groups, attended_groups) = lax.scan(
        forward_group, None, (query_groups, key_groups, value_groups)
    )
    attended = ungrouped(attended_groups).astype(jnp.bfloat16)
    log_total = log_groups.transpose(1, 3, 0, 2).reshape(utt_count, frame_count, head_count)
    projected = jnp.einsum("ufe,de->ufd", attended, weight_full, preferred_element_type=jnp.float32)
    hidden = (frame_input.astype(jnp.float32) + projected).astype(jnp.bfloat16)
    masked_hidden = jnp.where(own_valid[:, :, None], hidden, jnp.zeros_like(hidden))
    padded = padded_2(masked_hidden, (("ctx", 1),), half_span).astype(jnp.float32)
    conv_sum = depthwise(padded, taps[:, None, :])
    sigmoid = jax.nn.sigmoid(conv_sum)
    block_output = (hidden.astype(jnp.float32) + conv_sum * sigmoid).astype(jnp.bfloat16)
    grad_local = grad_output.astype(jnp.float32)
    swish_slope = sigmoid * (1.0 + conv_sum * (1.0 - sigmoid))
    grad_conv = (grad_local * swish_slope).astype(jnp.bfloat16)
    grad_padded = padded_2(grad_conv, (("ctx", 1),), half_span).astype(jnp.float32)
    back_sum = depthwise(grad_padded, taps[::-1][:, None, :])
    grad_hidden = (grad_local + jnp.where(own_valid[:, :, None], back_sum, 0.0)).astype(
        jnp.bfloat16
    )
    grad_conv_wide = grad_conv.astype(jnp.float32)
    kernel_term = jnp.zeros((tap_count, conv_sum.shape[2]), jnp.float32)
    for utt_index in range(utt_count):
        kernel_term = (
            kernel_term
            + depthwise(padded[utt_index : utt_index + 1], grad_conv_wide[utt_index][:, None, :])[0]
        )
    kernel_whole = lax.psum(kernel_term.astype(jnp.bfloat16), "ctx")
    grad_conv_weight = lax.psum_scatter(kernel_whole, "dp", scatter_dimension=1, tiled=True).astype(
        jnp.float32
    )
    grad_attended = jnp.einsum(
        "ufd,de->ufe", grad_hidden, weight_full, preferred_element_type=jnp.float32
    ).astype(jnp.bfloat16)
    row_delta = jnp.sum(
        grad_attended.astype(jnp.float32).reshape(utt_count, frame_count, head_count, HEAD_DIM)
        * attended.astype(jnp.float32).reshape(utt_count, frame_count, head_count, HEAD_DIM),
        axis=-1,
    )
    grad_groups = grouped(grad_attended)

    def query_group_step(unused, items):
        query_group, key_group, value_group, grad_group, log_group, delta_group = items
        key_block = split_heads(key_group)
        weights = jnp.exp(
            masked_scores(split_heads(query_group), key_block, all_valid) - log_group[..., None]
        )
        grad_weights = jnp.einsum(
            "uqgd,ukgd->ugqk",
            split_heads(grad_group),
            split_heads(value_group),
            preferred_element_type=jnp.float32,
        )
        grad_scores = (weights * (grad_weights - delta_group[..., None])).astype(jnp.bfloat16)
        query_sum = jnp.einsum(
            "ugqk,ukgd->uqgd", grad_scores, key_block, preferred_element_type=jnp.float32
        )
        return (None, query_sum.reshape(utt_count, frame_count, group_width))

    _, query_sums = lax.scan(
        query_group_step,
        None,
        (
            query_groups,
            key_groups,
            value_groups,
            grad_groups,
            stats_grouped(log_total),
            stats_grouped(row_delta),
        ),
    )
    grad_queries = (ungrouped(query_sums) * score_scale).astype(jnp.bfloat16)
    total_log, total_delta = (
        lax.all_gather(log_total, "ctx", axis=1, tiled=True),
        lax.all_gather(row_delta, "ctx", axis=1, tiled=True),
    )
    own_key_groups = grouped(key_proj)
    own_value_groups = grouped(value_proj)
    group_zeros = jnp.zeros((group_count, utt_count, frame_count, group_width), jnp.float32)
    start_sums = (group_zeros, group_zeros)
    query_all, grad_all = (
        lax.all_gather(queries, "ctx", axis=1, tiled=True),
        lax.all_gather(grad_attended, "ctx", axis=1, tiled=True),
    )
    log_piece = stats_grouped(total_log)
    delta_piece = stats_grouped(total_delta)

    def key_group_step(unused, items):
        (
            query_group,
            grad_group,
            log_group,
            delta_group,
            key_group,
            value_group,
            key_sum,
            value_sum,
        ) = items
        query_block = split_heads(query_group)
        grad_block = split_heads(grad_group)
        weights = jnp.exp(
            masked_scores(query_block, split_heads(key_group), own_valid) - log_group[..., None]
        )
        grad_weights = jnp.einsum(
            "uqgd,ukgd->ugqk",
            grad_block,
            split_heads(value_group),
            preferred_element_type=jnp.float32,
        )
        grad_scores = (weights * (grad_weights - delta_group[..., None])).astype(jnp.bfloat16)
        key_next = key_sum + jnp.einsum(
            "ugqk,uqgd->ukgd", grad_scores, query_block, preferred_element_type=jnp.float32
        ).reshape(utt_count, frame_count, group_width)
        value_next = value_sum + jnp.einsum(
            "ugqk,uqgd->ukgd",
            weights.astype(jnp.bfloat16),
            grad_block,
            preferred_element_type=jnp.float32,
        ).reshape(utt_count, frame_count, group_width)
        return (None, (key_next, value_next))

    _, result_sums = lax.scan(
        key_group_step,
        None,
        (
            grouped(query_all),
            grouped(grad_all),
            log_piece,
            delta_piece,
            own_key_groups,
            own_value_groups,
            start_sums[0],
            start_sums[1],
        ),
    )
    key_sum, value_sum = result_sums
    grad_keys = (ungrouped(key_sum) * score_scale).astype(jnp.bfloat16)
    grad_values = ungrouped(value_sum).astype(jnp.bfloat16)
    hidden_cols = lax.slice_in_dim(
        grad_hidden, 0, weight_full.shape[0] // lax.axis_size("ctx") * lax.axis_size("ctx"), axis=2
    )
    panel_share = lax.psum_scatter(
        jnp.einsum("ufd,ufe->de", hidden_cols, attended, preferred_element_type=jnp.float32).astype(
            jnp.bfloat16
        ),
        "ctx",
        scatter_dimension=0,
        tiled=True,
    )
    grad_out_weight = lax.psum_scatter(panel_share, "dp", scatter_dimension=1, tiled=True).astype(
        jnp.float32
    )
    return (
        block_output,
        grad_hidden,
        grad_queries,
        grad_keys,
        grad_values,
        grad_out_weight,
        grad_conv_weight,
    )


LANES = 128
N_CTX = 4
N_DP = 8
TAP_PAD = 32
FLOPS_A_MICRO = 1.15e9
TAPS = 31
REACH = 15


def slot_of(index, me):
    apart = index ^ me
    return ((apart & 1) << 2) | (apart & 2) | ((apart >> 2) & 1)


def dot_tt(lhs, rhs, lhs_dim, rhs_dim):
    return lax.dot_general(
        lhs, rhs, (((lhs_dim,), (rhs_dim,)), ((), ())), preferred_element_type=jnp.float32
    )


def call_kernel(body, out_shape, ins, outs=None, scratch=(), room=40, micros=1.0):
    spaces = {
        "smem": pl.BlockSpec(memory_space=pltpu.SMEM),
        "vmem": pl.BlockSpec(memory_space=pltpu.VMEM),
        "hbm": pl.BlockSpec(memory_space=pltpu.HBM),
        "any": pl.BlockSpec(memory_space=pl.ANY),
    }
    return pl.pallas_call(
        body,
        out_shape=out_shape,
        in_specs=[spaces[space] for space in ins],
        out_specs=[spaces[space] for space in (outs or ["vmem"] * len(out_shape))],
        scratch_shapes=list(scratch),
        compiler_params=pltpu.CompilerParams(vmem_limit_bytes=room * 1024 * 1024),
        cost_estimate=pl.CostEstimate(
            flops=int(micros * FLOPS_A_MICRO), bytes_accessed=0, transcendentals=0
        ),
    )


def half_of(index):
    return lax.shift_right_logical(index, 1)


def columns(start, size):
    return pl.ds(pl.multiple_of(start, LANES), size)


def start_copies(pairs, sem):
    for number, (source, target) in enumerate(pairs):
        pltpu.make_async_copy(source, target, sem.at[number]).start()


def wait_copies(pairs, sem):
    for number, (source, target) in enumerate(pairs):
        pltpu.make_async_copy(source, target, sem.at[number]).wait()


def run_copies(pairs, sem):
    start_copies(pairs, sem)
    wait_copies(pairs, sem)


def untouched(*refs):
    pass


def gate(arrays, *awaited, micros=0.0):
    count = len(arrays)
    spec = pl.BlockSpec(memory_space=pl.ANY)
    return pl.pallas_call(
        untouched,
        out_shape=tuple(jax.ShapeDtypeStruct(array.shape, array.dtype) for array in arrays),
        in_specs=[spec] * (count + len(awaited)),
        out_specs=(spec,) * count,
        input_output_aliases={number: number for number in range(count)},
        compiler_params=pltpu.CompilerParams(vmem_limit_bytes=1024 * 1024),
        cost_estimate=pl.CostEstimate(
            flops=int(micros * FLOPS_A_MICRO), bytes_accessed=0, transcendentals=0
        ),
    )(*arrays, *awaited)


def pack_heads(query_ref, key_ref, value_ref, *rest):
    outs, sem = rest[:N_CTX], rest[N_CTX]
    half = query_ref.shape[2] // 2
    place = lax.axis_index("ctx")
    pairs = []
    for apart in (2, 3, 1, 0):
        dest = place ^ apart
        cols = columns((dest & 1) * half, half)
        for slot, ref in enumerate((query_ref, key_ref, value_ref)):
            pairs.append((ref.at[half_of(dest), :, cols], outs[apart].at[slot]))
    run_copies(pairs, sem)


def pack_weights(panel_ref, taps_ref, awaited_ref, out_ref):
    entries = panel_ref.shape[0]
    taps = taps_ref[...].astype(jnp.float32)
    high = jnp.concatenate(
        [taps[TAP_PAD // 2 :], jnp.zeros((TAP_PAD - TAPS, taps.shape[1]), jnp.float32)], axis=0
    )
    out_ref[0, 0:entries] = panel_ref[...]
    joined = jnp.concatenate([taps[: TAP_PAD // 2], high], axis=1)
    out_ref[0, entries:] = joined.astype(jnp.bfloat16)


def pack_near(held_ref, came_ref, out_ref):
    entries = held_ref.shape[1] - TAP_PAD // 2
    for slot in range(2):
        for half, ref in enumerate((held_ref, came_ref)):
            first = (2 * half + slot) * entries
            out_ref[first : first + entries, :] = ref[slot, 0:entries]
    apart = lax.axis_index("ctx") ^ half_of(lax.axis_index("dp"))
    slot = half_of(apart)
    taps = [ref[slot, entries:].astype(jnp.float32) for ref in (held_ref, came_ref)]
    taps = jnp.where((apart & 1) == 1, taps[1], taps[0])
    out_ref[4 * entries :, :] = taps.astype(jnp.bfloat16)


def pack_channels(frame_ref, grad_ref, awaited_ref, *rest):
    across_ref, grad_outs, beside_ref, own_ref, sem = rest[0], rest[1:3], *rest[3:]
    width = frame_ref.shape[2] // N_CTX
    frames = frame_ref.shape[1]
    place = lax.axis_index("ctx")
    pairs = []
    for slot, ref in enumerate((frame_ref, grad_ref)):
        for apart in (2, 3, 1, 0):
            cols = columns((place ^ apart) * width, width)
            for utt in range(2):
                rows = slice(utt * frames, (utt + 1) * frames)
                if apart < 2:
                    target = (own_ref, beside_ref)[apart].at[slot, rows]
                elif slot == 0:
                    target = across_ref.at[apart - 2, rows]
                else:
                    target = grad_outs[apart - 2].at[rows]
                pairs.append((ref.at[utt, :, cols], target))
    run_copies(pairs, sem)


def make_sides(beside_ref, across_ref, out_ref):
    out_ref[0:2] = beside_ref[...]
    out_ref[2] = across_ref[1]


def unpack(*refs):
    ins, refs = refs[:N_CTX], refs[N_CTX:]
    own_ref, beside_ref, output_ref, input_ref = refs[:4]
    taps, heads, channels, taps_ref = refs[4:8], refs[8:11], refs[11:13], refs[13]
    held_ref, picked_ref, sem = refs[14:]
    half, width = ins[0].shape[2], own_ref.shape[3]
    frames = own_ref.shape[2]
    place = lax.axis_index("ctx")
    pairs = []
    for apart in range(N_CTX):
        source = place ^ apart
        cols = columns((source & 1) * half, half)
        for slot, ref in enumerate(heads):
            pairs.append((ins[apart].at[slot], ref.at[half_of(source), :, cols]))
    for slot, ref in enumerate(channels):
        for utt in range(2):
            part = pl.ds(utt * frames, frames)
            blocks = (
                own_ref.at[slot, utt],
                beside_ref.at[slot, part],
                (output_ref, input_ref)[slot].at[0, part],
                beside_ref.at[2 + slot, part],
            )
            for apart, block in enumerate(blocks):
                cols = columns((place ^ apart) * width, width)
                pairs.append((block, ref.at[utt, :, cols]))
    start_copies(pairs, sem)
    for apart in range(N_CTX):
        held_ref[apart] = taps[apart][...]
    mine = held_ref[place ^ half_of(lax.axis_index("dp"))]
    side = mine.shape[1] // 2
    picked_ref[...] = jnp.concatenate([mine[:, :side], mine[:, side:]], axis=0)[:TAPS]
    last = pltpu.make_async_copy(picked_ref, taps_ref, sem.at[len(pairs)])
    last.start()
    wait_copies(pairs, sem)
    last.wait()


def head_parts(refs, slot):
    return jnp.concatenate([ref[slot] for ref in refs], axis=0)


def half_masks(rows):
    lane = lax.broadcasted_iota(jnp.int32, (rows, LANES), 1)
    low = jnp.where(lane < HEAD_DIM, 1.0, 0.0)
    return low.astype(jnp.bfloat16), (1.0 - low).astype(jnp.bfloat16)


def weights_of(length_ref, key_pair, query_pair, mask, frames):
    place = lax.axis_index("ctx")
    rows = key_pair.shape[0]
    frame = lax.broadcasted_iota(jnp.int32, (rows, rows), 0) ^ (place * frames)
    scores = dot_tt(key_pair, query_pair * mask, 1, 1) * HEAD_DIM ** (-0.5)
    scores = jnp.where(frame < length_ref[half_of(place)], scores, masked_score)
    powers = jnp.exp(scores - jnp.max(scores, axis=0, keepdims=True))
    total = jnp.sum(powers, axis=0, keepdims=True)
    return (powers * (1.0 / total)).astype(jnp.bfloat16)


def attend(length_ref, *refs):
    ins, attended_ref = refs[:N_CTX], refs[N_CTX]
    frames, half = ins[0].shape[1], ins[0].shape[2]
    query, key, value = (head_parts(ins, slot) for slot in range(3))
    masks = half_masks(N_CTX * frames)
    for pair in range(half // LANES):
        cols = slice(pair * LANES, (pair + 1) * LANES)
        parts = []
        for side in range(2):
            low = weights_of(length_ref, key[:, cols], query[:, cols], masks[side], frames)
            mixed = dot_tt(value[:, cols], low, 0, 0)
            parts.append(mixed[side * HEAD_DIM : (side + 1) * HEAD_DIM])
        joined = jnp.concatenate(parts, axis=0).T.astype(jnp.bfloat16)
        attended_ref[:, :, cols] = joined.reshape(N_CTX, frames, LANES)


def weigh(length_ref, *refs):
    ins, weight_ref = refs[:N_CTX], refs[N_CTX + 1]
    frames, half = ins[0].shape[1], ins[0].shape[2]
    query, key = (head_parts(ins, slot) for slot in range(2))
    masks = half_masks(N_CTX * frames)
    for pair in range(half // LANES):
        cols = slice(pair * LANES, (pair + 1) * LANES)
        for side in range(2):
            weight_ref[2 * pair + side] = weights_of(
                length_ref, key[:, cols], query[:, cols], masks[side], frames
            )


def forward(length_ref, near_ref, other_ref, *refs):
    attended_refs, refs = refs[:N_CTX], refs[N_CTX:]
    own_ref, beside_ref, across_ref = refs[:3]
    out_refs, refs = refs[3:6], refs[6:]
    whole_ref, rows_ref, taps_ref, total_ref, masked_ref = refs[:5]
    hidden_ref, frame_ref, result_ref = refs[5:]
    frames, half = attended_refs[0].shape[1], attended_refs[0].shape[2]
    width = frame_ref.shape[3]
    rows = N_CTX * frames
    chunks = width // LANES
    entries = 2 * half // N_DP
    own = width // 2
    place = lax.axis_index("ctx")
    for apart in range(N_CTX):
        source = place ^ apart
        cols = columns((source & 1) * half, half)
        for block in range(N_CTX):
            whole_ref[half_of(source), block ^ source, :, cols] = attended_refs[apart][block]
        block = (own_ref, beside_ref, across_ref, beside_ref)[apart][(0, 0, 0, 2)[apart]]
        frame_ref[source] = block.reshape(frame_ref.shape[1:])
    group = lax.axis_index("dp")
    for slot, apart in enumerate((0, 4, 2, 6)):
        for odd, ref in enumerate((near_ref, other_ref)):
            first = pl.multiple_of((group ^ (apart + odd)) * entries, entries)
            rows_ref[pl.ds(first, entries)] = ref[slot * entries : (slot + 1) * entries]
    odd = (group & 1) == 1
    blocks = [ref[4 * entries :].astype(jnp.float32) for ref in (near_ref, other_ref)]
    blocks = (jnp.where(odd, blocks[1], blocks[0]), jnp.where(odd, blocks[0], blocks[1]))
    pieces = [jnp.concatenate([block[:, :own], block[:, own:]], axis=0) for block in blocks]
    taps = jnp.concatenate(pieces, axis=1)
    for chunk in range(chunks):
        for tap in range(TAPS):
            taps_ref[chunk, tap] = jnp.broadcast_to(
                taps[tap : tap + 1, chunk * LANES : (chunk + 1) * LANES], (8, LANES)
            )
    edge = jnp.zeros((2 * chunks, 16, LANES), jnp.float32)
    masked_ref[:, 0:16, :] = edge
    masked_ref[:, 16 + rows : 32 + rows, :] = edge
    for utt in range(2):
        real = lax.broadcasted_iota(jnp.int32, (rows, LANES), 0) < length_ref[utt]
        mixed = whole_ref[utt].reshape(rows, 2 * half)
        projected = dot_tt(mixed, rows_ref[...], 1, 0)
        hidden = frame_ref[:, utt].reshape(rows, width).astype(jnp.float32) + projected
        hidden = hidden.astype(jnp.bfloat16).astype(jnp.float32)
        for chunk in range(chunks):
            piece = hidden[:, chunk * LANES : (chunk + 1) * LANES]
            hidden_ref[utt * chunks + chunk] = piece
            masked_ref[utt * chunks + chunk, 16 : 16 + rows, :] = jnp.where(real, piece, 0.0)

    def convolve(step, carry):
        utt, chunk = step // chunks, step % chunks
        cols = columns(chunk * LANES, LANES)
        shape = (frames // 8, 8, LANES)
        for block in range(N_CTX):
            base = block * frames
            total = jnp.zeros(shape, jnp.float32)
            for tap in range(TAPS):
                first = base + tap + 16 - REACH
                piece = masked_ref[step, first : first + frames, :]
                total += taps_ref[chunk, tap][None] * piece.reshape(shape)
            total = total.reshape(frames, LANES)
            total_ref[step, base : base + frames, :] = total
            outer = hidden_ref[step, base : base + frames, :] + total * jax.nn.sigmoid(total)
            result_ref[block, utt, :, cols] = outer.astype(jnp.bfloat16)
        return carry

    lax.fori_loop(0, 2 * chunks, convolve, 0)
    for apart in range(2):
        out_refs[apart][...] = result_ref[place ^ apart]
        out_refs[2][apart] = result_ref[place ^ (2 + apart)].reshape(2 * frames, width)


def backward(length_ref, total_ref, taps_ref, rows_ref, *refs):
    own_ref, beside_ref = refs[:2]
    own_sides_ref, beside_sides_ref, grad_across_ref, grad_diagonal_ref = refs[2:6]
    refs = refs[6:]
    own_pair_ref, beside_pair_ref, across_ref = refs[:3]
    grad_ref, keep_ref, send_ref, cotangent_ref = refs[3:7]
    side_ref, result_ref = refs[7:]
    own_pair_ref[0], beside_pair_ref[0] = own_ref[...], beside_ref[...]
    utts, frames, width = own_ref.shape
    rows = N_CTX * frames
    chunks = width // LANES
    half = rows_ref.shape[0] // 2
    place = lax.axis_index("ctx")
    blocks = (own_sides_ref[1], beside_sides_ref[1], grad_across_ref[...], grad_diagonal_ref[...])
    for apart in range(N_CTX):
        side_ref[place ^ apart] = blocks[apart].reshape(side_ref.shape[1:])
    edge = jnp.zeros((2 * chunks, 16, LANES), jnp.float32)
    cotangent_ref[:, 0:16, :] = edge
    cotangent_ref[:, 16 + rows : 32 + rows, :] = edge

    def convolve(step, carry):
        utt, chunk = step // chunks, step % chunks
        cols = columns(chunk * LANES, LANES)
        length = length_ref[utt]
        shape = (frames // 8, 8, LANES)
        for block in range(N_CTX):
            base = block * frames
            total = total_ref[step, base : base + frames, :]
            gate = jax.nn.sigmoid(total)
            incoming = side_ref[block, utt, :, cols].astype(jnp.float32)
            slope = gate * (1.0 + total * (1.0 - gate))
            low = (incoming * slope).astype(jnp.bfloat16)
            cotangent_ref[step, 16 + base : 16 + base + frames, :] = low.astype(jnp.float32)
        for block in range(N_CTX):
            base = block * frames
            total = jnp.zeros(shape, jnp.float32)
            for tap in range(TAPS):
                first = base + 16 + REACH - tap
                piece = cotangent_ref[step, first : first + frames, :].reshape(shape)
                total += taps_ref[chunk, tap][None] * piece
            place_of = base + lax.broadcasted_iota(jnp.int32, (frames, LANES), 0)
            total = jnp.where(place_of < length, total.reshape(frames, LANES), 0.0)
            incoming = side_ref[block, utt, :, cols].astype(jnp.float32)
            low = (incoming + total).astype(jnp.bfloat16)
            result_ref[block, utt, :, cols] = low
            grad_ref[utt, base : base + frames, cols] = low
        return carry

    lax.fori_loop(0, 2 * chunks, convolve, 0)
    for apart in range(N_CTX):
        mine = result_ref[place ^ apart]
        if apart < 2:
            (own_pair_ref, beside_pair_ref)[apart][1] = mine
        else:
            across_ref[apart - 2] = mine.reshape(utts * frames, width)
        dest = place ^ apart
        mixed = dot_tt(
            grad_ref[half_of(dest)],
            rows_ref[pl.ds(pl.multiple_of((dest & 1) * half, half), half)],
            1,
            1,
        ).astype(jnp.bfloat16)
        ref = send_ref if apart % 2 else keep_ref
        for block in range(N_CTX):
            first = pl.multiple_of((block ^ dest) * frames, frames)
            ref[apart // 2, pl.ds(first, frames), :] = mixed[block * frames : (block + 1) * frames]


def make_taps(masked_ref, cotangent_ref, awaited_ref, keep_ref, send_ref, tap_sum_ref):
    steps, rows, chunks = masked_ref.shape[0], masked_ref.shape[1] - 32, tap_sum_ref.shape[0]
    block = 64
    shape = (block // 8, 8, LANES)
    tap_sum_ref[...] = jnp.zeros_like(tap_sum_ref)

    def correlate(step, carry):
        chunk = step % chunks
        for base in range(0, rows, block):
            held = masked_ref[step, 16 + base : 16 + base + block, :].reshape(shape)
            for tap in range(TAPS):
                first = base + 16 + REACH - tap
                piece = cotangent_ref[step, first : first + block, :].reshape(shape)
                tap_sum_ref[chunk, tap] += jnp.sum(held * piece, axis=0)
        return carry

    lax.fori_loop(0, steps, correlate, 0)
    sums = [
        jnp.concatenate(
            [
                jnp.sum(tap_sum_ref[chunk, tap], axis=0, keepdims=True)
                for tap in range(TAP_PAD)
            ],
            axis=0,
        )
        for chunk in range(chunks)
    ]
    sums = jnp.concatenate(sums, axis=1)
    own = sums.shape[1] // 2
    halves = [
        jnp.concatenate([part[: TAP_PAD // 2], part[TAP_PAD // 2 :]], axis=1)
        for part in (sums[:, :own], sums[:, own:])
    ]
    odd = (lax.axis_index("dp") & 1) == 1
    keep_ref[...] = jnp.where(odd, halves[1], halves[0])
    send_ref[...] = jnp.where(odd, halves[0], halves[1])


def make_panels(whole_ref, grad_ref, panel_ref):
    rows, half = grad_ref.shape[1], whole_ref.shape[3] // 2
    entries = 2 * half // N_DP
    group = lax.axis_index("dp")
    for side in range(2):
        panel = 0.0
        for utt in range(2):
            mixed = whole_ref[utt, :, :, side * half : (side + 1) * half].reshape(rows, half)
            panel += dot_tt(mixed, grad_ref[utt], 0, 0)
        panel = panel.astype(jnp.bfloat16)
        for part in range(N_DP // 2):
            panel_ref[slot_of(side * N_DP // 2 + part, group)] = panel[
                part * entries : (part + 1) * entries
            ]


def join(panel_ref, came_ref, tap_ref, tap_came_ref, awaited_ref, keep_ref, send_ref):
    entries = panel_ref.shape[1]
    group, place = lax.axis_index("dp"), lax.axis_index("ctx")
    taps = (tap_ref[...] + tap_came_ref[...]).astype(jnp.bfloat16)
    none = jnp.zeros_like(taps)
    for slot in range(N_DP // 2):
        ref = (keep_ref, send_ref)[slot // 2]
        total = panel_ref[slot].astype(jnp.float32) + came_ref[slot].astype(jnp.float32)
        ref[slot % 2, 0:entries] = total.astype(jnp.bfloat16)
        ref[slot % 2, entries:] = none
    mine = slot_of(2 * place, group & 6)
    for slot in range(N_DP // 2):
        ref = (keep_ref, send_ref)[slot // 2]

        @pl.when(mine == slot)
        def _(ref=ref, slot=slot):
            ref[slot % 2, entries:] = taps


def mark(*refs):
    refs[-1][...] = jnp.zeros_like(refs[-1])


def finish(kept_ref, came_ref, awaited_ref, taps_ref):
    first = kept_ref.shape[1] - TAP_PAD // 2
    taps_ref[...] = kept_ref[0, first:].astype(jnp.float32) + came_ref[...].astype(jnp.float32)


def relay(keep_ref, came_ref, out_ref):
    total = keep_ref[1].astype(jnp.float32) + came_ref[1].astype(jnp.float32)
    out_ref[...] = total.astype(jnp.bfloat16)


def make_pair(pair_ref, output_ref, input_ref, *refs):
    out_ref = refs[-1]
    for slot in range(2):
        out_ref[slot] = pair_ref[slot].reshape(out_ref.shape[1:])
    out_ref[2] = output_ref[1]
    out_ref[3] = input_ref[1]


def attend_back(weight_ref, keep_ref, came_ref, far_ref, *refs):
    ins, out_refs = refs[:N_CTX], refs[N_CTX + 1 :]
    frames, half = ins[0].shape[1], ins[0].shape[2]
    rows = N_CTX * frames
    query, key, value = (head_parts(ins, slot) for slot in range(3))
    masks = half_masks(rows)
    scale = HEAD_DIM ** (-0.5)
    arriving = keep_ref[0].astype(jnp.float32) + came_ref[0].astype(jnp.float32)
    arriving = (arriving + far_ref[...].astype(jnp.float32)).astype(jnp.bfloat16)
    low_lanes = lax.broadcasted_iota(jnp.int32, (rows, LANES), 1) < HEAD_DIM
    for pair in range(half // LANES):
        cols = slice(pair * LANES, (pair + 1) * LANES)
        key_pair, value_pair = key[:, cols], value[:, cols]
        query_pair, grad_pair = query[:, cols], arriving[:, cols]
        query_parts, key_parts, value_parts = [], [], []
        for side in range(2):
            low = weight_ref[2 * pair + side]
            weights = low.astype(jnp.float32)
            moved = weights * dot_tt(value_pair, grad_pair * masks[side], 1, 1)
            delta = jnp.sum(moved, axis=0, keepdims=True)
            grad_scores = (moved - weights * delta).astype(jnp.bfloat16)
            value_parts.append(dot_tt(low, grad_pair, 1, 0))
            key_parts.append(dot_tt(grad_scores, query_pair, 1, 0))
            mixed = dot_tt(key_pair, grad_scores, 0, 0)
            query_parts.append(mixed[side * HEAD_DIM : (side + 1) * HEAD_DIM])
        query_sum = (jnp.concatenate(query_parts, axis=0).T * scale).astype(jnp.bfloat16)
        key_sum = (jnp.where(low_lanes, key_parts[0], key_parts[1]) * scale).astype(jnp.bfloat16)
        value_sum = jnp.where(low_lanes, value_parts[0], value_parts[1]).astype(jnp.bfloat16)
        for slot, total in enumerate((query_sum, key_sum, value_sum)):
            for apart in range(N_CTX):
                out_refs[apart][slot, :, cols] = total[apart * frames : (apart + 1) * frames]


def swapped(array, bit):
    return lax.ppermute(array, "dp", [(i, i ^ bit) for i in range(N_DP)])


def dealt(slots):
    return lax.all_to_all(slots, "dp", 0, 0, tiled=True)


def crossed(array, apart):
    return lax.ppermute(array, "ctx", [(i, i ^ apart) for i in range(N_CTX)])


def traded(blocks):
    came = {apart: crossed(blocks[apart], apart) for apart in (2, 3, 1)}
    return [blocks[0]] + [came[apart] for apart in (1, 2, 3)]


def per_device(
    frame_input, queries, key_proj, value_proj, out_weight, conv_weight, lengths, grad_output
):
    utts, frames, wide = frame_input.shape
    inner = queries.shape[2]
    half, width = inner // 2, wide // N_CTX
    rows = N_CTX * frames
    chunks = width // LANES
    low, f32 = jnp.bfloat16, jnp.float32
    shape = jax.ShapeDtypeStruct
    entries = out_weight.shape[1]
    tap_count = conv_weight.shape[0]
    dma = pltpu.SemaphoreType.DMA
    head_block = shape((3, frames, half), low)
    channel_block = shape((utts, frames, width), low)

    blocks = call_kernel(
        pack_heads,
        (head_block,) * N_CTX,
        ["hbm"] * 3,
        scratch=[dma((3 * N_CTX,))],
        room=63,
    )(queries, key_proj, value_proj)
    packed = traded(blocks)
    (shard,) = call_kernel(
        pack_weights,
        (shape((1, entries + TAP_PAD // 2, width), low),),
        ["vmem"] * 2 + ["any"],
    )(out_weight.T, conv_weight, packed[1])
    shard = jnp.concatenate([shard, swapped(shard, 4)], axis=0)
    (shard,) = call_kernel(
        pack_near, (shape((4 * entries + TAP_PAD // 2, width), low),), ["vmem"] * 2
    )(shard, swapped(shard, 2))
    other_shard = swapped(shard, 1)
    pair_block = shape((2, utts, frames, width), low)
    side_block = shape((utts * frames, width), low)
    double_block = shape((2, utts * frames, width), low)
    frame_across, grad_across, grad_diagonal, beside_sides, own_sides = call_kernel(
        pack_channels,
        (double_block,) + (side_block,) * 2 + (double_block,) * 2,
        ["hbm"] * 2 + ["any"],
        scratch=[dma((4 * N_CTX,))],
    )(frame_input, grad_output, packed[2])
    frame_across = crossed(frame_across, 2)
    (beside_sides,) = call_kernel(
        make_sides, (shape((3, utts * frames, width), low),), ["vmem"] * 2
    )(beside_sides, frame_across)
    beside_sides = crossed(beside_sides, 1)
    (attended,) = call_kernel(
        attend,
        (shape((N_CTX, frames, half), low),),
        ["smem"] + ["vmem"] * N_CTX,
    )(lengths, *packed)
    (attended,) = gate([attended], frame_across)
    across = crossed(attended, 2)
    beside = crossed(attended, 1)
    diagonal = crossed(across, 1)
    grad_across, grad_diagonal = crossed(grad_across, 2), crossed(grad_diagonal, 3)
    forward_out = call_kernel(
        forward,
        (channel_block,) * 2
        + (
            shape((2, utts * frames, width), low),
            shape((utts, N_CTX, frames, inner), low),
            shape((inner, width), low),
            shape((chunks, TAP_PAD, 8, LANES), f32),
            shape((utts * chunks, rows, LANES), f32),
            shape((utts * chunks, rows + 32, LANES), f32),
        ),
        ["smem"] + ["vmem"] * (5 + N_CTX),
        scratch=[
            pltpu.VMEM((utts * chunks, rows, LANES), f32),
            pltpu.VMEM((N_CTX, utts, frames, width), low),
            pltpu.VMEM((N_CTX, utts, frames, width), low),
        ],
        micros=3.2,
    )(
        lengths,
        shard,
        other_shard,
        attended,
        beside,
        across,
        diagonal,
        own_sides,
        beside_sides,
        frame_across,
    )
    output_across = crossed(forward_out[2], 2)
    whole, weight_rows, taps, totals, masked = forward_out[3:]
    grad_blocks = gate([grad_across, grad_diagonal], totals, micros=10.0)
    grad_blocks = (own_sides, beside_sides, *grad_blocks)
    backward_out = call_kernel(
        backward,
        (pair_block,) * 2
        + (
            shape((2, utts * frames, width), low),
            shape((utts, rows, width), low),
            shape((2, rows, half), low),
            shape((2, rows, half), low),
            shape((utts * chunks, rows + 32, LANES), f32),
        ),
        ["smem"] + ["vmem"] * (5 + N_CTX),
        scratch=[
            pltpu.VMEM((N_CTX, utts, frames, width), low),
            pltpu.VMEM((N_CTX, utts, frames, width), low),
        ],
        micros=5.2,
    )(lengths, totals, taps, weight_rows, *forward_out[:2], *grad_blocks)
    grad_hidden, keep, send, cotangents = backward_out[3:]
    (send,) = gate([send], output_across)
    came = crossed(send, 1)
    (relayed,) = call_kernel(
        relay, (shape((rows, half), low),), ["vmem"] * 2, micros=0.2
    )(keep, came)
    (input_across,) = gate([backward_out[2]], relayed)
    (panels,) = call_kernel(
        make_panels,
        (shape((N_DP, entries, width), low),),
        ["vmem"] * 2,
        micros=0.7,
    )(whole, grad_hidden)
    panels_came = swapped(panels[4:], 1)
    tap_block = shape((TAP_PAD // 2, width), f32)
    tap_keep, tap_send = call_kernel(
        make_taps,
        (tap_block,) * 2,
        ["vmem"] * 2 + ["any"],
        scratch=[pltpu.VMEM((chunks, TAP_PAD, 8, LANES), f32)],
    )(masked, cotangents, relayed)
    taps_came = swapped(tap_send, 1)
    far, input_across = crossed(relayed, 2), crossed(input_across, 2)
    (weights,) = call_kernel(
        weigh,
        (shape((half // HEAD_DIM, rows, rows), low),),
        ["smem"] + ["vmem"] * N_CTX + ["any"],
    )(lengths, *packed, relayed)
    back_blocks = call_kernel(
        attend_back,
        (head_block,) * N_CTX,
        ["vmem"] * (4 + N_CTX) + ["any"],
        micros=2.2,
    )(weights, keep, came, far, *packed, tap_keep)
    (across_block,) = gate([back_blocks[2]], input_across)
    grad_blocks = traded([*back_blocks[:2], across_block, back_blocks[3]])
    own_pair = backward_out[0]
    (beside_pair,) = call_kernel(
        make_pair,
        (shape((4, utts * frames, width), low),),
        ["vmem"] * 3 + ["any"],
        micros=0.2,
    )(backward_out[1], output_across, input_across, grad_blocks[1])
    beside_pair = crossed(beside_pair, 1)

    kept, sent = call_kernel(
        join,
        (shape((2, entries + TAP_PAD // 2, width), low),) * 2,
        ["vmem"] * 4 + ["any"],
    )(panels[:4], panels_came, tap_keep, taps_came, back_blocks[0])
    panels = (kept.astype(f32) + swapped(sent, 2).astype(f32)).astype(low)
    taps_last = swapped(panels[1, entries:], 4)
    panels_last = swapped(panels[1, :entries], 4)
    (arrived,) = call_kernel(mark, (shape((8, LANES), f32),), ["any"] * 3)(
        *grad_blocks[2:], taps_last
    )
    (tap_sums,) = call_kernel(
        finish, (shape((TAP_PAD // 2, width), f32),), ["vmem"] * 2 + ["any"]
    )(panels, taps_last, arrived)
    grad_out_weight = (panels[0, :entries].astype(f32) + panels_last.astype(f32)).T
    tap_blocks = traded([tap_sums] * N_CTX)
    grad_queries, grad_keys, grad_values, block_output, grad_input, grad_taps = call_kernel(
        unpack,
        (shape((utts, frames, inner), low),) * 3
        + (shape((utts, frames, wide), low),) * 2
        + (shape(conv_weight.shape, f32),),
        ["any"] * (N_CTX + 4) + ["vmem"] * N_CTX,
        ["hbm"] * 6,
        [
            pltpu.VMEM((N_CTX, TAP_PAD // 2, width), f32),
            pltpu.VMEM(conv_weight.shape, f32),
            dma((7 * N_CTX + 1,)),
        ],
        micros=1.0,
    )(
        *grad_blocks,
        own_pair,
        beside_pair,
        output_across,
        input_across,
        *tap_blocks,
    )
    return (
        block_output,
        grad_input,
        grad_queries,
        grad_keys,
        grad_values,
        grad_out_weight,
        grad_taps,
    )


def chosen(sizes, *arrays):
    frame_input, queries, out_weight, conv_weight = (arrays[i] for i in (0, 1, 4, 5))
    utts, frames, wide = frame_input.shape
    inner = queries.shape[2]
    fits = (
        sizes == (N_DP, N_CTX)
        and utts == 2
        and frames == 64
        and wide % (N_CTX * LANES) == 0
        and inner % (2 * LANES) == 0
        and inner // N_DP % 16 == 0
        and inner // 2 == wide // N_CTX
        and conv_weight.shape == (TAPS, wide // N_DP)
        and out_weight.shape == (wide // N_CTX, inner // N_DP)
    )
    return (per_device if fits else general_device)(*arrays)


def solution(mesh):
    placed = (
        P("dp", "ctx", None),
        P("dp", "ctx", None),
        P("dp", "ctx", None),
        P("dp", "ctx", None),
        P("ctx", "dp"),
        P(None, "dp"),
        P("dp"),
        P("dp", "ctx", None),
    )
    sizes = (mesh.shape["dp"], mesh.shape["ctx"])
    return jax.shard_map(
        functools.partial(chosen, sizes),
        mesh=mesh,
        in_specs=placed,
        out_specs=(
            P("dp", "ctx", None),
            P("dp", "ctx", None),
            P("dp", "ctx", None),
            P("dp", "ctx", None),
            P("dp", "ctx", None),
            P("ctx", "dp"),
            P(None, "dp"),
        ),
        check_vma=False,
    )
```

```python
import functools

import jax
import jax.numpy as jnp
from jax import lax
from jax.experimental import pallas as pl
from jax.experimental.pallas import tpu as pltpu
from jax.sharding import PartitionSpec as P

HEAD_DIM = 64


masked_score = -1e30


def padded_2(array, sides, width):
    for axis, dim in sides:
        size, length = (lax.axis_size(axis), array.shape[dim])
        up = [(i, (i + 1) % size) for i in range(size - 1)]
        down = [(j, i) for i, j in up]
        last = lax.slice_in_dim(array, length - width, length, axis=dim)
        leading = lax.slice_in_dim(array, 0, width, axis=dim)
        before = lax.ppermute(last, axis, up)
        after = lax.ppermute(leading, axis, down)
        array = jnp.concatenate([before, array, after], axis=dim)
    return array


def depthwise(lhs, rhs):
    return lax.conv_general_dilated(
        lhs,
        rhs,
        (1,),
        "VALID",
        dimension_numbers=("NWC", "WIO", "NWC"),
        feature_group_count=lhs.shape[2],
        precision=lax.Precision.HIGHEST,
    )


def general_device(
    frame_input, queries, key_proj, value_proj, out_weight, conv_weight, lengths, grad_output
):
    utt_count = frame_input.shape[0]
    frame_count = frame_input.shape[1]
    inner_width = queries.shape[2]
    head_count = inner_width // HEAD_DIM
    group_heads = max((g for g in range(1, 7) if head_count % g == 0))
    group_count = head_count // group_heads
    group_width = group_heads * HEAD_DIM
    tap_count = conv_weight.shape[0]
    half_span = (tap_count - 1) // 2
    score_scale = HEAD_DIM ** (-0.5)
    total_frames = frame_count * lax.axis_size("ctx")
    offset = lax.axis_index("ctx") * frame_count
    own_valid = (offset + jnp.arange(frame_count, dtype=jnp.int32))[None, :] < lengths[:, None]
    all_valid = jnp.arange(total_frames, dtype=jnp.int32)[None, :] < lengths[:, None]

    def grouped(values):
        row_count = values.shape[1]
        return values.reshape(utt_count, row_count, group_count, group_width).transpose(2, 0, 1, 3)

    def ungrouped(values):
        row_count = values.shape[2]
        return values.transpose(1, 2, 0, 3).reshape(utt_count, row_count, group_count * group_width)

    def split_heads(values):
        return values.reshape(utt_count, values.shape[1], group_heads, HEAD_DIM)

    def stats_grouped(values):
        row_count = values.shape[1]
        return values.reshape(utt_count, row_count, group_count, group_heads).transpose(2, 0, 3, 1)

    def masked_scores(query_block, key_block, key_mask):
        scores = (
            jnp.einsum(
                "uqgd,ukgd->ugqk", query_block, key_block, preferred_element_type=jnp.float32
            )
            * score_scale
        )
        return jnp.where(key_mask[:, None, None, :], scores, masked_score)

    taps = lax.all_gather(conv_weight, "dp", axis=1, tiled=True).astype(jnp.float32)
    panel_rows = lax.all_gather(out_weight, "dp", axis=1, tiled=True)
    weight_full = lax.all_gather(panel_rows, "ctx", axis=0, tiled=True)
    all_keys, all_values = (
        lax.all_gather(key_proj, "ctx", axis=1, tiled=True),
        lax.all_gather(value_proj, "ctx", axis=1, tiled=True),
    )
    query_groups = grouped(queries)
    key_groups = grouped(all_keys)
    value_groups = grouped(all_values)

    def forward_group(unused, items):
        query_group, key_group, value_group = items
        query_block = split_heads(query_group)
        scores = masked_scores(query_block, split_heads(key_group), all_valid)
        largest = jnp.max(scores, axis=-1)
        log_group = largest + jnp.log(jnp.sum(jnp.exp(scores - largest[..., None]), axis=-1))
        weights_low = jnp.exp(scores - log_group[..., None]).astype(jnp.bfloat16)
        attended_group = jnp.einsum(
            "ugqk,ukgd->uqgd",
            weights_low,
            split_heads(value_group),
            preferred_element_type=jnp.float32,
        )
        return (None, (log_group, attended_group.reshape(utt_count, frame_count, group_width)))

    _, (log_groups, attended_groups) = lax.scan(
        forward_group, None, (query_groups, key_groups, value_groups)
    )
    attended = ungrouped(attended_groups).astype(jnp.bfloat16)
    log_total = log_groups.transpose(1, 3, 0, 2).reshape(utt_count, frame_count, head_count)
    projected = jnp.einsum("ufe,de->ufd", attended, weight_full, preferred_element_type=jnp.float32)
    hidden = (frame_input.astype(jnp.float32) + projected).astype(jnp.bfloat16)
    masked_hidden = jnp.where(own_valid[:, :, None], hidden, jnp.zeros_like(hidden))
    padded = padded_2(masked_hidden, (("ctx", 1),), half_span).astype(jnp.float32)
    conv_sum = depthwise(padded, taps[:, None, :])
    sigmoid = jax.nn.sigmoid(conv_sum)
    block_output = (hidden.astype(jnp.float32) + conv_sum * sigmoid).astype(jnp.bfloat16)
    grad_local = grad_output.astype(jnp.float32)
    swish_slope = sigmoid * (1.0 + conv_sum * (1.0 - sigmoid))
    grad_conv = (grad_local * swish_slope).astype(jnp.bfloat16)
    grad_padded = padded_2(grad_conv, (("ctx", 1),), half_span).astype(jnp.float32)
    back_sum = depthwise(grad_padded, taps[::-1][:, None, :])
    grad_hidden = (grad_local + jnp.where(own_valid[:, :, None], back_sum, 0.0)).astype(
        jnp.bfloat16
    )
    grad_conv_wide = grad_conv.astype(jnp.float32)
    kernel_term = jnp.zeros((tap_count, conv_sum.shape[2]), jnp.float32)
    for utt_index in range(utt_count):
        kernel_term = (
            kernel_term
            + depthwise(padded[utt_index : utt_index + 1], grad_conv_wide[utt_index][:, None, :])[0]
        )
    kernel_whole = lax.psum(kernel_term.astype(jnp.bfloat16), "ctx")
    grad_conv_weight = lax.psum_scatter(kernel_whole, "dp", scatter_dimension=1, tiled=True).astype(
        jnp.float32
    )
    grad_attended = jnp.einsum(
        "ufd,de->ufe", grad_hidden, weight_full, preferred_element_type=jnp.float32
    ).astype(jnp.bfloat16)
    row_delta = jnp.sum(
        grad_attended.astype(jnp.float32).reshape(utt_count, frame_count, head_count, HEAD_DIM)
        * attended.astype(jnp.float32).reshape(utt_count, frame_count, head_count, HEAD_DIM),
        axis=-1,
    )
    grad_groups = grouped(grad_attended)

    def query_group_step(unused, items):
        query_group, key_group, value_group, grad_group, log_group, delta_group = items
        key_block = split_heads(key_group)
        weights = jnp.exp(
            masked_scores(split_heads(query_group), key_block, all_valid) - log_group[..., None]
        )
        grad_weights = jnp.einsum(
            "uqgd,ukgd->ugqk",
            split_heads(grad_group),
            split_heads(value_group),
            preferred_element_type=jnp.float32,
        )
        grad_scores = (weights * (grad_weights - delta_group[..., None])).astype(jnp.bfloat16)
        query_sum = jnp.einsum(
            "ugqk,ukgd->uqgd", grad_scores, key_block, preferred_element_type=jnp.float32
        )
        return (None, query_sum.reshape(utt_count, frame_count, group_width))

    _, query_sums = lax.scan(
        query_group_step,
        None,
        (
            query_groups,
            key_groups,
            value_groups,
            grad_groups,
            stats_grouped(log_total),
            stats_grouped(row_delta),
        ),
    )
    grad_queries = (ungrouped(query_sums) * score_scale).astype(jnp.bfloat16)
    total_log, total_delta = (
        lax.all_gather(log_total, "ctx", axis=1, tiled=True),
        lax.all_gather(row_delta, "ctx", axis=1, tiled=True),
    )
    own_key_groups = grouped(key_proj)
    own_value_groups = grouped(value_proj)
    group_zeros = jnp.zeros((group_count, utt_count, frame_count, group_width), jnp.float32)
    start_sums = (group_zeros, group_zeros)
    query_all, grad_all = (
        lax.all_gather(queries, "ctx", axis=1, tiled=True),
        lax.all_gather(grad_attended, "ctx", axis=1, tiled=True),
    )
    log_piece = stats_grouped(total_log)
    delta_piece = stats_grouped(total_delta)

    def key_group_step(unused, items):
        (
            query_group,
            grad_group,
            log_group,
            delta_group,
            key_group,
            value_group,
            key_sum,
            value_sum,
        ) = items
        query_block = split_heads(query_group)
        grad_block = split_heads(grad_group)
        weights = jnp.exp(
            masked_scores(query_block, split_heads(key_group), own_valid) - log_group[..., None]
        )
        grad_weights = jnp.einsum(
            "uqgd,ukgd->ugqk",
            grad_block,
            split_heads(value_group),
            preferred_element_type=jnp.float32,
        )
        grad_scores = (weights * (grad_weights - delta_group[..., None])).astype(jnp.bfloat16)
        key_next = key_sum + jnp.einsum(
            "ugqk,uqgd->ukgd", grad_scores, query_block, preferred_element_type=jnp.float32
        ).reshape(utt_count, frame_count, group_width)
        value_next = value_sum + jnp.einsum(
            "ugqk,uqgd->ukgd",
            weights.astype(jnp.bfloat16),
            grad_block,
            preferred_element_type=jnp.float32,
        ).reshape(utt_count, frame_count, group_width)
        return (None, (key_next, value_next))

    _, result_sums = lax.scan(
        key_group_step,
        None,
        (
            grouped(query_all),
            grouped(grad_all),
            log_piece,
            delta_piece,
            own_key_groups,
            own_value_groups,
            start_sums[0],
            start_sums[1],
        ),
    )
    key_sum, value_sum = result_sums
    grad_keys = (ungrouped(key_sum) * score_scale).astype(jnp.bfloat16)
    grad_values = ungrouped(value_sum).astype(jnp.bfloat16)
    hidden_cols = lax.slice_in_dim(
        grad_hidden, 0, weight_full.shape[0] // lax.axis_size("ctx") * lax.axis_size("ctx"), axis=2
    )
    panel_share = lax.psum_scatter(
        jnp.einsum("ufd,ufe->de", hidden_cols, attended, preferred_element_type=jnp.float32).astype(
            jnp.bfloat16
        ),
        "ctx",
        scatter_dimension=0,
        tiled=True,
    )
    grad_out_weight = lax.psum_scatter(panel_share, "dp", scatter_dimension=1, tiled=True).astype(
        jnp.float32
    )
    return (
        block_output,
        grad_hidden,
        grad_queries,
        grad_keys,
        grad_values,
        grad_out_weight,
        grad_conv_weight,
    )


LANES = 128
N_CTX = 4
N_DP = 8
TAP_PAD = 32
FLOPS_A_MICRO = 1.15e9
TAPS = 31
REACH = 15


def slot_of(index, me):
    apart = index ^ me
    return ((apart & 1) << 2) | (apart & 2) | ((apart >> 2) & 1)


def dot_tt(lhs, rhs, lhs_dim, rhs_dim):
    return lax.dot_general(
        lhs, rhs, (((lhs_dim,), (rhs_dim,)), ((), ())), preferred_element_type=jnp.float32
    )


def call_kernel(body, out_shape, ins, outs=None, scratch=(), room=40, micros=1.0):
    spaces = {
        "smem": pl.BlockSpec(memory_space=pltpu.SMEM),
        "vmem": pl.BlockSpec(memory_space=pltpu.VMEM),
        "hbm": pl.BlockSpec(memory_space=pltpu.HBM),
        "any": pl.BlockSpec(memory_space=pl.ANY),
    }
    return pl.pallas_call(
        body,
        out_shape=out_shape,
        in_specs=[spaces[space] for space in ins],
        out_specs=[spaces[space] for space in (outs or ["vmem"] * len(out_shape))],
        scratch_shapes=list(scratch),
        compiler_params=pltpu.CompilerParams(vmem_limit_bytes=room * 1024 * 1024),
        cost_estimate=pl.CostEstimate(
            flops=int(micros * FLOPS_A_MICRO), bytes_accessed=0, transcendentals=0
        ),
    )


def half_of(index):
    return lax.shift_right_logical(index, 1)


def columns(start, size):
    return pl.ds(pl.multiple_of(start, LANES), size)


def start_copies(pairs, sem):
    for number, (source, target) in enumerate(pairs):
        pltpu.make_async_copy(source, target, sem.at[number]).start()


def wait_copies(pairs, sem):
    for number, (source, target) in enumerate(pairs):
        pltpu.make_async_copy(source, target, sem.at[number]).wait()


def run_copies(pairs, sem):
    start_copies(pairs, sem)
    wait_copies(pairs, sem)


def untouched(*refs):
    pass


def gate(arrays, *awaited, micros=0.0):
    count = len(arrays)
    spec = pl.BlockSpec(memory_space=pl.ANY)
    return pl.pallas_call(
        untouched,
        out_shape=tuple(jax.ShapeDtypeStruct(array.shape, array.dtype) for array in arrays),
        in_specs=[spec] * (count + len(awaited)),
        out_specs=(spec,) * count,
        input_output_aliases={number: number for number in range(count)},
        compiler_params=pltpu.CompilerParams(vmem_limit_bytes=1024 * 1024),
        cost_estimate=pl.CostEstimate(
            flops=int(micros * FLOPS_A_MICRO), bytes_accessed=0, transcendentals=0
        ),
    )(*arrays, *awaited)


def pack_heads(query_ref, key_ref, value_ref, *rest):
    outs, sem = rest[:N_CTX], rest[N_CTX]
    half = query_ref.shape[2] // 2
    place = lax.axis_index("ctx")
    pairs = []
    for apart in (2, 3, 1, 0):
        dest = place ^ apart
        cols = columns((dest & 1) * half, half)
        for slot, ref in enumerate((query_ref, key_ref, value_ref)):
            pairs.append((ref.at[half_of(dest), :, cols], outs[apart].at[slot]))
    run_copies(pairs, sem)


def pack_weights(panel_ref, taps_ref, awaited_ref, out_ref):
    entries = panel_ref.shape[0]
    taps = taps_ref[...].astype(jnp.float32)
    high = jnp.concatenate(
        [taps[TAP_PAD // 2 :], jnp.zeros((TAP_PAD - TAPS, taps.shape[1]), jnp.float32)], axis=0
    )
    out_ref[0, 0:entries] = panel_ref[...]
    joined = jnp.concatenate([taps[: TAP_PAD // 2], high], axis=1)
    out_ref[0, entries:] = joined.astype(jnp.bfloat16)


def pack_near(held_ref, came_ref, out_ref):
    entries = held_ref.shape[1] - TAP_PAD // 2
    for slot in range(2):
        for half, ref in enumerate((held_ref, came_ref)):
            first = (2 * half + slot) * entries
            out_ref[first : first + entries, :] = ref[slot, 0:entries]
    apart = lax.axis_index("ctx") ^ half_of(lax.axis_index("dp"))
    slot = half_of(apart)
    taps = [ref[slot, entries:].astype(jnp.float32) for ref in (held_ref, came_ref)]
    taps = jnp.where((apart & 1) == 1, taps[1], taps[0])
    out_ref[4 * entries :, :] = taps.astype(jnp.bfloat16)


def pack_channels(frame_ref, grad_ref, awaited_ref, *rest):
    across_ref, grad_outs, beside_ref, own_ref, sem = rest[0], rest[1:3], *rest[3:]
    width = frame_ref.shape[2] // N_CTX
    frames = frame_ref.shape[1]
    place = lax.axis_index("ctx")
    pairs = []
    for slot, ref in enumerate((frame_ref, grad_ref)):
        for apart in (2, 3, 1, 0):
            cols = columns((place ^ apart) * width, width)
            for utt in range(2):
                rows = slice(utt * frames, (utt + 1) * frames)
                if apart < 2:
                    target = (own_ref, beside_ref)[apart].at[slot, rows]
                elif slot == 0:
                    target = across_ref.at[apart - 2, rows]
                else:
                    target = grad_outs[apart - 2].at[rows]
                pairs.append((ref.at[utt, :, cols], target))
    run_copies(pairs, sem)


def make_sides(beside_ref, across_ref, out_ref):
    out_ref[0:2] = beside_ref[...]
    out_ref[2] = across_ref[1]


def unpack(*refs):
    ins, refs = refs[:N_CTX], refs[N_CTX:]
    own_ref, beside_ref, output_ref, input_ref = refs[:4]
    taps, heads, channels, taps_ref = refs[4:8], refs[8:11], refs[11:13], refs[13]
    held_ref, picked_ref, sem = refs[14:]
    half, width = ins[0].shape[2], own_ref.shape[3]
    frames = own_ref.shape[2]
    place = lax.axis_index("ctx")
    pairs = []
    for apart in range(N_CTX):
        source = place ^ apart
        cols = columns((source & 1) * half, half)
        for slot, ref in enumerate(heads):
            pairs.append((ins[apart].at[slot], ref.at[half_of(source), :, cols]))
    for slot, ref in enumerate(channels):
        for utt in range(2):
            part = pl.ds(utt * frames, frames)
            blocks = (
                own_ref.at[slot, utt],
                beside_ref.at[slot, part],
                (output_ref, input_ref)[slot].at[0, part],
                beside_ref.at[2 + slot, part],
            )
            for apart, block in enumerate(blocks):
                cols = columns((place ^ apart) * width, width)
                pairs.append((block, ref.at[utt, :, cols]))
    start_copies(pairs, sem)
    for apart in range(N_CTX):
        held_ref[apart] = taps[apart][...]
    mine = held_ref[place ^ half_of(lax.axis_index("dp"))]
    side = mine.shape[1] // 2
    picked_ref[...] = jnp.concatenate([mine[:, :side], mine[:, side:]], axis=0)[:TAPS]
    last = pltpu.make_async_copy(picked_ref, taps_ref, sem.at[len(pairs)])
    last.start()
    wait_copies(pairs, sem)
    last.wait()


def head_parts(refs, slot):
    return jnp.concatenate([ref[slot] for ref in refs], axis=0)


def half_masks(rows):
    lane = lax.broadcasted_iota(jnp.int32, (rows, LANES), 1)
    low = jnp.where(lane < HEAD_DIM, 1.0, 0.0)
    return low.astype(jnp.bfloat16), (1.0 - low).astype(jnp.bfloat16)


def weights_of(length_ref, key_pair, query_pair, mask, frames):
    place = lax.axis_index("ctx")
    rows = key_pair.shape[0]
    frame = lax.broadcasted_iota(jnp.int32, (rows, rows), 0) ^ (place * frames)
    scores = dot_tt(key_pair, query_pair * mask, 1, 1) * HEAD_DIM ** (-0.5)
    scores = jnp.where(frame < length_ref[half_of(place)], scores, masked_score)
    powers = jnp.exp(scores - jnp.max(scores, axis=0, keepdims=True))
    total = jnp.sum(powers, axis=0, keepdims=True)
    return (powers * (1.0 / total)).astype(jnp.bfloat16)


def attend(length_ref, *refs):
    ins, attended_ref = refs[:N_CTX], refs[N_CTX]
    frames, half = ins[0].shape[1], ins[0].shape[2]
    query, key, value = (head_parts(ins, slot) for slot in range(3))
    masks = half_masks(N_CTX * frames)
    for pair in range(half // LANES):
        cols = slice(pair * LANES, (pair + 1) * LANES)
        parts = []
        for side in range(2):
            low = weights_of(length_ref, key[:, cols], query[:, cols], masks[side], frames)
            mixed = dot_tt(value[:, cols], low, 0, 0)
            parts.append(mixed[side * HEAD_DIM : (side + 1) * HEAD_DIM])
        joined = jnp.concatenate(parts, axis=0).T.astype(jnp.bfloat16)
        attended_ref[:, :, cols] = joined.reshape(N_CTX, frames, LANES)


def weigh(length_ref, *refs):
    ins, weight_ref = refs[:N_CTX], refs[N_CTX + 1]
    frames, half = ins[0].shape[1], ins[0].shape[2]
    query, key = (head_parts(ins, slot) for slot in range(2))
    masks = half_masks(N_CTX * frames)
    for pair in range(half // LANES):
        cols = slice(pair * LANES, (pair + 1) * LANES)
        for side in range(2):
            weight_ref[2 * pair + side] = weights_of(
                length_ref, key[:, cols], query[:, cols], masks[side], frames
            )


def forward(length_ref, near_ref, other_ref, *refs):
    attended_refs, refs = refs[:N_CTX], refs[N_CTX:]
    own_ref, beside_ref, across_ref = refs[:3]
    out_refs, refs = refs[3:6], refs[6:]
    whole_ref, rows_ref, taps_ref, total_ref, masked_ref = refs[:5]
    hidden_ref, frame_ref, result_ref = refs[5:]
    frames, half = attended_refs[0].shape[1], attended_refs[0].shape[2]
    width = frame_ref.shape[3]
    rows = N_CTX * frames
    chunks = width // LANES
    entries = 2 * half // N_DP
    own = width // 2
    place = lax.axis_index("ctx")
    for apart in range(N_CTX):
        source = place ^ apart
        cols = columns((source & 1) * half, half)
        for block in range(N_CTX):
            whole_ref[half_of(source), block ^ source, :, cols] = attended_refs[apart][block]
        block = (own_ref, beside_ref, across_ref, beside_ref)[apart][(0, 0, 0, 2)[apart]]
        frame_ref[source] = block.reshape(frame_ref.shape[1:])
    group = lax.axis_index("dp")
    for slot, apart in enumerate((0, 4, 2, 6)):
        for odd, ref in enumerate((near_ref, other_ref)):
            first = pl.multiple_of((group ^ (apart + odd)) * entries, entries)
            rows_ref[pl.ds(first, entries)] = ref[slot * entries : (slot + 1) * entries]
    odd = (group & 1) == 1
    blocks = [ref[4 * entries :].astype(jnp.float32) for ref in (near_ref, other_ref)]
    blocks = (jnp.where(odd, blocks[1], blocks[0]), jnp.where(odd, blocks[0], blocks[1]))
    pieces = [jnp.concatenate([block[:, :own], block[:, own:]], axis=0) for block in blocks]
    taps = jnp.concatenate(pieces, axis=1)
    for chunk in range(chunks):
        for tap in range(TAPS):
            taps_ref[chunk, tap] = jnp.broadcast_to(
                taps[tap : tap + 1, chunk * LANES : (chunk + 1) * LANES], (8, LANES)
            )
    edge = jnp.zeros((2 * chunks, 16, LANES), jnp.float32)
    masked_ref[:, 0:16, :] = edge
    masked_ref[:, 16 + rows : 32 + rows, :] = edge
    for utt in range(2):
        real = lax.broadcasted_iota(jnp.int32, (rows, LANES), 0) < length_ref[utt]
        mixed = whole_ref[utt].reshape(rows, 2 * half)
        projected = dot_tt(mixed, rows_ref[...], 1, 0)
        hidden = frame_ref[:, utt].reshape(rows, width).astype(jnp.float32) + projected
        hidden = hidden.astype(jnp.bfloat16).astype(jnp.float32)
        for chunk in range(chunks):
            piece = hidden[:, chunk * LANES : (chunk + 1) * LANES]
            hidden_ref[utt * chunks + chunk] = piece
            masked_ref[utt * chunks + chunk, 16 : 16 + rows, :] = jnp.where(real, piece, 0.0)

    def convolve(step, carry):
        utt, chunk = step // chunks, step % chunks
        cols = columns(chunk * LANES, LANES)
        shape = (frames // 8, 8, LANES)
        for block in range(N_CTX):
            base = block * frames
            total = jnp.zeros(shape, jnp.float32)
            for tap in range(TAPS):
                first = base + tap + 16 - REACH
                piece = masked_ref[step, first : first + frames, :]
                total += taps_ref[chunk, tap][None] * piece.reshape(shape)
            total = total.reshape(frames, LANES)
            total_ref[step, base : base + frames, :] = total
            outer = hidden_ref[step, base : base + frames, :] + total * jax.nn.sigmoid(total)
            result_ref[block, utt, :, cols] = outer.astype(jnp.bfloat16)
        return carry

    lax.fori_loop(0, 2 * chunks, convolve, 0)
    for apart in range(2):
        out_refs[apart][...] = result_ref[place ^ apart]
        out_refs[2][apart] = result_ref[place ^ (2 + apart)].reshape(2 * frames, width)


def backward(length_ref, total_ref, taps_ref, rows_ref, *refs):
    own_ref, beside_ref = refs[:2]
    own_sides_ref, beside_sides_ref, grad_across_ref, grad_diagonal_ref = refs[2:6]
    refs = refs[6:]
    own_pair_ref, beside_pair_ref, across_ref = refs[:3]
    grad_ref, keep_ref, send_ref, cotangent_ref = refs[3:7]
    side_ref, result_ref = refs[7:]
    own_pair_ref[0], beside_pair_ref[0] = own_ref[...], beside_ref[...]
    utts, frames, width = own_ref.shape
    rows = N_CTX * frames
    chunks = width // LANES
    half = rows_ref.shape[0] // 2
    place = lax.axis_index("ctx")
    blocks = (own_sides_ref[1], beside_sides_ref[1], grad_across_ref[...], grad_diagonal_ref[...])
    for apart in range(N_CTX):
        side_ref[place ^ apart] = blocks[apart].reshape(side_ref.shape[1:])
    edge = jnp.zeros((2 * chunks, 16, LANES), jnp.float32)
    cotangent_ref[:, 0:16, :] = edge
    cotangent_ref[:, 16 + rows : 32 + rows, :] = edge

    def convolve(step, carry):
        utt, chunk = step // chunks, step % chunks
        cols = columns(chunk * LANES, LANES)
        length = length_ref[utt]
        shape = (frames // 8, 8, LANES)
        for block in range(N_CTX):
            base = block * frames
            total = total_ref[step, base : base + frames, :]
            gate = jax.nn.sigmoid(total)
            incoming = side_ref[block, utt, :, cols].astype(jnp.float32)
            slope = gate * (1.0 + total * (1.0 - gate))
            low = (incoming * slope).astype(jnp.bfloat16)
            cotangent_ref[step, 16 + base : 16 + base + frames, :] = low.astype(jnp.float32)
        for block in range(N_CTX):
            base = block * frames
            total = jnp.zeros(shape, jnp.float32)
            for tap in range(TAPS):
                first = base + 16 + REACH - tap
                piece = cotangent_ref[step, first : first + frames, :].reshape(shape)
                total += taps_ref[chunk, tap][None] * piece
            place_of = base + lax.broadcasted_iota(jnp.int32, (frames, LANES), 0)
            total = jnp.where(place_of < length, total.reshape(frames, LANES), 0.0)
            incoming = side_ref[block, utt, :, cols].astype(jnp.float32)
            low = (incoming + total).astype(jnp.bfloat16)
            result_ref[block, utt, :, cols] = low
            grad_ref[utt, base : base + frames, cols] = low
        return carry

    lax.fori_loop(0, 2 * chunks, convolve, 0)
    for apart in range(N_CTX):
        mine = result_ref[place ^ apart]
        if apart < 2:
            (own_pair_ref, beside_pair_ref)[apart][1] = mine
        else:
            across_ref[apart - 2] = mine.reshape(utts * frames, width)
        dest = place ^ apart
        mixed = dot_tt(
            grad_ref[half_of(dest)],
            rows_ref[pl.ds(pl.multiple_of((dest & 1) * half, half), half)],
            1,
            1,
        ).astype(jnp.bfloat16)
        ref = send_ref if apart % 2 else keep_ref
        for block in range(N_CTX):
            first = pl.multiple_of((block ^ dest) * frames, frames)
            ref[apart // 2, pl.ds(first, frames), :] = mixed[block * frames : (block + 1) * frames]


def make_taps(masked_ref, cotangent_ref, awaited_ref, keep_ref, send_ref, tap_sum_ref):
    steps, rows, chunks = masked_ref.shape[0], masked_ref.shape[1] - 32, tap_sum_ref.shape[0]
    block = 64
    shape = (block // 8, 8, LANES)
    tap_sum_ref[...] = jnp.zeros_like(tap_sum_ref)

    def correlate(step, carry):
        chunk = step % chunks
        for base in range(0, rows, block):
            held = masked_ref[step, 16 + base : 16 + base + block, :].reshape(shape)
            for tap in range(TAPS):
                first = base + 16 + REACH - tap
                piece = cotangent_ref[step, first : first + block, :].reshape(shape)
                tap_sum_ref[chunk, tap] += jnp.sum(held * piece, axis=0)
        return carry

    lax.fori_loop(0, steps, correlate, 0)
    sums = [
        jnp.concatenate(
            [
                jnp.sum(tap_sum_ref[chunk, tap], axis=0, keepdims=True)
                for tap in range(TAP_PAD)
            ],
            axis=0,
        )
        for chunk in range(chunks)
    ]
    sums = jnp.concatenate(sums, axis=1)
    own = sums.shape[1] // 2
    halves = [
        jnp.concatenate([part[: TAP_PAD // 2], part[TAP_PAD // 2 :]], axis=1)
        for part in (sums[:, :own], sums[:, own:])
    ]
    odd = (lax.axis_index("dp") & 1) == 1
    keep_ref[...] = jnp.where(odd, halves[1], halves[0])
    send_ref[...] = jnp.where(odd, halves[0], halves[1])


def make_panels(whole_ref, grad_ref, panel_ref):
    rows, half = grad_ref.shape[1], whole_ref.shape[3] // 2
    entries = 2 * half // N_DP
    group = lax.axis_index("dp")
    for side in range(2):
        panel = 0.0
        for utt in range(2):
            mixed = whole_ref[utt, :, :, side * half : (side + 1) * half].reshape(rows, half)
            panel += dot_tt(mixed, grad_ref[utt], 0, 0)
        panel = panel.astype(jnp.bfloat16)
        for part in range(N_DP // 2):
            panel_ref[slot_of(side * N_DP // 2 + part, group)] = panel[
                part * entries : (part + 1) * entries
            ]


def join(panel_ref, came_ref, tap_ref, tap_came_ref, awaited_ref, keep_ref, send_ref):
    entries = panel_ref.shape[1]
    group, place = lax.axis_index("dp"), lax.axis_index("ctx")
    taps = (tap_ref[...] + tap_came_ref[...]).astype(jnp.bfloat16)
    none = jnp.zeros_like(taps)
    for slot in range(N_DP // 2):
        ref = (keep_ref, send_ref)[slot // 2]
        total = panel_ref[slot].astype(jnp.float32) + came_ref[slot].astype(jnp.float32)
        ref[slot % 2, 0:entries] = total.astype(jnp.bfloat16)
        ref[slot % 2, entries:] = none
    mine = slot_of(2 * place, group & 6)
    for slot in range(N_DP // 2):
        ref = (keep_ref, send_ref)[slot // 2]

        @pl.when(mine == slot)
        def _(ref=ref, slot=slot):
            ref[slot % 2, entries:] = taps


def mark(*refs):
    refs[-1][...] = jnp.zeros_like(refs[-1])


def finish(kept_ref, came_ref, awaited_ref, taps_ref):
    first = kept_ref.shape[1] - TAP_PAD // 2
    taps_ref[...] = kept_ref[0, first:].astype(jnp.float32) + came_ref[...].astype(jnp.float32)


def relay(keep_ref, came_ref, out_ref):
    total = keep_ref[1].astype(jnp.float32) + came_ref[1].astype(jnp.float32)
    out_ref[...] = total.astype(jnp.bfloat16)


def make_pair(pair_ref, output_ref, input_ref, *refs):
    out_ref = refs[-1]
    for slot in range(2):
        out_ref[slot] = pair_ref[slot].reshape(out_ref.shape[1:])
    out_ref[2] = output_ref[1]
    out_ref[3] = input_ref[1]


def attend_back(weight_ref, keep_ref, came_ref, far_ref, *refs):
    ins, out_refs = refs[:N_CTX], refs[N_CTX + 1 :]
    frames, half = ins[0].shape[1], ins[0].shape[2]
    rows = N_CTX * frames
    query, key, value = (head_parts(ins, slot) for slot in range(3))
    masks = half_masks(rows)
    scale = HEAD_DIM ** (-0.5)
    arriving = keep_ref[0].astype(jnp.float32) + came_ref[0].astype(jnp.float32)
    arriving = (arriving + far_ref[...].astype(jnp.float32)).astype(jnp.bfloat16)
    low_lanes = lax.broadcasted_iota(jnp.int32, (rows, LANES), 1) < HEAD_DIM
    for pair in range(half // LANES):
        cols = slice(pair * LANES, (pair + 1) * LANES)
        key_pair, value_pair = key[:, cols], value[:, cols]
        query_pair, grad_pair = query[:, cols], arriving[:, cols]
        query_parts, key_parts, value_parts = [], [], []
        for side in range(2):
            low = weight_ref[2 * pair + side]
            weights = low.astype(jnp.float32)
            moved = weights * dot_tt(value_pair, grad_pair * masks[side], 1, 1)
            delta = jnp.sum(moved, axis=0, keepdims=True)
            grad_scores = (moved - weights * delta).astype(jnp.bfloat16)
            value_parts.append(dot_tt(low, grad_pair, 1, 0))
            key_parts.append(dot_tt(grad_scores, query_pair, 1, 0))
            mixed = dot_tt(key_pair, grad_scores, 0, 0)
            query_parts.append(mixed[side * HEAD_DIM : (side + 1) * HEAD_DIM])
        query_sum = (jnp.concatenate(query_parts, axis=0).T * scale).astype(jnp.bfloat16)
        key_sum = (jnp.where(low_lanes, key_parts[0], key_parts[1]) * scale).astype(jnp.bfloat16)
        value_sum = jnp.where(low_lanes, value_parts[0], value_parts[1]).astype(jnp.bfloat16)
        for slot, total in enumerate((query_sum, key_sum, value_sum)):
            for apart in range(N_CTX):
                out_refs[apart][slot, :, cols] = total[apart * frames : (apart + 1) * frames]


def swapped(array, bit):
    return lax.ppermute(array, "dp", [(i, i ^ bit) for i in range(N_DP)])


def dealt(slots):
    return lax.all_to_all(slots, "dp", 0, 0, tiled=True)


def crossed(array, apart):
    return lax.ppermute(array, "ctx", [(i, i ^ apart) for i in range(N_CTX)])


def traded(blocks):
    came = {apart: crossed(blocks[apart], apart) for apart in (2, 3, 1)}
    return [blocks[0]] + [came[apart] for apart in (1, 2, 3)]


def per_device(
    frame_input, queries, key_proj, value_proj, out_weight, conv_weight, lengths, grad_output
):
    utts, frames, wide = frame_input.shape
    inner = queries.shape[2]
    half, width = inner // 2, wide // N_CTX
    rows = N_CTX * frames
    chunks = width // LANES
    low, f32 = jnp.bfloat16, jnp.float32
    shape = jax.ShapeDtypeStruct
    entries = out_weight.shape[1]
    tap_count = conv_weight.shape[0]
    dma = pltpu.SemaphoreType.DMA
    head_block = shape((3, frames, half), low)
    channel_block = shape((utts, frames, width), low)

    blocks = call_kernel(
        pack_heads,
        (head_block,) * N_CTX,
        ["hbm"] * 3,
        scratch=[dma((3 * N_CTX,))],
        room=63,
    )(queries, key_proj, value_proj)
    packed = traded(blocks)
    (shard,) = call_kernel(
        pack_weights,
        (shape((1, entries + TAP_PAD // 2, width), low),),
        ["vmem"] * 2 + ["any"],
    )(out_weight.T, conv_weight, blocks[1])
    shard = jnp.concatenate([shard, swapped(shard, 4)], axis=0)
    (shard,) = call_kernel(
        pack_near, (shape((4 * entries + TAP_PAD // 2, width), low),), ["vmem"] * 2
    )(shard, swapped(shard, 2))
    other_shard = swapped(shard, 1)
    pair_block = shape((2, utts, frames, width), low)
    side_block = shape((utts * frames, width), low)
    double_block = shape((2, utts * frames, width), low)
    frame_across, grad_across, grad_diagonal, beside_sides, own_sides = call_kernel(
        pack_channels,
        (double_block,) + (side_block,) * 2 + (double_block,) * 2,
        ["hbm"] * 2 + ["any"],
        scratch=[dma((4 * N_CTX,))],
    )(frame_input, grad_output, packed[2])
    frame_across = crossed(frame_across, 2)
    (beside_sides,) = call_kernel(
        make_sides, (shape((3, utts * frames, width), low),), ["vmem"] * 2
    )(beside_sides, frame_across)
    beside_sides = crossed(beside_sides, 1)
    (attended,) = call_kernel(
        attend,
        (shape((N_CTX, frames, half), low),),
        ["smem"] + ["vmem"] * N_CTX,
    )(lengths, *packed)
    (attended,) = gate([attended], frame_across)
    across = crossed(attended, 2)
    beside = crossed(attended, 1)
    diagonal = crossed(across, 1)
    grad_across, grad_diagonal = crossed(grad_across, 2), crossed(grad_diagonal, 3)
    forward_out = call_kernel(
        forward,
        (channel_block,) * 2
        + (
            shape((2, utts * frames, width), low),
            shape((utts, N_CTX, frames, inner), low),
            shape((inner, width), low),
            shape((chunks, TAP_PAD, 8, LANES), f32),
            shape((utts * chunks, rows, LANES), f32),
            shape((utts * chunks, rows + 32, LANES), f32),
        ),
        ["smem"] + ["vmem"] * (5 + N_CTX),
        scratch=[
            pltpu.VMEM((utts * chunks, rows, LANES), f32),
            pltpu.VMEM((N_CTX, utts, frames, width), low),
            pltpu.VMEM((N_CTX, utts, frames, width), low),
        ],
        micros=3.2,
    )(
        lengths,
        shard,
        other_shard,
        attended,
        beside,
        across,
        diagonal,
        own_sides,
        beside_sides,
        frame_across,
    )
    output_across = crossed(forward_out[2], 2)
    whole, weight_rows, taps, totals, masked = forward_out[3:]
    grad_blocks = gate([grad_across, grad_diagonal], totals, micros=10.0)
    grad_blocks = (own_sides, beside_sides, *grad_blocks)
    backward_out = call_kernel(
        backward,
        (pair_block,) * 2
        + (
            shape((2, utts * frames, width), low),
            shape((utts, rows, width), low),
            shape((2, rows, half), low),
            shape((2, rows, half), low),
            shape((utts * chunks, rows + 32, LANES), f32),
        ),
        ["smem"] + ["vmem"] * (5 + N_CTX),
        scratch=[
            pltpu.VMEM((N_CTX, utts, frames, width), low),
            pltpu.VMEM((N_CTX, utts, frames, width), low),
        ],
        micros=5.2,
    )(lengths, totals, taps, weight_rows, *forward_out[:2], *grad_blocks)
    grad_hidden, keep, send, cotangents = backward_out[3:]
    (send,) = gate([send], output_across)
    came = crossed(send, 1)
    (relayed,) = call_kernel(
        relay, (shape((rows, half), low),), ["vmem"] * 2, micros=0.2
    )(keep, came)
    (input_across,) = gate([backward_out[2]], relayed)
    (panels,) = call_kernel(
        make_panels,
        (shape((N_DP, entries, width), low),),
        ["vmem"] * 2,
        micros=0.7,
    )(whole, grad_hidden)
    panels_came = swapped(panels[4:], 1)
    tap_block = shape((TAP_PAD // 2, width), f32)
    tap_keep, tap_send = call_kernel(
        make_taps,
        (tap_block,) * 2,
        ["vmem"] * 2 + ["any"],
        scratch=[pltpu.VMEM((chunks, TAP_PAD, 8, LANES), f32)],
    )(masked, cotangents, relayed)
    taps_came = swapped(tap_send, 1)
    far, input_across = crossed(relayed, 2), crossed(input_across, 2)
    (weights,) = call_kernel(
        weigh,
        (shape((half // HEAD_DIM, rows, rows), low),),
        ["smem"] + ["vmem"] * N_CTX + ["any"],
    )(lengths, *packed, relayed)
    back_blocks = call_kernel(
        attend_back,
        (head_block,) * N_CTX,
        ["vmem"] * (4 + N_CTX) + ["any"],
        micros=2.2,
    )(weights, keep, came, far, *packed, tap_keep)
    (across_block,) = gate([back_blocks[2]], input_across)
    grad_blocks = traded([*back_blocks[:2], across_block, back_blocks[3]])
    own_pair = backward_out[0]
    (beside_pair,) = call_kernel(
        make_pair,
        (shape((4, utts * frames, width), low),),
        ["vmem"] * 3 + ["any"],
        micros=0.2,
    )(backward_out[1], output_across, input_across, grad_blocks[1])
    beside_pair = crossed(beside_pair, 1)

    kept, sent = call_kernel(
        join,
        (shape((2, entries + TAP_PAD // 2, width), low),) * 2,
        ["vmem"] * 4 + ["any"],
    )(panels[:4], panels_came, tap_keep, taps_came, back_blocks[0])
    panels = (kept.astype(f32) + swapped(sent, 2).astype(f32)).astype(low)
    taps_last = swapped(panels[1, entries:], 4)
    panels_last = swapped(panels[1, :entries], 4)
    (arrived,) = call_kernel(mark, (shape((8, LANES), f32),), ["any"] * 3)(
        *grad_blocks[2:], taps_last
    )
    (tap_sums,) = call_kernel(
        finish, (shape((TAP_PAD // 2, width), f32),), ["vmem"] * 2 + ["any"]
    )(panels, taps_last, arrived)
    grad_out_weight = (panels[0, :entries].astype(f32) + panels_last.astype(f32)).T
    tap_blocks = traded([tap_sums] * N_CTX)
    grad_queries, grad_keys, grad_values, block_output, grad_input, grad_taps = call_kernel(
        unpack,
        (shape((utts, frames, inner), low),) * 3
        + (shape((utts, frames, wide), low),) * 2
        + (shape(conv_weight.shape, f32),),
        ["any"] * (N_CTX + 4) + ["vmem"] * N_CTX,
        ["hbm"] * 6,
        [
            pltpu.VMEM((N_CTX, TAP_PAD // 2, width), f32),
            pltpu.VMEM(conv_weight.shape, f32),
            dma((7 * N_CTX + 1,)),
        ],
        micros=1.0,
    )(
        *grad_blocks,
        own_pair,
        beside_pair,
        output_across,
        input_across,
        *tap_blocks,
    )
    return (
        block_output,
        grad_input,
        grad_queries,
        grad_keys,
        grad_values,
        grad_out_weight,
        grad_taps,
    )


def chosen(sizes, *arrays):
    frame_input, queries, out_weight, conv_weight = (arrays[i] for i in (0, 1, 4, 5))
    utts, frames, wide = frame_input.shape
    inner = queries.shape[2]
    fits = (
        sizes == (N_DP, N_CTX)
        and utts == 2
        and frames == 64
        and wide % (N_CTX * LANES) == 0
        and inner % (2 * LANES) == 0
        and inner // N_DP % 16 == 0
        and inner // 2 == wide // N_CTX
        and conv_weight.shape == (TAPS, wide // N_DP)
        and out_weight.shape == (wide // N_CTX, inner // N_DP)
    )
    return (per_device if fits else general_device)(*arrays)


def solution(mesh):
    placed = (
        P("dp", "ctx", None),
        P("dp", "ctx", None),
        P("dp", "ctx", None),
        P("dp", "ctx", None),
        P("ctx", "dp"),
        P(None, "dp"),
        P("dp"),
        P("dp", "ctx", None),
    )
    sizes = (mesh.shape["dp"], mesh.shape["ctx"])
    return jax.shard_map(
        functools.partial(chosen, sizes),
        mesh=mesh,
        in_specs=placed,
        out_specs=(
            P("dp", "ctx", None),
            P("dp", "ctx", None),
            P("dp", "ctx", None),
            P("dp", "ctx", None),
            P("dp", "ctx", None),
            P("ctx", "dp"),
            P(None, "dp"),
        ),
        check_vma=False,
    )
```

```python
import functools

import jax
import jax.numpy as jnp
from jax import lax
from jax.experimental import pallas as pl
from jax.experimental.pallas import tpu as pltpu
from jax.sharding import PartitionSpec as P

HEAD_DIM = 64


masked_score = -1e30


def padded_2(array, sides, width):
    for axis, dim in sides:
        size, length = (lax.axis_size(axis), array.shape[dim])
        up = [(i, (i + 1) % size) for i in range(size - 1)]
        down = [(j, i) for i, j in up]
        last = lax.slice_in_dim(array, length - width, length, axis=dim)
        leading = lax.slice_in_dim(array, 0, width, axis=dim)
        before = lax.ppermute(last, axis, up)
        after = lax.ppermute(leading, axis, down)
        array = jnp.concatenate([before, array, after], axis=dim)
    return array


def depthwise(lhs, rhs):
    return lax.conv_general_dilated(
        lhs,
        rhs,
        (1,),
        "VALID",
        dimension_numbers=("NWC", "WIO", "NWC"),
        feature_group_count=lhs.shape[2],
        precision=lax.Precision.HIGHEST,
    )


def general_device(
    frame_input, queries, key_proj, value_proj, out_weight, conv_weight, lengths, grad_output
):
    utt_count = frame_input.shape[0]
    frame_count = frame_input.shape[1]
    inner_width = queries.shape[2]
    head_count = inner_width // HEAD_DIM
    group_heads = max((g for g in range(1, 7) if head_count % g == 0))
    group_count = head_count // group_heads
    group_width = group_heads * HEAD_DIM
    tap_count = conv_weight.shape[0]
    half_span = (tap_count - 1) // 2
    score_scale = HEAD_DIM ** (-0.5)
    total_frames = frame_count * lax.axis_size("ctx")
    offset = lax.axis_index("ctx") * frame_count
    own_valid = (offset + jnp.arange(frame_count, dtype=jnp.int32))[None, :] < lengths[:, None]
    all_valid = jnp.arange(total_frames, dtype=jnp.int32)[None, :] < lengths[:, None]

    def grouped(values):
        row_count = values.shape[1]
        return values.reshape(utt_count, row_count, group_count, group_width).transpose(2, 0, 1, 3)

    def ungrouped(values):
        row_count = values.shape[2]
        return values.transpose(1, 2, 0, 3).reshape(utt_count, row_count, group_count * group_width)

    def split_heads(values):
        return values.reshape(utt_count, values.shape[1], group_heads, HEAD_DIM)

    def stats_grouped(values):
        row_count = values.shape[1]
        return values.reshape(utt_count, row_count, group_count, group_heads).transpose(2, 0, 3, 1)

    def masked_scores(query_block, key_block, key_mask):
        scores = (
            jnp.einsum(
                "uqgd,ukgd->ugqk", query_block, key_block, preferred_element_type=jnp.float32
            )
            * score_scale
        )
        return jnp.where(key_mask[:, None, None, :], scores, masked_score)

    taps = lax.all_gather(conv_weight, "dp", axis=1, tiled=True).astype(jnp.float32)
    panel_rows = lax.all_gather(out_weight, "dp", axis=1, tiled=True)
    weight_full = lax.all_gather(panel_rows, "ctx", axis=0, tiled=True)
    all_keys, all_values = (
        lax.all_gather(key_proj, "ctx", axis=1, tiled=True),
        lax.all_gather(value_proj, "ctx", axis=1, tiled=True),
    )
    query_groups = grouped(queries)
    key_groups = grouped(all_keys)
    value_groups = grouped(all_values)

    def forward_group(unused, items):
        query_group, key_group, value_group = items
        query_block = split_heads(query_group)
        scores = masked_scores(query_block, split_heads(key_group), all_valid)
        largest = jnp.max(scores, axis=-1)
        log_group = largest + jnp.log(jnp.sum(jnp.exp(scores - largest[..., None]), axis=-1))
        weights_low = jnp.exp(scores - log_group[..., None]).astype(jnp.bfloat16)
        attended_group = jnp.einsum(
            "ugqk,ukgd->uqgd",
            weights_low,
            split_heads(value_group),
            preferred_element_type=jnp.float32,
        )
        return (None, (log_group, attended_group.reshape(utt_count, frame_count, group_width)))

    _, (log_groups, attended_groups) = lax.scan(
        forward_group, None, (query_groups, key_groups, value_groups)
    )
    attended = ungrouped(attended_groups).astype(jnp.bfloat16)
    log_total = log_groups.transpose(1, 3, 0, 2).reshape(utt_count, frame_count, head_count)
    projected = jnp.einsum("ufe,de->ufd", attended, weight_full, preferred_element_type=jnp.float32)
    hidden = (frame_input.astype(jnp.float32) + projected).astype(jnp.bfloat16)
    masked_hidden = jnp.where(own_valid[:, :, None], hidden, jnp.zeros_like(hidden))
    padded = padded_2(masked_hidden, (("ctx", 1),), half_span).astype(jnp.float32)
    conv_sum = depthwise(padded, taps[:, None, :])
    sigmoid = jax.nn.sigmoid(conv_sum)
    block_output = (hidden.astype(jnp.float32) + conv_sum * sigmoid).astype(jnp.bfloat16)
    grad_local = grad_output.astype(jnp.float32)
    swish_slope = sigmoid * (1.0 + conv_sum * (1.0 - sigmoid))
    grad_conv = (grad_local * swish_slope).astype(jnp.bfloat16)
    grad_padded = padded_2(grad_conv, (("ctx", 1),), half_span).astype(jnp.float32)
    back_sum = depthwise(grad_padded, taps[::-1][:, None, :])
    grad_hidden = (grad_local + jnp.where(own_valid[:, :, None], back_sum, 0.0)).astype(
        jnp.bfloat16
    )
    grad_conv_wide = grad_conv.astype(jnp.float32)
    kernel_term = jnp.zeros((tap_count, conv_sum.shape[2]), jnp.float32)
    for utt_index in range(utt_count):
        kernel_term = (
            kernel_term
            + depthwise(padded[utt_index : utt_index + 1], grad_conv_wide[utt_index][:, None, :])[0]
        )
    kernel_whole = lax.psum(kernel_term.astype(jnp.bfloat16), "ctx")
    grad_conv_weight = lax.psum_scatter(kernel_whole, "dp", scatter_dimension=1, tiled=True).astype(
        jnp.float32
    )
    grad_attended = jnp.einsum(
        "ufd,de->ufe", grad_hidden, weight_full, preferred_element_type=jnp.float32
    ).astype(jnp.bfloat16)
    row_delta = jnp.sum(
        grad_attended.astype(jnp.float32).reshape(utt_count, frame_count, head_count, HEAD_DIM)
        * attended.astype(jnp.float32).reshape(utt_count, frame_count, head_count, HEAD_DIM),
        axis=-1,
    )
    grad_groups = grouped(grad_attended)

    def query_group_step(unused, items):
        query_group, key_group, value_group, grad_group, log_group, delta_group = items
        key_block = split_heads(key_group)
        weights = jnp.exp(
            masked_scores(split_heads(query_group), key_block, all_valid) - log_group[..., None]
        )
        grad_weights = jnp.einsum(
            "uqgd,ukgd->ugqk",
            split_heads(grad_group),
            split_heads(value_group),
            preferred_element_type=jnp.float32,
        )
        grad_scores = (weights * (grad_weights - delta_group[..., None])).astype(jnp.bfloat16)
        query_sum = jnp.einsum(
            "ugqk,ukgd->uqgd", grad_scores, key_block, preferred_element_type=jnp.float32
        )
        return (None, query_sum.reshape(utt_count, frame_count, group_width))

    _, query_sums = lax.scan(
        query_group_step,
        None,
        (
            query_groups,
            key_groups,
            value_groups,
            grad_groups,
            stats_grouped(log_total),
            stats_grouped(row_delta),
        ),
    )
    grad_queries = (ungrouped(query_sums) * score_scale).astype(jnp.bfloat16)
    total_log, total_delta = (
        lax.all_gather(log_total, "ctx", axis=1, tiled=True),
        lax.all_gather(row_delta, "ctx", axis=1, tiled=True),
    )
    own_key_groups = grouped(key_proj)
    own_value_groups = grouped(value_proj)
    group_zeros = jnp.zeros((group_count, utt_count, frame_count, group_width), jnp.float32)
    start_sums = (group_zeros, group_zeros)
    query_all, grad_all = (
        lax.all_gather(queries, "ctx", axis=1, tiled=True),
        lax.all_gather(grad_attended, "ctx", axis=1, tiled=True),
    )
    log_piece = stats_grouped(total_log)
    delta_piece = stats_grouped(total_delta)

    def key_group_step(unused, items):
        (
            query_group,
            grad_group,
            log_group,
            delta_group,
            key_group,
            value_group,
            key_sum,
            value_sum,
        ) = items
        query_block = split_heads(query_group)
        grad_block = split_heads(grad_group)
        weights = jnp.exp(
            masked_scores(query_block, split_heads(key_group), own_valid) - log_group[..., None]
        )
        grad_weights = jnp.einsum(
            "uqgd,ukgd->ugqk",
            grad_block,
            split_heads(value_group),
            preferred_element_type=jnp.float32,
        )
        grad_scores = (weights * (grad_weights - delta_group[..., None])).astype(jnp.bfloat16)
        key_next = key_sum + jnp.einsum(
            "ugqk,uqgd->ukgd", grad_scores, query_block, preferred_element_type=jnp.float32
        ).reshape(utt_count, frame_count, group_width)
        value_next = value_sum + jnp.einsum(
            "ugqk,uqgd->ukgd",
            weights.astype(jnp.bfloat16),
            grad_block,
            preferred_element_type=jnp.float32,
        ).reshape(utt_count, frame_count, group_width)
        return (None, (key_next, value_next))

    _, result_sums = lax.scan(
        key_group_step,
        None,
        (
            grouped(query_all),
            grouped(grad_all),
            log_piece,
            delta_piece,
            own_key_groups,
            own_value_groups,
            start_sums[0],
            start_sums[1],
        ),
    )
    key_sum, value_sum = result_sums
    grad_keys = (ungrouped(key_sum) * score_scale).astype(jnp.bfloat16)
    grad_values = ungrouped(value_sum).astype(jnp.bfloat16)
    hidden_cols = lax.slice_in_dim(
        grad_hidden, 0, weight_full.shape[0] // lax.axis_size("ctx") * lax.axis_size("ctx"), axis=2
    )
    panel_share = lax.psum_scatter(
        jnp.einsum("ufd,ufe->de", hidden_cols, attended, preferred_element_type=jnp.float32).astype(
            jnp.bfloat16
        ),
        "ctx",
        scatter_dimension=0,
        tiled=True,
    )
    grad_out_weight = lax.psum_scatter(panel_share, "dp", scatter_dimension=1, tiled=True).astype(
        jnp.float32
    )
    return (
        block_output,
        grad_hidden,
        grad_queries,
        grad_keys,
        grad_values,
        grad_out_weight,
        grad_conv_weight,
    )


LANES = 128
N_CTX = 4
N_DP = 8
TAP_PAD = 32
FLOPS_A_MICRO = 1.15e9
TAPS = 31
REACH = 15


def slot_of(index, me):
    apart = index ^ me
    return ((apart & 1) << 2) | (apart & 2) | ((apart >> 2) & 1)


def dot_tt(lhs, rhs, lhs_dim, rhs_dim):
    return lax.dot_general(
        lhs, rhs, (((lhs_dim,), (rhs_dim,)), ((), ())), preferred_element_type=jnp.float32
    )


def call_kernel(body, out_shape, ins, outs=None, scratch=(), room=40, micros=1.0):
    spaces = {
        "smem": pl.BlockSpec(memory_space=pltpu.SMEM),
        "vmem": pl.BlockSpec(memory_space=pltpu.VMEM),
        "hbm": pl.BlockSpec(memory_space=pltpu.HBM),
        "any": pl.BlockSpec(memory_space=pl.ANY),
    }
    return pl.pallas_call(
        body,
        out_shape=out_shape,
        in_specs=[spaces[space] for space in ins],
        out_specs=[spaces[space] for space in (outs or ["vmem"] * len(out_shape))],
        scratch_shapes=list(scratch),
        compiler_params=pltpu.CompilerParams(vmem_limit_bytes=room * 1024 * 1024),
        cost_estimate=pl.CostEstimate(
            flops=int(micros * FLOPS_A_MICRO), bytes_accessed=0, transcendentals=0
        ),
    )


def half_of(index):
    return lax.shift_right_logical(index, 1)


def columns(start, size):
    return pl.ds(pl.multiple_of(start, LANES), size)


def start_copies(pairs, sem):
    for number, (source, target) in enumerate(pairs):
        pltpu.make_async_copy(source, target, sem.at[number]).start()


def wait_copies(pairs, sem):
    for number, (source, target) in enumerate(pairs):
        pltpu.make_async_copy(source, target, sem.at[number]).wait()


def run_copies(pairs, sem):
    start_copies(pairs, sem)
    wait_copies(pairs, sem)


def untouched(*refs):
    pass


def gate(arrays, *awaited, micros=0.0):
    count = len(arrays)
    spec = pl.BlockSpec(memory_space=pl.ANY)
    return pl.pallas_call(
        untouched,
        out_shape=tuple(jax.ShapeDtypeStruct(array.shape, array.dtype) for array in arrays),
        in_specs=[spec] * (count + len(awaited)),
        out_specs=(spec,) * count,
        input_output_aliases={number: number for number in range(count)},
        compiler_params=pltpu.CompilerParams(vmem_limit_bytes=1024 * 1024),
        cost_estimate=pl.CostEstimate(
            flops=int(micros * FLOPS_A_MICRO), bytes_accessed=0, transcendentals=0
        ),
    )(*arrays, *awaited)


def pack_heads(query_ref, key_ref, value_ref, *rest):
    outs, sem = rest[:N_CTX], rest[N_CTX]
    half = query_ref.shape[2] // 2
    place = lax.axis_index("ctx")
    pairs = []
    for apart in (2, 3, 1, 0):
        dest = place ^ apart
        cols = columns((dest & 1) * half, half)
        for slot, ref in enumerate((query_ref, key_ref, value_ref)):
            pairs.append((ref.at[half_of(dest), :, cols], outs[apart].at[slot]))
    run_copies(pairs, sem)


def pack_weights(panel_ref, taps_ref, awaited_ref, out_ref):
    entries = panel_ref.shape[0]
    taps = taps_ref[...].astype(jnp.float32)
    high = jnp.concatenate(
        [taps[TAP_PAD // 2 :], jnp.zeros((TAP_PAD - TAPS, taps.shape[1]), jnp.float32)], axis=0
    )
    out_ref[0, 0:entries] = panel_ref[...]
    joined = jnp.concatenate([taps[: TAP_PAD // 2], high], axis=1)
    out_ref[0, entries:] = joined.astype(jnp.bfloat16)


def pack_near(held_ref, came_ref, out_ref):
    entries = held_ref.shape[1] - TAP_PAD // 2
    for slot in range(2):
        for half, ref in enumerate((held_ref, came_ref)):
            first = (2 * half + slot) * entries
            out_ref[first : first + entries, :] = ref[slot, 0:entries]
    apart = lax.axis_index("ctx") ^ half_of(lax.axis_index("dp"))
    slot = half_of(apart)
    taps = [ref[slot, entries:].astype(jnp.float32) for ref in (held_ref, came_ref)]
    taps = jnp.where((apart & 1) == 1, taps[1], taps[0])
    out_ref[4 * entries :, :] = taps.astype(jnp.bfloat16)


def pack_channels(frame_ref, grad_ref, awaited_ref, *rest):
    across_ref, grad_outs, beside_ref, own_ref, sem = rest[0], rest[1:3], *rest[3:]
    width = frame_ref.shape[2] // N_CTX
    frames = frame_ref.shape[1]
    place = lax.axis_index("ctx")
    pairs = []
    for slot, ref in enumerate((frame_ref, grad_ref)):
        for apart in (2, 3, 1, 0):
            cols = columns((place ^ apart) * width, width)
            for utt in range(2):
                rows = slice(utt * frames, (utt + 1) * frames)
                if apart < 2:
                    target = (own_ref, beside_ref)[apart].at[slot, rows]
                elif slot == 0:
                    target = across_ref.at[apart - 2, rows]
                else:
                    target = grad_outs[apart - 2].at[rows]
                pairs.append((ref.at[utt, :, cols], target))
    run_copies(pairs, sem)


def make_sides(beside_ref, across_ref, out_ref):
    out_ref[0:2] = beside_ref[...]
    out_ref[2] = across_ref[1]


def unpack(*refs):
    ins, refs = refs[:N_CTX], refs[N_CTX:]
    own_ref, beside_ref, output_ref, input_ref = refs[:4]
    taps, heads, channels, taps_ref = refs[4:8], refs[8:11], refs[11:13], refs[13]
    held_ref, picked_ref, sem = refs[14:]
    half, width = ins[0].shape[2], own_ref.shape[3]
    frames = own_ref.shape[2]
    place = lax.axis_index("ctx")
    pairs = []
    for apart in range(N_CTX):
        source = place ^ apart
        cols = columns((source & 1) * half, half)
        for slot, ref in enumerate(heads):
            pairs.append((ins[apart].at[slot], ref.at[half_of(source), :, cols]))
    for slot, ref in enumerate(channels):
        for utt in range(2):
            part = pl.ds(utt * frames, frames)
            blocks = (
                own_ref.at[slot, utt],
                beside_ref.at[slot, part],
                (output_ref, input_ref)[slot].at[0, part],
                beside_ref.at[2 + slot, part],
            )
            for apart, block in enumerate(blocks):
                cols = columns((place ^ apart) * width, width)
                pairs.append((block, ref.at[utt, :, cols]))
    start_copies(pairs, sem)
    for apart in range(N_CTX):
        held_ref[apart] = taps[apart][...]
    mine = held_ref[place ^ half_of(lax.axis_index("dp"))]
    side = mine.shape[1] // 2
    picked_ref[...] = jnp.concatenate([mine[:, :side], mine[:, side:]], axis=0)[:TAPS]
    last = pltpu.make_async_copy(picked_ref, taps_ref, sem.at[len(pairs)])
    last.start()
    wait_copies(pairs, sem)
    last.wait()


def head_parts(refs, slot):
    return jnp.concatenate([ref[slot] for ref in refs], axis=0)


def half_masks(rows):
    lane = lax.broadcasted_iota(jnp.int32, (rows, LANES), 1)
    low = jnp.where(lane < HEAD_DIM, 1.0, 0.0)
    return low.astype(jnp.bfloat16), (1.0 - low).astype(jnp.bfloat16)


def weights_of(length_ref, key_pair, query_pair, mask, frames):
    place = lax.axis_index("ctx")
    rows = key_pair.shape[0]
    frame = lax.broadcasted_iota(jnp.int32, (rows, rows), 0) ^ (place * frames)
    scores = dot_tt(key_pair, query_pair * (mask * HEAD_DIM ** (-0.5)), 1, 1)
    scores = jnp.where(frame < length_ref[half_of(place)], scores, masked_score)
    powers = jnp.exp(scores - jnp.max(scores, axis=0, keepdims=True))
    total = jnp.sum(powers, axis=0, keepdims=True)
    return (powers * (1.0 / total)).astype(jnp.bfloat16)


def attend(length_ref, *refs):
    ins, attended_ref = refs[:N_CTX], refs[N_CTX]
    frames, half = ins[0].shape[1], ins[0].shape[2]
    query, key, value = (head_parts(ins, slot) for slot in range(3))
    masks = half_masks(N_CTX * frames)
    for pair in range(half // LANES):
        cols = slice(pair * LANES, (pair + 1) * LANES)
        parts = []
        for side in range(2):
            low = weights_of(length_ref, key[:, cols], query[:, cols], masks[side], frames)
            mixed = dot_tt(value[:, cols], low, 0, 0)
            parts.append(mixed[side * HEAD_DIM : (side + 1) * HEAD_DIM])
        joined = jnp.concatenate(parts, axis=0).T.astype(jnp.bfloat16)
        attended_ref[:, :, cols] = joined.reshape(N_CTX, frames, LANES)


def weigh(length_ref, *refs):
    ins, weight_ref = refs[:N_CTX], refs[N_CTX + 1]
    frames, half = ins[0].shape[1], ins[0].shape[2]
    query, key = (head_parts(ins, slot) for slot in range(2))
    masks = half_masks(N_CTX * frames)
    for pair in range(half // LANES):
        cols = slice(pair * LANES, (pair + 1) * LANES)
        for side in range(2):
            weight_ref[2 * pair + side] = weights_of(
                length_ref, key[:, cols], query[:, cols], masks[side], frames
            )


def forward(length_ref, near_ref, other_ref, *refs):
    attended_refs, refs = refs[:N_CTX], refs[N_CTX:]
    own_ref, beside_ref, across_ref = refs[:3]
    out_refs, refs = refs[3:6], refs[6:]
    whole_ref, rows_ref, taps_ref, total_ref, masked_ref = refs[:5]
    hidden_ref, frame_ref, result_ref = refs[5:]
    frames, half = attended_refs[0].shape[1], attended_refs[0].shape[2]
    width = frame_ref.shape[3]
    rows = N_CTX * frames
    chunks = width // LANES
    entries = 2 * half // N_DP
    own = width // 2
    place = lax.axis_index("ctx")
    for apart in range(N_CTX):
        source = place ^ apart
        cols = columns((source & 1) * half, half)
        for block in range(N_CTX):
            whole_ref[half_of(source), block ^ source, :, cols] = attended_refs[apart][block]
        block = (own_ref, beside_ref, across_ref, beside_ref)[apart][(0, 0, 0, 2)[apart]]
        frame_ref[source] = block.reshape(frame_ref.shape[1:])
    group = lax.axis_index("dp")
    for slot, apart in enumerate((0, 4, 2, 6)):
        for odd, ref in enumerate((near_ref, other_ref)):
            first = pl.multiple_of((group ^ (apart + odd)) * entries, entries)
            rows_ref[pl.ds(first, entries)] = ref[slot * entries : (slot + 1) * entries]
    odd = (group & 1) == 1
    blocks = [ref[4 * entries :].astype(jnp.float32) for ref in (near_ref, other_ref)]
    blocks = (jnp.where(odd, blocks[1], blocks[0]), jnp.where(odd, blocks[0], blocks[1]))
    pieces = [jnp.concatenate([block[:, :own], block[:, own:]], axis=0) for block in blocks]
    taps = jnp.concatenate(pieces, axis=1)
    for chunk in range(chunks):
        for tap in range(TAPS):
            taps_ref[chunk, tap] = jnp.broadcast_to(
                taps[tap : tap + 1, chunk * LANES : (chunk + 1) * LANES], (8, LANES)
            )
    edge = jnp.zeros((2 * chunks, 16, LANES), jnp.float32)
    masked_ref[:, 0:16, :] = edge
    masked_ref[:, 16 + rows : 32 + rows, :] = edge
    for utt in range(2):
        real = lax.broadcasted_iota(jnp.int32, (rows, LANES), 0) < length_ref[utt]
        mixed = whole_ref[utt].reshape(rows, 2 * half)
        projected = dot_tt(mixed, rows_ref[...], 1, 0)
        hidden = frame_ref[:, utt].reshape(rows, width).astype(jnp.float32) + projected
        hidden = hidden.astype(jnp.bfloat16).astype(jnp.float32)
        for chunk in range(chunks):
            piece = hidden[:, chunk * LANES : (chunk + 1) * LANES]
            hidden_ref[utt * chunks + chunk] = piece
            masked_ref[utt * chunks + chunk, 16 : 16 + rows, :] = jnp.where(real, piece, 0.0)

    def convolve(step, carry):
        utt, chunk = step // chunks, step % chunks
        cols = columns(chunk * LANES, LANES)
        shape = (frames // 8, 8, LANES)
        for block in range(N_CTX):
            base = block * frames
            total = jnp.zeros(shape, jnp.float32)
            for tap in range(TAPS):
                first = base + tap + 16 - REACH
                piece = masked_ref[step, first : first + frames, :]
                total += taps_ref[chunk, tap][None] * piece.reshape(shape)
            total = total.reshape(frames, LANES)
            total_ref[step, base : base + frames, :] = total
            outer = hidden_ref[step, base : base + frames, :] + total * jax.nn.sigmoid(total)
            result_ref[block, utt, :, cols] = outer.astype(jnp.bfloat16)
        return carry

    lax.fori_loop(0, 2 * chunks, convolve, 0)
    for apart in range(2):
        out_refs[apart][...] = result_ref[place ^ apart]
        out_refs[2][apart] = result_ref[place ^ (2 + apart)].reshape(2 * frames, width)


def backward(length_ref, total_ref, taps_ref, rows_ref, *refs):
    own_ref, beside_ref = refs[:2]
    own_sides_ref, beside_sides_ref, grad_across_ref, grad_diagonal_ref = refs[2:6]
    refs = refs[6:]
    own_pair_ref, beside_pair_ref, across_ref = refs[:3]
    grad_ref, keep_ref, send_ref, cotangent_ref = refs[3:7]
    side_ref, result_ref = refs[7:]
    own_pair_ref[0], beside_pair_ref[0] = own_ref[...], beside_ref[...]
    utts, frames, width = own_ref.shape
    rows = N_CTX * frames
    chunks = width // LANES
    half = rows_ref.shape[0] // 2
    place = lax.axis_index("ctx")
    blocks = (own_sides_ref[1], beside_sides_ref[1], grad_across_ref[...], grad_diagonal_ref[...])
    for apart in range(N_CTX):
        side_ref[place ^ apart] = blocks[apart].reshape(side_ref.shape[1:])
    edge = jnp.zeros((2 * chunks, 16, LANES), jnp.float32)
    cotangent_ref[:, 0:16, :] = edge
    cotangent_ref[:, 16 + rows : 32 + rows, :] = edge

    def convolve(step, carry):
        utt, chunk = step // chunks, step % chunks
        cols = columns(chunk * LANES, LANES)
        length = length_ref[utt]
        shape = (frames // 8, 8, LANES)
        for block in range(N_CTX):
            base = block * frames
            total = total_ref[step, base : base + frames, :]
            gate = jax.nn.sigmoid(total)
            incoming = side_ref[block, utt, :, cols].astype(jnp.float32)
            slope = gate * (1.0 + total * (1.0 - gate))
            low = (incoming * slope).astype(jnp.bfloat16)
            cotangent_ref[step, 16 + base : 16 + base + frames, :] = low.astype(jnp.float32)
        for block in range(N_CTX):
            base = block * frames
            total = jnp.zeros(shape, jnp.float32)
            for tap in range(TAPS):
                first = base + 16 + REACH - tap
                piece = cotangent_ref[step, first : first + frames, :].reshape(shape)
                total += taps_ref[chunk, tap][None] * piece
            place_of = base + lax.broadcasted_iota(jnp.int32, (frames, LANES), 0)
            total = jnp.where(place_of < length, total.reshape(frames, LANES), 0.0)
            incoming = side_ref[block, utt, :, cols].astype(jnp.float32)
            low = (incoming + total).astype(jnp.bfloat16)
            result_ref[block, utt, :, cols] = low
            grad_ref[utt, base : base + frames, cols] = low
        return carry

    lax.fori_loop(0, 2 * chunks, convolve, 0)
    for apart in range(N_CTX):
        mine = result_ref[place ^ apart]
        if apart < 2:
            (own_pair_ref, beside_pair_ref)[apart][1] = mine
        else:
            across_ref[apart - 2] = mine.reshape(utts * frames, width)
        dest = place ^ apart
        mixed = dot_tt(
            grad_ref[half_of(dest)],
            rows_ref[pl.ds(pl.multiple_of((dest & 1) * half, half), half)],
            1,
            1,
        ).astype(jnp.bfloat16)
        ref = send_ref if apart % 2 else keep_ref
        for block in range(N_CTX):
            first = pl.multiple_of((block ^ dest) * frames, frames)
            ref[apart // 2, pl.ds(first, frames), :] = mixed[block * frames : (block + 1) * frames]


def make_taps(masked_ref, cotangent_ref, awaited_ref, keep_ref, send_ref, tap_sum_ref):
    steps, rows, chunks = masked_ref.shape[0], masked_ref.shape[1] - 32, tap_sum_ref.shape[0]
    block = 64
    shape = (block // 8, 8, LANES)
    tap_sum_ref[...] = jnp.zeros_like(tap_sum_ref)

    def correlate(step, carry):
        chunk = step % chunks
        for base in range(0, rows, block):
            held = masked_ref[step, 16 + base : 16 + base + block, :].reshape(shape)
            for tap in range(TAPS):
                first = base + 16 + REACH - tap
                piece = cotangent_ref[step, first : first + block, :].reshape(shape)
                tap_sum_ref[chunk, tap] += jnp.sum(held * piece, axis=0)
        return carry

    lax.fori_loop(0, steps, correlate, 0)
    sums = [
        jnp.concatenate(
            [
                jnp.sum(tap_sum_ref[chunk, tap], axis=0, keepdims=True)
                for tap in range(TAP_PAD)
            ],
            axis=0,
        )
        for chunk in range(chunks)
    ]
    sums = jnp.concatenate(sums, axis=1)
    own = sums.shape[1] // 2
    halves = [
        jnp.concatenate([part[: TAP_PAD // 2], part[TAP_PAD // 2 :]], axis=1)
        for part in (sums[:, :own], sums[:, own:])
    ]
    odd = (lax.axis_index("dp") & 1) == 1
    keep_ref[...] = jnp.where(odd, halves[1], halves[0])
    send_ref[...] = jnp.where(odd, halves[0], halves[1])


def make_panels(whole_ref, grad_ref, panel_ref):
    rows, half = grad_ref.shape[1], whole_ref.shape[3] // 2
    entries = 2 * half // N_DP
    group = lax.axis_index("dp")
    for side in range(2):
        panel = 0.0
        for utt in range(2):
            mixed = whole_ref[utt, :, :, side * half : (side + 1) * half].reshape(rows, half)
            panel += dot_tt(mixed, grad_ref[utt], 0, 0)
        panel = panel.astype(jnp.bfloat16)
        for part in range(N_DP // 2):
            panel_ref[slot_of(side * N_DP // 2 + part, group)] = panel[
                part * entries : (part + 1) * entries
            ]


def join(panel_ref, came_ref, tap_ref, tap_came_ref, awaited_ref, keep_ref, send_ref):
    entries = panel_ref.shape[1]
    group, place = lax.axis_index("dp"), lax.axis_index("ctx")
    taps = (tap_ref[...] + tap_came_ref[...]).astype(jnp.bfloat16)
    none = jnp.zeros_like(taps)
    for slot in range(N_DP // 2):
        ref = (keep_ref, send_ref)[slot // 2]
        total = panel_ref[slot].astype(jnp.float32) + came_ref[slot].astype(jnp.float32)
        ref[slot % 2, 0:entries] = total.astype(jnp.bfloat16)
        ref[slot % 2, entries:] = none
    mine = slot_of(2 * place, group & 6)
    for slot in range(N_DP // 2):
        ref = (keep_ref, send_ref)[slot // 2]

        @pl.when(mine == slot)
        def _(ref=ref, slot=slot):
            ref[slot % 2, entries:] = taps


def mark(*refs):
    refs[-1][...] = jnp.zeros_like(refs[-1])


def finish(kept_ref, came_ref, awaited_ref, taps_ref):
    first = kept_ref.shape[1] - TAP_PAD // 2
    taps_ref[...] = kept_ref[0, first:].astype(jnp.float32) + came_ref[...].astype(jnp.float32)


def relay(keep_ref, came_ref, out_ref):
    total = keep_ref[1].astype(jnp.float32) + came_ref[1].astype(jnp.float32)
    out_ref[...] = total.astype(jnp.bfloat16)


def make_pair(pair_ref, output_ref, input_ref, *refs):
    out_ref = refs[-1]
    for slot in range(2):
        out_ref[slot] = pair_ref[slot].reshape(out_ref.shape[1:])
    out_ref[2] = output_ref[1]
    out_ref[3] = input_ref[1]


def attend_back(weight_ref, keep_ref, came_ref, far_ref, *refs):
    ins, out_refs = refs[:N_CTX], refs[N_CTX + 1 :]
    frames, half = ins[0].shape[1], ins[0].shape[2]
    rows = N_CTX * frames
    query, key, value = (head_parts(ins, slot) for slot in range(3))
    masks = half_masks(rows)
    scale = HEAD_DIM ** (-0.5)
    arriving = keep_ref[0].astype(jnp.float32) + came_ref[0].astype(jnp.float32)
    arriving = (arriving + far_ref[...].astype(jnp.float32)).astype(jnp.bfloat16)
    low_lanes = lax.broadcasted_iota(jnp.int32, (rows, LANES), 1) < HEAD_DIM
    for pair in range(half // LANES):
        cols = slice(pair * LANES, (pair + 1) * LANES)
        key_pair, value_pair = key[:, cols], value[:, cols]
        query_pair, grad_pair = query[:, cols], arriving[:, cols]
        query_parts, key_parts, value_parts = [], [], []
        for side in range(2):
            low = weight_ref[2 * pair + side]
            weights = low.astype(jnp.float32)
            moved = weights * dot_tt(value_pair, grad_pair * masks[side], 1, 1)
            delta = jnp.sum(moved, axis=0, keepdims=True)
            grad_scores = (moved - weights * delta).astype(jnp.bfloat16)
            value_parts.append(dot_tt(low, grad_pair, 1, 0))
            key_parts.append(dot_tt(grad_scores, query_pair, 1, 0))
            mixed = dot_tt(key_pair, grad_scores, 0, 0)
            query_parts.append(mixed[side * HEAD_DIM : (side + 1) * HEAD_DIM])
        query_sum = (jnp.concatenate(query_parts, axis=0).T * scale).astype(jnp.bfloat16)
        key_sum = (jnp.where(low_lanes, key_parts[0], key_parts[1]) * scale).astype(jnp.bfloat16)
        value_sum = jnp.where(low_lanes, value_parts[0], value_parts[1]).astype(jnp.bfloat16)
        for slot, total in enumerate((query_sum, key_sum, value_sum)):
            for apart in range(N_CTX):
                out_refs[apart][slot, :, cols] = total[apart * frames : (apart + 1) * frames]


def swapped(array, bit):
    return lax.ppermute(array, "dp", [(i, i ^ bit) for i in range(N_DP)])


def dealt(slots):
    return lax.all_to_all(slots, "dp", 0, 0, tiled=True)


def crossed(array, apart):
    return lax.ppermute(array, "ctx", [(i, i ^ apart) for i in range(N_CTX)])


def traded(blocks):
    came = {apart: crossed(blocks[apart], apart) for apart in (2, 3, 1)}
    return [blocks[0]] + [came[apart] for apart in (1, 2, 3)]


def per_device(
    frame_input, queries, key_proj, value_proj, out_weight, conv_weight, lengths, grad_output
):
    utts, frames, wide = frame_input.shape
    inner = queries.shape[2]
    half, width = inner // 2, wide // N_CTX
    rows = N_CTX * frames
    chunks = width // LANES
    low, f32 = jnp.bfloat16, jnp.float32
    shape = jax.ShapeDtypeStruct
    entries = out_weight.shape[1]
    tap_count = conv_weight.shape[0]
    dma = pltpu.SemaphoreType.DMA
    head_block = shape((3, frames, half), low)
    channel_block = shape((utts, frames, width), low)

    blocks = call_kernel(
        pack_heads,
        (head_block,) * N_CTX,
        ["hbm"] * 3,
        scratch=[dma((3 * N_CTX,))],
        room=63,
    )(queries, key_proj, value_proj)
    packed = traded(blocks)
    (shard,) = call_kernel(
        pack_weights,
        (shape((1, entries + TAP_PAD // 2, width), low),),
        ["vmem"] * 2 + ["any"],
    )(out_weight.T, conv_weight, packed[1])
    shard = jnp.concatenate([shard, swapped(shard, 4)], axis=0)
    (shard,) = call_kernel(
        pack_near, (shape((4 * entries + TAP_PAD // 2, width), low),), ["vmem"] * 2
    )(shard, swapped(shard, 2))
    other_shard = swapped(shard, 1)
    pair_block = shape((2, utts, frames, width), low)
    side_block = shape((utts * frames, width), low)
    double_block = shape((2, utts * frames, width), low)
    frame_across, grad_across, grad_diagonal, beside_sides, own_sides = call_kernel(
        pack_channels,
        (double_block,) + (side_block,) * 2 + (double_block,) * 2,
        ["hbm"] * 2 + ["any"],
        scratch=[dma((4 * N_CTX,))],
    )(frame_input, grad_output, packed[2])
    frame_across = crossed(frame_across, 2)
    (beside_sides,) = call_kernel(
        make_sides, (shape((3, utts * frames, width), low),), ["vmem"] * 2
    )(beside_sides, frame_across)
    beside_sides = crossed(beside_sides, 1)
    (attended,) = call_kernel(
        attend,
        (shape((N_CTX, frames, half), low),),
        ["smem"] + ["vmem"] * N_CTX,
    )(lengths, *packed)
    (attended,) = gate([attended], frame_across)
    across = crossed(attended, 2)
    beside = crossed(attended, 1)
    diagonal = crossed(across, 1)
    grad_across, grad_diagonal = crossed(grad_across, 2), crossed(grad_diagonal, 3)
    forward_out = call_kernel(
        forward,
        (channel_block,) * 2
        + (
            shape((2, utts * frames, width), low),
            shape((utts, N_CTX, frames, inner), low),
            shape((inner, width), low),
            shape((chunks, TAP_PAD, 8, LANES), f32),
            shape((utts * chunks, rows, LANES), f32),
            shape((utts * chunks, rows + 32, LANES), f32),
        ),
        ["smem"] + ["vmem"] * (5 + N_CTX),
        scratch=[
            pltpu.VMEM((utts * chunks, rows, LANES), f32),
            pltpu.VMEM((N_CTX, utts, frames, width), low),
            pltpu.VMEM((N_CTX, utts, frames, width), low),
        ],
        micros=3.2,
    )(
        lengths,
        shard,
        other_shard,
        attended,
        beside,
        across,
        diagonal,
        own_sides,
        beside_sides,
        frame_across,
    )
    output_across = crossed(forward_out[2], 2)
    whole, weight_rows, taps, totals, masked = forward_out[3:]
    grad_blocks = gate([grad_across, grad_diagonal], totals, micros=10.0)
    grad_blocks = (own_sides, beside_sides, *grad_blocks)
    backward_out = call_kernel(
        backward,
        (pair_block,) * 2
        + (
            shape((2, utts * frames, width), low),
            shape((utts, rows, width), low),
            shape((2, rows, half), low),
            shape((2, rows, half), low),
            shape((utts * chunks, rows + 32, LANES), f32),
        ),
        ["smem"] + ["vmem"] * (5 + N_CTX),
        scratch=[
            pltpu.VMEM((N_CTX, utts, frames, width), low),
            pltpu.VMEM((N_CTX, utts, frames, width), low),
        ],
        micros=5.2,
    )(lengths, totals, taps, weight_rows, *forward_out[:2], *grad_blocks)
    grad_hidden, keep, send, cotangents = backward_out[3:]
    (send,) = gate([send], output_across)
    came = crossed(send, 1)
    (relayed,) = call_kernel(
        relay, (shape((rows, half), low),), ["vmem"] * 2, micros=0.2
    )(keep, came)
    (input_across,) = gate([backward_out[2]], relayed)
    (panels,) = call_kernel(
        make_panels,
        (shape((N_DP, entries, width), low),),
        ["vmem"] * 2,
        micros=0.7,
    )(whole, grad_hidden)
    panels_came = swapped(panels[4:], 1)
    tap_block = shape((TAP_PAD // 2, width), f32)
    tap_keep, tap_send = call_kernel(
        make_taps,
        (tap_block,) * 2,
        ["vmem"] * 2 + ["any"],
        scratch=[pltpu.VMEM((chunks, TAP_PAD, 8, LANES), f32)],
    )(masked, cotangents, relayed)
    taps_came = swapped(tap_send, 1)
    far, input_across = crossed(relayed, 2), crossed(input_across, 2)
    (weights,) = call_kernel(
        weigh,
        (shape((half // HEAD_DIM, rows, rows), low),),
        ["smem"] + ["vmem"] * N_CTX + ["any"],
    )(lengths, *packed, relayed)
    back_blocks = call_kernel(
        attend_back,
        (head_block,) * N_CTX,
        ["vmem"] * (4 + N_CTX) + ["any"],
        micros=2.2,
    )(weights, keep, came, far, *packed, tap_keep)
    (across_block,) = gate([back_blocks[2]], input_across)
    grad_blocks = traded([*back_blocks[:2], across_block, back_blocks[3]])
    own_pair = backward_out[0]
    (beside_pair,) = call_kernel(
        make_pair,
        (shape((4, utts * frames, width), low),),
        ["vmem"] * 3 + ["any"],
        micros=0.2,
    )(backward_out[1], output_across, input_across, grad_blocks[1])
    beside_pair = crossed(beside_pair, 1)

    kept, sent = call_kernel(
        join,
        (shape((2, entries + TAP_PAD // 2, width), low),) * 2,
        ["vmem"] * 4 + ["any"],
    )(panels[:4], panels_came, tap_keep, taps_came, back_blocks[0])
    panels = (kept.astype(f32) + swapped(sent, 2).astype(f32)).astype(low)
    taps_last = swapped(panels[1, entries:], 4)
    panels_last = swapped(panels[1, :entries], 4)
    (arrived,) = call_kernel(mark, (shape((8, LANES), f32),), ["any"] * 3)(
        *grad_blocks[2:], taps_last
    )
    (tap_sums,) = call_kernel(
        finish, (shape((TAP_PAD // 2, width), f32),), ["vmem"] * 2 + ["any"]
    )(panels, taps_last, arrived)
    grad_out_weight = (panels[0, :entries].astype(f32) + panels_last.astype(f32)).T
    tap_blocks = traded([tap_sums] * N_CTX)
    grad_queries, grad_keys, grad_values, block_output, grad_input, grad_taps = call_kernel(
        unpack,
        (shape((utts, frames, inner), low),) * 3
        + (shape((utts, frames, wide), low),) * 2
        + (shape(conv_weight.shape, f32),),
        ["any"] * (N_CTX + 4) + ["vmem"] * N_CTX,
        ["hbm"] * 6,
        [
            pltpu.VMEM((N_CTX, TAP_PAD // 2, width), f32),
            pltpu.VMEM(conv_weight.shape, f32),
            dma((7 * N_CTX + 1,)),
        ],
        micros=1.0,
    )(
        *grad_blocks,
        own_pair,
        beside_pair,
        output_across,
        input_across,
        *tap_blocks,
    )
    return (
        block_output,
        grad_input,
        grad_queries,
        grad_keys,
        grad_values,
        grad_out_weight,
        grad_taps,
    )


def chosen(sizes, *arrays):
    frame_input, queries, out_weight, conv_weight = (arrays[i] for i in (0, 1, 4, 5))
    utts, frames, wide = frame_input.shape
    inner = queries.shape[2]
    fits = (
        sizes == (N_DP, N_CTX)
        and utts == 2
        and frames == 64
        and wide % (N_CTX * LANES) == 0
        and inner % (2 * LANES) == 0
        and inner // N_DP % 16 == 0
        and inner // 2 == wide // N_CTX
        and conv_weight.shape == (TAPS, wide // N_DP)
        and out_weight.shape == (wide // N_CTX, inner // N_DP)
    )
    return (per_device if fits else general_device)(*arrays)


def solution(mesh):
    placed = (
        P("dp", "ctx", None),
        P("dp", "ctx", None),
        P("dp", "ctx", None),
        P("dp", "ctx", None),
        P("ctx", "dp"),
        P(None, "dp"),
        P("dp"),
        P("dp", "ctx", None),
    )
    sizes = (mesh.shape["dp"], mesh.shape["ctx"])
    return jax.shard_map(
        functools.partial(chosen, sizes),
        mesh=mesh,
        in_specs=placed,
        out_specs=(
            P("dp", "ctx", None),
            P("dp", "ctx", None),
            P("dp", "ctx", None),
            P("dp", "ctx", None),
            P("dp", "ctx", None),
            P("ctx", "dp"),
            P(None, "dp"),
        ),
        check_vma=False,
    )
```
